32 devices in a mesh: dp: 8 (over z, y), mp: 4 (over x, core).
Axes of the slice: x: 2, y: 2, z: 4, core: 2. Of those that a mesh axis runs over, the one named last changes fastest.
Arguments:
- tokens: bfloat16 [4, 8, 1024, 1024], P(None, 'dp', 'mp'), may hold values from -6 to 6
- cotangent: bfloat16 [4, 8, 1024, 1024], P(None, 'dp', 'mp'), may hold values from -6 to 6
- qkv_weight: float32 [3, 1024, 1024], P(None, 'dp', 'mp'), may hold values from -0.1875 to 0.1875
- qkv_first: float32 [3, 1024, 1024], P(None, 'dp', 'mp'), may hold values from -32 to 32
- qkv_second: float32 [3, 1024, 1024], P(None, 'dp', 'mp'), may hold values from 2.94912 to 11.79648
- out_weight: float32 [1024, 1024], P('mp', 'dp'), may hold values from -0.75 to 0.75
- out_first: float32 [1024, 1024], P('mp', 'dp'), may hold values from -32 to 32
- out_second: float32 [1024, 1024], P('mp', 'dp'), may hold values from 2.94912 to 11.79648
- up_weight: float32 [1024, 4, 1024], P('dp', None, 'mp'), may hold values from -0.1875 to 0.1875
- up_first: float32 [1024, 4, 1024], P('dp', None, 'mp'), may hold values from -32 to 32
- up_second: float32 [1024, 4, 1024], P('dp', None, 'mp'), may hold values from 2.94912 to 11.79648
- down_weight: float32 [4, 1024, 1024], P(None, 'mp', 'dp'), may hold values from -0.09375 to 0.09375
- down_first: float32 [4, 1024, 1024], P(None, 'mp', 'dp'), may hold values from -64 to 64
- down_second: float32 [4, 1024, 1024], P(None, 'mp', 'dp'), may hold values from 11.79648 to 47.18592
- head_biases: float32 [6, 1024], P(None, ('mp', 'dp')), may hold values from -3 to 3
- bias_first: float32 [6, 1024], P(None, ('mp', 'dp')), may hold values from -32 to 32
- bias_second: float32 [6, 1024], P(None, ('mp', 'dp')), may hold values from 2.94912 to 11.79648
- vectors: float32 [8, 1024], P(None, 'dp'), may hold values from 0.25 to 1.75
- vector_first: float32 [8, 1024], P(None, 'dp'), may hold values from -128 to 128
- vector_second: float32 [8, 1024], P(None, 'dp'), may hold values from 32.768 to 131.072
Outputs:
- layer_output: bfloat16 [4, 8, 1024, 1024], P(None, 'dp', 'mp')
- input_grad: float32 [4, 8, 1024, 1024], P(None, 'dp', 'mp')
- qkv_weight_new: float32 [3, 1024, 1024], P(None, 'dp', 'mp')
- qkv_first_new: float32 [3, 1024, 1024], P(None, 'dp', 'mp')
- qkv_second_new: float32 [3, 1024, 1024], P(None, 'dp', 'mp')
- out_weight_new: float32 [1024, 1024], P('mp', 'dp')
- out_first_new: float32 [1024, 1024], P('mp', 'dp')
- out_second_new: float32 [1024, 1024], P('mp', 'dp')
- up_weight_new: float32 [1024, 4, 1024], P('dp', None, 'mp')
- up_first_new: float32 [1024, 4, 1024], P('dp', None, 'mp')
- up_second_new: float32 [1024, 4, 1024], P('dp', None, 'mp')
- down_weight_new: float32 [4, 1024, 1024], P(None, 'mp', 'dp')
- down_first_new: float32 [4, 1024, 1024], P(None, 'mp', 'dp')
- down_second_new: float32 [4, 1024, 1024], P(None, 'mp', 'dp')
- head_biases_new: float32 [6, 1024], P(None, ('mp', 'dp'))
- bias_first_new: float32 [6, 1024], P(None, ('mp', 'dp'))
- bias_second_new: float32 [6, 1024], P(None, ('mp', 'dp'))
- vectors_new: float32 [8, 1024], P(None, 'dp')
- vector_first_new: float32 [8, 1024], P(None, 'dp')
- vector_second_new: float32 [8, 1024], P(None, 'dp')
The draws below stay inside these ranges and needn't reach their ends.
All inputs are finite; a program needn't handle non-finite values.
Results may differ from the reference program's by a relative error of at most 0.012.
The reference program's roundings to bfloat16 on the way count: a program that leaves them out, or rounds other values in their place, can miss the bound.
Values may be sent and summed in bfloat16 or wider, within the bound.
No kernel may reach another device: no remote copies, remote signals or barrier semaphores. Data moves between devices by JAX's collectives and lax.ppermute only.
A program may use at most 256 MiB of HBM per device.

```python
import math
import jax
import jax.numpy as jnp
from jax import lax

D = 1024
HEADS = 16
DH = 64
FF = 4096
SEQ = 1024
MICRO = 4
STEP = 10
FFR = 4
IMAGES = 8
TOTAL = 32768


def levels(own_key, extent, shards, smallest, top_value):
    level = 1.0
    for axis_at, shards_of in shards:
        draws = jax.random.uniform(jax.random.fold_in(jax.random.fold_in(own_key, 6), axis_at), (shards_of,), jnp.float32, smallest / len(shards), top_value / len(shards))
        level = level * jnp.repeat(jnp.exp(draws), extent[axis_at] // shards_of).reshape((-1,) + (1,) * (len(extent) - 1 - axis_at))
    return level


def noise(key, dims, scale, bound, shards=(), kind=jnp.bfloat16):
    result = jax.random.normal(key, dims, jnp.float32) * scale
    if len(shards) > 0:
        result = levels(key, dims, shards, -0.22, 0.18) * result
    return jnp.clip(result, min=-bound, max=bound).astype(kind)


def setup_inputs(seed: int = 0) -> dict:
    key_list = jax.random.split(jax.random.key(seed), 21)
    tokens = noise(key_list[0], (MICRO, IMAGES, SEQ, D), 1.0, 6.0, ((1, 8), (2, 4)))
    cotangent = noise(key_list[1], (MICRO, IMAGES, SEQ, D), 1.0, 6.0, ((1, 8), (2, 4)))
    qkv_weight = noise(key_list[2], (3, D, D), D ** -0.5, 0.1875, ((1, 8), (2, 4)), jnp.float32)
    qkv_first = noise(key_list[3], (3, D, D), (0.033 * TOTAL ** 0.5), 32.0, ((1, 8), (2, 4)), jnp.float32)
    qkv_second = jnp.clip(jnp.exp(math.log(11.79648) - 1.3862944 * jax.random.uniform(key_list[4], (3, D, D), jnp.float32) ** levels(key_list[4], (3, D, D), ((1, 8), (2, 4)), -0.2, 0.2)), 2.94912, 11.79648)
    out_weight = noise(key_list[5], (D, D), DH ** -0.5, 0.75, ((0, 4), (1, 8)), jnp.float32)
    out_first = noise(key_list[6], (D, D), (0.033 * TOTAL ** 0.5), 32.0, ((0, 4), (1, 8)), jnp.float32)
    out_second = jnp.clip(jnp.exp(math.log(11.79648) - 1.3862944 * jax.random.uniform(key_list[7], (D, D), jnp.float32) ** levels(key_list[7], (D, D), ((0, 4), (1, 8)), -0.2, 0.2)), 2.94912, 11.79648)
    up_weight = noise(key_list[8], (D, FFR, D), D ** -0.5, 0.1875, ((0, 8), (2, 4)), jnp.float32)
    up_first = noise(key_list[9], (D, FFR, D), (0.033 * TOTAL ** 0.5), 32.0, ((0, 8), (2, 4)), jnp.float32)
    up_second = jnp.clip(jnp.exp(math.log(11.79648) - 1.3862944 * jax.random.uniform(key_list[10], (D, FFR, D), jnp.float32) ** levels(key_list[10], (D, FFR, D), ((0, 8), (2, 4)), -0.2, 0.2)), 2.94912, 11.79648)
    down_weight = noise(key_list[11], (FFR, D, D), FF ** -0.5, 0.09375, ((1, 4), (2, 8)), jnp.float32)
    down_first = noise(key_list[12], (FFR, D, D), (0.067 * TOTAL ** 0.5), 64.0, ((1, 4), (2, 8)), jnp.float32)
    down_second = jnp.clip(jnp.exp(math.log(47.18592) - 1.3862944 * jax.random.uniform(key_list[13], (FFR, D, D), jnp.float32) ** levels(key_list[13], (FFR, D, D), ((1, 4), (2, 8)), -0.2, 0.2)), 11.79648, 47.18592)
    head_biases = noise(key_list[14], (2 + FFR, D), 0.5, 3.0, ((1, 32),), jnp.float32)
    bias_first = noise(key_list[15], (2 + FFR, D), (0.033 * TOTAL ** 0.5), 32.0, ((1, 32),), jnp.float32)
    bias_second = jnp.clip(jnp.exp(math.log(11.79648) - 1.3862944 * jax.random.uniform(key_list[16], (2 + FFR, D), jnp.float32) ** levels(key_list[16], (2 + FFR, D), ((1, 32),), -0.2, 0.2)), 2.94912, 11.79648)
    vectors = jnp.clip(1.0 + 0.15 * jax.random.normal(key_list[17], (8, D), jnp.float32), 0.25, 1.75)
    vector_first = noise(key_list[18], (8, D), (0.111 * TOTAL ** 0.5), 128.0, ((1, 8),), jnp.float32)
    vector_second = jnp.clip(jnp.exp(math.log(131.072) - 1.3862944 * jax.random.uniform(key_list[19], (8, D), jnp.float32) ** levels(key_list[19], (8, D), ((1, 8),), -0.2, 0.2)), 32.768, 131.072)
    return {"tokens": tokens, "cotangent": cotangent, "qkv_weight": qkv_weight, "qkv_first": qkv_first, "qkv_second": qkv_second, "out_weight": out_weight, "out_first": out_first, "out_second": out_second, "up_weight": up_weight, "up_first": up_first, "up_second": up_second, "down_weight": down_weight, "down_first": down_first, "down_second": down_second, "head_biases": head_biases, "bias_first": bias_first, "bias_second": bias_second, "vectors": vectors, "vector_first": vector_first, "vector_second": vector_second}


@jax.custom_vjp
def low(v):
    return lax.optimization_barrier(v.astype(jnp.bfloat16)).astype(jnp.float32)

@jax.custom_vjp
def low_back(v):
    return v

def low_keep(v):
    return (low(v), None)

def low_pass(kept, grad):
    return (grad,)

def back_keep(v):
    return (v, None)

def back_low(kept, grad):
    return (low(grad),)
low.defvjp(low_keep, low_pass)
low_back.defvjp(back_keep, back_low)
HIGHEST = lax.Precision.HIGHEST
RATES = (0.05, 0.2, 0.05, 0.03, 0.5, 0.5)

def layer_norm(values, gain, shift):
    center = values - lax.optimization_barrier(jnp.mean(values, -1, keepdims=True))
    spread = lax.optimization_barrier(jnp.mean(center * center, -1, keepdims=True))
    return center * lax.rsqrt(spread + 1e-06) * gain + shift

def block_forward(params, inputs):
    qkv_w, out_w, up_w, down_w, bias_rows, vector_rows = [low(each) for each in params]
    images = inputs.shape[0]
    head_shape = (images, SEQ, HEADS, DH)
    normed = low(layer_norm(inputs, vector_rows[0], vector_rows[1]))
    project = jnp.einsum('isd,tde->tise', normed, qkv_w, precision=HIGHEST)
    queries = low_back(low(project[0] + bias_rows[0])).reshape(head_shape)
    key_rows = low_back(low(project[1])).reshape(head_shape)
    values = low_back(low(project[2] + bias_rows[1])).reshape(head_shape)
    scores = low_back(jnp.einsum('ishe,ithe->ihst', queries, key_rows, precision=HIGHEST) * DH ** (-0.5))
    shifted = jnp.exp(scores - lax.optimization_barrier(jnp.max(scores, -1, keepdims=True)))
    softmax_rows = shifted / lax.optimization_barrier(jnp.sum(shifted, -1, keepdims=True))
    blended = jnp.einsum('ihst,ithe->ishe', low(softmax_rows), values, precision=HIGHEST).reshape(images, SEQ, D)
    blended = low_back(low(blended))
    projected = low_back(jnp.einsum('ise,ed->isd', blended, out_w, precision=HIGHEST))
    hidden = inputs + vector_rows[3] * (projected + vector_rows[2])
    normed_two = low(layer_norm(hidden, vector_rows[4], vector_rows[5]))
    pre_act = jnp.einsum('isd,df->isf', normed_two, up_w.reshape(D, FF), precision=HIGHEST)
    pre_act = low_back(pre_act + bias_rows[2:].reshape(FF))
    activ = low(jax.nn.gelu(pre_act, approximate=False))
    branch = low_back(jnp.einsum('isf,fd->isd', activ, down_w.reshape(FF, D), precision=HIGHEST))
    return hidden + vector_rows[7] * (branch + vector_rows[6])

def adam_update(weight, first, second, grad, rate):
    first_new = 0.9 * first + 0.1 * grad
    second_new = 0.999 * second + 0.001 * grad * grad
    corrected = first_new / (1.0 - 0.9 ** STEP)
    scaled = jnp.sqrt(second_new / (1.0 - 0.999 ** STEP))
    weight_new = weight - rate * (corrected / (scaled + 1e-08) + 0.05 * weight)
    return (weight_new, first_new, second_new)

def reference(tokens, cotangent, qkv_weight, qkv_first, qkv_second, out_weight, out_first, out_second, up_weight, up_first, up_second, down_weight, down_first, down_second, head_biases, bias_first, bias_second, vectors, vector_first, vector_second):
    all_images = MICRO * IMAGES
    group_size = min(max(1, 2048 // SEQ), all_images)
    while all_images % group_size:
        group_size = group_size - 1
    inputs = tokens.astype(jnp.float32).reshape(all_images // group_size, group_size, SEQ, D)
    backs = cotangent.astype(jnp.float32).reshape(all_images // group_size, group_size, SEQ, D)
    params = (qkv_weight, out_weight, up_weight, down_weight, head_biases, vectors)

    def one_group(carry, pair):
        outputs, pullback = jax.vjp(block_forward, params, pair[0])
        grads, grad_input = pullback(pair[1])
        carry = tuple((old_sum + new_part for old_sum, new_part in zip(carry, grads)))
        return (carry, (outputs.astype(jnp.bfloat16), grad_input))
    zeros_start = tuple((jnp.zeros(each.shape, jnp.float32) for each in params))
    grads, (outputs, grad_inputs) = lax.scan(one_group, zeros_start, (inputs, backs))
    layer_output = outputs.reshape(MICRO, IMAGES, SEQ, D)
    input_grad = grad_inputs.reshape(MICRO, IMAGES, SEQ, D)
    firsts = (qkv_first, out_first, up_first, down_first, bias_first, vector_first)
    seconds = (qkv_second, out_second, up_second, down_second, bias_second, vector_second)
    updated = [adam_update(params[slot], firsts[slot], seconds[slot], grads[slot], RATES[slot]) for slot in range(6)]
    return (layer_output, input_grad, updated[0][0], updated[0][1], updated[0][2], updated[1][0], updated[1][1], updated[1][2], updated[2][0], updated[2][1], updated[2][2], updated[3][0], updated[3][1], updated[3][2], updated[4][0], updated[4][1], updated[4][2], updated[5][0], updated[5][1], updated[5][2])
```

```python
import functools

import jax
import jax.numpy as jnp
from jax import lax
from jax.experimental import pallas as pl
from jax.experimental.pallas import tpu as pltpu
from jax.sharding import PartitionSpec as P

DH = 64
MICRO = 4
STEP = 10


RATES = (0.05, 0.2, 0.05, 0.03, 0.5, 0.5)


def layer_norm(values, gain, shift):
    center = values - jnp.mean(values, -1, keepdims=True)
    spread = jnp.mean(center * center, -1, keepdims=True)
    return center * lax.rsqrt(spread + 1e-06) * gain + shift


def exact_gelu(values):
    return jax.nn.gelu(values, approximate=False)


def adam_update(weight, first, second, grad, rate):
    first_new = 0.9 * first + 0.1 * grad
    second_new = 0.999 * second + 0.001 * grad * grad
    corrected = first_new / (1.0 - 0.9**STEP)
    scaled = jnp.sqrt(second_new / (1.0 - 0.999**STEP))
    weight_new = weight - rate * (corrected / (scaled + 1e-08) + 0.05 * weight)
    return (weight_new, first_new, second_new)


def attend_forward(queries, key_rows, values, block_rows):
    images, seq_rows, head_count, head_width = queries.shape
    block_count = seq_rows // block_rows
    factor = head_width ** (-0.5)
    query_blocks = jnp.moveaxis(
        queries.reshape(images, block_count, block_rows, head_count, head_width), 1, 0
    )

    def one_block(query_part):
        scores = (
            jnp.einsum("iqhe,ikhe->ihqk", query_part, key_rows, preferred_element_type=jnp.float32)
            * factor
        )
        row_peak = jnp.max(scores, -1, keepdims=True)
        shifted = jnp.exp(scores - row_peak)
        row_total = jnp.sum(shifted, -1, keepdims=True)
        softmax_rows = (shifted / row_total).astype(jnp.bfloat16)
        blended = jnp.einsum(
            "ihqk,ikhe->iqhe", softmax_rows, values, preferred_element_type=jnp.float32
        )
        return (blended, row_peak[..., 0] + jnp.log(row_total[..., 0]))

    blended, log_total = lax.map(one_block, query_blocks)
    blended = jnp.moveaxis(blended, 0, 1).reshape(images, seq_rows, head_count * head_width)
    return (blended.astype(jnp.bfloat16), log_total)


def attend_backward(queries, key_rows, values, grad_blended, log_total, block_rows):
    images, seq_rows, head_count, head_width = queries.shape
    block_count = seq_rows // block_rows
    factor = head_width ** (-0.5)
    split_shape = (images, block_count, block_rows, head_count, head_width)
    query_blocks = jnp.moveaxis(queries.reshape(split_shape), 1, 0)
    grad_blocks = jnp.moveaxis(grad_blended.reshape(split_shape), 1, 0)

    def one_block(carry, inputs_part):
        query_part, grad_part, total_part = inputs_part
        grad_keys, grad_values = carry
        scores = (
            jnp.einsum("iqhe,ikhe->ihqk", query_part, key_rows, preferred_element_type=jnp.float32)
            * factor
        )
        softmax_rows = jnp.exp(scores - total_part[..., None])
        grad_values = grad_values + jnp.einsum(
            "ihqk,iqhe->ikhe",
            softmax_rows.astype(jnp.bfloat16),
            grad_part,
            preferred_element_type=jnp.float32,
        )
        grad_rows = jnp.einsum(
            "iqhe,ikhe->ihqk", grad_part, values, preferred_element_type=jnp.float32
        )
        grad_scores = softmax_rows * (
            grad_rows - jnp.sum(grad_rows * softmax_rows, -1, keepdims=True)
        )
        grad_scores = grad_scores.astype(jnp.bfloat16)
        grad_query = (
            jnp.einsum("ihqk,ikhe->iqhe", grad_scores, key_rows, preferred_element_type=jnp.float32)
            * factor
        )
        grad_keys = (
            grad_keys
            + jnp.einsum(
                "ihqk,iqhe->ikhe", grad_scores, query_part, preferred_element_type=jnp.float32
            )
            * factor
        )
        return ((grad_keys, grad_values), grad_query)

    zero_grad = jnp.zeros(queries.shape, jnp.float32)
    (grad_keys, grad_values), grad_query = lax.scan(
        one_block, (zero_grad, zero_grad), (query_blocks, grad_blocks, log_total)
    )
    flat_shape = (images, seq_rows, head_count * head_width)
    grad_query = jnp.moveaxis(grad_query, 0, 1).reshape(flat_shape)
    stacked = jnp.stack(
        [grad_query, grad_keys.reshape(flat_shape), grad_values.reshape(flat_shape)]
    )
    return stacked.astype(jnp.bfloat16)


def rows_forward(part):
    return lax.all_gather(part, "mp", axis=1, tiled=True)


def rows_sum_forward(part):
    return lax.psum_scatter(part, "mp", scatter_dimension=1, tiled=True)


def rows_backward(part):
    return lax.all_gather(part, "mp", axis=1, tiled=True)


def rows_sum_backward(part):
    return lax.psum_scatter(part, "mp", scatter_dimension=1, tiled=True)


def forward(inputs, params):
    qkv_full, out_full, up_full, down_full, bias_full, vector_full = params
    base = inputs.astype(jnp.float32)
    normed = layer_norm(base, vector_full[0], vector_full[1]).astype(jnp.bfloat16)
    normed_all = rows_forward(normed)
    images, seq_rows = (normed_all.shape[0], normed_all.shape[1])
    head_shape = (images, seq_rows, -1, DH)
    project = jnp.einsum("isd,tde->tise", normed_all, qkv_full, preferred_element_type=jnp.float32)
    queries = (project[0] + bias_full[0]).astype(jnp.bfloat16).reshape(head_shape)
    key_rows = project[1].astype(jnp.bfloat16).reshape(head_shape)
    values = (project[2] + bias_full[1]).astype(jnp.bfloat16).reshape(head_shape)
    blended, log_total = attend_forward(queries, key_rows, values, min(512, seq_rows))
    projected = rows_sum_forward(
        jnp.einsum("ise,ed->isd", blended, out_full, preferred_element_type=jnp.float32)
    )
    branch_one = projected + vector_full[2]
    hidden = base + vector_full[3] * branch_one
    normed_two = layer_norm(hidden, vector_full[4], vector_full[5]).astype(jnp.bfloat16)
    normed_two_all = rows_forward(normed_two)
    pre_act = jnp.einsum(
        "isd,df->isf", normed_two_all, up_full, preferred_element_type=jnp.float32
    ) + bias_full[2:].reshape(-1)
    activ = exact_gelu(pre_act).astype(jnp.bfloat16)
    branch_two = (
        rows_sum_forward(
            jnp.einsum("isf,fd->isd", activ, down_full, preferred_element_type=jnp.float32)
        )
        + vector_full[6]
    )
    output = hidden + vector_full[7] * branch_two
    saved = (
        base,
        hidden,
        branch_one,
        branch_two,
        normed_all,
        queries,
        key_rows,
        values,
        log_total,
        blended,
        normed_two_all,
        pre_act,
        activ,
    )
    return (output.astype(jnp.bfloat16), saved)


def backward(grad_output, saved, params):
    qkv_full, out_full, up_full, down_full, bias_full, vector_full = params
    (
        base,
        hidden,
        branch_one,
        branch_two,
        normed_all,
        queries,
        key_rows,
        values,
        log_total,
        blended,
        normed_two_all,
        pre_act,
        activ,
    ) = saved
    local_width = qkv_full.shape[2]
    grad_out = grad_output.astype(jnp.float32)
    grad_scale_two = jnp.sum(grad_out * branch_two, axis=(0, 1))
    grad_bias_two = jnp.sum(grad_out, axis=(0, 1)) * vector_full[7]
    grad_branch = rows_backward((grad_out * vector_full[7]).astype(jnp.bfloat16))
    grad_down = jnp.einsum("isf,isd->fd", activ, grad_branch, preferred_element_type=jnp.float32)
    grad_activ = jnp.einsum(
        "isd,fd->isf", grad_branch, down_full, preferred_element_type=jnp.float32
    )
    grad_pre = jax.vjp(exact_gelu, pre_act)[1](grad_activ)[0].astype(jnp.bfloat16)
    grad_up_bias = jnp.sum(grad_pre, axis=(0, 1), dtype=jnp.float32)
    grad_up = jnp.einsum(
        "isd,isf->df", normed_two_all, grad_pre, preferred_element_type=jnp.float32
    )
    grad_normed_two = rows_sum_backward(
        jnp.einsum("isf,df->isd", grad_pre, up_full, preferred_element_type=jnp.float32)
    )
    norm_back_two = jax.vjp(layer_norm, hidden, vector_full[4], vector_full[5])[1]
    grad_hidden, grad_gain_two, grad_shift_two = norm_back_two(grad_normed_two)
    grad_hidden = grad_out + grad_hidden
    grad_scale_one = jnp.sum(grad_hidden * branch_one, axis=(0, 1))
    grad_out_bias = jnp.sum(grad_hidden, axis=(0, 1)) * vector_full[3]
    grad_projected = rows_backward((grad_hidden * vector_full[3]).astype(jnp.bfloat16))
    grad_out_weight = jnp.einsum(
        "ise,isd->ed", blended, grad_projected, preferred_element_type=jnp.float32
    )
    grad_blended = jnp.einsum(
        "isd,ed->ise", grad_projected, out_full, preferred_element_type=jnp.float32
    ).astype(jnp.bfloat16)
    grad_project = attend_backward(
        queries, key_rows, values, grad_blended, log_total, min(512, queries.shape[1])
    )
    grad_query_bias = jnp.sum(grad_project[0], axis=(0, 1), dtype=jnp.float32)
    grad_value_bias = jnp.sum(grad_project[2], axis=(0, 1), dtype=jnp.float32)
    grad_qkv = jnp.einsum(
        "isd,tise->tde", normed_all, grad_project, preferred_element_type=jnp.float32
    )
    grad_normed = rows_sum_backward(
        jnp.einsum("tise,tde->isd", grad_project, qkv_full, preferred_element_type=jnp.float32)
    )
    norm_back_one = jax.vjp(layer_norm, base, vector_full[0], vector_full[1])[1]
    grad_input_part, grad_gain_one, grad_shift_one = norm_back_one(grad_normed)
    grad_input = grad_hidden + grad_input_part
    grad_vectors = jnp.stack(
        [
            grad_gain_one,
            grad_shift_one,
            grad_out_bias,
            grad_scale_one,
            grad_gain_two,
            grad_shift_two,
            grad_bias_two,
            grad_scale_two,
        ]
    )
    grad_biases = jnp.concatenate(
        [jnp.stack([grad_query_bias, grad_value_bias]), grad_up_bias.reshape(-1, local_width)], 0
    )
    return (grad_input, (grad_qkv, grad_out_weight, grad_up, grad_down, grad_biases, grad_vectors))


def local_general(
    tokens,
    cotangent,
    qkv_weight,
    qkv_first,
    qkv_second,
    out_weight,
    out_first,
    out_second,
    up_weight,
    up_first,
    up_second,
    down_weight,
    down_first,
    down_second,
    head_biases,
    bias_first,
    bias_second,
    vectors,
    vector_first,
    vector_second,
):

    def gather_params():
        gathered = (
            lax.all_gather(qkv_weight.astype(jnp.bfloat16), "dp", axis=1, tiled=True),
            lax.all_gather(out_weight.astype(jnp.bfloat16), "dp", axis=1, tiled=True),
            lax.all_gather(up_weight.astype(jnp.bfloat16), "dp", axis=0, tiled=True),
            lax.all_gather(down_weight.astype(jnp.bfloat16), "dp", axis=2, tiled=True),
            lax.all_gather(head_biases.astype(jnp.bfloat16), "dp", axis=1, tiled=True),
            lax.all_gather(vectors.astype(jnp.bfloat16), "dp", axis=1, tiled=True),
        )
        qkv_full, out_full, up_full, down_full, bias_full, vector_full = gathered
        return (
            qkv_full,
            out_full,
            up_full.reshape(up_full.shape[0], -1),
            down_full.reshape(-1, down_full.shape[2]),
            bias_full.astype(jnp.float32),
            vector_full.astype(jnp.float32),
        )

    grad_sums = None
    outputs = []
    input_grads = []
    for micro_step in range(MICRO):
        params_fwd = gather_params()
        output, saved = forward(tokens[micro_step], params_fwd)
        outputs.append(output)
        params_back = gather_params()
        grad_input, grads = backward(cotangent[micro_step], saved, params_back)
        input_grads.append(grad_input)
        if grad_sums is None:
            grad_sums = grads
        else:
            grad_sums = tuple((old_sum + new_part for old_sum, new_part in zip(grad_sums, grads)))
    grad_qkv, grad_out_weight, grad_up, grad_down, grad_biases, grad_vectors = grad_sums
    grad_up = grad_up.reshape(-1, up_weight.shape[1], up_weight.shape[2])
    grad_down = grad_down.reshape(down_weight.shape[0], down_weight.shape[1], -1)
    reduced = (
        lax.psum_scatter(grad_qkv, "dp", scatter_dimension=1, tiled=True),
        lax.psum_scatter(grad_out_weight, "dp", scatter_dimension=1, tiled=True),
        lax.psum_scatter(grad_up, "dp", scatter_dimension=0, tiled=True),
        lax.psum_scatter(grad_down, "dp", scatter_dimension=2, tiled=True),
        lax.psum_scatter(grad_biases, "dp", scatter_dimension=1, tiled=True),
        lax.psum_scatter(grad_vectors, "dp", scatter_dimension=1, tiled=True),
    )
    vector_grad = lax.psum(reduced[5], "mp")
    grads = (reduced[0], reduced[1], reduced[2], reduced[3], reduced[4], vector_grad)
    params = (qkv_weight, out_weight, up_weight, down_weight, head_biases, vectors)
    firsts = (qkv_first, out_first, up_first, down_first, bias_first, vector_first)
    seconds = (qkv_second, out_second, up_second, down_second, bias_second, vector_second)
    updated = [
        adam_update(params[slot], firsts[slot], seconds[slot], grads[slot], RATES[slot])
        for slot in range(6)
    ]
    return (
        jnp.stack(outputs),
        jnp.stack(input_grads),
        updated[0][0],
        updated[0][1],
        updated[0][2],
        updated[1][0],
        updated[1][1],
        updated[1][2],
        updated[2][0],
        updated[2][1],
        updated[2][2],
        updated[3][0],
        updated[3][1],
        updated[3][2],
        updated[4][0],
        updated[4][1],
        updated[4][2],
        updated[5][0],
        updated[5][1],
        updated[5][2],
    )


ZS, YS, MP = (4, 2, 4)
DP = ZS * YS
LANES = 128
BF = jnp.bfloat16
F32 = jnp.float32


def swap_z(part, step):
    return lax.ppermute(
        part, "dp", [(z * YS + y, (z ^ step) * YS + y) for z in range(ZS) for y in range(YS)]
    )


def swap_y(part):
    return lax.ppermute(part, "dp", [(each, each ^ 1) for each in range(DP)])


def swap_mp(part, step):
    return lax.ppermute(part, "mp", [(each, each ^ step) for each in range(MP)])


def gather_rows_z(shard):
    return jnp.concatenate([shard] + [swap_z(shard, step) for step in range(1, ZS)], 0)


def gather_weight(shard, y_first):
    rows = gather_rows_z(shard)
    if y_first:
        rows = jnp.concatenate([rows, swap_y(rows)], 0)
        rows = jnp.concatenate([rows, swap_mp(rows, 2)], 1)
    else:
        rows = jnp.concatenate([rows, swap_mp(rows, 2)], 1)
        rows = jnp.concatenate([rows, swap_y(rows)], 0)
    return (rows, swap_mp(rows, 1))


def add_low(first, second):
    return (first.astype(F32) + second.astype(F32)).astype(BF)


def reduce_x(total):
    width = total.shape[1] // 2
    return add_low(total[:, :width], swap_mp(total[:, width:], 2))


def reduce_y(total):
    rows = total.shape[0] // 2
    return add_low(total[:rows], swap_y(total[rows:]))


def reduce_weight(own_part, other_part, x_first):
    total = add_low(own_part, swap_mp(other_part, 1))
    if x_first:
        total = reduce_y(reduce_x(total))
    else:
        total = reduce_x(reduce_y(total))
    rows = total.shape[0] // ZS
    result = total[:rows].astype(F32)
    for step in range(1, ZS):
        result = result + swap_z(total[step * rows : (step + 1) * rows], step).astype(F32)
    return result


def assemble_kernel(place_ref, own_ref, *refs):
    chunk_rows = own_ref.shape[1]
    out_ref = refs[-1]
    out_ref[0:chunk_rows, :] = own_ref[0]
    for at, part_ref in enumerate(refs[:-1]):
        out_ref[(at + 1) * chunk_rows : (at + 2) * chunk_rows, :] = part_ref[...]


def assemble_image(place, arrays, parts):
    chunk_rows, width = parts[0].shape
    return pl.pallas_call(
        assemble_kernel,
        grid_spec=pltpu.PrefetchScalarGridSpec(
            num_scalar_prefetch=1,
            grid=(width // LANES,),
            in_specs=[
                pl.BlockSpec((1, chunk_rows, LANES), lambda j, place_ref: (place_ref[DP], 0, place_ref[j]))
            ]
            + [pl.BlockSpec((chunk_rows, LANES), lambda j, place_ref: (0, place_ref[j]))] * len(parts),
            out_specs=pl.BlockSpec((chunk_rows * MP, LANES), lambda j, place_ref: (0, j)),
        ),
        out_shape=jax.ShapeDtypeStruct((chunk_rows * MP, width), arrays.dtype),
        name="assemble_image",
    )(place, arrays, *parts)


def spread_kernel(place_ref, own_ref, *refs):
    out_ref = refs[-1]
    mine = place_ref[DP]
    out_ref[mine] = own_ref[...].astype(out_ref.dtype)
    for at, part_ref in enumerate(refs[:-1]):
        out_ref[mine ^ (at + 1)] = part_ref[...].astype(out_ref.dtype)


def spread_image(place, own, parts, dtype):
    chunk_rows, width = parts[0].shape
    block = pl.BlockSpec((chunk_rows, LANES), lambda j, place_ref: (0, j))
    return pl.pallas_call(
        spread_kernel,
        grid_spec=pltpu.PrefetchScalarGridSpec(
            num_scalar_prefetch=1,
            grid=(width // LANES,),
            in_specs=[block] * (1 + len(parts)),
            out_specs=pl.BlockSpec((MP, chunk_rows, LANES), lambda j, place_ref: (0, 0, place_ref[j])),
        ),
        out_shape=jax.ShapeDtypeStruct((MP, chunk_rows, width), dtype),
        name="spread_image",
    )(place, own, *parts)


def lane_dot(left, right):
    return lax.dot_general(left, right, (((1,), (1,)), ((), ())), preferred_element_type=F32)


def head_masks(width):
    lane = lax.broadcasted_iota(jnp.int32, (1, width), 1)
    return [lane // DH == head for head in range(width // DH)]


def attend_kernel(block_rows, q_ref, k_ref, v_ref, o_ref, lse_ref):
    masks = head_masks(LANES)
    key_rows = k_ref[...]
    values = v_ref[...]
    zero = jnp.zeros((), BF)
    for block in range(q_ref.shape[0] // block_rows):
        rows = slice(block * block_rows, (block + 1) * block_rows)
        queries = q_ref[rows, :] * jnp.asarray(DH**-0.5, BF)
        blended = []
        for head, mask in enumerate(masks):
            scores = lane_dot(jnp.where(mask, queries, zero), key_rows)
            peak = jnp.max(scores, 1, keepdims=True)
            shifted = jnp.exp(scores - peak)
            total = jnp.sum(shifted, 1, keepdims=True)
            part = jnp.dot(shifted.astype(BF), values, preferred_element_type=F32)
            blended.append(part * (1.0 / total))
            log_total = jnp.broadcast_to(peak + jnp.log(total), (block_rows, LANES))
            lse_ref[0, head : head + 1, rows] = jnp.transpose(log_total)[0:1, :]
        o_ref[rows, :] = jnp.where(masks[0], blended[0], blended[1]).astype(BF)


def attend_back_kernel(
    block_rows, q_ref, k_ref, v_ref, g_ref, lse_ref, dq_ref, dk_ref, dv_ref, dk_acc, dv_acc
):
    masks = head_masks(LANES)
    key_rows = k_ref[...]
    values = v_ref[...]
    zero = jnp.zeros((), BF)
    factor = DH**-0.5
    key_heads = [jnp.where(mask, key_rows, zero) for mask in masks]
    for block in range(q_ref.shape[0] // block_rows):
        rows = slice(block * block_rows, (block + 1) * block_rows)
        queries = q_ref[rows, :] * jnp.asarray(factor, BF)
        grads = g_ref[rows, :]
        grad_query = None
        grad_keys = None
        grad_values = None
        for head, mask in enumerate(masks):
            query_head = jnp.where(mask, queries, zero)
            grad_head = jnp.where(mask, grads, zero)
            scores = lane_dot(key_rows, query_head)
            weights = jnp.exp(scores - lse_ref[0, head : head + 1, rows])
            value_part = jnp.dot(weights.astype(BF), grad_head, preferred_element_type=F32)
            grad_rows = lane_dot(values, grad_head)
            delta = jnp.sum(grad_rows * weights, 0, keepdims=True)
            grad_scores = (weights * (grad_rows - delta)).astype(BF)
            key_part = jnp.dot(grad_scores, query_head, preferred_element_type=F32)
            query_part = lax.dot_general(
                grad_scores, key_heads[head], (((0,), (0,)), ((), ())), preferred_element_type=F32
            )
            grad_query = query_part if head == 0 else grad_query + query_part
            grad_keys = key_part if head == 0 else grad_keys + key_part
            grad_values = value_part if head == 0 else grad_values + value_part
        dq_ref[rows, :] = (grad_query * factor).astype(BF)
        if block == 0:
            dk_acc[...] = grad_keys
            dv_acc[...] = grad_values
        else:
            dk_acc[...] += grad_keys
            dv_acc[...] += grad_values
    dk_ref[...] = dk_acc[...].astype(BF)
    dv_ref[...] = dv_acc[...].astype(BF)


def pair_spec(rows, first):
    kinds, kind = first
    return pl.BlockSpec((rows, LANES), lambda p: (0, (p // 2) * (2 * kinds) + 2 * kind + p % 2))


def attend(query_keys, values):
    rows, width = values.shape
    pairs = width // LANES
    scores_size = rows * rows * 2 * pairs
    return pl.pallas_call(
        functools.partial(attend_kernel, 256),
        grid=(pairs,),
        in_specs=[pair_spec(rows, (2, 0)), pair_spec(rows, (2, 1)), pair_spec(rows, (1, 0))],
        out_specs=[pair_spec(rows, (1, 0)), pl.BlockSpec((1, 8, rows), lambda p: (p, 0, 0))],
        out_shape=[
            jax.ShapeDtypeStruct((rows, width), BF),
            jax.ShapeDtypeStruct((pairs, 8, rows), F32),
        ],
        compiler_params=pltpu.CompilerParams(vmem_limit_bytes=32 * 2**20),
        cost_estimate=pl.CostEstimate(
            flops=scores_size * 2 * 512, bytes_accessed=rows * width * 8, transcendentals=scores_size
        ),
        name="attend",
    )(query_keys, query_keys, values)


def attend_back(query_keys, values, grad_blended, log_total):
    rows, width = values.shape
    pairs = width // LANES
    scores_size = rows * rows * 2 * pairs
    single = pair_spec(rows, (1, 0))
    return pl.pallas_call(
        functools.partial(attend_back_kernel, 256),
        grid=(pairs,),
        in_specs=[
            pair_spec(rows, (2, 0)),
            pair_spec(rows, (2, 1)),
            single,
            single,
            pl.BlockSpec((1, 8, rows), lambda p: (p, 0, 0)),
        ],
        out_specs=[single] * 3,
        out_shape=[jax.ShapeDtypeStruct((rows, width), BF)] * 3,
        scratch_shapes=[pltpu.VMEM((rows, LANES), F32)] * 2,
        compiler_params=pltpu.CompilerParams(vmem_limit_bytes=32 * 2**20),
        cost_estimate=pl.CostEstimate(
            flops=scores_size * 2 * 1280, bytes_accessed=rows * width * 14, transcendentals=scores_size
        ),
        name="attend_back",
    )(query_keys, query_keys, values, grad_blended, log_total)


def dot_nn(left, right):
    return lax.dot_general(left, right, (((1,), (0,)), ((), ())), preferred_element_type=F32)


def dot_nt(left, right):
    return lax.dot_general(left, right, (((1,), (1,)), ((), ())), preferred_element_type=F32)


def dot_tn(left, right):
    return lax.dot_general(left, right, (((0,), (0,)), ((), ())), preferred_element_type=F32)


def norm_parts(values):
    center = values - jnp.mean(values, -1, keepdims=True)
    spread = lax.rsqrt(jnp.mean(center * center, -1, keepdims=True) + 1e-06)
    return (center * spread, spread)


def norm_back(grad, normal, spread, gain):
    scaled = grad * gain
    inner = scaled - jnp.mean(scaled, -1, keepdims=True)
    inner = inner - normal * jnp.mean(scaled * normal, -1, keepdims=True)
    return (spread * inner, jnp.sum(grad * normal, 0), jnp.sum(grad, 0))


def gelu_pair(values):
    share = 0.5 * (1.0 + lax.erf(values * 0.7071067811865476))
    slope = share + values * (0.3989422804014327 * jnp.exp(-0.5 * values * values))
    return ((values * share).astype(BF), slope.astype(BF))


def local_image(
    tokens,
    cotangent,
    qkv_weight,
    qkv_first,
    qkv_second,
    out_weight,
    out_first,
    out_second,
    up_weight,
    up_first,
    up_second,
    down_weight,
    down_first,
    down_second,
    head_biases,
    bias_first,
    bias_second,
    vectors,
    vector_first,
    vector_second,
):
    dp_at = lax.axis_index("dp")
    mp_at = lax.axis_index("mp")
    units = up_weight.shape[1]
    block_width = qkv_weight.shape[2]
    depth = qkv_weight.shape[1]
    bias_width = head_biases.shape[1]
    chunk_rows, width = tokens.shape[2:]
    order = [((zk * YS) + yk) for yk in range(YS) for zk in range(ZS)]
    places = [dp_at ^ each for each in order]
    place = jnp.stack(places + [mp_at]).astype(jnp.int32)

    def fetch_image(array):
        chunks = array[:, 0]
        parts = [
            swap_mp(lax.dynamic_index_in_dim(chunks, mp_at ^ step, 0, keepdims=False), step)
            for step in range(1, MP)
        ]
        return assemble_image(place, chunks, parts)

    small = jnp.concatenate(
        [vectors.astype(BF).reshape(-1), head_biases.astype(BF).reshape(-1)]
    ).reshape(1, -1)
    vector_size = vectors.size
    small = gather_rows_z(small)
    small = jnp.concatenate([small, swap_y(small)], 0)
    vector_full = (
        small[:, :vector_size].reshape(DP, vectors.shape[0], LANES).transpose(1, 0, 2)
    ).reshape(vectors.shape[0], width).astype(F32)
    bias_small = small[:, vector_size:]
    bias_small = jnp.stack([bias_small, swap_mp(bias_small, 2)], 0)
    bias_small = jnp.stack([bias_small, swap_mp(bias_small, 1)], 0)
    back_places = jnp.stack([((each ^ dp_at) & 1) * ZS + ((each ^ dp_at) >> 1) for each in range(DP)])
    bias_rows = jnp.take(bias_small, back_places, axis=2).reshape(2, 2, DP, -1, bias_width)
    bias_full = bias_rows.transpose(0, 3, 1, 2, 4).reshape(2, head_biases.shape[0], 2, block_width)
    bias_full = bias_full.astype(F32)

    inputs = fetch_image(tokens)
    qkv_low = qkv_weight.astype(BF)
    up_low = up_weight.astype(BF)
    half_units = units // 2
    down_low = down_weight.transpose(2, 0, 1).astype(BF)
    w_qk = gather_weight(jnp.concatenate([qkv_low[0], qkv_low[1]], 1), False)
    w_v = gather_weight(qkv_low[2], True)
    w_out = gather_weight(out_weight.T.astype(BF), True)
    w_up = [
        gather_weight(up_low[:, at : at + half_units].reshape(depth, -1), at == 0)
        for at in (0, half_units)
    ]
    w_down = [
        gather_weight(down_low[:, at : at + half_units].reshape(depth, -1), at == 0)
        for at in (0, half_units)
    ]
    cores = (0, 1)
    gain_one, shift_one, out_bias, scale_one, gain_two, shift_two, down_bias, scale_two = vector_full

    base = inputs.astype(F32)
    normal_one, spread_one = norm_parts(base)
    normed_one = (normal_one * gain_one + shift_one).astype(BF)
    query_keys, values, blended, log_total = ([], [], [], [])
    for core in cores:
        query_bias = jnp.stack([bias_full[core, 0], jnp.zeros_like(bias_full[core, 0])], 1).reshape(-1)
        query_keys.append((dot_nn(normed_one, w_qk[core]) + query_bias).astype(BF))
        values.append((dot_nn(normed_one, w_v[core]) + bias_full[core, 1].reshape(-1)).astype(BF))
    for core in cores:
        part, part_total = attend(query_keys[core], values[core])
        blended.append(part)
        log_total.append(part_total)
    branch_one = dot_nt(blended[0], w_out[0]) + dot_nt(blended[1], w_out[1]) + out_bias
    hidden = base + scale_one * branch_one
    normal_two, spread_two = norm_parts(hidden)
    normed_two = (normal_two * gain_two + shift_two).astype(BF)
    parts = [(half, core) for half in (0, 1) for core in cores]
    activ, slope = ({}, {})
    branch_two = down_bias
    for half, core in parts:
        rows = bias_full[core, 2 + half * half_units : 2 + (half + 1) * half_units]
        unit_bias = rows.transpose(1, 0, 2).reshape(-1)
        pre_act = dot_nn(normed_two, w_up[half][core]) + unit_bias
        activ[half, core], slope[half, core] = gelu_pair(pre_act)
        branch_two = branch_two + dot_nt(activ[half, core], w_down[half][core])
    output = (hidden + scale_two * branch_two).astype(BF)

    def send_back(array, dtype):
        low = array.astype(BF)
        back = [
            swap_mp(low[step * chunk_rows : (step + 1) * chunk_rows], step) for step in range(1, MP)
        ]
        return spread_image(place, array[:chunk_rows], back, dtype)[:, None]

    layer_output = send_back(output, BF)

    grad_out = fetch_image(cotangent).astype(F32)
    grad_scale_two = jnp.sum(grad_out * branch_two, 0)
    grad_down_bias = jnp.sum(grad_out, 0) * scale_two
    grad_branch = (grad_out * scale_two).astype(BF)
    sums = {}
    for half in (0, 1):
        own, other = [dot_tn(grad_branch, activ[half, core]).astype(BF) for core in cores]
        sums["down", half] = reduce_weight(own, other, half == 0)
    grad_pre = {}
    grad_normed_two = 0.0
    for half in (0, 1):
        for core in cores:
            grad_activ = dot_nn(grad_branch, w_down[half][core])
            grad_pre[half, core] = (grad_activ * slope[half, core].astype(F32)).astype(BF)
        own, other = [dot_tn(normed_two, grad_pre[half, core]).astype(BF) for core in cores]
        sums["up", half] = reduce_weight(own, other, half == 0)
        for core in cores:
            grad_normed_two = grad_normed_two + dot_nt(grad_pre[half, core], w_up[half][core])
    grad_unit_bias = {key: jnp.sum(grad_pre[key].astype(F32), 0) for key in parts}
    grad_hidden, grad_gain_two, grad_shift_two = norm_back(
        grad_normed_two, normal_two, spread_two, gain_two
    )
    grad_hidden = grad_out + grad_hidden
    grad_scale_one = jnp.sum(grad_hidden * branch_one, 0)
    grad_out_bias = jnp.sum(grad_hidden, 0) * scale_one
    grad_projected = (grad_hidden * scale_one).astype(BF)
    own, other = [dot_tn(grad_projected, blended[core]).astype(BF) for core in cores]
    sums["out"] = reduce_weight(own, other, True)
    grad_qk, grad_v = ([], [])
    for core in cores:
        grad_blended = dot_nn(grad_projected, w_out[core]).astype(BF)
        grad_query, grad_key, grad_value = attend_back(
            query_keys[core], values[core], grad_blended, log_total[core]
        )
        pair_shape = (grad_query.shape[0], 2, -1)
        stacked = jnp.stack([grad_query.reshape(pair_shape), grad_key.reshape(pair_shape)], 2)
        grad_qk.append(stacked.reshape(grad_query.shape[0], -1))
        grad_v.append(grad_value)
    own, other = [dot_tn(normed_one, grad_qk[core]).astype(BF) for core in cores]
    sums["qk"] = reduce_weight(own, other, False)
    own, other = [dot_tn(normed_one, grad_v[core]).astype(BF) for core in cores]
    sums["v"] = reduce_weight(own, other, True)
    grad_normed_one = 0.0
    for core in cores:
        grad_normed_one = grad_normed_one + dot_nt(grad_qk[core], w_qk[core])
        grad_normed_one = grad_normed_one + dot_nt(grad_v[core], w_v[core])
    grad_input, grad_gain_one, grad_shift_one = norm_back(
        grad_normed_one, normal_one, spread_one, gain_one
    )
    input_grad = send_back(grad_hidden + grad_input, F32)

    grad_vectors = jnp.stack(
        [
            grad_gain_one,
            grad_shift_one,
            grad_out_bias,
            grad_scale_one,
            grad_gain_two,
            grad_shift_two,
            grad_down_bias,
            grad_scale_two,
        ]
    )
    grad_vectors = grad_vectors.reshape(-1, DP, LANES).transpose(1, 0, 2).reshape(DP, -1)
    bias_parts = []
    for core in cores:
        query_part = jnp.sum(grad_qk[core].astype(F32), 0).reshape(2, 2, block_width)[:, 0]
        value_part = jnp.sum(grad_v[core].astype(F32), 0).reshape(2, block_width)
        rows = [query_part, value_part]
        for half in (0, 1):
            unit_part = grad_unit_bias[half, core].reshape(2, half_units, block_width)
            rows += [unit_part[:, at] for at in range(half_units)]
        bias_parts.append(jnp.stack(rows, 1))
    grad_biases = jnp.stack(bias_parts).reshape(2, 2, -1, DP, bias_width).transpose(0, 1, 3, 2, 4)
    grad_biases = jnp.take(grad_biases, place[:DP], axis=2).reshape(2, 2, DP, -1)
    total_vectors = grad_vectors + swap_mp(grad_vectors, 1)
    total_biases = grad_biases[0] + swap_mp(grad_biases[1], 1)
    total_vectors = total_vectors + swap_mp(total_vectors, 2)
    total_biases = total_biases[0] + swap_mp(total_biases[1], 2)
    small_grads = jnp.concatenate([total_vectors, total_biases], 1)
    small_grads = small_grads[:ZS] + swap_y(small_grads[ZS:])
    small_total = small_grads[0]
    for step in range(1, ZS):
        small_total = small_total + swap_z(small_grads[step], step)
    vector_grad = small_total[:vector_size].reshape(vectors.shape)
    bias_grad = small_total[vector_size:].reshape(head_biases.shape)

    qk_sum = sums["qk"].reshape(depth, 2, block_width).transpose(1, 0, 2)
    qkv_grad = jnp.concatenate([qk_sum, sums["v"][None]], 0)
    up_grad = jnp.concatenate(
        [sums["up", half].reshape(depth, half_units, block_width) for half in (0, 1)], 1
    )
    down_grad = jnp.concatenate(
        [sums["down", half].reshape(depth, half_units, block_width) for half in (0, 1)], 1
    ).transpose(1, 2, 0)
    grads = (qkv_grad, sums["out"].T, up_grad, down_grad, bias_grad, vector_grad)
    params = (qkv_weight, out_weight, up_weight, down_weight, head_biases, vectors)
    firsts = (qkv_first, out_first, up_first, down_first, bias_first, vector_first)
    seconds = (qkv_second, out_second, up_second, down_second, bias_second, vector_second)
    results = [layer_output, input_grad]
    for slot in range(6):
        results.extend(
            adam_update(params[slot], firsts[slot], seconds[slot], grads[slot], RATES[slot])
        )
    return tuple(results)


def solution(mesh):
    whole_image = mesh.shape["mp"] == MICRO == MP and mesh.shape["dp"] == DP
    return jax.shard_map(
        local_image if whole_image else local_general,
        mesh=mesh,
        in_specs=(
            P(None, "dp", "mp", None),
            P(None, "dp", "mp", None),
            P(None, "dp", "mp"),
            P(None, "dp", "mp"),
            P(None, "dp", "mp"),
            P("mp", "dp"),
            P("mp", "dp"),
            P("mp", "dp"),
            P("dp", None, "mp"),
            P("dp", None, "mp"),
            P("dp", None, "mp"),
            P(None, "mp", "dp"),
            P(None, "mp", "dp"),
            P(None, "mp", "dp"),
            P(None, ("mp", "dp")),
            P(None, ("mp", "dp")),
            P(None, ("mp", "dp")),
            P(None, "dp"),
            P(None, "dp"),
            P(None, "dp"),
        ),
        out_specs=(
            P(None, "dp", "mp", None),
            P(None, "dp", "mp", None),
            P(None, "dp", "mp"),
            P(None, "dp", "mp"),
            P(None, "dp", "mp"),
            P("mp", "dp"),
            P("mp", "dp"),
            P("mp", "dp"),
            P("dp", None, "mp"),
            P("dp", None, "mp"),
            P("dp", None, "mp"),
            P(None, "mp", "dp"),
            P(None, "mp", "dp"),
            P(None, "mp", "dp"),
            P(None, ("mp", "dp")),
            P(None, ("mp", "dp")),
            P(None, ("mp", "dp")),
            P(None, "dp"),
            P(None, "dp"),
            P(None, "dp"),
        ),
        check_vma=False,
    )
```

```python
import functools

import jax
import jax.numpy as jnp
from jax import lax
from jax.experimental import pallas as pl
from jax.experimental.pallas import tpu as pltpu
from jax.sharding import PartitionSpec as P

DH = 64
MICRO = 4
STEP = 10


RATES = (0.05, 0.2, 0.05, 0.03, 0.5, 0.5)


def layer_norm(values, gain, shift):
    center = values - jnp.mean(values, -1, keepdims=True)
    spread = jnp.mean(center * center, -1, keepdims=True)
    return center * lax.rsqrt(spread + 1e-06) * gain + shift


def exact_gelu(values):
    return jax.nn.gelu(values, approximate=False)


def adam_update(weight, first, second, grad, rate):
    first_new = 0.9 * first + 0.1 * grad
    second_new = 0.999 * second + 0.001 * grad * grad
    corrected = first_new / (1.0 - 0.9**STEP)
    scaled = jnp.sqrt(second_new / (1.0 - 0.999**STEP))
    weight_new = weight - rate * (corrected / (scaled + 1e-08) + 0.05 * weight)
    return (weight_new, first_new, second_new)


def attend_forward(queries, key_rows, values, block_rows):
    images, seq_rows, head_count, head_width = queries.shape
    block_count = seq_rows // block_rows
    factor = head_width ** (-0.5)
    query_blocks = jnp.moveaxis(
        queries.reshape(images, block_count, block_rows, head_count, head_width), 1, 0
    )

    def one_block(query_part):
        scores = (
            jnp.einsum("iqhe,ikhe->ihqk", query_part, key_rows, preferred_element_type=jnp.float32)
            * factor
        )
        row_peak = jnp.max(scores, -1, keepdims=True)
        shifted = jnp.exp(scores - row_peak)
        row_total = jnp.sum(shifted, -1, keepdims=True)
        softmax_rows = (shifted / row_total).astype(jnp.bfloat16)
        blended = jnp.einsum(
            "ihqk,ikhe->iqhe", softmax_rows, values, preferred_element_type=jnp.float32
        )
        return (blended, row_peak[..., 0] + jnp.log(row_total[..., 0]))

    blended, log_total = lax.map(one_block, query_blocks)
    blended = jnp.moveaxis(blended, 0, 1).reshape(images, seq_rows, head_count * head_width)
    return (blended.astype(jnp.bfloat16), log_total)


def attend_backward(queries, key_rows, values, grad_blended, log_total, block_rows):
    images, seq_rows, head_count, head_width = queries.shape
    block_count = seq_rows // block_rows
    factor = head_width ** (-0.5)
    split_shape = (images, block_count, block_rows, head_count, head_width)
    query_blocks = jnp.moveaxis(queries.reshape(split_shape), 1, 0)
    grad_blocks = jnp.moveaxis(grad_blended.reshape(split_shape), 1, 0)

    def one_block(carry, inputs_part):
        query_part, grad_part, total_part = inputs_part
        grad_keys, grad_values = carry
        scores = (
            jnp.einsum("iqhe,ikhe->ihqk", query_part, key_rows, preferred_element_type=jnp.float32)
            * factor
        )
        softmax_rows = jnp.exp(scores - total_part[..., None])
        grad_values = grad_values + jnp.einsum(
            "ihqk,iqhe->ikhe",
            softmax_rows.astype(jnp.bfloat16),
            grad_part,
            preferred_element_type=jnp.float32,
        )
        grad_rows = jnp.einsum(
            "iqhe,ikhe->ihqk", grad_part, values, preferred_element_type=jnp.float32
        )
        grad_scores = softmax_rows * (
            grad_rows - jnp.sum(grad_rows * softmax_rows, -1, keepdims=True)
        )
        grad_scores = grad_scores.astype(jnp.bfloat16)
        grad_query = (
            jnp.einsum("ihqk,ikhe->iqhe", grad_scores, key_rows, preferred_element_type=jnp.float32)
            * factor
        )
        grad_keys = (
            grad_keys
            + jnp.einsum(
                "ihqk,iqhe->ikhe", grad_scores, query_part, preferred_element_type=jnp.float32
            )
            * factor
        )
        return ((grad_keys, grad_values), grad_query)

    zero_grad = jnp.zeros(queries.shape, jnp.float32)
    (grad_keys, grad_values), grad_query = lax.scan(
        one_block, (zero_grad, zero_grad), (query_blocks, grad_blocks, log_total)
    )
    flat_shape = (images, seq_rows, head_count * head_width)
    grad_query = jnp.moveaxis(grad_query, 0, 1).reshape(flat_shape)
    stacked = jnp.stack(
        [grad_query, grad_keys.reshape(flat_shape), grad_values.reshape(flat_shape)]
    )
    return stacked.astype(jnp.bfloat16)


def rows_forward(part):
    return lax.all_gather(part, "mp", axis=1, tiled=True)


def rows_sum_forward(part):
    return lax.psum_scatter(part, "mp", scatter_dimension=1, tiled=True)


def rows_backward(part):
    return lax.all_gather(part, "mp", axis=1, tiled=True)


def rows_sum_backward(part):
    return lax.psum_scatter(part, "mp", scatter_dimension=1, tiled=True)


def forward(inputs, params):
    qkv_full, out_full, up_full, down_full, bias_full, vector_full = params
    base = inputs.astype(jnp.float32)
    normed = layer_norm(base, vector_full[0], vector_full[1]).astype(jnp.bfloat16)
    normed_all = rows_forward(normed)
    images, seq_rows = (normed_all.shape[0], normed_all.shape[1])
    head_shape = (images, seq_rows, -1, DH)
    project = jnp.einsum("isd,tde->tise", normed_all, qkv_full, preferred_element_type=jnp.float32)
    queries = (project[0] + bias_full[0]).astype(jnp.bfloat16).reshape(head_shape)
    key_rows = project[1].astype(jnp.bfloat16).reshape(head_shape)
    values = (project[2] + bias_full[1]).astype(jnp.bfloat16).reshape(head_shape)
    blended, log_total = attend_forward(queries, key_rows, values, min(512, seq_rows))
    projected = rows_sum_forward(
        jnp.einsum("ise,ed->isd", blended, out_full, preferred_element_type=jnp.float32)
    )
    branch_one = projected + vector_full[2]
    hidden = base + vector_full[3] * branch_one
    normed_two = layer_norm(hidden, vector_full[4], vector_full[5]).astype(jnp.bfloat16)
    normed_two_all = rows_forward(normed_two)
    pre_act = jnp.einsum(
        "isd,df->isf", normed_two_all, up_full, preferred_element_type=jnp.float32
    ) + bias_full[2:].reshape(-1)
    activ = exact_gelu(pre_act).astype(jnp.bfloat16)
    branch_two = (
        rows_sum_forward(
            jnp.einsum("isf,fd->isd", activ, down_full, preferred_element_type=jnp.float32)
        )
        + vector_full[6]
    )
    output = hidden + vector_full[7] * branch_two
    saved = (
        base,
        hidden,
        branch_one,
        branch_two,
        normed_all,
        queries,
        key_rows,
        values,
        log_total,
        blended,
        normed_two_all,
        pre_act,
        activ,
    )
    return (output.astype(jnp.bfloat16), saved)


def backward(grad_output, saved, params):
    qkv_full, out_full, up_full, down_full, bias_full, vector_full = params
    (
        base,
        hidden,
        branch_one,
        branch_two,
        normed_all,
        queries,
        key_rows,
        values,
        log_total,
        blended,
        normed_two_all,
        pre_act,
        activ,
    ) = saved
    local_width = qkv_full.shape[2]
    grad_out = grad_output.astype(jnp.float32)
    grad_scale_two = jnp.sum(grad_out * branch_two, axis=(0, 1))
    grad_bias_two = jnp.sum(grad_out, axis=(0, 1)) * vector_full[7]
    grad_branch = rows_backward((grad_out * vector_full[7]).astype(jnp.bfloat16))
    grad_down = jnp.einsum("isf,isd->fd", activ, grad_branch, preferred_element_type=jnp.float32)
    grad_activ = jnp.einsum(
        "isd,fd->isf", grad_branch, down_full, preferred_element_type=jnp.float32
    )
    grad_pre = jax.vjp(exact_gelu, pre_act)[1](grad_activ)[0].astype(jnp.bfloat16)
    grad_up_bias = jnp.sum(grad_pre, axis=(0, 1), dtype=jnp.float32)
    grad_up = jnp.einsum(
        "isd,isf->df", normed_two_all, grad_pre, preferred_element_type=jnp.float32
    )
    grad_normed_two = rows_sum_backward(
        jnp.einsum("isf,df->isd", grad_pre, up_full, preferred_element_type=jnp.float32)
    )
    norm_back_two = jax.vjp(layer_norm, hidden, vector_full[4], vector_full[5])[1]
    grad_hidden, grad_gain_two, grad_shift_two = norm_back_two(grad_normed_two)
    grad_hidden = grad_out + grad_hidden
    grad_scale_one = jnp.sum(grad_hidden * branch_one, axis=(0, 1))
    grad_out_bias = jnp.sum(grad_hidden, axis=(0, 1)) * vector_full[3]
    grad_projected = rows_backward((grad_hidden * vector_full[3]).astype(jnp.bfloat16))
    grad_out_weight = jnp.einsum(
        "ise,isd->ed", blended, grad_projected, preferred_element_type=jnp.float32
    )
    grad_blended = jnp.einsum(
        "isd,ed->ise", grad_projected, out_full, preferred_element_type=jnp.float32
    ).astype(jnp.bfloat16)
    grad_project = attend_backward(
        queries, key_rows, values, grad_blended, log_total, min(512, queries.shape[1])
    )
    grad_query_bias = jnp.sum(grad_project[0], axis=(0, 1), dtype=jnp.float32)
    grad_value_bias = jnp.sum(grad_project[2], axis=(0, 1), dtype=jnp.float32)
    grad_qkv = jnp.einsum(
        "isd,tise->tde", normed_all, grad_project, preferred_element_type=jnp.float32
    )
    grad_normed = rows_sum_backward(
        jnp.einsum("tise,tde->isd", grad_project, qkv_full, preferred_element_type=jnp.float32)
    )
    norm_back_one = jax.vjp(layer_norm, base, vector_full[0], vector_full[1])[1]
    grad_input_part, grad_gain_one, grad_shift_one = norm_back_one(grad_normed)
    grad_input = grad_hidden + grad_input_part
    grad_vectors = jnp.stack(
        [
            grad_gain_one,
            grad_shift_one,
            grad_out_bias,
            grad_scale_one,
            grad_gain_two,
            grad_shift_two,
            grad_bias_two,
            grad_scale_two,
        ]
    )
    grad_biases = jnp.concatenate(
        [jnp.stack([grad_query_bias, grad_value_bias]), grad_up_bias.reshape(-1, local_width)], 0
    )
    return (grad_input, (grad_qkv, grad_out_weight, grad_up, grad_down, grad_biases, grad_vectors))


def local_general(
    tokens,
    cotangent,
    qkv_weight,
    qkv_first,
    qkv_second,
    out_weight,
    out_first,
    out_second,
    up_weight,
    up_first,
    up_second,
    down_weight,
    down_first,
    down_second,
    head_biases,
    bias_first,
    bias_second,
    vectors,
    vector_first,
    vector_second,
):

    def gather_params():
        gathered = (
            lax.all_gather(qkv_weight.astype(jnp.bfloat16), "dp", axis=1, tiled=True),
            lax.all_gather(out_weight.astype(jnp.bfloat16), "dp", axis=1, tiled=True),
            lax.all_gather(up_weight.astype(jnp.bfloat16), "dp", axis=0, tiled=True),
            lax.all_gather(down_weight.astype(jnp.bfloat16), "dp", axis=2, tiled=True),
            lax.all_gather(head_biases.astype(jnp.bfloat16), "dp", axis=1, tiled=True),
            lax.all_gather(vectors.astype(jnp.bfloat16), "dp", axis=1, tiled=True),
        )
        qkv_full, out_full, up_full, down_full, bias_full, vector_full = gathered
        return (
            qkv_full,
            out_full,
            up_full.reshape(up_full.shape[0], -1),
            down_full.reshape(-1, down_full.shape[2]),
            bias_full.astype(jnp.float32),
            vector_full.astype(jnp.float32),
        )

    grad_sums = None
    outputs = []
    input_grads = []
    for micro_step in range(MICRO):
        params_fwd = gather_params()
        output, saved = forward(tokens[micro_step], params_fwd)
        outputs.append(output)
        params_back = gather_params()
        grad_input, grads = backward(cotangent[micro_step], saved, params_back)
        input_grads.append(grad_input)
        if grad_sums is None:
            grad_sums = grads
        else:
            grad_sums = tuple((old_sum + new_part for old_sum, new_part in zip(grad_sums, grads)))
    grad_qkv, grad_out_weight, grad_up, grad_down, grad_biases, grad_vectors = grad_sums
    grad_up = grad_up.reshape(-1, up_weight.shape[1], up_weight.shape[2])
    grad_down = grad_down.reshape(down_weight.shape[0], down_weight.shape[1], -1)
    reduced = (
        lax.psum_scatter(grad_qkv, "dp", scatter_dimension=1, tiled=True),
        lax.psum_scatter(grad_out_weight, "dp", scatter_dimension=1, tiled=True),
        lax.psum_scatter(grad_up, "dp", scatter_dimension=0, tiled=True),
        lax.psum_scatter(grad_down, "dp", scatter_dimension=2, tiled=True),
        lax.psum_scatter(grad_biases, "dp", scatter_dimension=1, tiled=True),
        lax.psum_scatter(grad_vectors, "dp", scatter_dimension=1, tiled=True),
    )
    vector_grad = lax.psum(reduced[5], "mp")
    grads = (reduced[0], reduced[1], reduced[2], reduced[3], reduced[4], vector_grad)
    params = (qkv_weight, out_weight, up_weight, down_weight, head_biases, vectors)
    firsts = (qkv_first, out_first, up_first, down_first, bias_first, vector_first)
    seconds = (qkv_second, out_second, up_second, down_second, bias_second, vector_second)
    updated = [
        adam_update(params[slot], firsts[slot], seconds[slot], grads[slot], RATES[slot])
        for slot in range(6)
    ]
    return (
        jnp.stack(outputs),
        jnp.stack(input_grads),
        updated[0][0],
        updated[0][1],
        updated[0][2],
        updated[1][0],
        updated[1][1],
        updated[1][2],
        updated[2][0],
        updated[2][1],
        updated[2][2],
        updated[3][0],
        updated[3][1],
        updated[3][2],
        updated[4][0],
        updated[4][1],
        updated[4][2],
        updated[5][0],
        updated[5][1],
        updated[5][2],
    )


ZS, YS, MP = (4, 2, 4)
DP = ZS * YS
LANES = 128
BF = jnp.bfloat16
F32 = jnp.float32


def swap_z(part, step):
    return lax.ppermute(
        part, "dp", [(z * YS + y, (z ^ step) * YS + y) for z in range(ZS) for y in range(YS)]
    )


def swap_y(part):
    return lax.ppermute(part, "dp", [(each, each ^ 1) for each in range(DP)])


def swap_mp(part, step):
    return lax.ppermute(part, "mp", [(each, each ^ step) for each in range(MP)])


class Chain:
    def __init__(self, steps, *args):
        self.own = None
        self.result = None
        self.steps = steps(self, *args)
        self.flight = next(self.steps)

    def land(self, arrived):
        try:
            self.flight = self.steps.send(arrived)
        except StopIteration as end:
            self.flight = None
            self.result = end.value


def meet(values, *chains):
    values, flights = lax.optimization_barrier((values, [each.flight for each in chains]))
    for each, flight in zip(chains, flights):
        each.land(flight)
    return values


def gather_steps(chain, shard, order):
    rows = shard
    for axis in order:
        if axis == "z":
            arrived = yield [swap_z(rows, step) for step in range(1, ZS)]
            rows = jnp.concatenate([rows] + arrived, 0)
        elif axis == "y":
            arrived = yield [swap_y(rows)]
            rows = jnp.concatenate([rows] + arrived, 0)
        else:
            arrived = yield [swap_mp(rows, 2)]
            rows = jnp.concatenate([rows] + arrived, 1)
    chain.own = rows
    arrived = yield [swap_mp(rows, 1)]
    return (rows, arrived[0])


def add_low(first, second):
    return (first.astype(F32) + second.astype(F32)).astype(BF)


def reduce_steps(chain, other_part, order):
    arrived = yield [swap_mp(other_part, 1)]
    total = add_low(chain.own, arrived[0])
    for axis in order:
        rows, width = total.shape[-2:]
        if axis == "z":
            rows = rows // ZS
            arrived = yield [
                swap_z(total[..., step * rows : (step + 1) * rows, :], step) for step in range(1, ZS)
            ]
            total = total[..., :rows, :].astype(F32)
            for each in arrived:
                total = total + each.astype(F32)
        elif axis == "y":
            arrived = yield [swap_y(total[..., rows // 2 :, :])]
            total = add_low(total[..., : rows // 2, :], arrived[0])
        else:
            arrived = yield [swap_mp(total[..., width // 2 :], 2)]
            total = add_low(total[..., : width // 2], arrived[0])
    return total


def mp_steps(chain, parts):
    arrived = yield [swap_mp(part, step + 1) for step, part in enumerate(parts)]
    return arrived


def small_steps(chain, shard, vector_size):
    arrived = yield [swap_z(shard, step) for step in range(1, ZS)]
    rows = jnp.concatenate([shard] + arrived, 0)
    arrived = yield [swap_y(rows)]
    rows = jnp.concatenate([rows] + arrived, 0)
    arrived = yield [swap_mp(rows[:, vector_size:], step) for step in range(1, MP)]
    return (rows[:, :vector_size], jnp.stack([rows[:, vector_size:]] + arrived, 0))


def small_reduce_steps(chain, vector_part, bias_part):
    arrived = yield [swap_mp(vector_part, 1), swap_mp(bias_part[1], 1), swap_mp(bias_part[3], 1)]
    vector_part = vector_part + arrived[0]
    even, odd = (bias_part[0] + arrived[1], bias_part[2] + arrived[2])
    arrived = yield [swap_mp(vector_part, 2), swap_mp(odd, 2)]
    total = jnp.concatenate([vector_part + arrived[0], even + arrived[1]], 1)
    arrived = yield [swap_y(total[ZS:])]
    total = total[:ZS] + arrived[0]
    arrived = yield [swap_z(total[step], step) for step in range(1, ZS)]
    total = total[0]
    for each in arrived:
        total = total + each
    return total


def assemble_kernel(place_ref, own_ref, *refs):
    chunk_rows = own_ref.shape[1]
    out_ref = refs[-1]
    out_ref[0:chunk_rows, :] = own_ref[0]
    for at, part_ref in enumerate(refs[:-1]):
        out_ref[(at + 1) * chunk_rows : (at + 2) * chunk_rows, :] = part_ref[...]


def assemble_image(place, arrays, parts):
    chunk_rows, width = parts[0].shape
    return pl.pallas_call(
        assemble_kernel,
        grid_spec=pltpu.PrefetchScalarGridSpec(
            num_scalar_prefetch=1,
            grid=(width // LANES,),
            in_specs=[
                pl.BlockSpec((1, chunk_rows, LANES), lambda j, place_ref: (place_ref[DP], 0, place_ref[j]))
            ]
            + [pl.BlockSpec((chunk_rows, LANES), lambda j, place_ref: (0, place_ref[j]))] * len(parts),
            out_specs=pl.BlockSpec((chunk_rows * MP, LANES), lambda j, place_ref: (0, j)),
        ),
        out_shape=jax.ShapeDtypeStruct((chunk_rows * MP, width), arrays.dtype),
        name="assemble_image",
    )(place, arrays, *parts)


def spread_kernel(place_ref, own_ref, *refs):
    out_ref = refs[-1]
    mine = place_ref[DP]
    out_ref[mine] = own_ref[...].astype(out_ref.dtype)
    for at, part_ref in enumerate(refs[:-1]):
        out_ref[mine ^ (at + 1)] = part_ref[...].astype(out_ref.dtype)


def spread_image(place, own, parts, dtype):
    chunk_rows, width = parts[0].shape
    block = pl.BlockSpec((chunk_rows, LANES), lambda j, place_ref: (0, j))
    return pl.pallas_call(
        spread_kernel,
        grid_spec=pltpu.PrefetchScalarGridSpec(
            num_scalar_prefetch=1,
            grid=(width // LANES,),
            in_specs=[block] * (1 + len(parts)),
            out_specs=pl.BlockSpec((MP, chunk_rows, LANES), lambda j, place_ref: (0, 0, place_ref[j])),
        ),
        out_shape=jax.ShapeDtypeStruct((MP, chunk_rows, width), dtype),
        name="spread_image",
    )(place, own, *parts)


def lane_dot(left, right):
    return lax.dot_general(left, right, (((1,), (1,)), ((), ())), preferred_element_type=F32)


def head_masks(width):
    lane = lax.broadcasted_iota(jnp.int32, (1, width), 1)
    return [lane // DH == head for head in range(width // DH)]


def attend_kernel(block_rows, q_ref, k_ref, v_ref, o_ref, lse_ref):
    masks = head_masks(LANES)
    key_rows = k_ref[...]
    values = v_ref[...]
    zero = jnp.zeros((), BF)
    for block in range(q_ref.shape[0] // block_rows):
        rows = slice(block * block_rows, (block + 1) * block_rows)
        queries = q_ref[rows, :] * jnp.asarray(DH**-0.5, BF)
        blended = []
        for head, mask in enumerate(masks):
            scores = lane_dot(jnp.where(mask, queries, zero), key_rows)
            peak = jnp.max(scores, 1, keepdims=True)
            shifted = jnp.exp(scores - peak)
            total = jnp.sum(shifted, 1, keepdims=True)
            part = jnp.dot(shifted.astype(BF), values, preferred_element_type=F32)
            blended.append(part * (1.0 / total))
            log_total = jnp.broadcast_to(peak + jnp.log(total), (block_rows, LANES))
            lse_ref[0, head : head + 1, rows] = jnp.transpose(log_total)[0:1, :]
        o_ref[rows, :] = jnp.where(masks[0], blended[0], blended[1]).astype(BF)


def attend_back_kernel(
    block_rows, q_ref, k_ref, v_ref, g_ref, lse_ref, out_ref, dk_acc, dv_acc
):
    masks = head_masks(LANES)
    key_rows = k_ref[...]
    values = v_ref[...]
    zero = jnp.zeros((), BF)
    factor = DH**-0.5
    key_heads = [jnp.where(mask, key_rows, zero) for mask in masks]
    for block in range(q_ref.shape[0] // block_rows):
        rows = slice(block * block_rows, (block + 1) * block_rows)
        queries = q_ref[rows, :] * jnp.asarray(factor, BF)
        grads = g_ref[rows, :]
        grad_query = None
        grad_keys = None
        grad_values = None
        for head, mask in enumerate(masks):
            query_head = jnp.where(mask, queries, zero)
            grad_head = jnp.where(mask, grads, zero)
            scores = lane_dot(key_rows, query_head)
            weights = jnp.exp(scores - lse_ref[0, head : head + 1, rows])
            value_part = jnp.dot(weights.astype(BF), grad_head, preferred_element_type=F32)
            grad_rows = lane_dot(values, grad_head)
            delta = jnp.sum(grad_rows * weights, 0, keepdims=True)
            grad_scores = (weights * (grad_rows - delta)).astype(BF)
            key_part = jnp.dot(grad_scores, query_head, preferred_element_type=F32)
            query_part = lax.dot_general(
                grad_scores, key_heads[head], (((0,), (0,)), ((), ())), preferred_element_type=F32
            )
            grad_query = query_part if head == 0 else grad_query + query_part
            grad_keys = key_part if head == 0 else grad_keys + key_part
            grad_values = value_part if head == 0 else grad_values + value_part
        out_ref[0, rows, :] = (grad_query * factor).astype(BF)
        if block == 0:
            dk_acc[...] = grad_keys
            dv_acc[...] = grad_values
        else:
            dk_acc[...] += grad_keys
            dv_acc[...] += grad_values
    out_ref[1] = dk_acc[...].astype(BF)
    out_ref[2] = dv_acc[...].astype(BF)


def pair_spec(rows):
    return pl.BlockSpec((rows, LANES), lambda p: (0, p))


def attend(queries, key_rows, values):
    rows, width = values.shape
    pairs = width // LANES
    scores_size = rows * rows * 2 * pairs
    return pl.pallas_call(
        functools.partial(attend_kernel, 256),
        grid=(pairs,),
        in_specs=[pair_spec(rows)] * 3,
        out_specs=[pair_spec(rows), pl.BlockSpec((1, 8, rows), lambda p: (p, 0, 0))],
        out_shape=[
            jax.ShapeDtypeStruct((rows, width), BF),
            jax.ShapeDtypeStruct((pairs, 8, rows), F32),
        ],
        compiler_params=pltpu.CompilerParams(vmem_limit_bytes=32 * 2**20),
        cost_estimate=pl.CostEstimate(
            flops=scores_size * 2 * 512, bytes_accessed=rows * width * 8, transcendentals=scores_size
        ),
        name="attend",
    )(queries, key_rows, values)


def attend_back(queries, key_rows, values, grad_blended, log_total):
    rows, width = values.shape
    pairs = width // LANES
    scores_size = rows * rows * 2 * pairs
    return pl.pallas_call(
        functools.partial(attend_back_kernel, 256),
        grid=(pairs,),
        in_specs=[pair_spec(rows)] * 4 + [pl.BlockSpec((1, 8, rows), lambda p: (p, 0, 0))],
        out_specs=pl.BlockSpec((3, rows, LANES), lambda p: (0, 0, p)),
        out_shape=jax.ShapeDtypeStruct((3, rows, width), BF),
        scratch_shapes=[pltpu.VMEM((rows, LANES), F32)] * 2,
        compiler_params=pltpu.CompilerParams(vmem_limit_bytes=32 * 2**20),
        cost_estimate=pl.CostEstimate(
            flops=scores_size * 2 * 1280, bytes_accessed=rows * width * 14, transcendentals=scores_size
        ),
        name="attend_back",
    )(queries, key_rows, values, grad_blended, log_total)


def dot_nn(left, right):
    return lax.dot_general(left, right, (((1,), (0,)), ((), ())), preferred_element_type=F32)


def dot_nt(left, right):
    return lax.dot_general(left, right, (((1,), (1,)), ((), ())), preferred_element_type=F32)


def dot_tn(left, right):
    return lax.dot_general(left, right, (((0,), (0,)), ((), ())), preferred_element_type=F32)


def norm_parts(values):
    center = values - jnp.mean(values, -1, keepdims=True)
    spread = lax.rsqrt(jnp.mean(center * center, -1, keepdims=True) + 1e-06)
    return (center * spread, spread)


def norm_back(grad, normal, spread, gain):
    scaled = grad * gain
    inner = scaled - jnp.mean(scaled, -1, keepdims=True)
    inner = inner - normal * jnp.mean(scaled * normal, -1, keepdims=True)
    return (spread * inner, jnp.sum(grad * normal, 0), jnp.sum(grad, 0))


def gelu_pair(values):
    share = 0.5 * (1.0 + lax.erf(values * 0.7071067811865476))
    slope = share + values * (0.3989422804014327 * jnp.exp(-0.5 * values * values))
    return ((values * share).astype(BF), slope.astype(BF))


def local_image(
    tokens,
    cotangent,
    qkv_weight,
    qkv_first,
    qkv_second,
    out_weight,
    out_first,
    out_second,
    up_weight,
    up_first,
    up_second,
    down_weight,
    down_first,
    down_second,
    head_biases,
    bias_first,
    bias_second,
    vectors,
    vector_first,
    vector_second,
):
    dp_at = lax.axis_index("dp")
    mp_at = lax.axis_index("mp")
    units = up_weight.shape[1]
    half_units = units // 2
    block_width = qkv_weight.shape[2]
    depth = qkv_weight.shape[1]
    bias_width = head_biases.shape[1]
    chunk_rows, width = tokens.shape[2:]
    order = [((zk * YS) + yk) for yk in range(YS) for zk in range(ZS)]
    place = jnp.stack([dp_at ^ each for each in order] + [mp_at]).astype(jnp.int32)
    cores = (0, 1)

    def fetch_image(array):
        chunks = array[:, 0]
        return Chain(
            mp_steps,
            [
                lax.dynamic_index_in_dim(chunks, mp_at ^ step, 0, keepdims=False)
                for step in range(1, MP)
            ],
        )

    def send_back(array):
        low = array.astype(BF)
        return Chain(
            mp_steps, [low[step * chunk_rows : (step + 1) * chunk_rows] for step in range(1, MP)]
        )

    small_shard = jnp.concatenate(
        [vectors.astype(BF).reshape(-1), head_biases.astype(BF).reshape(-1)]
    ).reshape(1, -1)
    vector_size = vectors.size
    qkv_low = qkv_weight.astype(BF)
    up_low = up_weight.astype(BF)
    down_low = down_weight.transpose(2, 0, 1).astype(BF)
    out_low = out_weight.T.astype(BF)
    up_shards = [up_low[:, at : at + half_units].reshape(depth, -1) for at in (0, half_units)]
    down_shards = [down_low[:, at : at + half_units].reshape(depth, -1) for at in (0, half_units)]

    small = Chain(small_steps, small_shard, vector_size)
    get_q = Chain(gather_steps, qkv_low[0], "zxy")
    get_k = Chain(gather_steps, qkv_low[1], "zxy")
    get_v = Chain(gather_steps, qkv_low[2], "zyx")
    fetch_tokens = fetch_image(tokens)
    out_low, up_shards, down_shards = meet((out_low, up_shards, down_shards), small, get_q, get_k, get_v)
    get_out = Chain(gather_steps, out_low, "zyx")
    up_shards, down_shards = meet((up_shards, down_shards), small, get_q, get_k, get_v, get_out)
    get_up = [Chain(gather_steps, up_shards[0], "zxy"), None]
    tokens, down_shards, up_shards = meet(
        (tokens, down_shards, up_shards), small, fetch_tokens, get_k, get_q
    )
    get_up[1] = Chain(gather_steps, up_shards[1], "zxy")

    vector_full, bias_small = small.result
    vector_full = vector_full.reshape(DP, vectors.shape[0], LANES).transpose(1, 0, 2)
    vector_full = vector_full.reshape(vectors.shape[0], width).astype(F32)
    back_places = jnp.stack([((each ^ dp_at) & 1) * ZS + ((each ^ dp_at) >> 1) for each in range(DP)])
    bias_rows = jnp.take(bias_small, back_places, axis=1).reshape(2, 2, DP, -1, bias_width)
    bias_full = bias_rows.transpose(1, 3, 0, 2, 4).reshape(2, head_biases.shape[0], 2, block_width)
    bias_full = bias_full.astype(F32)
    gain_one, shift_one, out_bias, scale_one, gain_two, shift_two, down_bias, scale_two = vector_full

    base = assemble_image(place, tokens[:, 0], fetch_tokens.result).astype(F32)
    normal_one, spread_one = norm_parts(base)
    normed_one = (normal_one * gain_one + shift_one).astype(BF)
    normed_one = meet(normed_one, get_v, get_up[0], get_out)

    def project(core, weights):
        w_q, w_k, w_v = weights
        return (
            (dot_nn(normed_one, w_q) + bias_full[core, 0].reshape(-1)).astype(BF),
            dot_nn(normed_one, w_k).astype(BF),
            (dot_nn(normed_one, w_v) + bias_full[core, 1].reshape(-1)).astype(BF),
        )

    heads, blended, log_total = ([None, None], [None, None], [None, None])
    heads[0] = project(0, (get_q.own, get_k.own, get_v.own))
    heads[0] = meet(heads[0], get_q, get_k, get_v, get_up[1])
    blended[0], log_total[0] = attend(*heads[0])
    blended[0], normed_one, down_shards, cotangent = meet(
        (blended[0], normed_one, down_shards, cotangent), get_up[0], get_out
    )
    get_down = [Chain(gather_steps, down_shards[0], "zxy"), None]
    heads[1] = project(1, (get_q.result[1], get_k.result[1], get_v.result[1]))
    blended[1], log_total[1] = attend(*heads[1])
    blended, down_shards = meet((blended, down_shards), get_up[0], get_up[1], get_out, get_down[0])
    get_down[1] = Chain(gather_steps, down_shards[1], "zxy")
    w_out = get_out.result
    branch_one = dot_nt(blended[0], w_out[0]) + dot_nt(blended[1], w_out[1]) + out_bias
    hidden = base + scale_one * branch_one
    normal_two, spread_two = norm_parts(hidden)
    normed_two = (normal_two * gain_two + shift_two).astype(BF)
    normed_two, cotangent = meet(
        (normed_two, cotangent), get_up[0], get_up[1], get_down[0], get_down[1]
    )
    fetch_cotangent = fetch_image(cotangent)
    w_up = [get_up[0].result, None]
    activ, slope = ({}, {})

    def expand(half, core):
        rows = bias_full[core, 2 + half * half_units : 2 + (half + 1) * half_units]
        pre_act = dot_nn(normed_two, w_up[half][core]) + rows.transpose(1, 0, 2).reshape(-1)
        activ[half, core], slope[half, core] = gelu_pair(pre_act)

    expand(0, 0)
    expand(0, 1)
    activ, normed_two, slope = meet((activ, normed_two, slope), get_up[1], get_down[0])
    w_up[1] = get_up[1].result
    expand(1, 0)
    expand(1, 1)
    activ, slope, cotangent = meet(
        (activ, slope, cotangent), get_down[0], get_down[1], fetch_cotangent
    )

    grad_out = assemble_image(place, cotangent[:, 0], fetch_cotangent.result).astype(F32)
    grad_branch = (grad_out * scale_two).astype(BF)
    sum_down, sum_up = ([None, None], [None, None])

    def grads_down(half):
        sum_down[half] = Chain(reduce_steps, dot_tn(grad_branch, activ[half, 1]).astype(BF), "yxz")
        sum_down[half].own = dot_tn(grad_branch, activ[half, 0]).astype(BF)

    grads_down(0)
    grad_branch, activ = meet((grad_branch, activ), sum_down[0], get_down[1])
    grads_down(1)
    activ = meet(activ, get_down[1])
    w_down = [get_down[0].result, get_down[1].result]
    branch_two = down_bias
    for half in (0, 1):
        for core in cores:
            branch_two = branch_two + dot_nt(activ[half, core], w_down[half][core])
    output = (hidden + scale_two * branch_two).astype(BF)
    grad_branch, output, normed_two = meet((grad_branch, output, normed_two), sum_down[1])
    send_output = send_back(output)
    grad_pre = {}

    def grads_up(half):
        for core in (1, 0):
            grad_activ = dot_nn(grad_branch, w_down[half][core])
            grad_pre[half, core] = (grad_activ * slope[half, core].astype(F32)).astype(BF)
        sum_up[half] = Chain(reduce_steps, dot_tn(normed_two, grad_pre[half, 1]).astype(BF), "yxz")
        sum_up[half].own = dot_tn(normed_two, grad_pre[half, 0]).astype(BF)

    grads_up(0)
    grad_branch, normed_two, grad_pre = meet((grad_branch, normed_two, grad_pre), sum_down[0], sum_up[0])
    grads_up(1)
    grad_normed_two = 0.0
    for half in (0, 1):
        for core in cores:
            grad_normed_two = grad_normed_two + dot_nt(grad_pre[half, core], w_up[half][core])
    grad_hidden, grad_gain_two, grad_shift_two = norm_back(
        grad_normed_two, normal_two, spread_two, gain_two
    )
    grad_hidden = grad_out + grad_hidden
    grad_projected = (grad_hidden * scale_one).astype(BF)
    grad_projected = meet(
        grad_projected, sum_down[0], sum_down[1], sum_up[0], sum_up[1], send_output
    )
    sum_out = Chain(reduce_steps, dot_tn(grad_projected, blended[1]).astype(BF), "xyz")
    sum_out.own = dot_tn(grad_projected, blended[0]).astype(BF)
    sums_qkv = None
    grad_heads = [None, None]

    def back_heads(core):
        grad_blended = dot_nn(grad_projected, w_out[core]).astype(BF)
        grad_heads[core] = attend_back(*heads[core], grad_blended, log_total[core])
        return jnp.einsum(
            "sd,tse->tde", normed_one, grad_heads[core], preferred_element_type=F32
        ).astype(BF)

    grad_other = back_heads(1)
    grad_other, grad_projected = meet(
        (grad_other, grad_projected), sum_down[0], sum_down[1], sum_up[0], sum_up[1], sum_out
    )
    sum_qkv = Chain(reduce_steps, grad_other, "yxz")
    sum_qkv.own = back_heads(0)
    grad_heads, normed_one = meet((grad_heads, normed_one), sum_qkv, sum_up[0], sum_up[1], sum_out, sum_down[1])
    weights = [[each.own for each in (get_q, get_k, get_v)], [each.result[1] for each in (get_q, get_k, get_v)]]
    grad_normed_one = 0.0
    for core in cores:
        for kind in range(3):
            grad_normed_one = grad_normed_one + dot_nt(grad_heads[core][kind], weights[core][kind])
    grad_input, grad_gain_one, grad_shift_one = norm_back(
        grad_normed_one, normal_one, spread_one, gain_one
    )
    grad_input = grad_hidden + grad_input

    grad_vectors = jnp.stack(
        [
            grad_gain_one,
            grad_shift_one,
            jnp.sum(grad_hidden, 0) * scale_one,
            jnp.sum(grad_hidden * branch_one, 0),
            grad_gain_two,
            grad_shift_two,
            jnp.sum(grad_out, 0) * scale_two,
            jnp.sum(grad_out * branch_two, 0),
        ]
    )
    grad_vectors = grad_vectors.reshape(-1, DP, LANES).transpose(1, 0, 2).reshape(DP, -1)
    bias_parts = []
    for core in cores:
        rows = [
            jnp.sum(grad_heads[core][kind].astype(F32), 0).reshape(2, block_width) for kind in (0, 2)
        ]
        for half in (0, 1):
            unit_part = jnp.sum(grad_pre[half, core].astype(F32), 0)
            unit_part = unit_part.reshape(2, half_units, block_width)
            rows += [unit_part[:, at] for at in range(half_units)]
        bias_parts.append(jnp.stack(rows, 1))
    grad_biases = jnp.stack(bias_parts, 1).reshape(MP, -1, DP, bias_width).transpose(0, 2, 1, 3)
    grad_biases = jnp.take(grad_biases, place[:DP], axis=1).reshape(MP, DP, -1)
    sum_small = Chain(small_reduce_steps, grad_vectors, grad_biases)
    send_grad = send_back(grad_input)
    grad_input = meet(grad_input, sum_qkv, sum_small, sum_up[1], sum_out)
    grad_input = meet(grad_input, sum_qkv, sum_small, sum_out, send_grad)
    grad_input = meet(grad_input, sum_qkv, sum_small)
    meet((), sum_small)
    layer_output = spread_image(place, output[:chunk_rows], send_output.result, BF)[:, None]
    input_grad = spread_image(place, grad_input[:chunk_rows], send_grad.result, F32)[:, None]

    small_total = sum_small.result
    vector_grad = small_total[:vector_size].reshape(vectors.shape)
    bias_grad = small_total[vector_size:].reshape(head_biases.shape)
    up_grad = jnp.concatenate(
        [each.result.reshape(depth, half_units, block_width) for each in sum_up], 1
    )
    down_grad = jnp.concatenate(
        [each.result.reshape(depth, half_units, block_width) for each in sum_down], 1
    ).transpose(1, 2, 0)
    grads = (sum_qkv.result, sum_out.result.T, up_grad, down_grad, bias_grad, vector_grad)
    params = (qkv_weight, out_weight, up_weight, down_weight, head_biases, vectors)
    firsts = (qkv_first, out_first, up_first, down_first, bias_first, vector_first)
    seconds = (qkv_second, out_second, up_second, down_second, bias_second, vector_second)
    results = [layer_output, input_grad]
    for slot in range(6):
        results.extend(
            adam_update(params[slot], firsts[slot], seconds[slot], grads[slot], RATES[slot])
        )
    return tuple(results)


def solution(mesh):
    whole_image = mesh.shape["mp"] == MICRO == MP and mesh.shape["dp"] == DP
    return jax.shard_map(
        local_image if whole_image else local_general,
        mesh=mesh,
        in_specs=(
            P(None, "dp", "mp", None),
            P(None, "dp", "mp", None),
            P(None, "dp", "mp"),
            P(None, "dp", "mp"),
            P(None, "dp", "mp"),
            P("mp", "dp"),
            P("mp", "dp"),
            P("mp", "dp"),
            P("dp", None, "mp"),
            P("dp", None, "mp"),
            P("dp", None, "mp"),
            P(None, "mp", "dp"),
            P(None, "mp", "dp"),
            P(None, "mp", "dp"),
            P(None, ("mp", "dp")),
            P(None, ("mp", "dp")),
            P(None, ("mp", "dp")),
            P(None, "dp"),
            P(None, "dp"),
            P(None, "dp"),
        ),
        out_specs=(
            P(None, "dp", "mp", None),
            P(None, "dp", "mp", None),
            P(None, "dp", "mp"),
            P(None, "dp", "mp"),
            P(None, "dp", "mp"),
            P("mp", "dp"),
            P("mp", "dp"),
            P("mp", "dp"),
            P("dp", None, "mp"),
            P("dp", None, "mp"),
            P("dp", None, "mp"),
            P(None, "mp", "dp"),
            P(None, "mp", "dp"),
            P(None, "mp", "dp"),
            P(None, ("mp", "dp")),
            P(None, ("mp", "dp")),
            P(None, ("mp", "dp")),
            P(None, "dp"),
            P(None, "dp"),
            P(None, "dp"),
        ),
        check_vma=False,
    )
```

```python
import functools

import jax
import jax.numpy as jnp
from jax import lax
from jax.experimental import pallas as pl
from jax.experimental.pallas import tpu as pltpu
from jax.sharding import PartitionSpec as P

DH = 64
MICRO = 4
STEP = 10


RATES = (0.05, 0.2, 0.05, 0.03, 0.5, 0.5)


def layer_norm(values, gain, shift):
    center = values - jnp.mean(values, -1, keepdims=True)
    spread = jnp.mean(center * center, -1, keepdims=True)
    return center * lax.rsqrt(spread + 1e-06) * gain + shift


def exact_gelu(values):
    return jax.nn.gelu(values, approximate=False)


def adam_update(weight, first, second, grad, rate):
    first_new = 0.9 * first + 0.1 * grad
    second_new = 0.999 * second + 0.001 * grad * grad
    corrected = first_new / (1.0 - 0.9**STEP)
    scaled = jnp.sqrt(second_new / (1.0 - 0.999**STEP))
    weight_new = weight - rate * (corrected / (scaled + 1e-08) + 0.05 * weight)
    return (weight_new, first_new, second_new)


def attend_forward(queries, key_rows, values, block_rows):
    images, seq_rows, head_count, head_width = queries.shape
    block_count = seq_rows // block_rows
    factor = head_width ** (-0.5)
    query_blocks = jnp.moveaxis(
        queries.reshape(images, block_count, block_rows, head_count, head_width), 1, 0
    )

    def one_block(query_part):
        scores = (
            jnp.einsum("iqhe,ikhe->ihqk", query_part, key_rows, preferred_element_type=jnp.float32)
            * factor
        )
        row_peak = jnp.max(scores, -1, keepdims=True)
        shifted = jnp.exp(scores - row_peak)
        row_total = jnp.sum(shifted, -1, keepdims=True)
        softmax_rows = (shifted / row_total).astype(jnp.bfloat16)
        blended = jnp.einsum(
            "ihqk,ikhe->iqhe", softmax_rows, values, preferred_element_type=jnp.float32
        )
        return (blended, row_peak[..., 0] + jnp.log(row_total[..., 0]))

    blended, log_total = lax.map(one_block, query_blocks)
    blended = jnp.moveaxis(blended, 0, 1).reshape(images, seq_rows, head_count * head_width)
    return (blended.astype(jnp.bfloat16), log_total)


def attend_backward(queries, key_rows, values, grad_blended, log_total, block_rows):
    images, seq_rows, head_count, head_width = queries.shape
    block_count = seq_rows // block_rows
    factor = head_width ** (-0.5)
    split_shape = (images, block_count, block_rows, head_count, head_width)
    query_blocks = jnp.moveaxis(queries.reshape(split_shape), 1, 0)
    grad_blocks = jnp.moveaxis(grad_blended.reshape(split_shape), 1, 0)

    def one_block(carry, inputs_part):
        query_part, grad_part, total_part = inputs_part
        grad_keys, grad_values = carry
        scores = (
            jnp.einsum("iqhe,ikhe->ihqk", query_part, key_rows, preferred_element_type=jnp.float32)
            * factor
        )
        softmax_rows = jnp.exp(scores - total_part[..., None])
        grad_values = grad_values + jnp.einsum(
            "ihqk,iqhe->ikhe",
            softmax_rows.astype(jnp.bfloat16),
            grad_part,
            preferred_element_type=jnp.float32,
        )
        grad_rows = jnp.einsum(
            "iqhe,ikhe->ihqk", grad_part, values, preferred_element_type=jnp.float32
        )
        grad_scores = softmax_rows * (
            grad_rows - jnp.sum(grad_rows * softmax_rows, -1, keepdims=True)
        )
        grad_scores = grad_scores.astype(jnp.bfloat16)
        grad_query = (
            jnp.einsum("ihqk,ikhe->iqhe", grad_scores, key_rows, preferred_element_type=jnp.float32)
            * factor
        )
        grad_keys = (
            grad_keys
            + jnp.einsum(
                "ihqk,iqhe->ikhe", grad_scores, query_part, preferred_element_type=jnp.float32
            )
            * factor
        )
        return ((grad_keys, grad_values), grad_query)

    zero_grad = jnp.zeros(queries.shape, jnp.float32)
    (grad_keys, grad_values), grad_query = lax.scan(
        one_block, (zero_grad, zero_grad), (query_blocks, grad_blocks, log_total)
    )
    flat_shape = (images, seq_rows, head_count * head_width)
    grad_query = jnp.moveaxis(grad_query, 0, 1).reshape(flat_shape)
    stacked = jnp.stack(
        [grad_query, grad_keys.reshape(flat_shape), grad_values.reshape(flat_shape)]
    )
    return stacked.astype(jnp.bfloat16)


def rows_forward(part):
    return lax.all_gather(part, "mp", axis=1, tiled=True)


def rows_sum_forward(part):
    return lax.psum_scatter(part, "mp", scatter_dimension=1, tiled=True)


def rows_backward(part):
    return lax.all_gather(part, "mp", axis=1, tiled=True)


def rows_sum_backward(part):
    return lax.psum_scatter(part, "mp", scatter_dimension=1, tiled=True)


def forward(inputs, params):
    qkv_full, out_full, up_full, down_full, bias_full, vector_full = params
    base = inputs.astype(jnp.float32)
    normed = layer_norm(base, vector_full[0], vector_full[1]).astype(jnp.bfloat16)
    normed_all = rows_forward(normed)
    images, seq_rows = (normed_all.shape[0], normed_all.shape[1])
    head_shape = (images, seq_rows, -1, DH)
    project = jnp.einsum("isd,tde->tise", normed_all, qkv_full, preferred_element_type=jnp.float32)
    queries = (project[0] + bias_full[0]).astype(jnp.bfloat16).reshape(head_shape)
    key_rows = project[1].astype(jnp.bfloat16).reshape(head_shape)
    values = (project[2] + bias_full[1]).astype(jnp.bfloat16).reshape(head_shape)
    blended, log_total = attend_forward(queries, key_rows, values, min(512, seq_rows))
    projected = rows_sum_forward(
        jnp.einsum("ise,ed->isd", blended, out_full, preferred_element_type=jnp.float32)
    )
    branch_one = projected + vector_full[2]
    hidden = base + vector_full[3] * branch_one
    normed_two = layer_norm(hidden, vector_full[4], vector_full[5]).astype(jnp.bfloat16)
    normed_two_all = rows_forward(normed_two)
    pre_act = jnp.einsum(
        "isd,df->isf", normed_two_all, up_full, preferred_element_type=jnp.float32
    ) + bias_full[2:].reshape(-1)
    activ = exact_gelu(pre_act).astype(jnp.bfloat16)
    branch_two = (
        rows_sum_forward(
            jnp.einsum("isf,fd->isd", activ, down_full, preferred_element_type=jnp.float32)
        )
        + vector_full[6]
    )
    output = hidden + vector_full[7] * branch_two
    saved = (
        base,
        hidden,
        branch_one,
        branch_two,
        normed_all,
        queries,
        key_rows,
        values,
        log_total,
        blended,
        normed_two_all,
        pre_act,
        activ,
    )
    return (output.astype(jnp.bfloat16), saved)


def backward(grad_output, saved, params):
    qkv_full, out_full, up_full, down_full, bias_full, vector_full = params
    (
        base,
        hidden,
        branch_one,
        branch_two,
        normed_all,
        queries,
        key_rows,
        values,
        log_total,
        blended,
        normed_two_all,
        pre_act,
        activ,
    ) = saved
    local_width = qkv_full.shape[2]
    grad_out = grad_output.astype(jnp.float32)
    grad_scale_two = jnp.sum(grad_out * branch_two, axis=(0, 1))
    grad_bias_two = jnp.sum(grad_out, axis=(0, 1)) * vector_full[7]
    grad_branch = rows_backward((grad_out * vector_full[7]).astype(jnp.bfloat16))
    grad_down = jnp.einsum("isf,isd->fd", activ, grad_branch, preferred_element_type=jnp.float32)
    grad_activ = jnp.einsum(
        "isd,fd->isf", grad_branch, down_full, preferred_element_type=jnp.float32
    )
    grad_pre = jax.vjp(exact_gelu, pre_act)[1](grad_activ)[0].astype(jnp.bfloat16)
    grad_up_bias = jnp.sum(grad_pre, axis=(0, 1), dtype=jnp.float32)
    grad_up = jnp.einsum(
        "isd,isf->df", normed_two_all, grad_pre, preferred_element_type=jnp.float32
    )
    grad_normed_two = rows_sum_backward(
        jnp.einsum("isf,df->isd", grad_pre, up_full, preferred_element_type=jnp.float32)
    )
    norm_back_two = jax.vjp(layer_norm, hidden, vector_full[4], vector_full[5])[1]
    grad_hidden, grad_gain_two, grad_shift_two = norm_back_two(grad_normed_two)
    grad_hidden = grad_out + grad_hidden
    grad_scale_one = jnp.sum(grad_hidden * branch_one, axis=(0, 1))
    grad_out_bias = jnp.sum(grad_hidden, axis=(0, 1)) * vector_full[3]
    grad_projected = rows_backward((grad_hidden * vector_full[3]).astype(jnp.bfloat16))
    grad_out_weight = jnp.einsum(
        "ise,isd->ed", blended, grad_projected, preferred_element_type=jnp.float32
    )
    grad_blended = jnp.einsum(
        "isd,ed->ise", grad_projected, out_full, preferred_element_type=jnp.float32
    ).astype(jnp.bfloat16)
    grad_project = attend_backward(
        queries, key_rows, values, grad_blended, log_total, min(512, queries.shape[1])
    )
    grad_query_bias = jnp.sum(grad_project[0], axis=(0, 1), dtype=jnp.float32)
    grad_value_bias = jnp.sum(grad_project[2], axis=(0, 1), dtype=jnp.float32)
    grad_qkv = jnp.einsum(
        "isd,tise->tde", normed_all, grad_project, preferred_element_type=jnp.float32
    )
    grad_normed = rows_sum_backward(
        jnp.einsum("tise,tde->isd", grad_project, qkv_full, preferred_element_type=jnp.float32)
    )
    norm_back_one = jax.vjp(layer_norm, base, vector_full[0], vector_full[1])[1]
    grad_input_part, grad_gain_one, grad_shift_one = norm_back_one(grad_normed)
    grad_input = grad_hidden + grad_input_part
    grad_vectors = jnp.stack(
        [
            grad_gain_one,
            grad_shift_one,
            grad_out_bias,
            grad_scale_one,
            grad_gain_two,
            grad_shift_two,
            grad_bias_two,
            grad_scale_two,
        ]
    )
    grad_biases = jnp.concatenate(
        [jnp.stack([grad_query_bias, grad_value_bias]), grad_up_bias.reshape(-1, local_width)], 0
    )
    return (grad_input, (grad_qkv, grad_out_weight, grad_up, grad_down, grad_biases, grad_vectors))


def local_general(
    tokens,
    cotangent,
    qkv_weight,
    qkv_first,
    qkv_second,
    out_weight,
    out_first,
    out_second,
    up_weight,
    up_first,
    up_second,
    down_weight,
    down_first,
    down_second,
    head_biases,
    bias_first,
    bias_second,
    vectors,
    vector_first,
    vector_second,
):

    def gather_params():
        gathered = (
            lax.all_gather(qkv_weight.astype(jnp.bfloat16), "dp", axis=1, tiled=True),
            lax.all_gather(out_weight.astype(jnp.bfloat16), "dp", axis=1, tiled=True),
            lax.all_gather(up_weight.astype(jnp.bfloat16), "dp", axis=0, tiled=True),
            lax.all_gather(down_weight.astype(jnp.bfloat16), "dp", axis=2, tiled=True),
            lax.all_gather(head_biases.astype(jnp.bfloat16), "dp", axis=1, tiled=True),
            lax.all_gather(vectors.astype(jnp.bfloat16), "dp", axis=1, tiled=True),
        )
        qkv_full, out_full, up_full, down_full, bias_full, vector_full = gathered
        return (
            qkv_full,
            out_full,
            up_full.reshape(up_full.shape[0], -1),
            down_full.reshape(-1, down_full.shape[2]),
            bias_full.astype(jnp.float32),
            vector_full.astype(jnp.float32),
        )

    grad_sums = None
    outputs = []
    input_grads = []
    for micro_step in range(MICRO):
        params_fwd = gather_params()
        output, saved = forward(tokens[micro_step], params_fwd)
        outputs.append(output)
        params_back = gather_params()
        grad_input, grads = backward(cotangent[micro_step], saved, params_back)
        input_grads.append(grad_input)
        if grad_sums is None:
            grad_sums = grads
        else:
            grad_sums = tuple((old_sum + new_part for old_sum, new_part in zip(grad_sums, grads)))
    grad_qkv, grad_out_weight, grad_up, grad_down, grad_biases, grad_vectors = grad_sums
    grad_up = grad_up.reshape(-1, up_weight.shape[1], up_weight.shape[2])
    grad_down = grad_down.reshape(down_weight.shape[0], down_weight.shape[1], -1)
    reduced = (
        lax.psum_scatter(grad_qkv, "dp", scatter_dimension=1, tiled=True),
        lax.psum_scatter(grad_out_weight, "dp", scatter_dimension=1, tiled=True),
        lax.psum_scatter(grad_up, "dp", scatter_dimension=0, tiled=True),
        lax.psum_scatter(grad_down, "dp", scatter_dimension=2, tiled=True),
        lax.psum_scatter(grad_biases, "dp", scatter_dimension=1, tiled=True),
        lax.psum_scatter(grad_vectors, "dp", scatter_dimension=1, tiled=True),
    )
    vector_grad = lax.psum(reduced[5], "mp")
    grads = (reduced[0], reduced[1], reduced[2], reduced[3], reduced[4], vector_grad)
    params = (qkv_weight, out_weight, up_weight, down_weight, head_biases, vectors)
    firsts = (qkv_first, out_first, up_first, down_first, bias_first, vector_first)
    seconds = (qkv_second, out_second, up_second, down_second, bias_second, vector_second)
    updated = [
        adam_update(params[slot], firsts[slot], seconds[slot], grads[slot], RATES[slot])
        for slot in range(6)
    ]
    return (
        jnp.stack(outputs),
        jnp.stack(input_grads),
        updated[0][0],
        updated[0][1],
        updated[0][2],
        updated[1][0],
        updated[1][1],
        updated[1][2],
        updated[2][0],
        updated[2][1],
        updated[2][2],
        updated[3][0],
        updated[3][1],
        updated[3][2],
        updated[4][0],
        updated[4][1],
        updated[4][2],
        updated[5][0],
        updated[5][1],
        updated[5][2],
    )


ZS, YS, MP = (4, 2, 4)
DP = ZS * YS
LANES = 128
BF = jnp.bfloat16
F32 = jnp.float32


def swap_z(part, step):
    return lax.ppermute(
        part, "dp", [(z * YS + y, (z ^ step) * YS + y) for z in range(ZS) for y in range(YS)]
    )


def swap_y(part):
    return lax.ppermute(part, "dp", [(each, each ^ 1) for each in range(DP)])


def swap_mp(part, step):
    return lax.ppermute(part, "mp", [(each, each ^ step) for each in range(MP)])


class Chain:
    def __init__(self, steps, *args):
        self.own = None
        self.result = None
        self.steps = steps(self, *args)
        self.flight = next(self.steps)

    def land(self, arrived):
        try:
            self.flight = self.steps.send(arrived)
        except StopIteration as end:
            self.flight = None
            self.result = end.value


def meet(values, *chains):
    values, flights = lax.optimization_barrier((values, [each.flight for each in chains]))
    for each, flight in zip(chains, flights):
        each.land(flight)
    return values


def join(rows, arrived, axis):
    return jnp.concatenate([rows, arrived], -2 if axis == "y" else -1)


def swap_plane(part, axis):
    return swap_y(part) if axis == "y" else swap_mp(part, 2)


def rows_z_steps(chain, shard):
    arrived = yield [swap_z(shard, step) for step in range(1, ZS)]
    return jnp.concatenate([shard] + arrived, 0)


def gather_steps(chain, parts, orders):
    for axes in zip(*orders):
        arrived = yield [swap_plane(part, axis) for part, axis in zip(parts, axes)]
        parts = [join(part, each, axis) for part, each, axis in zip(parts, arrived, axes)]
    chain.own = parts
    arrived = yield [swap_mp(part, 1) for part in parts]
    return arrived


def add_low(first, second):
    return (first.astype(F32) + second.astype(F32)).astype(BF)


def halve(total, axis):
    rows, width = total.shape[-2:]
    if axis == "y":
        return (total[..., : rows // 2, :], total[..., rows // 2 :, :])
    return (total[..., : width // 2], total[..., width // 2 :])


def reduce_steps(chain, other_parts, orders):
    arrived = yield [swap_mp(part, 1) for part in other_parts]
    totals = [add_low(own, each) for own, each in zip(chain.own, arrived)]
    for axes in zip(*orders):
        halves = [halve(total, axis) for total, axis in zip(totals, axes)]
        arrived = yield [swap_plane(half[1], axis) for half, axis in zip(halves, axes)]
        totals = [add_low(half[0], each) for half, each in zip(halves, arrived)]
    return totals


def sum_z_steps(chain, total):
    rows = total.shape[0] // ZS
    arrived = yield [swap_z(total[step * rows : (step + 1) * rows], step) for step in range(1, ZS)]
    total = total[:rows].astype(F32)
    for each in arrived:
        total = total + each.astype(F32)
    return total


def mp_steps(chain, parts):
    arrived = yield [swap_mp(part, step + 1) for step, part in enumerate(parts)]
    return arrived


def small_steps(chain, shard, vector_size):
    arrived = yield [swap_z(shard, step) for step in range(1, ZS)]
    rows = jnp.concatenate([shard] + arrived, 0)
    arrived = yield [swap_y(rows)]
    rows = jnp.concatenate([rows] + arrived, 0)
    arrived = yield [swap_mp(rows[:, vector_size:], step) for step in range(1, MP)]
    return (rows[:, :vector_size], jnp.stack([rows[:, vector_size:]] + arrived, 0))


def small_reduce_steps(chain, vector_part, bias_part):
    packed = [jnp.concatenate([vector_part, each], 1) for each in bias_part]
    arrived = yield [swap_mp(packed[step], step) for step in range(1, MP)]
    total = (packed[0] + arrived[0]) + (arrived[1] + arrived[2])
    arrived = yield [swap_y(total[ZS:])]
    total = total[:ZS] + arrived[0]
    arrived = yield [swap_z(total[step], step) for step in range(1, ZS)]
    total = total[0]
    for each in arrived:
        total = total + each
    return total


def assemble_kernel(place_ref, own_ref, *refs):
    chunk_rows = own_ref.shape[1]
    out_ref = refs[-1]
    out_ref[0:chunk_rows, :] = own_ref[0]
    for at, part_ref in enumerate(refs[:-1]):
        out_ref[(at + 1) * chunk_rows : (at + 2) * chunk_rows, :] = part_ref[...]


def assemble_image(place, arrays, parts):
    chunk_rows, width = parts[0].shape
    return pl.pallas_call(
        assemble_kernel,
        grid_spec=pltpu.PrefetchScalarGridSpec(
            num_scalar_prefetch=1,
            grid=(width // LANES,),
            in_specs=[
                pl.BlockSpec((1, chunk_rows, LANES), lambda j, place_ref: (place_ref[DP], 0, place_ref[j]))
            ]
            + [pl.BlockSpec((chunk_rows, LANES), lambda j, place_ref: (0, place_ref[j]))] * len(parts),
            out_specs=pl.BlockSpec((chunk_rows * MP, LANES), lambda j, place_ref: (0, j)),
        ),
        out_shape=jax.ShapeDtypeStruct((chunk_rows * MP, width), arrays.dtype),
        name="assemble_image",
    )(place, arrays, *parts)


def spread_kernel(place_ref, own_ref, *refs):
    out_ref = refs[-1]
    mine = place_ref[DP]
    out_ref[mine] = own_ref[...].astype(out_ref.dtype)
    for at, part_ref in enumerate(refs[:-1]):
        out_ref[mine ^ (at + 1)] = part_ref[...].astype(out_ref.dtype)


def spread_image(place, own, parts, dtype):
    chunk_rows, width = parts[0].shape
    block = pl.BlockSpec((chunk_rows, LANES), lambda j, place_ref: (0, j))
    return pl.pallas_call(
        spread_kernel,
        grid_spec=pltpu.PrefetchScalarGridSpec(
            num_scalar_prefetch=1,
            grid=(width // LANES,),
            in_specs=[block] * (1 + len(parts)),
            out_specs=pl.BlockSpec((MP, chunk_rows, LANES), lambda j, place_ref: (0, 0, place_ref[j])),
        ),
        out_shape=jax.ShapeDtypeStruct((MP, chunk_rows, width), dtype),
        name="spread_image",
    )(place, own, *parts)


def lane_dot(left, right):
    return lax.dot_general(left, right, (((1,), (1,)), ((), ())), preferred_element_type=F32)


def head_masks(width):
    lane = lax.broadcasted_iota(jnp.int32, (1, width), 1)
    return [lane // DH == head for head in range(width // DH)]


def attend_kernel(block_rows, q_ref, k_ref, v_ref, o_ref, lse_ref):
    masks = head_masks(LANES)
    key_rows = k_ref[...]
    values = v_ref[...]
    zero = jnp.zeros((), BF)
    for block in range(q_ref.shape[0] // block_rows):
        rows = slice(block * block_rows, (block + 1) * block_rows)
        queries = q_ref[rows, :] * jnp.asarray(DH**-0.5, BF)
        blended = []
        for head, mask in enumerate(masks):
            scores = lane_dot(jnp.where(mask, queries, zero), key_rows)
            peak = jnp.max(scores, 1, keepdims=True)
            shifted = jnp.exp(scores - peak)
            total = jnp.sum(shifted, 1, keepdims=True)
            part = jnp.dot(shifted.astype(BF), values, preferred_element_type=F32)
            blended.append(part * (1.0 / total))
            log_total = jnp.broadcast_to(peak + jnp.log(total), (block_rows, LANES))
            lse_ref[0, head : head + 1, rows] = jnp.transpose(log_total)[0:1, :]
        o_ref[rows, :] = jnp.where(masks[0], blended[0], blended[1]).astype(BF)


def attend_back_kernel(
    block_rows, q_ref, k_ref, v_ref, g_ref, lse_ref, out_ref, dk_acc, dv_acc
):
    masks = head_masks(LANES)
    key_rows = k_ref[...]
    values = v_ref[...]
    zero = jnp.zeros((), BF)
    factor = DH**-0.5
    key_heads = [jnp.where(mask, key_rows, zero) for mask in masks]
    for block in range(q_ref.shape[0] // block_rows):
        rows = slice(block * block_rows, (block + 1) * block_rows)
        queries = q_ref[rows, :] * jnp.asarray(factor, BF)
        grads = g_ref[rows, :]
        grad_query = None
        grad_keys = None
        grad_values = None
        for head, mask in enumerate(masks):
            query_head = jnp.where(mask, queries, zero)
            grad_head = jnp.where(mask, grads, zero)
            scores = lane_dot(key_rows, query_head)
            weights = jnp.exp(scores - lse_ref[0, head : head + 1, rows])
            value_part = jnp.dot(weights.astype(BF), grad_head, preferred_element_type=F32)
            grad_rows = lane_dot(values, grad_head)
            delta = jnp.sum(grad_rows * weights, 0, keepdims=True)
            grad_scores = (weights * (grad_rows - delta)).astype(BF)
            key_part = jnp.dot(grad_scores, query_head, preferred_element_type=F32)
            query_part = lax.dot_general(
                grad_scores, key_heads[head], (((0,), (0,)), ((), ())), preferred_element_type=F32
            )
            grad_query = query_part if head == 0 else grad_query + query_part
            grad_keys = key_part if head == 0 else grad_keys + key_part
            grad_values = value_part if head == 0 else grad_values + value_part
        out_ref[rows, 0:LANES] = (grad_query * factor).astype(BF)
        if block == 0:
            dk_acc[...] = grad_keys
            dv_acc[...] = grad_values
        else:
            dk_acc[...] += grad_keys
            dv_acc[...] += grad_values
    out_ref[:, LANES : 2 * LANES] = dk_acc[...].astype(BF)
    out_ref[:, 2 * LANES : 3 * LANES] = dv_acc[...].astype(BF)


def kind_spec(rows, kind):
    return pl.BlockSpec((rows, LANES), lambda p: (0, p * 3 + kind))


def attend(heads):
    rows, width = heads.shape
    pairs = width // LANES // 3
    scores_size = rows * rows * 2 * pairs
    return pl.pallas_call(
        functools.partial(attend_kernel, 256),
        grid=(pairs,),
        in_specs=[kind_spec(rows, kind) for kind in range(3)],
        out_specs=[
            pl.BlockSpec((rows, LANES), lambda p: (0, p)),
            pl.BlockSpec((1, 8, rows), lambda p: (p, 0, 0)),
        ],
        out_shape=[
            jax.ShapeDtypeStruct((rows, pairs * LANES), BF),
            jax.ShapeDtypeStruct((pairs, 8, rows), F32),
        ],
        compiler_params=pltpu.CompilerParams(vmem_limit_bytes=32 * 2**20),
        cost_estimate=pl.CostEstimate(
            flops=scores_size * 2 * 512, bytes_accessed=rows * width * 8, transcendentals=scores_size
        ),
        name="attend",
    )(heads, heads, heads)


def attend_back(heads, grad_blended, log_total):
    rows, width = heads.shape
    pairs = width // LANES // 3
    scores_size = rows * rows * 2 * pairs
    return pl.pallas_call(
        functools.partial(attend_back_kernel, 256),
        grid=(pairs,),
        in_specs=[kind_spec(rows, kind) for kind in range(3)]
        + [
            pl.BlockSpec((rows, LANES), lambda p: (0, p)),
            pl.BlockSpec((1, 8, rows), lambda p: (p, 0, 0)),
        ],
        out_specs=pl.BlockSpec((rows, 3 * LANES), lambda p: (0, p)),
        out_shape=jax.ShapeDtypeStruct((rows, width), BF),
        scratch_shapes=[pltpu.VMEM((rows, LANES), F32)] * 2,
        compiler_params=pltpu.CompilerParams(vmem_limit_bytes=32 * 2**20),
        cost_estimate=pl.CostEstimate(
            flops=scores_size * 2 * 1280, bytes_accessed=rows * width * 14, transcendentals=scores_size
        ),
        name="attend_back",
    )(heads, heads, heads, grad_blended, log_total)


def dot_nn(left, right):
    return lax.dot_general(left, right, (((1,), (0,)), ((), ())), preferred_element_type=F32)


def dot_nt(left, right):
    return lax.dot_general(left, right, (((1,), (1,)), ((), ())), preferred_element_type=F32)


def dot_tn(left, right):
    return lax.dot_general(left, right, (((0,), (0,)), ((), ())), preferred_element_type=F32)


def norm_parts(values):
    center = values - jnp.mean(values, -1, keepdims=True)
    spread = lax.rsqrt(jnp.mean(center * center, -1, keepdims=True) + 1e-06)
    return (center * spread, spread)


def norm_back(grad, normal, spread, gain):
    scaled = grad * gain
    inner = scaled - jnp.mean(scaled, -1, keepdims=True)
    inner = inner - normal * jnp.mean(scaled * normal, -1, keepdims=True)
    return (spread * inner, jnp.sum(grad * normal, 0), jnp.sum(grad, 0))


def gelu_pair(values):
    share = 0.5 * (1.0 + lax.erf(values * 0.7071067811865476))
    slope = share + values * (0.3989422804014327 * jnp.exp(-0.5 * values * values))
    return ((values * share).astype(BF), slope.astype(BF))


def local_image(
    tokens,
    cotangent,
    qkv_weight,
    qkv_first,
    qkv_second,
    out_weight,
    out_first,
    out_second,
    up_weight,
    up_first,
    up_second,
    down_weight,
    down_first,
    down_second,
    head_biases,
    bias_first,
    bias_second,
    vectors,
    vector_first,
    vector_second,
):
    dp_at = lax.axis_index("dp")
    mp_at = lax.axis_index("mp")
    units = up_weight.shape[1]
    half_units = units // 2
    block_width = qkv_weight.shape[2]
    depth = qkv_weight.shape[1]
    bias_width = head_biases.shape[1]
    chunk_rows, width = tokens.shape[2:]
    order = [((zk * YS) + yk) for yk in range(YS) for zk in range(ZS)]
    place = jnp.stack([dp_at ^ each for each in order] + [mp_at]).astype(jnp.int32)
    cores = (0, 1)

    def fetch_image(array):
        chunks = array[:, 0]
        return Chain(
            mp_steps,
            [
                lax.dynamic_index_in_dim(chunks, mp_at ^ step, 0, keepdims=False)
                for step in range(1, MP)
            ],
        )

    def send_back(array):
        low = array.astype(BF)
        return Chain(
            mp_steps, [low[step * chunk_rows : (step + 1) * chunk_rows] for step in range(1, MP)]
        )

    small_shard = jnp.concatenate(
        [vectors.astype(BF).reshape(-1), head_biases.astype(BF).reshape(-1)]
    ).reshape(1, -1)
    vector_size = vectors.size
    kinds = qkv_weight.shape[0]
    qkv_shard = qkv_weight.astype(BF).reshape(kinds, depth, 2, LANES).transpose(1, 2, 0, 3)
    qkv_shard = qkv_shard.reshape(depth, -1)
    rest_shard = jnp.concatenate(
        [
            out_weight.T.astype(BF),
            up_weight.astype(BF).reshape(depth, -1),
            down_weight.transpose(2, 0, 1).astype(BF).reshape(depth, -1),
        ],
        1,
    )
    both = ("xy", "yx")
    small = Chain(small_steps, small_shard, vector_size)
    rows_qkv = Chain(rows_z_steps, qkv_shard)
    fetch_tokens = fetch_image(tokens)
    rest_shard = meet(rest_shard, small, rows_qkv)
    rows_rest = Chain(rows_z_steps, rest_shard)
    get_qkv = Chain(gather_steps, jnp.split(rows_qkv.result, 2, 1), both)
    meet((), small, get_qkv)
    tokens = meet(tokens, small, fetch_tokens, rows_rest)
    out_rows, up_rows, down_rows = jnp.split(
        rows_rest.result, [block_width, block_width * (1 + units)], 1
    )
    get_out = Chain(gather_steps, [jnp.stack(jnp.split(out_rows, 2, 1))], ("yx",))
    get_up = Chain(gather_steps, jnp.split(up_rows, 2, 1), both)

    vector_full, bias_small = small.result
    vector_full = vector_full.reshape(DP, vectors.shape[0], LANES).transpose(1, 0, 2)
    vector_full = vector_full.reshape(vectors.shape[0], width).astype(F32)
    back_places = jnp.stack([((each ^ dp_at) & 1) * ZS + ((each ^ dp_at) >> 1) for each in range(DP)])
    bias_rows = jnp.take(bias_small, back_places, axis=1).reshape(2, 2, DP, -1, bias_width)
    bias_full = bias_rows.transpose(1, 3, 0, 2, 4).reshape(2, head_biases.shape[0], 2, block_width)
    bias_full = bias_full.astype(F32)
    gain_one, shift_one, out_bias, scale_one, gain_two, shift_two, down_bias, scale_two = vector_full

    base = assemble_image(place, tokens[:, 0], fetch_tokens.result).astype(F32)
    normal_one, spread_one = norm_parts(base)
    normed_one = (normal_one * gain_one + shift_one).astype(BF)
    normed_one = meet(normed_one, get_qkv, get_up, get_out)

    def project(core, weights):
        results = []
        for half in (0, 1):
            lanes = slice(half * LANES, (half + 1) * LANES)
            zero = jnp.zeros((2, LANES), F32)
            bias = jnp.stack([bias_full[core, 0, :, lanes], zero, bias_full[core, 1, :, lanes]], 1)
            results.append((dot_nn(normed_one, weights[half]) + bias.reshape(-1)).astype(BF))
        return results

    heads, blended, log_total = ([None, None], [None, None], [None, None])
    heads[0] = project(0, get_qkv.own)
    heads[0] = meet(heads[0], get_qkv, get_out)
    w_qkv = [get_qkv.own, get_qkv.result]
    blended[0], log_total[0] = zip(*[attend(each) for each in heads[0]])
    blended[0], normed_one, down_rows, cotangent = meet(
        (blended[0], normed_one, down_rows, cotangent), get_up, get_out
    )
    get_down = Chain(gather_steps, jnp.split(down_rows, 2, 1), both)
    fetch_cotangent = fetch_image(cotangent)
    heads[1] = project(1, w_qkv[1])
    blended[1], log_total[1] = zip(*[attend(each) for each in heads[1]])
    blended = meet(blended, get_up, get_down)
    w_up = [get_up.own, get_up.result]
    blended = [jnp.concatenate(each, 1) for each in blended]
    w_out = [jnp.concatenate([each[0][0], each[0][1]], 1) for each in (get_out.own, get_out.result)]
    branch_one = dot_nt(jnp.concatenate(blended, 1), jnp.concatenate(w_out, 1)) + out_bias
    hidden = base + scale_one * branch_one
    normal_two, spread_two = norm_parts(hidden)
    normed_two = (normal_two * gain_two + shift_two).astype(BF)
    normed_two = meet(normed_two, fetch_cotangent)
    grad_out = assemble_image(place, cotangent[:, 0], fetch_cotangent.result).astype(F32)
    grad_branch = (grad_out * scale_two).astype(BF)
    parts = [(half, core) for core in (1, 0) for half in (0, 1)]
    activ, slope = ({}, {})
    for half, core in parts:
        rows = bias_full[core, 2 + half * half_units : 2 + (half + 1) * half_units]
        pre_act = dot_nn(normed_two, w_up[core][half]) + rows.transpose(1, 0, 2).reshape(-1)
        activ[half, core], slope[half, core] = gelu_pair(pre_act)
    activ, slope, grad_branch = meet((activ, slope, grad_branch), get_down)

    def reduce_pairs(left, rights):
        chain = Chain(reduce_steps, [dot_tn(left, rights[half, 1]).astype(BF) for half in (0, 1)], both[::-1])
        chain.own = [dot_tn(left, rights[half, 0]).astype(BF) for half in (0, 1)]
        return chain

    sum_down = reduce_pairs(grad_branch, activ)
    grad_branch, activ = meet((grad_branch, activ), sum_down, get_down)
    w_down = [get_down.own, get_down.result]
    branch_two = down_bias
    for half, core in parts:
        branch_two = branch_two + dot_nt(activ[half, core], w_down[core][half])
    output = (hidden + scale_two * branch_two).astype(BF)
    output, grad_branch, slope = meet((output, grad_branch, slope))
    send_output = send_back(output)
    grad_pre = {}
    for half, core in parts:
        grad_activ = dot_nn(grad_branch, w_down[core][half])
        grad_pre[half, core] = (grad_activ * slope[half, core].astype(F32)).astype(BF)
    grad_pre, normed_two = meet((grad_pre, normed_two), sum_down)
    sum_up = reduce_pairs(normed_two, grad_pre)
    grad_normed_two = 0.0
    for half, core in parts:
        grad_normed_two = grad_normed_two + dot_nt(grad_pre[half, core], w_up[core][half])
    grad_hidden, grad_gain_two, grad_shift_two = norm_back(
        grad_normed_two, normal_two, spread_two, gain_two
    )
    grad_hidden = grad_out + grad_hidden
    grad_projected = (grad_hidden * scale_one).astype(BF)
    grad_projected = meet(grad_projected, sum_up, sum_down, send_output)
    rows_down = Chain(sum_z_steps, jnp.concatenate(sum_down.result, 1))
    grad_w_out = [jnp.stack(jnp.split(dot_tn(grad_projected, each).astype(BF), 2, 1)) for each in blended]
    sum_out = Chain(reduce_steps, [grad_w_out[1]], ("xy",))
    sum_out.own = [grad_w_out[0]]
    grad_blended = [jnp.split(dot_nn(grad_projected, each).astype(BF), 2, 1) for each in w_out]
    grad_heads = [[None, None], [None, None]]

    def back_heads(core, half):
        grad_heads[core][half] = attend_back(
            heads[core][half], grad_blended[core][half], log_total[core][half]
        )
        return dot_tn(normed_one, grad_heads[core][half]).astype(BF)

    other = back_heads(1, 0)
    other, grad_blended = meet((other, grad_blended), sum_up, sum_out, rows_down)
    sum_qkv = [Chain(reduce_steps, [other], ("yx",)), None]
    sum_qkv[0].own = [back_heads(0, 0)]
    grad_heads[0][0], grad_blended = meet((grad_heads[0][0], grad_blended), sum_qkv[0], sum_out, sum_up)
    other = back_heads(1, 1)
    other, grad_blended = meet((other, grad_blended), sum_out)
    sum_qkv[1] = Chain(reduce_steps, [other], ("xy",))
    out_rows = jnp.concatenate([sum_out.result[0][0], sum_out.result[0][1]], 1)
    rows_rest = Chain(sum_z_steps, jnp.concatenate(sum_up.result + [out_rows], 1))
    sum_qkv[1].own = [back_heads(0, 1)]
    grad_heads = meet(grad_heads, sum_qkv[0], sum_qkv[1])
    grad_normed_one = 0.0
    for core in cores:
        for half in (0, 1):
            grad_normed_one = grad_normed_one + dot_nt(grad_heads[core][half], w_qkv[core][half])
    grad_input, grad_gain_one, grad_shift_one = norm_back(
        grad_normed_one, normal_one, spread_one, gain_one
    )
    grad_input = grad_hidden + grad_input

    grad_vectors = jnp.stack(
        [
            grad_gain_one,
            grad_shift_one,
            jnp.sum(grad_hidden, 0) * scale_one,
            jnp.sum(grad_hidden * branch_one, 0),
            grad_gain_two,
            grad_shift_two,
            jnp.sum(grad_out, 0) * scale_two,
            jnp.sum(grad_out * branch_two, 0),
        ]
    )
    grad_vectors = grad_vectors.reshape(-1, DP, LANES).transpose(1, 0, 2).reshape(DP, -1)
    bias_parts = []
    for core in cores:
        head_part = [
            jnp.sum(each.astype(F32), 0).reshape(2, kinds, LANES) for each in grad_heads[core]
        ]
        rows = [jnp.concatenate([each[:, kind] for each in head_part], 1) for kind in (0, 2)]
        for half in (0, 1):
            unit_part = jnp.sum(grad_pre[half, core].astype(F32), 0)
            unit_part = unit_part.reshape(2, half_units, block_width)
            rows += [unit_part[:, at] for at in range(half_units)]
        bias_parts.append(jnp.stack(rows, 1))
    grad_biases = jnp.stack(bias_parts, 1).reshape(MP, -1, DP, bias_width).transpose(0, 2, 1, 3)
    grad_biases = jnp.take(grad_biases, place[:DP], axis=1).reshape(MP, DP, -1)
    sum_small = Chain(small_reduce_steps, grad_vectors, grad_biases)
    send_grad = send_back(grad_input)
    meet((), sum_qkv[0], sum_qkv[1], sum_small, rows_rest)
    meet((), sum_qkv[1], sum_small)
    rows_qkv = Chain(sum_z_steps, jnp.concatenate(sum_qkv[0].result + sum_qkv[1].result, 1))
    meet((), rows_qkv, sum_small, send_grad)
    layer_output = spread_image(place, output[:chunk_rows], send_output.result, BF)[:, None]
    input_grad = spread_image(place, grad_input[:chunk_rows], send_grad.result, F32)[:, None]

    small_total = sum_small.result
    vector_grad = small_total[:vector_size].reshape(vectors.shape)
    bias_grad = small_total[vector_size:].reshape(head_biases.shape)
    qkv_grad = rows_qkv.result.reshape(depth, 2, kinds, LANES).transpose(2, 0, 1, 3)
    up_size = block_width * units
    up_grad = rows_rest.result[:, :up_size].reshape(depth, units, block_width)
    down_grad = rows_down.result.reshape(depth, units, block_width).transpose(1, 2, 0)
    grads = (
        qkv_grad.reshape(qkv_weight.shape),
        rows_rest.result[:, up_size:].T,
        up_grad,
        down_grad,
        bias_grad,
        vector_grad,
    )
    params = (qkv_weight, out_weight, up_weight, down_weight, head_biases, vectors)
    firsts = (qkv_first, out_first, up_first, down_first, bias_first, vector_first)
    seconds = (qkv_second, out_second, up_second, down_second, bias_second, vector_second)
    results = [layer_output, input_grad]
    for slot in range(6):
        results.extend(
            adam_update(params[slot], firsts[slot], seconds[slot], grads[slot], RATES[slot])
        )
    return tuple(results)


def solution(mesh):
    whole_image = mesh.shape["mp"] == MICRO == MP and mesh.shape["dp"] == DP
    return jax.shard_map(
        local_image if whole_image else local_general,
        mesh=mesh,
        in_specs=(
            P(None, "dp", "mp", None),
            P(None, "dp", "mp", None),
            P(None, "dp", "mp"),
            P(None, "dp", "mp"),
            P(None, "dp", "mp"),
            P("mp", "dp"),
            P("mp", "dp"),
            P("mp", "dp"),
            P("dp", None, "mp"),
            P("dp", None, "mp"),
            P("dp", None, "mp"),
            P(None, "mp", "dp"),
            P(None, "mp", "dp"),
            P(None, "mp", "dp"),
            P(None, ("mp", "dp")),
            P(None, ("mp", "dp")),
            P(None, ("mp", "dp")),
            P(None, "dp"),
            P(None, "dp"),
            P(None, "dp"),
        ),
        out_specs=(
            P(None, "dp", "mp", None),
            P(None, "dp", "mp", None),
            P(None, "dp", "mp"),
            P(None, "dp", "mp"),
            P(None, "dp", "mp"),
            P("mp", "dp"),
            P("mp", "dp"),
            P("mp", "dp"),
            P("dp", None, "mp"),
            P("dp", None, "mp"),
            P("dp", None, "mp"),
            P(None, "mp", "dp"),
            P(None, "mp", "dp"),
            P(None, "mp", "dp"),
            P(None, ("mp", "dp")),
            P(None, ("mp", "dp")),
            P(None, ("mp", "dp")),
            P(None, "dp"),
            P(None, "dp"),
            P(None, "dp"),
        ),
        check_vma=False,
    )
```

```python
import functools

import jax
import jax.numpy as jnp
from jax import lax
from jax.experimental import pallas as pl
from jax.experimental.pallas import tpu as pltpu
from jax.sharding import PartitionSpec as P

DH = 64
MICRO = 4
STEP = 10


RATES = (0.05, 0.2, 0.05, 0.03, 0.5, 0.5)


def layer_norm(values, gain, shift):
    center = values - jnp.mean(values, -1, keepdims=True)
    spread = jnp.mean(center * center, -1, keepdims=True)
    return center * lax.rsqrt(spread + 1e-06) * gain + shift


def exact_gelu(values):
    return jax.nn.gelu(values, approximate=False)


def adam_update(weight, first, second, grad, rate):
    first_new = 0.9 * first + 0.1 * grad
    second_new = 0.999 * second + 0.001 * grad * grad
    corrected = first_new / (1.0 - 0.9**STEP)
    scaled = jnp.sqrt(second_new / (1.0 - 0.999**STEP))
    weight_new = weight - rate * (corrected / (scaled + 1e-08) + 0.05 * weight)
    return (weight_new, first_new, second_new)


def attend_forward(queries, key_rows, values, block_rows):
    images, seq_rows, head_count, head_width = queries.shape
    block_count = seq_rows // block_rows
    factor = head_width ** (-0.5)
    query_blocks = jnp.moveaxis(
        queries.reshape(images, block_count, block_rows, head_count, head_width), 1, 0
    )

    def one_block(query_part):
        scores = (
            jnp.einsum("iqhe,ikhe->ihqk", query_part, key_rows, preferred_element_type=jnp.float32)
            * factor
        )
        row_peak = jnp.max(scores, -1, keepdims=True)
        shifted = jnp.exp(scores - row_peak)
        row_total = jnp.sum(shifted, -1, keepdims=True)
        softmax_rows = (shifted / row_total).astype(jnp.bfloat16)
        blended = jnp.einsum(
            "ihqk,ikhe->iqhe", softmax_rows, values, preferred_element_type=jnp.float32
        )
        return (blended, row_peak[..., 0] + jnp.log(row_total[..., 0]))

    blended, log_total = lax.map(one_block, query_blocks)
    blended = jnp.moveaxis(blended, 0, 1).reshape(images, seq_rows, head_count * head_width)
    return (blended.astype(jnp.bfloat16), log_total)


def attend_backward(queries, key_rows, values, grad_blended, log_total, block_rows):
    images, seq_rows, head_count, head_width = queries.shape
    block_count = seq_rows // block_rows
    factor = head_width ** (-0.5)
    split_shape = (images, block_count, block_rows, head_count, head_width)
    query_blocks = jnp.moveaxis(queries.reshape(split_shape), 1, 0)
    grad_blocks = jnp.moveaxis(grad_blended.reshape(split_shape), 1, 0)

    def one_block(carry, inputs_part):
        query_part, grad_part, total_part = inputs_part
        grad_keys, grad_values = carry
        scores = (
            jnp.einsum("iqhe,ikhe->ihqk", query_part, key_rows, preferred_element_type=jnp.float32)
            * factor
        )
        softmax_rows = jnp.exp(scores - total_part[..., None])
        grad_values = grad_values + jnp.einsum(
            "ihqk,iqhe->ikhe",
            softmax_rows.astype(jnp.bfloat16),
            grad_part,
            preferred_element_type=jnp.float32,
        )
        grad_rows = jnp.einsum(
            "iqhe,ikhe->ihqk", grad_part, values, preferred_element_type=jnp.float32
        )
        grad_scores = softmax_rows * (
            grad_rows - jnp.sum(grad_rows * softmax_rows, -1, keepdims=True)
        )
        grad_scores = grad_scores.astype(jnp.bfloat16)
        grad_query = (
            jnp.einsum("ihqk,ikhe->iqhe", grad_scores, key_rows, preferred_element_type=jnp.float32)
            * factor
        )
        grad_keys = (
            grad_keys
            + jnp.einsum(
                "ihqk,iqhe->ikhe", grad_scores, query_part, preferred_element_type=jnp.float32
            )
            * factor
        )
        return ((grad_keys, grad_values), grad_query)

    zero_grad = jnp.zeros(queries.shape, jnp.float32)
    (grad_keys, grad_values), grad_query = lax.scan(
        one_block, (zero_grad, zero_grad), (query_blocks, grad_blocks, log_total)
    )
    flat_shape = (images, seq_rows, head_count * head_width)
    grad_query = jnp.moveaxis(grad_query, 0, 1).reshape(flat_shape)
    stacked = jnp.stack(
        [grad_query, grad_keys.reshape(flat_shape), grad_values.reshape(flat_shape)]
    )
    return stacked.astype(jnp.bfloat16)


def rows_forward(part):
    return lax.all_gather(part, "mp", axis=1, tiled=True)


def rows_sum_forward(part):
    return lax.psum_scatter(part, "mp", scatter_dimension=1, tiled=True)


def rows_backward(part):
    return lax.all_gather(part, "mp", axis=1, tiled=True)


def rows_sum_backward(part):
    return lax.psum_scatter(part, "mp", scatter_dimension=1, tiled=True)


def forward(inputs, params):
    qkv_full, out_full, up_full, down_full, bias_full, vector_full = params
    base = inputs.astype(jnp.float32)
    normed = layer_norm(base, vector_full[0], vector_full[1]).astype(jnp.bfloat16)
    normed_all = rows_forward(normed)
    images, seq_rows = (normed_all.shape[0], normed_all.shape[1])
    head_shape = (images, seq_rows, -1, DH)
    project = jnp.einsum("isd,tde->tise", normed_all, qkv_full, preferred_element_type=jnp.float32)
    queries = (project[0] + bias_full[0]).astype(jnp.bfloat16).reshape(head_shape)
    key_rows = project[1].astype(jnp.bfloat16).reshape(head_shape)
    values = (project[2] + bias_full[1]).astype(jnp.bfloat16).reshape(head_shape)
    blended, log_total = attend_forward(queries, key_rows, values, min(512, seq_rows))
    projected = rows_sum_forward(
        jnp.einsum("ise,ed->isd", blended, out_full, preferred_element_type=jnp.float32)
    )
    branch_one = projected + vector_full[2]
    hidden = base + vector_full[3] * branch_one
    normed_two = layer_norm(hidden, vector_full[4], vector_full[5]).astype(jnp.bfloat16)
    normed_two_all = rows_forward(normed_two)
    pre_act = jnp.einsum(
        "isd,df->isf", normed_two_all, up_full, preferred_element_type=jnp.float32
    ) + bias_full[2:].reshape(-1)
    activ = exact_gelu(pre_act).astype(jnp.bfloat16)
    branch_two = (
        rows_sum_forward(
            jnp.einsum("isf,fd->isd", activ, down_full, preferred_element_type=jnp.float32)
        )
        + vector_full[6]
    )
    output = hidden + vector_full[7] * branch_two
    saved = (
        base,
        hidden,
        branch_one,
        branch_two,
        normed_all,
        queries,
        key_rows,
        values,
        log_total,
        blended,
        normed_two_all,
        pre_act,
        activ,
    )
    return (output.astype(jnp.bfloat16), saved)


def backward(grad_output, saved, params):
    qkv_full, out_full, up_full, down_full, bias_full, vector_full = params
    (
        base,
        hidden,
        branch_one,
        branch_two,
        normed_all,
        queries,
        key_rows,
        values,
        log_total,
        blended,
        normed_two_all,
        pre_act,
        activ,
    ) = saved
    local_width = qkv_full.shape[2]
    grad_out = grad_output.astype(jnp.float32)
    grad_scale_two = jnp.sum(grad_out * branch_two, axis=(0, 1))
    grad_bias_two = jnp.sum(grad_out, axis=(0, 1)) * vector_full[7]
    grad_branch = rows_backward((grad_out * vector_full[7]).astype(jnp.bfloat16))
    grad_down = jnp.einsum("isf,isd->fd", activ, grad_branch, preferred_element_type=jnp.float32)
    grad_activ = jnp.einsum(
        "isd,fd->isf", grad_branch, down_full, preferred_element_type=jnp.float32
    )
    grad_pre = jax.vjp(exact_gelu, pre_act)[1](grad_activ)[0].astype(jnp.bfloat16)
    grad_up_bias = jnp.sum(grad_pre, axis=(0, 1), dtype=jnp.float32)
    grad_up = jnp.einsum(
        "isd,isf->df", normed_two_all, grad_pre, preferred_element_type=jnp.float32
    )
    grad_normed_two = rows_sum_backward(
        jnp.einsum("isf,df->isd", grad_pre, up_full, preferred_element_type=jnp.float32)
    )
    norm_back_two = jax.vjp(layer_norm, hidden, vector_full[4], vector_full[5])[1]
    grad_hidden, grad_gain_two, grad_shift_two = norm_back_two(grad_normed_two)
    grad_hidden = grad_out + grad_hidden
    grad_scale_one = jnp.sum(grad_hidden * branch_one, axis=(0, 1))
    grad_out_bias = jnp.sum(grad_hidden, axis=(0, 1)) * vector_full[3]
    grad_projected = rows_backward((grad_hidden * vector_full[3]).astype(jnp.bfloat16))
    grad_out_weight = jnp.einsum(
        "ise,isd->ed", blended, grad_projected, preferred_element_type=jnp.float32
    )
    grad_blended = jnp.einsum(
        "isd,ed->ise", grad_projected, out_full, preferred_element_type=jnp.float32
    ).astype(jnp.bfloat16)
    grad_project = attend_backward(
        queries, key_rows, values, grad_blended, log_total, min(512, queries.shape[1])
    )
    grad_query_bias = jnp.sum(grad_project[0], axis=(0, 1), dtype=jnp.float32)
    grad_value_bias = jnp.sum(grad_project[2], axis=(0, 1), dtype=jnp.float32)
    grad_qkv = jnp.einsum(
        "isd,tise->tde", normed_all, grad_project, preferred_element_type=jnp.float32
    )
    grad_normed = rows_sum_backward(
        jnp.einsum("tise,tde->isd", grad_project, qkv_full, preferred_element_type=jnp.float32)
    )
    norm_back_one = jax.vjp(layer_norm, base, vector_full[0], vector_full[1])[1]
    grad_input_part, grad_gain_one, grad_shift_one = norm_back_one(grad_normed)
    grad_input = grad_hidden + grad_input_part
    grad_vectors = jnp.stack(
        [
            grad_gain_one,
            grad_shift_one,
            grad_out_bias,
            grad_scale_one,
            grad_gain_two,
            grad_shift_two,
            grad_bias_two,
            grad_scale_two,
        ]
    )
    grad_biases = jnp.concatenate(
        [jnp.stack([grad_query_bias, grad_value_bias]), grad_up_bias.reshape(-1, local_width)], 0
    )
    return (grad_input, (grad_qkv, grad_out_weight, grad_up, grad_down, grad_biases, grad_vectors))


def local_general(
    tokens,
    cotangent,
    qkv_weight,
    qkv_first,
    qkv_second,
    out_weight,
    out_first,
    out_second,
    up_weight,
    up_first,
    up_second,
    down_weight,
    down_first,
    down_second,
    head_biases,
    bias_first,
    bias_second,
    vectors,
    vector_first,
    vector_second,
):

    def gather_params():
        gathered = (
            lax.all_gather(qkv_weight.astype(jnp.bfloat16), "dp", axis=1, tiled=True),
            lax.all_gather(out_weight.astype(jnp.bfloat16), "dp", axis=1, tiled=True),
            lax.all_gather(up_weight.astype(jnp.bfloat16), "dp", axis=0, tiled=True),
            lax.all_gather(down_weight.astype(jnp.bfloat16), "dp", axis=2, tiled=True),
            lax.all_gather(head_biases.astype(jnp.bfloat16), "dp", axis=1, tiled=True),
            lax.all_gather(vectors.astype(jnp.bfloat16), "dp", axis=1, tiled=True),
        )
        qkv_full, out_full, up_full, down_full, bias_full, vector_full = gathered
        return (
            qkv_full,
            out_full,
            up_full.reshape(up_full.shape[0], -1),
            down_full.reshape(-1, down_full.shape[2]),
            bias_full.astype(jnp.float32),
            vector_full.astype(jnp.float32),
        )

    grad_sums = None
    outputs = []
    input_grads = []
    for micro_step in range(MICRO):
        params_fwd = gather_params()
        output, saved = forward(tokens[micro_step], params_fwd)
        outputs.append(output)
        params_back = gather_params()
        grad_input, grads = backward(cotangent[micro_step], saved, params_back)
        input_grads.append(grad_input)
        if grad_sums is None:
            grad_sums = grads
        else:
            grad_sums = tuple((old_sum + new_part for old_sum, new_part in zip(grad_sums, grads)))
    grad_qkv, grad_out_weight, grad_up, grad_down, grad_biases, grad_vectors = grad_sums
    grad_up = grad_up.reshape(-1, up_weight.shape[1], up_weight.shape[2])
    grad_down = grad_down.reshape(down_weight.shape[0], down_weight.shape[1], -1)
    reduced = (
        lax.psum_scatter(grad_qkv, "dp", scatter_dimension=1, tiled=True),
        lax.psum_scatter(grad_out_weight, "dp", scatter_dimension=1, tiled=True),
        lax.psum_scatter(grad_up, "dp", scatter_dimension=0, tiled=True),
        lax.psum_scatter(grad_down, "dp", scatter_dimension=2, tiled=True),
        lax.psum_scatter(grad_biases, "dp", scatter_dimension=1, tiled=True),
        lax.psum_scatter(grad_vectors, "dp", scatter_dimension=1, tiled=True),
    )
    vector_grad = lax.psum(reduced[5], "mp")
    grads = (reduced[0], reduced[1], reduced[2], reduced[3], reduced[4], vector_grad)
    params = (qkv_weight, out_weight, up_weight, down_weight, head_biases, vectors)
    firsts = (qkv_first, out_first, up_first, down_first, bias_first, vector_first)
    seconds = (qkv_second, out_second, up_second, down_second, bias_second, vector_second)
    updated = [
        adam_update(params[slot], firsts[slot], seconds[slot], grads[slot], RATES[slot])
        for slot in range(6)
    ]
    return (
        jnp.stack(outputs),
        jnp.stack(input_grads),
        updated[0][0],
        updated[0][1],
        updated[0][2],
        updated[1][0],
        updated[1][1],
        updated[1][2],
        updated[2][0],
        updated[2][1],
        updated[2][2],
        updated[3][0],
        updated[3][1],
        updated[3][2],
        updated[4][0],
        updated[4][1],
        updated[4][2],
        updated[5][0],
        updated[5][1],
        updated[5][2],
    )


ZS, YS, MP = (4, 2, 4)
DP = ZS * YS
LANES = 128
BF = jnp.bfloat16
F32 = jnp.float32


def swap_z(part, step):
    return lax.ppermute(
        part, "dp", [(z * YS + y, (z ^ step) * YS + y) for z in range(ZS) for y in range(YS)]
    )


def swap_y(part):
    return lax.ppermute(part, "dp", [(each, each ^ 1) for each in range(DP)])


def swap_mp(part, step):
    return lax.ppermute(part, "mp", [(each, each ^ step) for each in range(MP)])


class Chain:
    def __init__(self, steps, *args):
        self.own = None
        self.result = None
        self.steps = steps(self, *args)
        self.flight = next(self.steps)

    def land(self, arrived):
        try:
            self.flight = self.steps.send(arrived)
        except StopIteration as end:
            self.flight = None
            self.result = end.value


def meet(values, *chains):
    values, flights = lax.optimization_barrier((values, [each.flight for each in chains]))
    for each, flight in zip(chains, flights):
        each.land(flight)
    return values


def join(rows, arrived, axis):
    return jnp.concatenate([rows, arrived], -2 if axis == "y" else -1)


def swap_plane(part, axis):
    return swap_y(part) if axis == "y" else swap_mp(part, 2)


def rows_z_steps(chain, shard):
    arrived = yield [swap_z(shard, step) for step in range(1, ZS)]
    return jnp.concatenate([shard] + arrived, 0)


def gather_steps(chain, parts, orders):
    for axes in zip(*orders):
        arrived = yield [swap_plane(part, axis) for part, axis in zip(parts, axes)]
        parts = [join(part, each, axis) for part, each, axis in zip(parts, arrived, axes)]
    chain.own = parts
    arrived = yield [swap_mp(part, 1) for part in parts]
    return arrived


def add_low(first, second):
    return (first.astype(F32) + second.astype(F32)).astype(BF)


def halve(total, axis):
    rows, width = total.shape[-2:]
    if axis == "y":
        return (total[..., : rows // 2, :], total[..., rows // 2 :, :])
    return (total[..., : width // 2], total[..., width // 2 :])


def reduce_steps(chain, other_parts, orders):
    arrived = yield [swap_mp(part, 1) for part in other_parts]
    totals = [add_low(own, each) for own, each in zip(chain.own, arrived)]
    for axes in zip(*orders):
        halves = [halve(total, axis) for total, axis in zip(totals, axes)]
        arrived = yield [swap_plane(half[1], axis) for half, axis in zip(halves, axes)]
        totals = [add_low(half[0], each) for half, each in zip(halves, arrived)]
    return totals


def sum_z_steps(chain, total):
    rows = total.shape[0] // ZS
    arrived = yield [swap_z(total[step * rows : (step + 1) * rows], step) for step in range(1, ZS)]
    total = total[:rows].astype(F32)
    for each in arrived:
        total = total + each.astype(F32)
    return total


def mp_steps(chain, parts):
    arrived = yield [swap_mp(part, step + 1) for step, part in enumerate(parts)]
    return arrived


def small_steps(chain, shard, vector_size):
    arrived = yield [swap_z(shard, step) for step in range(1, ZS)]
    rows = jnp.concatenate([shard] + arrived, 0)
    arrived = yield [swap_y(rows)]
    rows = jnp.concatenate([rows] + arrived, 0)
    arrived = yield [swap_mp(rows[:, vector_size:], step) for step in range(1, MP)]
    return (rows[:, :vector_size], jnp.stack([rows[:, vector_size:]] + arrived, 0))


def small_reduce_steps(chain, vector_part, bias_part):
    packed = [jnp.concatenate([vector_part, each], 1) for each in bias_part]
    arrived = yield [swap_mp(packed[step], step) for step in range(1, MP)]
    total = (packed[0] + arrived[0]) + (arrived[1] + arrived[2])
    arrived = yield [swap_y(total[ZS:])]
    total = total[:ZS] + arrived[0]
    arrived = yield [swap_z(total[step], step) for step in range(1, ZS)]
    total = total[0]
    for each in arrived:
        total = total + each
    return total


def norm_parts(values):
    center = values - jnp.mean(values, -1, keepdims=True)
    spread = lax.rsqrt(jnp.mean(center * center, -1, keepdims=True) + 1e-06)
    return (center * spread, spread)


def norm_back(grad, normal, spread, gain):
    scaled = grad * gain
    inner = scaled - jnp.mean(scaled, -1, keepdims=True)
    return spread * (inner - normal * jnp.mean(scaled * normal, -1, keepdims=True))


GAIN_ONE, SHIFT_ONE, OUT_BIAS, SCALE_ONE, GAIN_TWO, SHIFT_TWO, DOWN_BIAS, SCALE_TWO = range(8)


def vector_row(vector_ref, at):
    return vector_ref[at : at + 1, :]


def assemble_kernel(with_norm, place_ref, vector_ref, own_ref, *refs):
    out_ref, second_ref = refs[-2:]
    part_refs = [own_ref.at[0]] + list(refs[:-2])
    for at, part_ref in enumerate(part_refs):
        for block in range(DP):
            lanes = pl.ds(pl.multiple_of(place_ref[block] * LANES, LANES), LANES)
            out_ref[at, :, block * LANES : (block + 1) * LANES] = part_ref[:, lanes]
        values = out_ref[at].astype(F32)
        if with_norm:
            normal, _ = norm_parts(values)
            values = normal * vector_row(vector_ref, GAIN_ONE) + vector_row(vector_ref, SHIFT_ONE)
        else:
            values = values * vector_row(vector_ref, SCALE_TWO)
        second_ref[at] = values.astype(BF)


def assemble_image(place, vector_full, arrays, parts, with_norm):
    chunk_rows, width = parts[0].shape
    rows = chunk_rows // 4
    block = pl.BlockSpec((rows, width), lambda i, place_ref: (i, 0))
    result = pl.BlockSpec((MP, rows, width), lambda i, place_ref: (0, i, 0))
    shape = jax.ShapeDtypeStruct((MP, chunk_rows, width), BF)
    image, second = pl.pallas_call(
        functools.partial(assemble_kernel, with_norm),
        grid_spec=pltpu.PrefetchScalarGridSpec(
            num_scalar_prefetch=1,
            grid=(4,),
            in_specs=[
                pl.BlockSpec(vector_full.shape, lambda i, place_ref: (0, 0)),
                pl.BlockSpec((1, rows, width), lambda i, place_ref: (place_ref[DP], i, 0)),
            ]
            + [block] * len(parts),
            out_specs=[result] * 2,
        ),
        out_shape=[shape] * 2,
        compiler_params=pltpu.CompilerParams(vmem_limit_bytes=32 * 2**20),
        cost_estimate=pl.CostEstimate(
            flops=chunk_rows * width * 40, bytes_accessed=chunk_rows * width * 24, transcendentals=0
        ),
        name="assemble_image",
    )(place, vector_full, arrays, *parts)
    return (image.reshape(-1, width), second.reshape(-1, width))


def spread_kernel(place_ref, own_ref, *refs):
    out_ref = refs[-1]
    mine = place_ref[DP]
    for at, part_ref in enumerate([own_ref] + list(refs[:-1])):
        for block in range(DP):
            lanes = pl.ds(pl.multiple_of(place_ref[block] * LANES, LANES), LANES)
            part = part_ref[:, block * LANES : (block + 1) * LANES]
            out_ref[mine ^ at, :, lanes] = part.astype(out_ref.dtype)


def spread_image(place, own, parts, dtype):
    chunk_rows, width = parts[0].shape
    rows = chunk_rows // 4
    block = pl.BlockSpec((rows, width), lambda i, place_ref: (i, 0))
    return pl.pallas_call(
        spread_kernel,
        grid_spec=pltpu.PrefetchScalarGridSpec(
            num_scalar_prefetch=1,
            grid=(4,),
            in_specs=[block] * (1 + len(parts)),
            out_specs=pl.BlockSpec((MP, rows, width), lambda i, place_ref: (0, i, 0)),
        ),
        out_shape=jax.ShapeDtypeStruct((MP, chunk_rows, width), dtype),
        compiler_params=pltpu.CompilerParams(vmem_limit_bytes=32 * 2**20),
        cost_estimate=pl.CostEstimate(
            flops=chunk_rows * width * 4, bytes_accessed=chunk_rows * width * 20, transcendentals=0
        ),
        name="spread_image",
    )(place, own, *parts)


ROWS = 256


def product_nt(left_refs, right_refs):
    total = None
    for left_ref, right_ref in zip(left_refs, right_refs):
        part = lax.dot_general(
            left_ref[...], right_ref[...], (((1,), (1,)), ((), ())), preferred_element_type=F32
        )
        total = part if total is None else total + part
    return total


def add_rows(sums_ref, rows):
    @pl.when(pl.program_id(0) == 0)
    def _():
        sums_ref[...] = jnp.zeros_like(sums_ref)

    for at, each in enumerate(rows):
        sums_ref[at : at + 1, :] += jnp.sum(each, 0, keepdims=True)


def out_kernel(count, *refs):
    lefts, rights = (refs[:count], refs[count : 2 * count])
    vector_ref, base_ref, branch_ref, hidden_ref, normed_ref = refs[2 * count :]
    branch = product_nt(lefts, rights) + vector_row(vector_ref, OUT_BIAS)
    hidden = base_ref[...].astype(F32) + vector_row(vector_ref, SCALE_ONE) * branch
    normal, _ = norm_parts(hidden)
    branch_ref[...] = branch
    hidden_ref[...] = hidden
    normed = normal * vector_row(vector_ref, GAIN_TWO) + vector_row(vector_ref, SHIFT_TWO)
    normed_ref[...] = normed.astype(BF)


def down_kernel(count, *refs):
    lefts, rights = (refs[:count], refs[count : 2 * count])
    vector_ref, hidden_ref, grad_ref, output_ref, sums_ref = refs[2 * count :]
    branch = product_nt(lefts, rights) + vector_row(vector_ref, DOWN_BIAS)
    output = hidden_ref[...] + vector_row(vector_ref, SCALE_TWO) * branch
    output_ref[...] = output.astype(BF)
    grad = grad_ref[...].astype(F32)
    add_rows(sums_ref, [grad * branch, grad])


def up_back_kernel(count, *refs):
    lefts, rights = (refs[:count], refs[count : 2 * count])
    vector_ref, hidden_ref, branch_ref, grad_ref, out_ref, low_ref, sums_ref = refs[2 * count :]
    grad_normed = product_nt(lefts, rights)
    normal, spread = norm_parts(hidden_ref[...])
    grad = norm_back(grad_normed, normal, spread, vector_row(vector_ref, GAIN_TWO))
    grad = grad + grad_ref[...].astype(F32)
    out_ref[...] = grad
    low_ref[...] = (grad * vector_row(vector_ref, SCALE_ONE)).astype(BF)
    add_rows(sums_ref, [grad_normed * normal, grad_normed, grad * branch_ref[...], grad])


def in_back_kernel(count, *refs):
    lefts, rights = (refs[:count], refs[count : 2 * count])
    vector_ref, base_ref, grad_ref, own_ref, low_ref, sums_ref = refs[2 * count :]
    grad_normed = product_nt(lefts, rights)
    normal, spread = norm_parts(base_ref[...].astype(F32))
    grad = norm_back(grad_normed, normal, spread, vector_row(vector_ref, GAIN_ONE))
    grad = grad + grad_ref[...]
    low_ref[...] = grad.astype(BF)

    @pl.when(pl.program_id(0) == 0)
    def _():
        own_ref[...] = grad

    add_rows(sums_ref, [grad_normed * normal, grad_normed])


def row_call(kernel, name, lefts, rights, vector_full, row_inputs, outs):
    rows, width = row_inputs[0].shape
    once = pl.Buffered(1)
    block = pl.BlockSpec((ROWS, width), lambda i: (i, 0))
    specs = {
        "sums": (pl.BlockSpec((8, width), lambda i: (0, 0)), jax.ShapeDtypeStruct((8, width), F32)),
        "own": (
            pl.BlockSpec((ROWS, width), lambda i: (0, 0)),
            jax.ShapeDtypeStruct((ROWS, width), F32),
        ),
    }
    pairs = [
        specs[each] if isinstance(each, str) else (block, jax.ShapeDtypeStruct((rows, width), each))
        for each in outs
    ]
    depth = sum(each.shape[1] for each in lefts)
    return pl.pallas_call(
        functools.partial(kernel, len(lefts)),
        grid=(rows // ROWS,),
        in_specs=[pl.BlockSpec((ROWS, each.shape[1]), lambda i: (i, 0)) for each in lefts]
        + [pl.BlockSpec(each.shape, lambda i: (0, 0), pipeline_mode=once) for each in rights]
        + [pl.BlockSpec(vector_full.shape, lambda i: (0, 0))]
        + [block] * len(row_inputs),
        out_specs=[each[0] for each in pairs],
        out_shape=[each[1] for each in pairs],
        compiler_params=pltpu.CompilerParams(vmem_limit_bytes=48 * 2**20),
        cost_estimate=pl.CostEstimate(
            flops=2 * rows * width * depth, bytes_accessed=rows * width * 24, transcendentals=0
        ),
        name=name,
    )(*lefts, *rights, vector_full, *row_inputs)


def lane_dot(left, right):
    return lax.dot_general(left, right, (((1,), (1,)), ((), ())), preferred_element_type=F32)


def head_masks(width):
    lane = lax.broadcasted_iota(jnp.int32, (1, width), 1)
    return [lane // DH == head for head in range(width // DH)]


def attend_kernel(block_rows, q_ref, k_ref, v_ref, o_ref, lse_ref):
    masks = head_masks(LANES)
    key_rows = k_ref[...]
    values = v_ref[...]
    zero = jnp.zeros((), BF)
    for block in range(q_ref.shape[0] // block_rows):
        rows = slice(block * block_rows, (block + 1) * block_rows)
        queries = q_ref[rows, :] * jnp.asarray(DH**-0.5, BF)
        blended = []
        for head, mask in enumerate(masks):
            scores = lane_dot(jnp.where(mask, queries, zero), key_rows)
            peak = jnp.max(scores, 1, keepdims=True)
            shifted = jnp.exp(scores - peak)
            total = jnp.sum(shifted, 1, keepdims=True)
            part = jnp.dot(shifted.astype(BF), values, preferred_element_type=F32)
            blended.append(part * (1.0 / total))
            log_total = jnp.broadcast_to(peak + jnp.log(total), (block_rows, LANES))
            lse_ref[0, head : head + 1, rows] = jnp.transpose(log_total)[0:1, :]
        o_ref[rows, :] = jnp.where(masks[0], blended[0], blended[1]).astype(BF)


def attend_back_kernel(
    block_rows, q_ref, k_ref, v_ref, g_ref, lse_ref, out_ref, dk_acc, dv_acc
):
    masks = head_masks(LANES)
    key_rows = k_ref[...]
    values = v_ref[...]
    zero = jnp.zeros((), BF)
    factor = DH**-0.5
    key_heads = [jnp.where(mask, key_rows, zero) for mask in masks]
    for block in range(q_ref.shape[0] // block_rows):
        rows = slice(block * block_rows, (block + 1) * block_rows)
        queries = q_ref[rows, :] * jnp.asarray(factor, BF)
        grads = g_ref[rows, :]
        grad_query = None
        grad_keys = None
        grad_values = None
        for head, mask in enumerate(masks):
            query_head = jnp.where(mask, queries, zero)
            grad_head = jnp.where(mask, grads, zero)
            scores = lane_dot(key_rows, query_head)
            weights = jnp.exp(scores - lse_ref[0, head : head + 1, rows])
            value_part = jnp.dot(weights.astype(BF), grad_head, preferred_element_type=F32)
            grad_rows = lane_dot(values, grad_head)
            delta = jnp.sum(grad_rows * weights, 0, keepdims=True)
            grad_scores = (weights * (grad_rows - delta)).astype(BF)
            key_part = jnp.dot(grad_scores, query_head, preferred_element_type=F32)
            query_part = lax.dot_general(
                grad_scores, key_heads[head], (((0,), (0,)), ((), ())), preferred_element_type=F32
            )
            grad_query = query_part if head == 0 else grad_query + query_part
            grad_keys = key_part if head == 0 else grad_keys + key_part
            grad_values = value_part if head == 0 else grad_values + value_part
        out_ref[rows, 0:LANES] = (grad_query * factor).astype(BF)
        if block == 0:
            dk_acc[...] = grad_keys
            dv_acc[...] = grad_values
        else:
            dk_acc[...] += grad_keys
            dv_acc[...] += grad_values
    out_ref[:, LANES : 2 * LANES] = dk_acc[...].astype(BF)
    out_ref[:, 2 * LANES : 3 * LANES] = dv_acc[...].astype(BF)


def kind_spec(rows, kind):
    return pl.BlockSpec((rows, LANES), lambda p: (0, p * 3 + kind))


def attend(heads):
    rows, width = heads.shape
    pairs = width // LANES // 3
    scores_size = rows * rows * 2 * pairs
    return pl.pallas_call(
        functools.partial(attend_kernel, 256),
        grid=(pairs,),
        in_specs=[kind_spec(rows, kind) for kind in range(3)],
        out_specs=[
            pl.BlockSpec((rows, LANES), lambda p: (0, p)),
            pl.BlockSpec((1, 8, rows), lambda p: (p, 0, 0)),
        ],
        out_shape=[
            jax.ShapeDtypeStruct((rows, pairs * LANES), BF),
            jax.ShapeDtypeStruct((pairs, 8, rows), F32),
        ],
        compiler_params=pltpu.CompilerParams(vmem_limit_bytes=32 * 2**20),
        cost_estimate=pl.CostEstimate(
            flops=scores_size * 2 * 512, bytes_accessed=rows * width * 8, transcendentals=scores_size
        ),
        name="attend",
    )(heads, heads, heads)


def attend_back(heads, grad_blended, log_total):
    rows, width = heads.shape
    pairs = width // LANES // 3
    scores_size = rows * rows * 2 * pairs
    return pl.pallas_call(
        functools.partial(attend_back_kernel, 256),
        grid=(pairs,),
        in_specs=[kind_spec(rows, kind) for kind in range(3)]
        + [
            pl.BlockSpec((rows, LANES), lambda p: (0, p)),
            pl.BlockSpec((1, 8, rows), lambda p: (p, 0, 0)),
        ],
        out_specs=pl.BlockSpec((rows, 3 * LANES), lambda p: (0, p)),
        out_shape=jax.ShapeDtypeStruct((rows, width), BF),
        scratch_shapes=[pltpu.VMEM((rows, LANES), F32)] * 2,
        compiler_params=pltpu.CompilerParams(vmem_limit_bytes=32 * 2**20),
        cost_estimate=pl.CostEstimate(
            flops=scores_size * 2 * 1280, bytes_accessed=rows * width * 14, transcendentals=scores_size
        ),
        name="attend_back",
    )(heads, heads, heads, grad_blended, log_total)


def dot_nn(left, right):
    return lax.dot_general(left, right, (((1,), (0,)), ((), ())), preferred_element_type=F32)


def dot_nt(left, right):
    return lax.dot_general(left, right, (((1,), (1,)), ((), ())), preferred_element_type=F32)


def dot_tn(left, right):
    return lax.dot_general(left, right, (((0,), (0,)), ((), ())), preferred_element_type=F32)


def gelu_pair(values):
    share = 0.5 * (1.0 + lax.erf(values * 0.7071067811865476))
    slope = share + values * (0.3989422804014327 * jnp.exp(-0.5 * values * values))
    return ((values * share).astype(BF), slope.astype(BF))


def local_image(
    tokens,
    cotangent,
    qkv_weight,
    qkv_first,
    qkv_second,
    out_weight,
    out_first,
    out_second,
    up_weight,
    up_first,
    up_second,
    down_weight,
    down_first,
    down_second,
    head_biases,
    bias_first,
    bias_second,
    vectors,
    vector_first,
    vector_second,
):
    dp_at = lax.axis_index("dp")
    mp_at = lax.axis_index("mp")
    units = up_weight.shape[1]
    half_units = units // 2
    block_width = qkv_weight.shape[2]
    depth = qkv_weight.shape[1]
    bias_width = head_biases.shape[1]
    chunk_rows, width = tokens.shape[2:]
    order = [((zk * YS) + yk) for yk in range(YS) for zk in range(ZS)]
    place = jnp.stack([dp_at ^ each for each in order] + [mp_at]).astype(jnp.int32)
    cores = (0, 1)

    def fetch_image(array):
        chunks = array[:, 0]
        return Chain(
            mp_steps,
            [
                lax.dynamic_index_in_dim(chunks, mp_at ^ step, 0, keepdims=False)
                for step in range(1, MP)
            ],
        )

    def send_back(array):
        low = array.astype(BF)
        return Chain(
            mp_steps, [low[step * chunk_rows : (step + 1) * chunk_rows] for step in range(1, MP)]
        )

    small_shard = jnp.concatenate(
        [vectors.astype(BF).reshape(-1), head_biases.astype(BF).reshape(-1)]
    ).reshape(1, -1)
    vector_size = vectors.size
    kinds = qkv_weight.shape[0]
    qkv_shard = qkv_weight.astype(BF).reshape(kinds, depth, 2, LANES).transpose(1, 2, 0, 3)
    qkv_shard = qkv_shard.reshape(depth, -1)
    rest_shard = jnp.concatenate(
        [
            out_weight.T.astype(BF),
            up_weight.astype(BF).reshape(depth, -1),
            down_weight.transpose(2, 0, 1).astype(BF).reshape(depth, -1),
        ],
        1,
    )
    both = ("xy", "yx")
    rows_qkv = [Chain(rows_z_steps, each) for each in jnp.split(qkv_shard, 2, 1)]
    small = Chain(small_steps, small_shard, vector_size)
    fetch_tokens = fetch_image(tokens)
    rest_shard = meet(rest_shard, rows_qkv[0], small)
    get_qkv = [Chain(gather_steps, [rows_qkv[0].result], ("xy",)), None]
    rest_shard = meet(rest_shard, small, rows_qkv[1])
    get_qkv[1] = Chain(gather_steps, [rows_qkv[1].result], ("yx",))
    rows_rest = Chain(rows_z_steps, rest_shard)
    tokens = meet(tokens, small, get_qkv[0], fetch_tokens)

    vector_full, bias_small = small.result
    vector_full = vector_full.reshape(DP, vectors.shape[0], LANES).transpose(1, 0, 2)
    vector_full = vector_full.reshape(vectors.shape[0], width).astype(F32)
    back_places = jnp.stack([((each ^ dp_at) & 1) * ZS + ((each ^ dp_at) >> 1) for each in range(DP)])
    bias_rows = jnp.take(bias_small, back_places, axis=1).reshape(2, 2, DP, -1, bias_width)
    bias_full = bias_rows.transpose(1, 3, 0, 2, 4).reshape(2, head_biases.shape[0], 2, block_width)
    bias_full = bias_full.astype(F32)

    base, normed_one = assemble_image(place, vector_full, tokens[:, 0], fetch_tokens.result, True)
    normed_one = meet(normed_one, *get_qkv, rows_rest)
    out_rows, up_rows, down_rows = jnp.split(
        rows_rest.result, [block_width, block_width * (1 + units)], 1
    )
    get_out = Chain(gather_steps, [jnp.stack(jnp.split(out_rows, 2, 1))], ("yx",))
    get_up = Chain(gather_steps, jnp.split(up_rows, 2, 1), both)

    def project(core, half, weight):
        lanes = slice(half * LANES, (half + 1) * LANES)
        zero = jnp.zeros((2, LANES), F32)
        bias = jnp.stack([bias_full[core, 0, :, lanes], zero, bias_full[core, 1, :, lanes]], 1)
        return (dot_nn(normed_one, weight) + bias.reshape(-1)).astype(BF)

    heads, blended, log_total = ([[None, None], [None, None]] for _ in range(3))

    def forward_heads(core, half):
        blended[core][half], log_total[core][half] = attend(heads[core][half])

    heads[0][0] = project(0, 0, get_qkv[0].own[0])
    forward_heads(0, 0)
    blended[0][0], normed_one = meet((blended[0][0], normed_one), *get_qkv, get_out, get_up)
    heads[0][1] = project(0, 1, get_qkv[1].own[0])
    forward_heads(0, 1)
    blended[0][1], normed_one, down_rows = meet((blended[0][1], normed_one, down_rows), get_qkv[1], get_out)
    w_qkv = [[each.own[0] for each in get_qkv], [each.result[0] for each in get_qkv]]
    get_down = Chain(gather_steps, jnp.split(down_rows, 2, 1), both)
    heads[1][0] = project(1, 0, w_qkv[1][0])
    forward_heads(1, 0)
    blended[1][0], normed_one, cotangent = meet(
        (blended[1][0], normed_one, cotangent), get_up, get_out
    )
    fetch_cotangent = fetch_image(cotangent)
    heads[1][1] = project(1, 1, w_qkv[1][1])
    forward_heads(1, 1)
    blended = meet(blended, get_up, get_down)
    w_up = [get_up.own, get_up.result]
    w_out = [[each[0][half] for half in (0, 1)] for each in (get_out.own, get_out.result)]
    pairs = [(core, half) for core in cores for half in (0, 1)]
    branch_one, hidden, normed_two = row_call(
        out_kernel,
        "out_norm",
        [blended[core][half] for core, half in pairs],
        [w_out[core][half] for core, half in pairs],
        vector_full,
        [base],
        [F32, F32, BF],
    )
    parts = [(half, core) for core in (1, 0) for half in (0, 1)]
    activ, slope = ({}, {})
    for half, core in parts:
        rows = bias_full[core, 2 + half * half_units : 2 + (half + 1) * half_units]
        pre_act = dot_nn(normed_two, w_up[core][half]) + rows.transpose(1, 0, 2).reshape(-1)
        activ[half, core], slope[half, core] = gelu_pair(pre_act)
    activ, slope, cotangent = meet((activ, slope, cotangent), get_down, fetch_cotangent)
    grad_out, grad_branch = assemble_image(
        place, vector_full, cotangent[:, 0], fetch_cotangent.result, False
    )

    def reduce_pairs(left, rights):
        chain = Chain(reduce_steps, [dot_tn(left, rights[half, 1]).astype(BF) for half in (0, 1)], both[::-1])
        chain.own = [dot_tn(left, rights[half, 0]).astype(BF) for half in (0, 1)]
        return chain

    sum_down = reduce_pairs(grad_branch, activ)
    grad_branch, activ = meet((grad_branch, activ), sum_down, get_down)
    w_down = [get_down.own, get_down.result]
    output, sums_two = row_call(
        down_kernel,
        "down_output",
        [activ[each] for each in parts],
        [w_down[core][half] for half, core in parts],
        vector_full,
        [hidden, grad_out],
        [BF, "sums"],
    )
    output, grad_branch, slope = meet((output, grad_branch, slope))
    send_output = send_back(output)
    grad_pre = {}
    for half, core in parts:
        grad_activ = dot_nn(grad_branch, w_down[core][half])
        grad_pre[half, core] = (grad_activ * slope[half, core].astype(F32)).astype(BF)
    grad_pre, normed_two = meet((grad_pre, normed_two), sum_down)
    sum_up = reduce_pairs(normed_two, grad_pre)
    grad_hidden, grad_projected, sums_one = row_call(
        up_back_kernel,
        "up_norm_back",
        [grad_pre[each] for each in parts],
        [w_up[core][half] for half, core in parts],
        vector_full,
        [hidden, branch_one, grad_out],
        [F32, BF, "sums"],
    )
    grad_projected = meet(grad_projected, sum_up, sum_down, send_output)
    rows_down = Chain(sum_z_steps, jnp.concatenate(sum_down.result, 1))
    grad_w_out = [
        jnp.stack([dot_tn(grad_projected, each).astype(BF) for each in blended[core]]) for core in cores
    ]
    sum_out = Chain(reduce_steps, [grad_w_out[1]], ("xy",))
    sum_out.own = [grad_w_out[0]]
    grad_blended = [[dot_nn(grad_projected, each).astype(BF) for each in w_out[core]] for core in cores]
    grad_heads = [[None, None], [None, None]]

    def back_heads(core, half):
        grad_heads[core][half] = attend_back(
            heads[core][half], grad_blended[core][half], log_total[core][half]
        )
        return dot_tn(normed_one, grad_heads[core][half]).astype(BF)

    other = back_heads(1, 0)
    other, grad_blended = meet((other, grad_blended), sum_up, sum_out, rows_down)
    sum_qkv = [Chain(reduce_steps, [other], ("yx",)), None]
    sum_qkv[0].own = [back_heads(0, 0)]
    grad_heads[0][0], grad_blended = meet((grad_heads[0][0], grad_blended), sum_qkv[0], sum_out, sum_up)
    other = back_heads(1, 1)
    other, grad_blended = meet((other, grad_blended), sum_out)
    sum_qkv[1] = Chain(reduce_steps, [other], ("xy",))
    out_rows = jnp.concatenate([sum_out.result[0][0], sum_out.result[0][1]], 1)
    rows_rest = Chain(sum_z_steps, jnp.concatenate(sum_up.result + [out_rows], 1))
    sum_qkv[1].own = [back_heads(0, 1)]
    grad_heads = meet(grad_heads, sum_qkv[0], sum_qkv[1])
    own_grad, grad_input, sums_input = row_call(
        in_back_kernel,
        "in_norm_back",
        [grad_heads[core][half] for core, half in pairs],
        [w_qkv[core][half] for core, half in pairs],
        vector_full,
        [base, grad_hidden],
        ["own", BF, "sums"],
    )

    grad_vectors = jnp.stack(
        [
            sums_input[0],
            sums_input[1],
            sums_one[3] * vector_full[SCALE_ONE],
            sums_one[2],
            sums_one[0],
            sums_one[1],
            sums_two[1] * vector_full[SCALE_TWO],
            sums_two[0],
        ]
    )
    grad_vectors = grad_vectors.reshape(-1, DP, LANES).transpose(1, 0, 2).reshape(DP, -1)
    bias_parts = []
    for core in cores:
        head_part = [
            jnp.sum(each.astype(F32), 0).reshape(2, kinds, LANES) for each in grad_heads[core]
        ]
        rows = [jnp.concatenate([each[:, kind] for each in head_part], 1) for kind in (0, 2)]
        for half in (0, 1):
            unit_part = jnp.sum(grad_pre[half, core].astype(F32), 0)
            unit_part = unit_part.reshape(2, half_units, block_width)
            rows += [unit_part[:, at] for at in range(half_units)]
        bias_parts.append(jnp.stack(rows, 1))
    grad_biases = jnp.stack(bias_parts, 1).reshape(MP, -1, DP, bias_width).transpose(0, 2, 1, 3)
    grad_biases = jnp.take(grad_biases, place[:DP], axis=1).reshape(MP, DP, -1)
    sum_small = Chain(small_reduce_steps, grad_vectors, grad_biases)
    send_grad = send_back(grad_input)
    meet((), sum_qkv[0], sum_qkv[1], sum_small, rows_rest)
    meet((), sum_qkv[1], sum_small)
    rows_qkv = Chain(sum_z_steps, jnp.concatenate(sum_qkv[0].result + sum_qkv[1].result, 1))
    meet((), rows_qkv, sum_small, send_grad)
    layer_output = spread_image(place, output[:chunk_rows], send_output.result, BF)[:, None]
    input_grad = spread_image(place, own_grad, send_grad.result, F32)[:, None]

    small_total = sum_small.result
    vector_grad = small_total[:vector_size].reshape(vectors.shape)
    bias_grad = small_total[vector_size:].reshape(head_biases.shape)
    qkv_grad = rows_qkv.result.reshape(depth, 2, kinds, LANES).transpose(2, 0, 1, 3)
    up_size = block_width * units
    up_grad = rows_rest.result[:, :up_size].reshape(depth, units, block_width)
    down_grad = rows_down.result.reshape(depth, units, block_width).transpose(1, 2, 0)
    grads = (
        qkv_grad.reshape(qkv_weight.shape),
        rows_rest.result[:, up_size:].T,
        up_grad,
        down_grad,
        bias_grad,
        vector_grad,
    )
    params = (qkv_weight, out_weight, up_weight, down_weight, head_biases, vectors)
    firsts = (qkv_first, out_first, up_first, down_first, bias_first, vector_first)
    seconds = (qkv_second, out_second, up_second, down_second, bias_second, vector_second)
    results = [layer_output, input_grad]
    for slot in range(6):
        results.extend(
            adam_update(params[slot], firsts[slot], seconds[slot], grads[slot], RATES[slot])
        )
    return tuple(results)


def solution(mesh):
    whole_image = mesh.shape["mp"] == MICRO == MP and mesh.shape["dp"] == DP
    return jax.shard_map(
        local_image if whole_image else local_general,
        mesh=mesh,
        in_specs=(
            P(None, "dp", "mp", None),
            P(None, "dp", "mp", None),
            P(None, "dp", "mp"),
            P(None, "dp", "mp"),
            P(None, "dp", "mp"),
            P("mp", "dp"),
            P("mp", "dp"),
            P("mp", "dp"),
            P("dp", None, "mp"),
            P("dp", None, "mp"),
            P("dp", None, "mp"),
            P(None, "mp", "dp"),
            P(None, "mp", "dp"),
            P(None, "mp", "dp"),
            P(None, ("mp", "dp")),
            P(None, ("mp", "dp")),
            P(None, ("mp", "dp")),
            P(None, "dp"),
            P(None, "dp"),
            P(None, "dp"),
        ),
        out_specs=(
            P(None, "dp", "mp", None),
            P(None, "dp", "mp", None),
            P(None, "dp", "mp"),
            P(None, "dp", "mp"),
            P(None, "dp", "mp"),
            P("mp", "dp"),
            P("mp", "dp"),
            P("mp", "dp"),
            P("dp", None, "mp"),
            P("dp", None, "mp"),
            P("dp", None, "mp"),
            P(None, "mp", "dp"),
            P(None, "mp", "dp"),
            P(None, "mp", "dp"),
            P(None, ("mp", "dp")),
            P(None, ("mp", "dp")),
            P(None, ("mp", "dp")),
            P(None, "dp"),
            P(None, "dp"),
            P(None, "dp"),
        ),
        check_vma=False,
    )
```

```python
import functools

import jax
import jax.numpy as jnp
from jax import lax
from jax.experimental import pallas as pl
from jax.experimental.pallas import tpu as pltpu
from jax.sharding import PartitionSpec as P

DH = 64
MICRO = 4
STEP = 10


RATES = (0.05, 0.2, 0.05, 0.03, 0.5, 0.5)


def layer_norm(values, gain, shift):
    center = values - jnp.mean(values, -1, keepdims=True)
    spread = jnp.mean(center * center, -1, keepdims=True)
    return center * lax.rsqrt(spread + 1e-06) * gain + shift


def exact_gelu(values):
    return jax.nn.gelu(values, approximate=False)


def adam_update(weight, first, second, grad, rate):
    first_new = 0.9 * first + 0.1 * grad
    second_new = 0.999 * second + 0.001 * grad * grad
    corrected = first_new / (1.0 - 0.9**STEP)
    scaled = jnp.sqrt(second_new / (1.0 - 0.999**STEP))
    weight_new = weight - rate * (corrected / (scaled + 1e-08) + 0.05 * weight)
    return (weight_new, first_new, second_new)


def attend_forward(queries, key_rows, values, block_rows):
    images, seq_rows, head_count, head_width = queries.shape
    block_count = seq_rows // block_rows
    factor = head_width ** (-0.5)
    query_blocks = jnp.moveaxis(
        queries.reshape(images, block_count, block_rows, head_count, head_width), 1, 0
    )

    def one_block(query_part):
        scores = (
            jnp.einsum("iqhe,ikhe->ihqk", query_part, key_rows, preferred_element_type=jnp.float32)
            * factor
        )
        row_peak = jnp.max(scores, -1, keepdims=True)
        shifted = jnp.exp(scores - row_peak)
        row_total = jnp.sum(shifted, -1, keepdims=True)
        softmax_rows = (shifted / row_total).astype(jnp.bfloat16)
        blended = jnp.einsum(
            "ihqk,ikhe->iqhe", softmax_rows, values, preferred_element_type=jnp.float32
        )
        return (blended, row_peak[..., 0] + jnp.log(row_total[..., 0]))

    blended, log_total = lax.map(one_block, query_blocks)
    blended = jnp.moveaxis(blended, 0, 1).reshape(images, seq_rows, head_count * head_width)
    return (blended.astype(jnp.bfloat16), log_total)


def attend_backward(queries, key_rows, values, grad_blended, log_total, block_rows):
    images, seq_rows, head_count, head_width = queries.shape
    block_count = seq_rows // block_rows
    factor = head_width ** (-0.5)
    split_shape = (images, block_count, block_rows, head_count, head_width)
    query_blocks = jnp.moveaxis(queries.reshape(split_shape), 1, 0)
    grad_blocks = jnp.moveaxis(grad_blended.reshape(split_shape), 1, 0)

    def one_block(carry, inputs_part):
        query_part, grad_part, total_part = inputs_part
        grad_keys, grad_values = carry
        scores = (
            jnp.einsum("iqhe,ikhe->ihqk", query_part, key_rows, preferred_element_type=jnp.float32)
            * factor
        )
        softmax_rows = jnp.exp(scores - total_part[..., None])
        grad_values = grad_values + jnp.einsum(
            "ihqk,iqhe->ikhe",
            softmax_rows.astype(jnp.bfloat16),
            grad_part,
            preferred_element_type=jnp.float32,
        )
        grad_rows = jnp.einsum(
            "iqhe,ikhe->ihqk", grad_part, values, preferred_element_type=jnp.float32
        )
        grad_scores = softmax_rows * (
            grad_rows - jnp.sum(grad_rows * softmax_rows, -1, keepdims=True)
        )
        grad_scores = grad_scores.astype(jnp.bfloat16)
        grad_query = (
            jnp.einsum("ihqk,ikhe->iqhe", grad_scores, key_rows, preferred_element_type=jnp.float32)
            * factor
        )
        grad_keys = (
            grad_keys
            + jnp.einsum(
                "ihqk,iqhe->ikhe", grad_scores, query_part, preferred_element_type=jnp.float32
            )
            * factor
        )
        return ((grad_keys, grad_values), grad_query)

    zero_grad = jnp.zeros(queries.shape, jnp.float32)
    (grad_keys, grad_values), grad_query = lax.scan(
        one_block, (zero_grad, zero_grad), (query_blocks, grad_blocks, log_total)
    )
    flat_shape = (images, seq_rows, head_count * head_width)
    grad_query = jnp.moveaxis(grad_query, 0, 1).reshape(flat_shape)
    stacked = jnp.stack(
        [grad_query, grad_keys.reshape(flat_shape), grad_values.reshape(flat_shape)]
    )
    return stacked.astype(jnp.bfloat16)


def rows_forward(part):
    return lax.all_gather(part, "mp", axis=1, tiled=True)


def rows_sum_forward(part):
    return lax.psum_scatter(part, "mp", scatter_dimension=1, tiled=True)


def rows_backward(part):
    return lax.all_gather(part, "mp", axis=1, tiled=True)


def rows_sum_backward(part):
    return lax.psum_scatter(part, "mp", scatter_dimension=1, tiled=True)


def forward(inputs, params):
    qkv_full, out_full, up_full, down_full, bias_full, vector_full = params
    base = inputs.astype(jnp.float32)
    normed = layer_norm(base, vector_full[0], vector_full[1]).astype(jnp.bfloat16)
    normed_all = rows_forward(normed)
    images, seq_rows = (normed_all.shape[0], normed_all.shape[1])
    head_shape = (images, seq_rows, -1, DH)
    project = jnp.einsum("isd,tde->tise", normed_all, qkv_full, preferred_element_type=jnp.float32)
    queries = (project[0] + bias_full[0]).astype(jnp.bfloat16).reshape(head_shape)
    key_rows = project[1].astype(jnp.bfloat16).reshape(head_shape)
    values = (project[2] + bias_full[1]).astype(jnp.bfloat16).reshape(head_shape)
    blended, log_total = attend_forward(queries, key_rows, values, min(512, seq_rows))
    projected = rows_sum_forward(
        jnp.einsum("ise,ed->isd", blended, out_full, preferred_element_type=jnp.float32)
    )
    branch_one = projected + vector_full[2]
    hidden = base + vector_full[3] * branch_one
    normed_two = layer_norm(hidden, vector_full[4], vector_full[5]).astype(jnp.bfloat16)
    normed_two_all = rows_forward(normed_two)
    pre_act = jnp.einsum(
        "isd,df->isf", normed_two_all, up_full, preferred_element_type=jnp.float32
    ) + bias_full[2:].reshape(-1)
    activ = exact_gelu(pre_act).astype(jnp.bfloat16)
    branch_two = (
        rows_sum_forward(
            jnp.einsum("isf,fd->isd", activ, down_full, preferred_element_type=jnp.float32)
        )
        + vector_full[6]
    )
    output = hidden + vector_full[7] * branch_two
    saved = (
        base,
        hidden,
        branch_one,
        branch_two,
        normed_all,
        queries,
        key_rows,
        values,
        log_total,
        blended,
        normed_two_all,
        pre_act,
        activ,
    )
    return (output.astype(jnp.bfloat16), saved)


def backward(grad_output, saved, params):
    qkv_full, out_full, up_full, down_full, bias_full, vector_full = params
    (
        base,
        hidden,
        branch_one,
        branch_two,
        normed_all,
        queries,
        key_rows,
        values,
        log_total,
        blended,
        normed_two_all,
        pre_act,
        activ,
    ) = saved
    local_width = qkv_full.shape[2]
    grad_out = grad_output.astype(jnp.float32)
    grad_scale_two = jnp.sum(grad_out * branch_two, axis=(0, 1))
    grad_bias_two = jnp.sum(grad_out, axis=(0, 1)) * vector_full[7]
    grad_branch = rows_backward((grad_out * vector_full[7]).astype(jnp.bfloat16))
    grad_down = jnp.einsum("isf,isd->fd", activ, grad_branch, preferred_element_type=jnp.float32)
    grad_activ = jnp.einsum(
        "isd,fd->isf", grad_branch, down_full, preferred_element_type=jnp.float32
    )
    grad_pre = jax.vjp(exact_gelu, pre_act)[1](grad_activ)[0].astype(jnp.bfloat16)
    grad_up_bias = jnp.sum(grad_pre, axis=(0, 1), dtype=jnp.float32)
    grad_up = jnp.einsum(
        "isd,isf->df", normed_two_all, grad_pre, preferred_element_type=jnp.float32
    )
    grad_normed_two = rows_sum_backward(
        jnp.einsum("isf,df->isd", grad_pre, up_full, preferred_element_type=jnp.float32)
    )
    norm_back_two = jax.vjp(layer_norm, hidden, vector_full[4], vector_full[5])[1]
    grad_hidden, grad_gain_two, grad_shift_two = norm_back_two(grad_normed_two)
    grad_hidden = grad_out + grad_hidden
    grad_scale_one = jnp.sum(grad_hidden * branch_one, axis=(0, 1))
    grad_out_bias = jnp.sum(grad_hidden, axis=(0, 1)) * vector_full[3]
    grad_projected = rows_backward((grad_hidden * vector_full[3]).astype(jnp.bfloat16))
    grad_out_weight = jnp.einsum(
        "ise,isd->ed", blended, grad_projected, preferred_element_type=jnp.float32
    )
    grad_blended = jnp.einsum(
        "isd,ed->ise", grad_projected, out_full, preferred_element_type=jnp.float32
    ).astype(jnp.bfloat16)
    grad_project = attend_backward(
        queries, key_rows, values, grad_blended, log_total, min(512, queries.shape[1])
    )
    grad_query_bias = jnp.sum(grad_project[0], axis=(0, 1), dtype=jnp.float32)
    grad_value_bias = jnp.sum(grad_project[2], axis=(0, 1), dtype=jnp.float32)
    grad_qkv = jnp.einsum(
        "isd,tise->tde", normed_all, grad_project, preferred_element_type=jnp.float32
    )
    grad_normed = rows_sum_backward(
        jnp.einsum("tise,tde->isd", grad_project, qkv_full, preferred_element_type=jnp.float32)
    )
    norm_back_one = jax.vjp(layer_norm, base, vector_full[0], vector_full[1])[1]
    grad_input_part, grad_gain_one, grad_shift_one = norm_back_one(grad_normed)
    grad_input = grad_hidden + grad_input_part
    grad_vectors = jnp.stack(
        [
            grad_gain_one,
            grad_shift_one,
            grad_out_bias,
            grad_scale_one,
            grad_gain_two,
            grad_shift_two,
            grad_bias_two,
            grad_scale_two,
        ]
    )
    grad_biases = jnp.concatenate(
        [jnp.stack([grad_query_bias, grad_value_bias]), grad_up_bias.reshape(-1, local_width)], 0
    )
    return (grad_input, (grad_qkv, grad_out_weight, grad_up, grad_down, grad_biases, grad_vectors))


def local_general(
    tokens,
    cotangent,
    qkv_weight,
    qkv_first,
    qkv_second,
    out_weight,
    out_first,
    out_second,
    up_weight,
    up_first,
    up_second,
    down_weight,
    down_first,
    down_second,
    head_biases,
    bias_first,
    bias_second,
    vectors,
    vector_first,
    vector_second,
):

    def gather_params():
        gathered = (
            lax.all_gather(qkv_weight.astype(jnp.bfloat16), "dp", axis=1, tiled=True),
            lax.all_gather(out_weight.astype(jnp.bfloat16), "dp", axis=1, tiled=True),
            lax.all_gather(up_weight.astype(jnp.bfloat16), "dp", axis=0, tiled=True),
            lax.all_gather(down_weight.astype(jnp.bfloat16), "dp", axis=2, tiled=True),
            lax.all_gather(head_biases.astype(jnp.bfloat16), "dp", axis=1, tiled=True),
            lax.all_gather(vectors.astype(jnp.bfloat16), "dp", axis=1, tiled=True),
        )
        qkv_full, out_full, up_full, down_full, bias_full, vector_full = gathered
        return (
            qkv_full,
            out_full,
            up_full.reshape(up_full.shape[0], -1),
            down_full.reshape(-1, down_full.shape[2]),
            bias_full.astype(jnp.float32),
            vector_full.astype(jnp.float32),
        )

    grad_sums = None
    outputs = []
    input_grads = []
    for micro_step in range(MICRO):
        params_fwd = gather_params()
        output, saved = forward(tokens[micro_step], params_fwd)
        outputs.append(output)
        params_back = gather_params()
        grad_input, grads = backward(cotangent[micro_step], saved, params_back)
        input_grads.append(grad_input)
        if grad_sums is None:
            grad_sums = grads
        else:
            grad_sums = tuple((old_sum + new_part for old_sum, new_part in zip(grad_sums, grads)))
    grad_qkv, grad_out_weight, grad_up, grad_down, grad_biases, grad_vectors = grad_sums
    grad_up = grad_up.reshape(-1, up_weight.shape[1], up_weight.shape[2])
    grad_down = grad_down.reshape(down_weight.shape[0], down_weight.shape[1], -1)
    reduced = (
        lax.psum_scatter(grad_qkv, "dp", scatter_dimension=1, tiled=True),
        lax.psum_scatter(grad_out_weight, "dp", scatter_dimension=1, tiled=True),
        lax.psum_scatter(grad_up, "dp", scatter_dimension=0, tiled=True),
        lax.psum_scatter(grad_down, "dp", scatter_dimension=2, tiled=True),
        lax.psum_scatter(grad_biases, "dp", scatter_dimension=1, tiled=True),
        lax.psum_scatter(grad_vectors, "dp", scatter_dimension=1, tiled=True),
    )
    vector_grad = lax.psum(reduced[5], "mp")
    grads = (reduced[0], reduced[1], reduced[2], reduced[3], reduced[4], vector_grad)
    params = (qkv_weight, out_weight, up_weight, down_weight, head_biases, vectors)
    firsts = (qkv_first, out_first, up_first, down_first, bias_first, vector_first)
    seconds = (qkv_second, out_second, up_second, down_second, bias_second, vector_second)
    updated = [
        adam_update(params[slot], firsts[slot], seconds[slot], grads[slot], RATES[slot])
        for slot in range(6)
    ]
    return (
        jnp.stack(outputs),
        jnp.stack(input_grads),
        updated[0][0],
        updated[0][1],
        updated[0][2],
        updated[1][0],
        updated[1][1],
        updated[1][2],
        updated[2][0],
        updated[2][1],
        updated[2][2],
        updated[3][0],
        updated[3][1],
        updated[3][2],
        updated[4][0],
        updated[4][1],
        updated[4][2],
        updated[5][0],
        updated[5][1],
        updated[5][2],
    )


ZS, YS, MP = (4, 2, 4)
DP = ZS * YS
LANES = 128
BF = jnp.bfloat16
F32 = jnp.float32


def swap_z(part, step):
    return lax.ppermute(
        part, "dp", [(z * YS + y, (z ^ step) * YS + y) for z in range(ZS) for y in range(YS)]
    )


def swap_y(part):
    return lax.ppermute(part, "dp", [(each, each ^ 1) for each in range(DP)])


def swap_mp(part, step):
    return lax.ppermute(part, "mp", [(each, each ^ step) for each in range(MP)])


class Chain:
    def __init__(self, steps, *args):
        self.own = None
        self.result = None
        self.steps = steps(self, *args)
        self.flight = next(self.steps)

    def land(self, arrived):
        try:
            self.flight = self.steps.send(arrived)
        except StopIteration as end:
            self.flight = None
            self.result = end.value


def meet(values, *chains):
    values, flights = lax.optimization_barrier((values, [each.flight for each in chains]))
    for each, flight in zip(chains, flights):
        each.land(flight)
    return values


def join(rows, arrived, axis):
    return jnp.concatenate([rows, arrived], -2 if axis == "y" else -1)


def swap_plane(part, axis):
    return swap_y(part) if axis == "y" else swap_mp(part, 2)


def rows_z_steps(chain, shard):
    arrived = yield [swap_z(shard, step) for step in range(1, ZS)]
    return jnp.concatenate([shard] + arrived, 0)


def gather_steps(chain, parts, orders):
    for axes in zip(*orders):
        arrived = yield [swap_plane(part, axis) for part, axis in zip(parts, axes)]
        parts = [join(part, each, axis) for part, each, axis in zip(parts, arrived, axes)]
    chain.own = parts
    arrived = yield [swap_mp(part, 1) for part in parts]
    return arrived


def add_low(first, second):
    return (first.astype(F32) + second.astype(F32)).astype(BF)


def halve(total, axis):
    rows, width = total.shape[-2:]
    if axis == "y":
        return (total[..., : rows // 2, :], total[..., rows // 2 :, :])
    return (total[..., : width // 2], total[..., width // 2 :])


def reduce_steps(chain, other_parts, orders):
    arrived = yield [swap_mp(part, 1) for part in other_parts]
    totals = [add_low(own, each) for own, each in zip(chain.own, arrived)]
    for axes in zip(*orders):
        halves = [halve(total, axis) for total, axis in zip(totals, axes)]
        arrived = yield [swap_plane(half[1], axis) for half, axis in zip(halves, axes)]
        totals = [add_low(half[0], each) for half, each in zip(halves, arrived)]
    return totals


def sum_z_steps(chain, total):
    rows = total.shape[0] // ZS
    arrived = yield [swap_z(total[step * rows : (step + 1) * rows], step) for step in range(1, ZS)]
    total = total[:rows].astype(F32)
    for each in arrived:
        total = total + each.astype(F32)
    return total


def mp_steps(chain, parts, first=1):
    arrived = yield [swap_mp(part, step + first) for step, part in enumerate(parts)]
    return arrived


def small_steps(chain, shard, vector_size):
    biases = shard[:, vector_size:]
    arrived = yield [swap_mp(biases, step) for step in range(1, MP)]
    rows = jnp.concatenate([shard] + arrived, 1)
    arrived = yield [swap_z(rows, step) for step in range(1, ZS)]
    rows = jnp.concatenate([rows] + arrived, 0)
    arrived = yield [swap_y(rows)]
    rows = jnp.concatenate([rows] + arrived, 0)
    biases = rows[:, vector_size:].reshape(DP, MP, -1).transpose(1, 0, 2)
    return (rows[:, :vector_size], biases)


def small_reduce_steps(chain, vector_part, bias_part):
    packed = [jnp.concatenate([vector_part, each], 1) for each in bias_part]
    arrived = yield [swap_mp(packed[step], step) for step in range(1, MP)]
    total = (packed[0] + arrived[0]) + (arrived[1] + arrived[2])
    arrived = yield [swap_y(total[ZS:])]
    total = total[:ZS] + arrived[0]
    arrived = yield [swap_z(total[step], step) for step in range(1, ZS)]
    total = total[0]
    for each in arrived:
        total = total + each
    return total


def norm_parts(values):
    center = values - jnp.mean(values, -1, keepdims=True)
    spread = lax.rsqrt(jnp.mean(center * center, -1, keepdims=True) + 1e-06)
    return (center * spread, spread)


def norm_back(grad, normal, spread, gain):
    scaled = grad * gain
    inner = scaled - jnp.mean(scaled, -1, keepdims=True)
    return spread * (inner - normal * jnp.mean(scaled * normal, -1, keepdims=True))


GAIN_ONE, SHIFT_ONE, OUT_BIAS, SCALE_ONE, GAIN_TWO, SHIFT_TWO, DOWN_BIAS, SCALE_TWO = range(8)


def vector_row(vector_ref, at):
    return vector_ref[at : at + 1, :]


def assemble_kernel(with_norm, place_ref, vector_ref, own_ref, *refs):
    out_ref, second_ref = refs[-2:]
    part_refs = [own_ref.at[0]] + list(refs[:-2])
    for at, part_ref in enumerate(part_refs):
        for block in range(DP):
            lanes = pl.ds(pl.multiple_of(place_ref[block] * LANES, LANES), LANES)
            out_ref[at, :, block * LANES : (block + 1) * LANES] = part_ref[:, lanes]
        values = out_ref[at].astype(F32)
        if with_norm:
            normal, _ = norm_parts(values)
            values = normal * vector_row(vector_ref, GAIN_ONE) + vector_row(vector_ref, SHIFT_ONE)
        else:
            values = values * vector_row(vector_ref, SCALE_TWO)
        second_ref[at] = values.astype(BF)


def assemble_image(place, vector_full, arrays, parts, with_norm):
    chunk_rows, width = parts[0].shape
    rows = chunk_rows // 4
    block = pl.BlockSpec((rows, width), lambda i, place_ref: (i, 0))
    result = pl.BlockSpec((MP, rows, width), lambda i, place_ref: (0, i, 0))
    shape = jax.ShapeDtypeStruct((MP, chunk_rows, width), BF)
    image, second = pl.pallas_call(
        functools.partial(assemble_kernel, with_norm),
        grid_spec=pltpu.PrefetchScalarGridSpec(
            num_scalar_prefetch=1,
            grid=(4,),
            in_specs=[
                pl.BlockSpec(vector_full.shape, lambda i, place_ref: (0, 0)),
                pl.BlockSpec((1, rows, width), lambda i, place_ref: (place_ref[DP], i, 0)),
            ]
            + [block] * len(parts),
            out_specs=[result] * 2,
        ),
        out_shape=[shape] * 2,
        compiler_params=pltpu.CompilerParams(vmem_limit_bytes=32 * 2**20),
        cost_estimate=pl.CostEstimate(
            flops=chunk_rows * width * 40, bytes_accessed=chunk_rows * width * 24, transcendentals=0
        ),
        name="assemble_image",
    )(place, vector_full, arrays, *parts)
    return (image.reshape(-1, width), second.reshape(-1, width))


def spread_kernel(place_ref, own_ref, *refs):
    out_ref = refs[-1]
    mine = place_ref[DP]
    for at, part_ref in enumerate([own_ref] + list(refs[:-1])):
        for block in range(DP):
            lanes = pl.ds(pl.multiple_of(place_ref[block] * LANES, LANES), LANES)
            part = part_ref[:, block * LANES : (block + 1) * LANES]
            out_ref[mine ^ at, :, lanes] = part.astype(out_ref.dtype)


def spread_image(place, own, parts, dtype):
    chunk_rows, width = parts[0].shape
    rows = chunk_rows // 4
    block = pl.BlockSpec((rows, width), lambda i, place_ref: (i, 0))
    return pl.pallas_call(
        spread_kernel,
        grid_spec=pltpu.PrefetchScalarGridSpec(
            num_scalar_prefetch=1,
            grid=(4,),
            in_specs=[block] * (1 + len(parts)),
            out_specs=pl.BlockSpec((MP, rows, width), lambda i, place_ref: (0, i, 0)),
        ),
        out_shape=jax.ShapeDtypeStruct((MP, chunk_rows, width), dtype),
        compiler_params=pltpu.CompilerParams(vmem_limit_bytes=32 * 2**20),
        cost_estimate=pl.CostEstimate(
            flops=chunk_rows * width * 4, bytes_accessed=chunk_rows * width * 20, transcendentals=0
        ),
        name="spread_image",
    )(place, own, *parts)


ROWS = 512


def product_nt(left_refs, right_refs):
    total = None
    for left_ref, right_ref in zip(left_refs, right_refs):
        part = lax.dot_general(
            left_ref[...], right_ref[...], (((1,), (1,)), ((), ())), preferred_element_type=F32
        )
        total = part if total is None else total + part
    return total


def add_rows(sums_ref, rows):
    @pl.when(pl.program_id(0) == 0)
    def _():
        sums_ref[...] = jnp.zeros_like(sums_ref)

    for at, each in enumerate(rows):
        sums_ref[at : at + 1, :] += jnp.sum(each, 0, keepdims=True)


def out_kernel(count, *refs):
    lefts, rights = (refs[:count], refs[count : 2 * count])
    vector_ref, base_ref, branch_ref, hidden_ref, normed_ref = refs[2 * count :]
    branch = product_nt(lefts, rights) + vector_row(vector_ref, OUT_BIAS)
    hidden = base_ref[...].astype(F32) + vector_row(vector_ref, SCALE_ONE) * branch
    normal, _ = norm_parts(hidden)
    branch_ref[...] = branch
    hidden_ref[...] = hidden
    normed = normal * vector_row(vector_ref, GAIN_TWO) + vector_row(vector_ref, SHIFT_TWO)
    normed_ref[...] = normed.astype(BF)


def down_kernel(count, *refs):
    lefts, rights = (refs[:count], refs[count : 2 * count])
    vector_ref, hidden_ref, grad_ref, output_ref, sums_ref = refs[2 * count :]
    branch = product_nt(lefts, rights) + vector_row(vector_ref, DOWN_BIAS)
    output = hidden_ref[...] + vector_row(vector_ref, SCALE_TWO) * branch
    output_ref[...] = output.astype(BF)
    grad = grad_ref[...].astype(F32)
    add_rows(sums_ref, [grad * branch, grad])


def up_back_kernel(count, *refs):
    lefts, rights = (refs[:count], refs[count : 2 * count])
    vector_ref, hidden_ref, branch_ref, grad_ref, out_ref, low_ref, sums_ref = refs[2 * count :]
    grad_normed = product_nt(lefts, rights)
    normal, spread = norm_parts(hidden_ref[...])
    grad = norm_back(grad_normed, normal, spread, vector_row(vector_ref, GAIN_TWO))
    grad = grad + grad_ref[...].astype(F32)
    out_ref[...] = grad
    low_ref[...] = (grad * vector_row(vector_ref, SCALE_ONE)).astype(BF)
    add_rows(sums_ref, [grad_normed * normal, grad_normed, grad * branch_ref[...], grad])


def in_back_kernel(count, *refs):
    lefts, rights = (refs[:count], refs[count : 2 * count])
    vector_ref, base_ref, grad_ref, low_ref, sums_ref = refs[2 * count : 2 * count + 5]
    grad_normed = product_nt(lefts, rights)
    normal, spread = norm_parts(base_ref[...].astype(F32))
    grad = norm_back(grad_normed, normal, spread, vector_row(vector_ref, GAIN_ONE))
    grad = grad + grad_ref[...]
    low_ref[...] = grad.astype(BF)

    for own_ref in refs[2 * count + 5 :]:
        own_ref[...] = grad[: own_ref.shape[0]]
    add_rows(sums_ref, [grad_normed * normal, grad_normed])


def expand_kernel(left_ref, right_ref, bias_ref, activ_ref, slope_ref):
    values = jnp.dot(left_ref[...], right_ref[...], preferred_element_type=F32) + bias_ref[0:1, :]
    share = 0.5 * (1.0 + lax.erf(values * 0.7071067811865476))
    activ_ref[...] = (values * share).astype(BF)
    slope = share + values * (0.3989422804014327 * jnp.exp(-0.5 * values * values))
    slope_ref[...] = slope.astype(BF)


def expand(left, right, bias):
    rows, depth = left.shape
    width = right.shape[1]
    block = pl.BlockSpec((256, width), lambda i: (i, 0))
    return pl.pallas_call(
        expand_kernel,
        grid=(rows // 256,),
        in_specs=[
            pl.BlockSpec((256, depth), lambda i: (i, 0)),
            pl.BlockSpec((depth, width), lambda i: (0, 0), pipeline_mode=pl.Buffered(1)),
            pl.BlockSpec((1, width), lambda i: (0, 0)),
        ],
        out_specs=[block] * 2,
        out_shape=[jax.ShapeDtypeStruct((rows, width), BF)] * 2,
        compiler_params=pltpu.CompilerParams(vmem_limit_bytes=32 * 2**20),
        cost_estimate=pl.CostEstimate(
            flops=2 * rows * width * depth, bytes_accessed=rows * width * 8, transcendentals=rows * width
        ),
        name="expand",
    )(left, right, bias.reshape(1, width))


def row_call(kernel, name, lefts, rights, vector_full, row_inputs, outs, span=None, own_rows=0):
    rows, width = row_inputs[0].shape
    first, count = span or (0, rows // ROWS)
    rows = count * ROWS
    once = pl.Buffered(1)
    block = pl.BlockSpec((ROWS, width), lambda i: (i, 0))
    source = pl.BlockSpec((ROWS, width), lambda i: (i + first, 0))
    specs = {
        "sums": (pl.BlockSpec((8, width), lambda i: (0, 0)), jax.ShapeDtypeStruct((8, width), F32)),
        "own": (
            pl.BlockSpec((own_rows, width), lambda i: (0, 0)),
            jax.ShapeDtypeStruct((own_rows, width), F32),
        ),
    }
    pairs = [
        specs[each] if isinstance(each, str) else (block, jax.ShapeDtypeStruct((rows, width), each))
        for each in outs
    ]
    depth = sum(each.shape[1] for each in lefts)
    return pl.pallas_call(
        functools.partial(kernel, len(lefts)),
        grid=(count,),
        in_specs=[pl.BlockSpec((ROWS, each.shape[1]), lambda i: (i + first, 0)) for each in lefts]
        + [pl.BlockSpec(each.shape, lambda i: (0, 0), pipeline_mode=once) for each in rights]
        + [pl.BlockSpec(vector_full.shape, lambda i: (0, 0))]
        + [source] * len(row_inputs),
        out_specs=[each[0] for each in pairs],
        out_shape=[each[1] for each in pairs],
        compiler_params=pltpu.CompilerParams(vmem_limit_bytes=48 * 2**20),
        cost_estimate=None
        if span
        else pl.CostEstimate(
            flops=2 * rows * width * depth, bytes_accessed=rows * width * 24, transcendentals=0
        ),
        name=name,
    )(*lefts, *rights, vector_full, *row_inputs)


def lane_dot(left, right):
    return lax.dot_general(left, right, (((1,), (1,)), ((), ())), preferred_element_type=F32)


def head_masks(width):
    lane = lax.broadcasted_iota(jnp.int32, (1, width), 1)
    return [lane // DH == head for head in range(width // DH)]


def attend_kernel(block_rows, q_ref, k_ref, v_ref, o_ref, lse_ref):
    masks = head_masks(LANES)
    key_rows = k_ref[...]
    values = v_ref[...]
    zero = jnp.zeros((), BF)
    for block in range(q_ref.shape[0] // block_rows):
        rows = slice(block * block_rows, (block + 1) * block_rows)
        queries = q_ref[rows, :] * jnp.asarray(DH**-0.5, BF)
        blended = []
        for head, mask in enumerate(masks):
            scores = lane_dot(jnp.where(mask, queries, zero), key_rows)
            peak = jnp.max(scores, 1, keepdims=True)
            shifted = jnp.exp(scores - peak)
            total = jnp.sum(shifted, 1, keepdims=True)
            part = jnp.dot(shifted.astype(BF), values, preferred_element_type=F32)
            blended.append(part * (1.0 / total))
            log_total = jnp.broadcast_to(peak + jnp.log(total), (block_rows, LANES))
            lse_ref[0, head : head + 1, rows] = jnp.transpose(log_total)[0:1, :]
        o_ref[rows, :] = jnp.where(masks[0], blended[0], blended[1]).astype(BF)


def attend_back_kernel(
    block_rows, q_ref, k_ref, v_ref, g_ref, lse_ref, out_ref, dk_acc, dv_acc
):
    masks = head_masks(LANES)
    key_rows = k_ref[...]
    values = v_ref[...]
    zero = jnp.zeros((), BF)
    factor = DH**-0.5
    key_heads = [jnp.where(mask, key_rows, zero) for mask in masks]
    for block in range(q_ref.shape[0] // block_rows):
        rows = slice(block * block_rows, (block + 1) * block_rows)
        queries = q_ref[rows, :] * jnp.asarray(factor, BF)
        grads = g_ref[rows, :]
        grad_query = None
        grad_keys = None
        grad_values = None
        for head, mask in enumerate(masks):
            query_head = jnp.where(mask, queries, zero)
            grad_head = jnp.where(mask, grads, zero)
            scores = lane_dot(key_rows, query_head)
            weights = jnp.exp(scores - lse_ref[0, head : head + 1, rows])
            value_part = jnp.dot(weights.astype(BF), grad_head, preferred_element_type=F32)
            grad_rows = lane_dot(values, grad_head)
            delta = jnp.sum(grad_rows * weights, 0, keepdims=True)
            grad_scores = (weights * (grad_rows - delta)).astype(BF)
            key_part = jnp.dot(grad_scores, query_head, preferred_element_type=F32)
            query_part = lax.dot_general(
                grad_scores, key_heads[head], (((0,), (0,)), ((), ())), preferred_element_type=F32
            )
            grad_query = query_part if head == 0 else grad_query + query_part
            grad_keys = key_part if head == 0 else grad_keys + key_part
            grad_values = value_part if head == 0 else grad_values + value_part
        out_ref[rows, 0:LANES] = (grad_query * factor).astype(BF)
        if block == 0:
            dk_acc[...] = grad_keys
            dv_acc[...] = grad_values
        else:
            dk_acc[...] += grad_keys
            dv_acc[...] += grad_values
    out_ref[:, LANES : 2 * LANES] = dk_acc[...].astype(BF)
    out_ref[:, 2 * LANES : 3 * LANES] = dv_acc[...].astype(BF)


def kind_spec(rows, kind):
    return pl.BlockSpec((rows, LANES), lambda p: (0, p * 3 + kind))


def attend(heads):
    rows, width = heads.shape
    pairs = width // LANES // 3
    scores_size = rows * rows * 2 * pairs
    return pl.pallas_call(
        functools.partial(attend_kernel, 256),
        grid=(pairs,),
        in_specs=[kind_spec(rows, kind) for kind in range(3)],
        out_specs=[
            pl.BlockSpec((rows, LANES), lambda p: (0, p)),
            pl.BlockSpec((1, 8, rows), lambda p: (p, 0, 0)),
        ],
        out_shape=[
            jax.ShapeDtypeStruct((rows, pairs * LANES), BF),
            jax.ShapeDtypeStruct((pairs, 8, rows), F32),
        ],
        compiler_params=pltpu.CompilerParams(vmem_limit_bytes=32 * 2**20),
        cost_estimate=pl.CostEstimate(
            flops=scores_size * 2 * 512, bytes_accessed=rows * width * 8, transcendentals=scores_size
        ),
        name="attend",
    )(heads, heads, heads)


def attend_back(heads, grad_blended, log_total):
    rows, width = heads.shape
    pairs = width // LANES // 3
    scores_size = rows * rows * 2 * pairs
    return pl.pallas_call(
        functools.partial(attend_back_kernel, 256),
        grid=(pairs,),
        in_specs=[kind_spec(rows, kind) for kind in range(3)]
        + [
            pl.BlockSpec((rows, LANES), lambda p: (0, p)),
            pl.BlockSpec((1, 8, rows), lambda p: (p, 0, 0)),
        ],
        out_specs=pl.BlockSpec((rows, 3 * LANES), lambda p: (0, p)),
        out_shape=jax.ShapeDtypeStruct((rows, width), BF),
        scratch_shapes=[pltpu.VMEM((rows, LANES), F32)] * 2,
        compiler_params=pltpu.CompilerParams(vmem_limit_bytes=32 * 2**20),
        cost_estimate=pl.CostEstimate(
            flops=scores_size * 2 * 1280, bytes_accessed=rows * width * 14, transcendentals=scores_size
        ),
        name="attend_back",
    )(heads, heads, heads, grad_blended, log_total)


def dot_nn(left, right):
    return lax.dot_general(left, right, (((1,), (0,)), ((), ())), preferred_element_type=F32)


def dot_nt(left, right):
    return lax.dot_general(left, right, (((1,), (1,)), ((), ())), preferred_element_type=F32)


def dot_tn(left, right):
    return lax.dot_general(left, right, (((0,), (0,)), ((), ())), preferred_element_type=F32)


def local_image(
    tokens,
    cotangent,
    qkv_weight,
    qkv_first,
    qkv_second,
    out_weight,
    out_first,
    out_second,
    up_weight,
    up_first,
    up_second,
    down_weight,
    down_first,
    down_second,
    head_biases,
    bias_first,
    bias_second,
    vectors,
    vector_first,
    vector_second,
):
    dp_at = lax.axis_index("dp")
    mp_at = lax.axis_index("mp")
    units = up_weight.shape[1]
    half_units = units // 2
    block_width = qkv_weight.shape[2]
    depth = qkv_weight.shape[1]
    bias_width = head_biases.shape[1]
    chunk_rows, width = tokens.shape[2:]
    order = [((zk * YS) + yk) for yk in range(YS) for zk in range(ZS)]
    place = jnp.stack([dp_at ^ each for each in order] + [mp_at]).astype(jnp.int32)
    cores = (0, 1)

    def fetch_image(array):
        chunks = array[:, 0]
        return Chain(
            mp_steps,
            [
                lax.dynamic_index_in_dim(chunks, mp_at ^ step, 0, keepdims=False)
                for step in range(1, MP)
            ],
        )

    def send_back(array):
        low = array.astype(BF)
        return Chain(
            mp_steps, [low[step * chunk_rows : (step + 1) * chunk_rows] for step in range(1, MP)]
        )

    small_shard = jnp.concatenate(
        [vectors.astype(BF).reshape(-1), head_biases.astype(BF).reshape(-1)]
    ).reshape(1, -1)
    vector_size = vectors.size
    kinds = qkv_weight.shape[0]
    qkv_shard = qkv_weight.astype(BF).reshape(kinds, depth, 2, LANES).transpose(1, 2, 0, 3)
    qkv_shard = qkv_shard.reshape(depth, -1)
    rest_shard = jnp.concatenate(
        [
            out_weight.T.astype(BF),
            up_weight.astype(BF).reshape(depth, -1),
            down_weight.transpose(2, 0, 1).astype(BF).reshape(depth, -1),
        ],
        1,
    )
    both = ("xy", "yx")
    rows_qkv = [Chain(rows_z_steps, each) for each in jnp.split(qkv_shard, 2, 1)]
    small = Chain(small_steps, small_shard, vector_size)
    fetch_tokens = fetch_image(tokens)
    rest_shard = meet(rest_shard, rows_qkv[0], small)
    get_qkv = [Chain(gather_steps, [rows_qkv[0].result], ("yx",)), None]
    rest_shard = meet(rest_shard, small, rows_qkv[1])
    get_qkv[1] = Chain(gather_steps, [rows_qkv[1].result], ("xy",))
    rows_rest = Chain(rows_z_steps, rest_shard)
    tokens = meet(tokens, small, get_qkv[0], fetch_tokens)

    vector_full, bias_small = small.result
    vector_full = vector_full.reshape(DP, vectors.shape[0], LANES).transpose(1, 0, 2)
    vector_full = vector_full.reshape(vectors.shape[0], width).astype(F32)
    back_places = jnp.stack([((each ^ dp_at) & 1) * ZS + ((each ^ dp_at) >> 1) for each in range(DP)])
    bias_rows = jnp.take(bias_small, back_places, axis=1).reshape(2, 2, DP, -1, bias_width)
    bias_full = bias_rows.transpose(1, 3, 0, 2, 4).reshape(2, head_biases.shape[0], 2, block_width)
    bias_full = bias_full.astype(F32)

    base, normed_one = assemble_image(place, vector_full, tokens[:, 0], fetch_tokens.result, True)
    normed_one = meet(normed_one, *get_qkv)

    def project(core, half, weight):
        lanes = slice(half * LANES, (half + 1) * LANES)
        zero = jnp.zeros((2, LANES), F32)
        bias = jnp.stack([bias_full[core, 0, :, lanes], zero, bias_full[core, 1, :, lanes]], 1)
        return (dot_nn(normed_one, weight) + bias.reshape(-1)).astype(BF)

    heads, blended, log_total = ([[None, None], [None, None]] for _ in range(3))

    def forward_heads(core, half):
        blended[core][half], log_total[core][half] = attend(heads[core][half])

    heads[0][0] = project(0, 0, get_qkv[0].own[0])
    forward_heads(0, 0)
    blended[0][0], normed_one = meet((blended[0][0], normed_one), *get_qkv, rows_rest)
    out_rows, up_rows, down_rows = jnp.split(
        rows_rest.result, [block_width, block_width * (1 + units)], 1
    )
    get_out = Chain(gather_steps, [jnp.stack(jnp.split(out_rows, 2, 1))], ("yx",))
    get_up = Chain(gather_steps, jnp.split(up_rows, 2, 1), both)
    heads[0][1] = project(0, 1, get_qkv[1].own[0])
    forward_heads(0, 1)
    blended[0][1], normed_one, down_rows = meet(
        (blended[0][1], normed_one, down_rows), get_qkv[1], get_out, get_up
    )
    w_qkv = [[each.own[0] for each in get_qkv], [each.result[0] for each in get_qkv]]
    get_down = Chain(gather_steps, jnp.split(down_rows, 2, 1), both)
    heads[1][0] = project(1, 0, w_qkv[1][0])
    forward_heads(1, 0)
    blended[1][0], normed_one, cotangent = meet(
        (blended[1][0], normed_one, cotangent), get_up, get_out
    )
    fetch_cotangent = fetch_image(cotangent)
    heads[1][1] = project(1, 1, w_qkv[1][1])
    forward_heads(1, 1)
    blended = meet(blended, get_up, get_out, get_down)
    w_up = [get_up.own, get_up.result]
    w_out = [[each[0][half] for half in (0, 1)] for each in (get_out.own, get_out.result)]
    pairs = [(core, half) for core in cores for half in (0, 1)]
    branch_one, hidden, normed_two = row_call(
        out_kernel,
        "out_norm",
        [blended[core][half] for core, half in pairs],
        [w_out[core][half] for core, half in pairs],
        vector_full,
        [base],
        [F32, F32, BF],
    )
    parts = [(half, core) for core in (1, 0) for half in (0, 1)]
    activ, slope = ({}, {})
    for half, core in parts:
        rows = bias_full[core, 2 + half * half_units : 2 + (half + 1) * half_units]
        unit_bias = rows.transpose(1, 0, 2).reshape(-1)
        activ[half, core], slope[half, core] = expand(normed_two, w_up[core][half], unit_bias)
        if (half, core) == (0, 0):
            activ, normed_two = meet((activ, normed_two), get_down)
    activ, slope, cotangent = meet((activ, slope, cotangent), fetch_cotangent)
    grad_out, grad_branch = assemble_image(
        place, vector_full, cotangent[:, 0], fetch_cotangent.result, False
    )

    def reduce_pairs(left, rights):
        chain = Chain(reduce_steps, [dot_tn(left, rights[half, 1]).astype(BF) for half in (0, 1)], both[::-1])
        chain.own = [dot_tn(left, rights[half, 0]).astype(BF) for half in (0, 1)]
        return chain

    sum_down = reduce_pairs(grad_branch, activ)
    grad_branch, activ = meet((grad_branch, activ), sum_down, get_down)
    w_down = [get_down.own, get_down.result]
    output, sums_two = row_call(
        down_kernel,
        "down_output",
        [activ[each] for each in parts],
        [w_down[core][half] for half, core in parts],
        vector_full,
        [hidden, grad_out],
        [BF, "sums"],
    )
    output, grad_branch, slope = meet((output, grad_branch, slope))
    send_output = send_back(output)
    grad_pre = {}
    for half, core in parts:
        grad_activ = dot_nn(grad_branch, w_down[core][half])
        grad_pre[half, core] = (grad_activ * slope[half, core].astype(F32)).astype(BF)
    grad_pre, normed_two = meet((grad_pre, normed_two))
    sum_up = reduce_pairs(normed_two, grad_pre)
    grad_hidden, grad_projected, sums_one = row_call(
        up_back_kernel,
        "up_norm_back",
        [grad_pre[each] for each in parts],
        [w_up[core][half] for half, core in parts],
        vector_full,
        [hidden, branch_one, grad_out],
        [F32, BF, "sums"],
    )
    grad_projected = meet(grad_projected, sum_up, sum_down, send_output)
    grad_w_out = [
        jnp.stack([dot_tn(grad_projected, each).astype(BF) for each in blended[core]]) for core in cores
    ]
    sum_out = Chain(reduce_steps, [grad_w_out[1]], ("xy",))
    sum_out.own = [grad_w_out[0]]
    grad_blended = [[dot_nn(grad_projected, each).astype(BF) for each in w_out[core]] for core in cores]
    grad_heads = [[None, None], [None, None]]

    def back_heads(core, half):
        grad_heads[core][half] = attend_back(
            heads[core][half], grad_blended[core][half], log_total[core][half]
        )
        return dot_tn(normed_one, grad_heads[core][half]).astype(BF)

    other = back_heads(1, 0)
    other, grad_blended = meet((other, grad_blended), sum_up, sum_out, sum_down)
    sum_qkv = [Chain(reduce_steps, [other], ("xy",)), None]
    sum_qkv[0].own = [back_heads(0, 0)]
    grad_heads[0][0], grad_blended = meet((grad_heads[0][0], grad_blended), sum_qkv[0], sum_out, sum_up)
    other = back_heads(1, 1)
    other, grad_blended = meet((other, grad_blended), sum_out, sum_qkv[0])
    sum_qkv[1] = Chain(reduce_steps, [other], ("yx",))
    out_rows = jnp.concatenate([sum_out.result[0][0], sum_out.result[0][1]], 1)
    rows_rest = Chain(sum_z_steps, jnp.concatenate(sum_up.result + sum_down.result + [out_rows], 1))
    sum_qkv[1].own = [back_heads(0, 1)]
    grad_heads = meet(grad_heads, sum_qkv[0], sum_qkv[1])

    def input_back(span, outs):
        return row_call(
            in_back_kernel,
            "in_norm_back",
            [grad_heads[core][half] for core, half in pairs],
            [w_qkv[core][half] for core, half in pairs],
            vector_full,
            [base, grad_hidden],
            outs,
            span,
            chunk_rows,
        )

    grad_far, sums_far = input_back((1, 1), [BF, "sums"])
    send_far = Chain(mp_steps, [grad_far[:chunk_rows], grad_far[chunk_rows:]], 2)
    grad_heads = meet(grad_heads, sum_qkv[1])
    grad_near, sums_near, own_grad = input_back((0, 1), [BF, "sums", "own"])
    send_near = Chain(mp_steps, [grad_near[chunk_rows:]], 1)
    sums_input = sums_far + sums_near

    grad_vectors = jnp.stack(
        [
            sums_input[0],
            sums_input[1],
            sums_one[3] * vector_full[SCALE_ONE],
            sums_one[2],
            sums_one[0],
            sums_one[1],
            sums_two[1] * vector_full[SCALE_TWO],
            sums_two[0],
        ]
    )
    grad_vectors = grad_vectors.reshape(-1, DP, LANES).transpose(1, 0, 2).reshape(DP, -1)
    bias_parts = []
    for core in cores:
        head_part = [
            jnp.sum(each.astype(F32), 0).reshape(2, kinds, LANES) for each in grad_heads[core]
        ]
        rows = [jnp.concatenate([each[:, kind] for each in head_part], 1) for kind in (0, 2)]
        for half in (0, 1):
            unit_part = jnp.sum(grad_pre[half, core].astype(F32), 0)
            unit_part = unit_part.reshape(2, half_units, block_width)
            rows += [unit_part[:, at] for at in range(half_units)]
        bias_parts.append(jnp.stack(rows, 1))
    grad_biases = jnp.stack(bias_parts, 1).reshape(MP, -1, DP, bias_width).transpose(0, 2, 1, 3)
    grad_biases = jnp.take(grad_biases, place[:DP], axis=1).reshape(MP, DP, -1)
    sum_small = Chain(small_reduce_steps, grad_vectors, grad_biases)
    meet((), sum_qkv[1])
    rows_qkv = Chain(sum_z_steps, jnp.concatenate(sum_qkv[0].result + sum_qkv[1].result, 1))
    meet((), send_far)
    meet((), rows_rest)
    meet((), rows_qkv)
    meet((), send_near)
    for _ in range(3):
        meet((), sum_small)
    layer_output = spread_image(place, output[:chunk_rows], send_output.result, BF)[:, None]
    input_grad = spread_image(place, own_grad, send_near.result + send_far.result, F32)[:, None]

    small_total = sum_small.result
    vector_grad = small_total[:vector_size].reshape(vectors.shape)
    bias_grad = small_total[vector_size:].reshape(head_biases.shape)
    qkv_grad = rows_qkv.result.reshape(depth, 2, kinds, LANES).transpose(2, 0, 1, 3)
    up_size = block_width * units
    up_grad = rows_rest.result[:, :up_size].reshape(depth, units, block_width)
    down_grad = rows_rest.result[:, up_size : 2 * up_size].reshape(depth, units, block_width).transpose(1, 2, 0)
    grads = (
        qkv_grad.reshape(qkv_weight.shape),
        rows_rest.result[:, 2 * up_size :].T,
        up_grad,
        down_grad,
        bias_grad,
        vector_grad,
    )
    params = (qkv_weight, out_weight, up_weight, down_weight, head_biases, vectors)
    firsts = (qkv_first, out_first, up_first, down_first, bias_first, vector_first)
    seconds = (qkv_second, out_second, up_second, down_second, bias_second, vector_second)
    results = [layer_output, input_grad]
    for slot in range(6):
        results.extend(
            adam_update(params[slot], firsts[slot], seconds[slot], grads[slot], RATES[slot])
        )
    return tuple(results)


def solution(mesh):
    whole_image = mesh.shape["mp"] == MICRO == MP and mesh.shape["dp"] == DP
    return jax.shard_map(
        local_image if whole_image else local_general,
        mesh=mesh,
        in_specs=(
            P(None, "dp", "mp", None),
            P(None, "dp", "mp", None),
            P(None, "dp", "mp"),
            P(None, "dp", "mp"),
            P(None, "dp", "mp"),
            P("mp", "dp"),
            P("mp", "dp"),
            P("mp", "dp"),
            P("dp", None, "mp"),
            P("dp", None, "mp"),
            P("dp", None, "mp"),
            P(None, "mp", "dp"),
            P(None, "mp", "dp"),
            P(None, "mp", "dp"),
            P(None, ("mp", "dp")),
            P(None, ("mp", "dp")),
            P(None, ("mp", "dp")),
            P(None, "dp"),
            P(None, "dp"),
            P(None, "dp"),
        ),
        out_specs=(
            P(None, "dp", "mp", None),
            P(None, "dp", "mp", None),
            P(None, "dp", "mp"),
            P(None, "dp", "mp"),
            P(None, "dp", "mp"),
            P("mp", "dp"),
            P("mp", "dp"),
            P("mp", "dp"),
            P("dp", None, "mp"),
            P("dp", None, "mp"),
            P("dp", None, "mp"),
            P(None, "mp", "dp"),
            P(None, "mp", "dp"),
            P(None, "mp", "dp"),
            P(None, ("mp", "dp")),
            P(None, ("mp", "dp")),
            P(None, ("mp", "dp")),
            P(None, "dp"),
            P(None, "dp"),
            P(None, "dp"),
        ),
        check_vma=False,
    )
```

```python
import functools

import jax
import jax.numpy as jnp
from jax import lax
from jax.experimental import pallas as pl
from jax.experimental.pallas import tpu as pltpu
from jax.sharding import PartitionSpec as P

DH = 64
MICRO = 4
STEP = 10


RATES = (0.05, 0.2, 0.05, 0.03, 0.5, 0.5)


def layer_norm(values, gain, shift):
    center = values - jnp.mean(values, -1, keepdims=True)
    spread = jnp.mean(center * center, -1, keepdims=True)
    return center * lax.rsqrt(spread + 1e-06) * gain + shift


def exact_gelu(values):
    return jax.nn.gelu(values, approximate=False)


def adam_update(weight, first, second, grad, rate):
    first_new = 0.9 * first + 0.1 * grad
    second_new = 0.999 * second + 0.001 * grad * grad
    corrected = first_new / (1.0 - 0.9**STEP)
    scaled = jnp.sqrt(second_new / (1.0 - 0.999**STEP))
    weight_new = weight - rate * (corrected / (scaled + 1e-08) + 0.05 * weight)
    return (weight_new, first_new, second_new)


def attend_forward(queries, key_rows, values, block_rows):
    images, seq_rows, head_count, head_width = queries.shape
    block_count = seq_rows // block_rows
    factor = head_width ** (-0.5)
    query_blocks = jnp.moveaxis(
        queries.reshape(images, block_count, block_rows, head_count, head_width), 1, 0
    )

    def one_block(query_part):
        scores = (
            jnp.einsum("iqhe,ikhe->ihqk", query_part, key_rows, preferred_element_type=jnp.float32)
            * factor
        )
        row_peak = jnp.max(scores, -1, keepdims=True)
        shifted = jnp.exp(scores - row_peak)
        row_total = jnp.sum(shifted, -1, keepdims=True)
        softmax_rows = (shifted / row_total).astype(jnp.bfloat16)
        blended = jnp.einsum(
            "ihqk,ikhe->iqhe", softmax_rows, values, preferred_element_type=jnp.float32
        )
        return (blended, row_peak[..., 0] + jnp.log(row_total[..., 0]))

    blended, log_total = lax.map(one_block, query_blocks)
    blended = jnp.moveaxis(blended, 0, 1).reshape(images, seq_rows, head_count * head_width)
    return (blended.astype(jnp.bfloat16), log_total)


def attend_backward(queries, key_rows, values, grad_blended, log_total, block_rows):
    images, seq_rows, head_count, head_width = queries.shape
    block_count = seq_rows // block_rows
    factor = head_width ** (-0.5)
    split_shape = (images, block_count, block_rows, head_count, head_width)
    query_blocks = jnp.moveaxis(queries.reshape(split_shape), 1, 0)
    grad_blocks = jnp.moveaxis(grad_blended.reshape(split_shape), 1, 0)

    def one_block(carry, inputs_part):
        query_part, grad_part, total_part = inputs_part
        grad_keys, grad_values = carry
        scores = (
            jnp.einsum("iqhe,ikhe->ihqk", query_part, key_rows, preferred_element_type=jnp.float32)
            * factor
        )
        softmax_rows = jnp.exp(scores - total_part[..., None])
        grad_values = grad_values + jnp.einsum(
            "ihqk,iqhe->ikhe",
            softmax_rows.astype(jnp.bfloat16),
            grad_part,
            preferred_element_type=jnp.float32,
        )
        grad_rows = jnp.einsum(
            "iqhe,ikhe->ihqk", grad_part, values, preferred_element_type=jnp.float32
        )
        grad_scores = softmax_rows * (
            grad_rows - jnp.sum(grad_rows * softmax_rows, -1, keepdims=True)
        )
        grad_scores = grad_scores.astype(jnp.bfloat16)
        grad_query = (
            jnp.einsum("ihqk,ikhe->iqhe", grad_scores, key_rows, preferred_element_type=jnp.float32)
            * factor
        )
        grad_keys = (
            grad_keys
            + jnp.einsum(
                "ihqk,iqhe->ikhe", grad_scores, query_part, preferred_element_type=jnp.float32
            )
            * factor
        )
        return ((grad_keys, grad_values), grad_query)

    zero_grad = jnp.zeros(queries.shape, jnp.float32)
    (grad_keys, grad_values), grad_query = lax.scan(
        one_block, (zero_grad, zero_grad), (query_blocks, grad_blocks, log_total)
    )
    flat_shape = (images, seq_rows, head_count * head_width)
    grad_query = jnp.moveaxis(grad_query, 0, 1).reshape(flat_shape)
    stacked = jnp.stack(
        [grad_query, grad_keys.reshape(flat_shape), grad_values.reshape(flat_shape)]
    )
    return stacked.astype(jnp.bfloat16)


def rows_forward(part):
    return lax.all_gather(part, "mp", axis=1, tiled=True)


def rows_sum_forward(part):
    return lax.psum_scatter(part, "mp", scatter_dimension=1, tiled=True)


def rows_backward(part):
    return lax.all_gather(part, "mp", axis=1, tiled=True)


def rows_sum_backward(part):
    return lax.psum_scatter(part, "mp", scatter_dimension=1, tiled=True)


def forward(inputs, params):
    qkv_full, out_full, up_full, down_full, bias_full, vector_full = params
    base = inputs.astype(jnp.float32)
    normed = layer_norm(base, vector_full[0], vector_full[1]).astype(jnp.bfloat16)
    normed_all = rows_forward(normed)
    images, seq_rows = (normed_all.shape[0], normed_all.shape[1])
    head_shape = (images, seq_rows, -1, DH)
    project = jnp.einsum("isd,tde->tise", normed_all, qkv_full, preferred_element_type=jnp.float32)
    queries = (project[0] + bias_full[0]).astype(jnp.bfloat16).reshape(head_shape)
    key_rows = project[1].astype(jnp.bfloat16).reshape(head_shape)
    values = (project[2] + bias_full[1]).astype(jnp.bfloat16).reshape(head_shape)
    blended, log_total = attend_forward(queries, key_rows, values, min(512, seq_rows))
    projected = rows_sum_forward(
        jnp.einsum("ise,ed->isd", blended, out_full, preferred_element_type=jnp.float32)
    )
    branch_one = projected + vector_full[2]
    hidden = base + vector_full[3] * branch_one
    normed_two = layer_norm(hidden, vector_full[4], vector_full[5]).astype(jnp.bfloat16)
    normed_two_all = rows_forward(normed_two)
    pre_act = jnp.einsum(
        "isd,df->isf", normed_two_all, up_full, preferred_element_type=jnp.float32
    ) + bias_full[2:].reshape(-1)
    activ = exact_gelu(pre_act).astype(jnp.bfloat16)
    branch_two = (
        rows_sum_forward(
            jnp.einsum("isf,fd->isd", activ, down_full, preferred_element_type=jnp.float32)
        )
        + vector_full[6]
    )
    output = hidden + vector_full[7] * branch_two
    saved = (
        base,
        hidden,
        branch_one,
        branch_two,
        normed_all,
        queries,
        key_rows,
        values,
        log_total,
        blended,
        normed_two_all,
        pre_act,
        activ,
    )
    return (output.astype(jnp.bfloat16), saved)


def backward(grad_output, saved, params):
    qkv_full, out_full, up_full, down_full, bias_full, vector_full = params
    (
        base,
        hidden,
        branch_one,
        branch_two,
        normed_all,
        queries,
        key_rows,
        values,
        log_total,
        blended,
        normed_two_all,
        pre_act,
        activ,
    ) = saved
    local_width = qkv_full.shape[2]
    grad_out = grad_output.astype(jnp.float32)
    grad_scale_two = jnp.sum(grad_out * branch_two, axis=(0, 1))
    grad_bias_two = jnp.sum(grad_out, axis=(0, 1)) * vector_full[7]
    grad_branch = rows_backward((grad_out * vector_full[7]).astype(jnp.bfloat16))
    grad_down = jnp.einsum("isf,isd->fd", activ, grad_branch, preferred_element_type=jnp.float32)
    grad_activ = jnp.einsum(
        "isd,fd->isf", grad_branch, down_full, preferred_element_type=jnp.float32
    )
    grad_pre = jax.vjp(exact_gelu, pre_act)[1](grad_activ)[0].astype(jnp.bfloat16)
    grad_up_bias = jnp.sum(grad_pre, axis=(0, 1), dtype=jnp.float32)
    grad_up = jnp.einsum(
        "isd,isf->df", normed_two_all, grad_pre, preferred_element_type=jnp.float32
    )
    grad_normed_two = rows_sum_backward(
        jnp.einsum("isf,df->isd", grad_pre, up_full, preferred_element_type=jnp.float32)
    )
    norm_back_two = jax.vjp(layer_norm, hidden, vector_full[4], vector_full[5])[1]
    grad_hidden, grad_gain_two, grad_shift_two = norm_back_two(grad_normed_two)
    grad_hidden = grad_out + grad_hidden
    grad_scale_one = jnp.sum(grad_hidden * branch_one, axis=(0, 1))
    grad_out_bias = jnp.sum(grad_hidden, axis=(0, 1)) * vector_full[3]
    grad_projected = rows_backward((grad_hidden * vector_full[3]).astype(jnp.bfloat16))
    grad_out_weight = jnp.einsum(
        "ise,isd->ed", blended, grad_projected, preferred_element_type=jnp.float32
    )
    grad_blended = jnp.einsum(
        "isd,ed->ise", grad_projected, out_full, preferred_element_type=jnp.float32
    ).astype(jnp.bfloat16)
    grad_project = attend_backward(
        queries, key_rows, values, grad_blended, log_total, min(512, queries.shape[1])
    )
    grad_query_bias = jnp.sum(grad_project[0], axis=(0, 1), dtype=jnp.float32)
    grad_value_bias = jnp.sum(grad_project[2], axis=(0, 1), dtype=jnp.float32)
    grad_qkv = jnp.einsum(
        "isd,tise->tde", normed_all, grad_project, preferred_element_type=jnp.float32
    )
    grad_normed = rows_sum_backward(
        jnp.einsum("tise,tde->isd", grad_project, qkv_full, preferred_element_type=jnp.float32)
    )
    norm_back_one = jax.vjp(layer_norm, base, vector_full[0], vector_full[1])[1]
    grad_input_part, grad_gain_one, grad_shift_one = norm_back_one(grad_normed)
    grad_input = grad_hidden + grad_input_part
    grad_vectors = jnp.stack(
        [
            grad_gain_one,
            grad_shift_one,
            grad_out_bias,
            grad_scale_one,
            grad_gain_two,
            grad_shift_two,
            grad_bias_two,
            grad_scale_two,
        ]
    )
    grad_biases = jnp.concatenate(
        [jnp.stack([grad_query_bias, grad_value_bias]), grad_up_bias.reshape(-1, local_width)], 0
    )
    return (grad_input, (grad_qkv, grad_out_weight, grad_up, grad_down, grad_biases, grad_vectors))


def local_general(
    tokens,
    cotangent,
    qkv_weight,
    qkv_first,
    qkv_second,
    out_weight,
    out_first,
    out_second,
    up_weight,
    up_first,
    up_second,
    down_weight,
    down_first,
    down_second,
    head_biases,
    bias_first,
    bias_second,
    vectors,
    vector_first,
    vector_second,
):

    def gather_params():
        gathered = (
            lax.all_gather(qkv_weight.astype(jnp.bfloat16), "dp", axis=1, tiled=True),
            lax.all_gather(out_weight.astype(jnp.bfloat16), "dp", axis=1, tiled=True),
            lax.all_gather(up_weight.astype(jnp.bfloat16), "dp", axis=0, tiled=True),
            lax.all_gather(down_weight.astype(jnp.bfloat16), "dp", axis=2, tiled=True),
            lax.all_gather(head_biases.astype(jnp.bfloat16), "dp", axis=1, tiled=True),
            lax.all_gather(vectors.astype(jnp.bfloat16), "dp", axis=1, tiled=True),
        )
        qkv_full, out_full, up_full, down_full, bias_full, vector_full = gathered
        return (
            qkv_full,
            out_full,
            up_full.reshape(up_full.shape[0], -1),
            down_full.reshape(-1, down_full.shape[2]),
            bias_full.astype(jnp.float32),
            vector_full.astype(jnp.float32),
        )

    grad_sums = None
    outputs = []
    input_grads = []
    for micro_step in range(MICRO):
        params_fwd = gather_params()
        output, saved = forward(tokens[micro_step], params_fwd)
        outputs.append(output)
        params_back = gather_params()
        grad_input, grads = backward(cotangent[micro_step], saved, params_back)
        input_grads.append(grad_input)
        if grad_sums is None:
            grad_sums = grads
        else:
            grad_sums = tuple((old_sum + new_part for old_sum, new_part in zip(grad_sums, grads)))
    grad_qkv, grad_out_weight, grad_up, grad_down, grad_biases, grad_vectors = grad_sums
    grad_up = grad_up.reshape(-1, up_weight.shape[1], up_weight.shape[2])
    grad_down = grad_down.reshape(down_weight.shape[0], down_weight.shape[1], -1)
    reduced = (
        lax.psum_scatter(grad_qkv, "dp", scatter_dimension=1, tiled=True),
        lax.psum_scatter(grad_out_weight, "dp", scatter_dimension=1, tiled=True),
        lax.psum_scatter(grad_up, "dp", scatter_dimension=0, tiled=True),
        lax.psum_scatter(grad_down, "dp", scatter_dimension=2, tiled=True),
        lax.psum_scatter(grad_biases, "dp", scatter_dimension=1, tiled=True),
        lax.psum_scatter(grad_vectors, "dp", scatter_dimension=1, tiled=True),
    )
    vector_grad = lax.psum(reduced[5], "mp")
    grads = (reduced[0], reduced[1], reduced[2], reduced[3], reduced[4], vector_grad)
    params = (qkv_weight, out_weight, up_weight, down_weight, head_biases, vectors)
    firsts = (qkv_first, out_first, up_first, down_first, bias_first, vector_first)
    seconds = (qkv_second, out_second, up_second, down_second, bias_second, vector_second)
    updated = [
        adam_update(params[slot], firsts[slot], seconds[slot], grads[slot], RATES[slot])
        for slot in range(6)
    ]
    return (
        jnp.stack(outputs),
        jnp.stack(input_grads),
        updated[0][0],
        updated[0][1],
        updated[0][2],
        updated[1][0],
        updated[1][1],
        updated[1][2],
        updated[2][0],
        updated[2][1],
        updated[2][2],
        updated[3][0],
        updated[3][1],
        updated[3][2],
        updated[4][0],
        updated[4][1],
        updated[4][2],
        updated[5][0],
        updated[5][1],
        updated[5][2],
    )


ZS, YS, MP = (4, 2, 4)
DP = ZS * YS
LANES = 128
BF = jnp.bfloat16
F32 = jnp.float32


def swap_z(part, step):
    return lax.ppermute(
        part, "dp", [(z * YS + y, (z ^ step) * YS + y) for z in range(ZS) for y in range(YS)]
    )


def swap_y(part):
    return lax.ppermute(part, "dp", [(each, each ^ 1) for each in range(DP)])


def swap_mp(part, step):
    return lax.ppermute(part, "mp", [(each, each ^ step) for each in range(MP)])


class Chain:
    def __init__(self, steps, *args):
        self.own = None
        self.result = None
        self.steps = steps(self, *args)
        self.flight = next(self.steps)

    def land(self, arrived):
        try:
            self.flight = self.steps.send(arrived)
        except StopIteration as end:
            self.flight = None
            self.result = end.value


def meet(values, *chains):
    values, flights = lax.optimization_barrier((values, [each.flight for each in chains]))
    for each, flight in zip(chains, flights):
        each.land(flight)
    return values


def join(rows, arrived, axis):
    return jnp.concatenate([rows, arrived], -2 if axis == "y" else -1)


def swap_plane(part, axis):
    return swap_y(part) if axis == "y" else swap_mp(part, 2)


def rows_z_steps(chain, shard):
    arrived = yield [swap_z(shard, step) for step in range(1, ZS)]
    return jnp.concatenate([shard] + arrived, 0)


def gather_steps(chain, parts, orders):
    for axes in zip(*orders):
        arrived = yield [swap_plane(part, axis) for part, axis in zip(parts, axes)]
        parts = [join(part, each, axis) for part, each, axis in zip(parts, arrived, axes)]
    chain.own = parts
    arrived = yield [swap_mp(part, 1) for part in parts]
    return arrived


def add_low(first, second):
    return (first.astype(F32) + second.astype(F32)).astype(BF)


def halve(total, axis):
    rows, width = total.shape[-2:]
    if axis == "y":
        return (total[..., : rows // 2, :], total[..., rows // 2 :, :])
    return (total[..., : width // 2], total[..., width // 2 :])


def reduce_steps(chain, other_parts, orders):
    arrived = yield [swap_mp(part, 1) for part in other_parts]
    totals = [add_low(own, each) for own, each in zip(chain.own, arrived)]
    for axes in zip(*orders):
        halves = [halve(total, axis) for total, axis in zip(totals, axes)]
        arrived = yield [swap_plane(half[1], axis) for half, axis in zip(halves, axes)]
        totals = [add_low(half[0], each) for half, each in zip(halves, arrived)]
    return totals


def sum_z_steps(chain, total):
    rows = total.shape[0] // ZS
    arrived = yield [swap_z(total[step * rows : (step + 1) * rows], step) for step in range(1, ZS)]
    total = total[:rows].astype(F32)
    for each in arrived:
        total = total + each.astype(F32)
    return total


def sum_z_halves_steps(chain, total):
    half = total.shape[0] // 2
    (arrived,) = yield [swap_z(total[half:], 2)]
    total = add_low(total[:half], arrived)
    (arrived,) = yield [swap_z(total[half // 2 :], 1)]
    return total[: half // 2].astype(F32) + arrived.astype(F32)


def image_steps(chain, far, near):
    (arrived,) = yield [swap_mp(far, 2)]
    second, passing = arrived
    (arrived,) = yield [swap_mp(jnp.stack([near(), passing]), 1)]
    return [arrived[0], second, arrived[1]]


def small_steps(chain, shard, vector_size):
    biases = shard[:, vector_size:]
    arrived = yield [swap_mp(biases, step) for step in range(1, MP)]
    rows = jnp.concatenate([shard] + arrived, 1)
    arrived = yield [swap_z(rows, step) for step in range(1, ZS)]
    rows = jnp.concatenate([rows] + arrived, 0)
    arrived = yield [swap_y(rows)]
    rows = jnp.concatenate([rows] + arrived, 0)
    biases = rows[:, vector_size:].reshape(DP, MP, -1).transpose(1, 0, 2)
    return (rows[:, :vector_size], biases)


def small_reduce_steps(chain, vector_part, bias_part):
    packed = [jnp.concatenate([vector_part, each], 1) for each in bias_part]
    arrived = yield [swap_mp(packed[step], step) for step in range(1, MP)]
    total = (packed[0] + arrived[0]) + (arrived[1] + arrived[2])
    arrived = yield [swap_y(total[ZS:])]
    total = total[:ZS] + arrived[0]
    arrived = yield [swap_z(total[step], step) for step in range(1, ZS)]
    total = total[0]
    for each in arrived:
        total = total + each
    return total


def norm_parts(values):
    center = values - jnp.mean(values, -1, keepdims=True)
    spread = lax.rsqrt(jnp.mean(center * center, -1, keepdims=True) + 1e-06)
    return (center * spread, spread)


def norm_back(grad, normal, spread, gain):
    scaled = grad * gain
    inner = scaled - jnp.mean(scaled, -1, keepdims=True)
    return spread * (inner - normal * jnp.mean(scaled * normal, -1, keepdims=True))


GAIN_ONE, SHIFT_ONE, OUT_BIAS, SCALE_ONE, GAIN_TWO, SHIFT_TWO, DOWN_BIAS, SCALE_TWO = range(8)


def vector_row(vector_ref, at):
    return vector_ref[at : at + 1, :]


def assemble_kernel(with_norm, place_ref, vector_ref, own_ref, *refs):
    out_ref, second_ref = refs[-2:]
    part_refs = [own_ref.at[0]] + list(refs[:-2])
    for at, part_ref in enumerate(part_refs):
        for block in range(DP):
            lanes = pl.ds(pl.multiple_of(place_ref[block] * LANES, LANES), LANES)
            out_ref[at, :, block * LANES : (block + 1) * LANES] = part_ref[:, lanes]
        values = out_ref[at].astype(F32)
        if with_norm:
            normal, _ = norm_parts(values)
            values = normal * vector_row(vector_ref, GAIN_ONE) + vector_row(vector_ref, SHIFT_ONE)
        else:
            values = values * vector_row(vector_ref, SCALE_TWO)
        second_ref[at] = values.astype(BF)


def assemble_image(place, vector_full, arrays, parts, with_norm):
    chunk_rows, width = parts[0].shape
    rows = chunk_rows // 4
    block = pl.BlockSpec((rows, width), lambda i, place_ref: (i, 0))
    result = pl.BlockSpec((MP, rows, width), lambda i, place_ref: (0, i, 0))
    shape = jax.ShapeDtypeStruct((MP, chunk_rows, width), BF)
    image, second = pl.pallas_call(
        functools.partial(assemble_kernel, with_norm),
        grid_spec=pltpu.PrefetchScalarGridSpec(
            num_scalar_prefetch=1,
            grid=(4,),
            in_specs=[
                pl.BlockSpec(vector_full.shape, lambda i, place_ref: (0, 0)),
                pl.BlockSpec((1, rows, width), lambda i, place_ref: (place_ref[DP], i, 0)),
            ]
            + [block] * len(parts),
            out_specs=[result] * 2,
        ),
        out_shape=[shape] * 2,
        compiler_params=pltpu.CompilerParams(vmem_limit_bytes=32 * 2**20),
        name="assemble_image",
    )(place, vector_full, arrays, *parts)
    return (image.reshape(-1, width), second.reshape(-1, width))


def spread_kernel(place_ref, own_ref, *refs):
    out_ref = refs[-1]
    mine = place_ref[DP]
    for at, part_ref in enumerate([own_ref] + list(refs[:-1])):
        for block in range(DP):
            lanes = pl.ds(pl.multiple_of(place_ref[block] * LANES, LANES), LANES)
            part = part_ref[:, block * LANES : (block + 1) * LANES]
            out_ref[mine ^ at, :, lanes] = part.astype(out_ref.dtype)


def spread_image(place, own, parts, dtype):
    chunk_rows, width = parts[0].shape
    rows = chunk_rows // 4
    block = pl.BlockSpec((rows, width), lambda i, place_ref: (i, 0))
    return pl.pallas_call(
        spread_kernel,
        grid_spec=pltpu.PrefetchScalarGridSpec(
            num_scalar_prefetch=1,
            grid=(4,),
            in_specs=[block] * (1 + len(parts)),
            out_specs=pl.BlockSpec((MP, rows, width), lambda i, place_ref: (0, i, 0)),
        ),
        out_shape=jax.ShapeDtypeStruct((MP, chunk_rows, width), dtype),
        compiler_params=pltpu.CompilerParams(vmem_limit_bytes=32 * 2**20),
        name="spread_image",
    )(place, own, *parts)


ROWS = 512


def product_nt(left_refs, right_refs):
    total = None
    for left_ref, right_ref in zip(left_refs, right_refs):
        part = lax.dot_general(
            left_ref[...], right_ref[...], (((1,), (1,)), ((), ())), preferred_element_type=F32
        )
        total = part if total is None else total + part
    return total


def add_rows(sums_ref, rows):
    @pl.when(pl.program_id(0) == 0)
    def _():
        sums_ref[...] = jnp.zeros_like(sums_ref)

    for at, each in enumerate(rows):
        sums_ref[at : at + 1, :] += jnp.sum(each, 0, keepdims=True)


def out_kernel(count, *refs):
    lefts, rights = (refs[:count], refs[count : 2 * count])
    vector_ref, base_ref, branch_ref, hidden_ref, normed_ref = refs[2 * count :]
    branch = product_nt(lefts, rights) + vector_row(vector_ref, OUT_BIAS)
    hidden = base_ref[...].astype(F32) + vector_row(vector_ref, SCALE_ONE) * branch
    normal, _ = norm_parts(hidden)
    branch_ref[...] = branch
    hidden_ref[...] = hidden
    normed = normal * vector_row(vector_ref, GAIN_TWO) + vector_row(vector_ref, SHIFT_TWO)
    normed_ref[...] = normed.astype(BF)


def down_kernel(count, *refs):
    lefts, rights = (refs[:count], refs[count : 2 * count])
    vector_ref, hidden_ref, grad_ref, output_ref, sums_ref = refs[2 * count :]
    branch = product_nt(lefts, rights) + vector_row(vector_ref, DOWN_BIAS)
    output = hidden_ref[...] + vector_row(vector_ref, SCALE_TWO) * branch
    output_ref[...] = output.astype(BF)
    grad = grad_ref[...].astype(F32)
    add_rows(sums_ref, [grad * branch, grad])


def up_back_kernel(count, *refs):
    lefts, rights = (refs[:count], refs[count : 2 * count])
    vector_ref, hidden_ref, branch_ref, grad_ref, out_ref, low_ref, sums_ref = refs[2 * count :]
    grad_normed = product_nt(lefts, rights)
    normal, spread = norm_parts(hidden_ref[...])
    grad = norm_back(grad_normed, normal, spread, vector_row(vector_ref, GAIN_TWO))
    grad = grad + grad_ref[...].astype(F32)
    out_ref[...] = grad
    low_ref[...] = (grad * vector_row(vector_ref, SCALE_ONE)).astype(BF)
    add_rows(sums_ref, [grad_normed * normal, grad_normed, grad * branch_ref[...], grad])


def in_back_kernel(count, *refs):
    lefts, rights = (refs[:count], refs[count : 2 * count])
    vector_ref, base_ref, grad_ref, low_ref, sums_ref = refs[2 * count : 2 * count + 5]
    grad_normed = product_nt(lefts, rights)
    normal, spread = norm_parts(base_ref[...].astype(F32))
    grad = norm_back(grad_normed, normal, spread, vector_row(vector_ref, GAIN_ONE))
    grad = grad + grad_ref[...]
    low_ref[...] = grad.astype(BF)

    for own_ref in refs[2 * count + 5 :]:
        own_ref[...] = grad[: own_ref.shape[0]]
    add_rows(sums_ref, [grad_normed * normal, grad_normed])


def expand_kernel(left_ref, right_ref, bias_ref, activ_ref, slope_ref):
    values = jnp.dot(left_ref[...], right_ref[...], preferred_element_type=F32) + bias_ref[0:1, :]
    share = 0.5 * (1.0 + lax.erf(values * 0.7071067811865476))
    activ_ref[...] = (values * share).astype(BF)
    slope = share + values * (0.3989422804014327 * jnp.exp(-0.5 * values * values))
    slope_ref[...] = slope.astype(BF)


def expand(left, right, bias):
    rows, depth = left.shape
    width = right.shape[1]
    block = pl.BlockSpec((256, width), lambda i: (i, 0))
    return pl.pallas_call(
        expand_kernel,
        grid=(rows // 256,),
        in_specs=[
            pl.BlockSpec((256, depth), lambda i: (i, 0)),
            pl.BlockSpec((depth, width), lambda i: (0, 0), pipeline_mode=pl.Buffered(1)),
            pl.BlockSpec((1, width), lambda i: (0, 0)),
        ],
        out_specs=[block] * 2,
        out_shape=[jax.ShapeDtypeStruct((rows, width), BF)] * 2,
        compiler_params=pltpu.CompilerParams(vmem_limit_bytes=32 * 2**20),
        name="expand",
    )(left, right, bias.reshape(1, width))


def slope_kernel(left_ref, right_ref, slope_ref, grad_ref, sums_ref):
    grad = jnp.dot(left_ref[...], right_ref[...], preferred_element_type=F32)
    low = (grad * slope_ref[...].astype(F32)).astype(BF)
    grad_ref[...] = low
    add_rows(sums_ref, [low.astype(F32)])


def slope_product(left, right, slope):
    rows, depth = left.shape
    width = right.shape[1]
    block = pl.BlockSpec((256, width), lambda i: (i, 0))
    return pl.pallas_call(
        slope_kernel,
        grid=(rows // 256,),
        in_specs=[
            pl.BlockSpec((256, depth), lambda i: (i, 0)),
            pl.BlockSpec((depth, width), lambda i: (0, 0), pipeline_mode=pl.Buffered(1)),
            block,
        ],
        out_specs=[block, pl.BlockSpec((8, width), lambda i: (0, 0))],
        out_shape=[jax.ShapeDtypeStruct((rows, width), BF), jax.ShapeDtypeStruct((8, width), F32)],
        compiler_params=pltpu.CompilerParams(vmem_limit_bytes=32 * 2**20),
        name="slope_product",
    )(left, right, slope)


def row_call(kernel, name, lefts, rights, vector_full, row_inputs, outs, span=None, own_rows=0):
    rows, width = row_inputs[0].shape
    first, count = span or (0, rows // ROWS)
    rows = count * ROWS
    once = pl.Buffered(1)
    block = pl.BlockSpec((ROWS, width), lambda i: (i, 0))
    source = pl.BlockSpec((ROWS, width), lambda i: (i + first, 0))
    specs = {
        "sums": (pl.BlockSpec((8, width), lambda i: (0, 0)), jax.ShapeDtypeStruct((8, width), F32)),
        "own": (
            pl.BlockSpec((own_rows, width), lambda i: (0, 0)),
            jax.ShapeDtypeStruct((own_rows, width), F32),
        ),
    }
    pairs = [
        specs[each] if isinstance(each, str) else (block, jax.ShapeDtypeStruct((rows, width), each))
        for each in outs
    ]
    return pl.pallas_call(
        functools.partial(kernel, len(lefts)),
        grid=(count,),
        in_specs=[pl.BlockSpec((ROWS, each.shape[1]), lambda i: (i + first, 0)) for each in lefts]
        + [pl.BlockSpec(each.shape, lambda i: (0, 0), pipeline_mode=once) for each in rights]
        + [pl.BlockSpec(vector_full.shape, lambda i: (0, 0))]
        + [source] * len(row_inputs),
        out_specs=[each[0] for each in pairs],
        out_shape=[each[1] for each in pairs],
        compiler_params=pltpu.CompilerParams(vmem_limit_bytes=48 * 2**20),
        name=name,
    )(*lefts, *rights, vector_full, *row_inputs)


def lane_dot(left, right):
    return lax.dot_general(left, right, (((1,), (1,)), ((), ())), preferred_element_type=F32)


def head_masks(width):
    lane = lax.broadcasted_iota(jnp.int32, (1, width), 1)
    return [lane // DH == head for head in range(width // DH)]


def attend_kernel(block_rows, q_ref, k_ref, v_ref, o_ref, lse_ref):
    masks = head_masks(LANES)
    key_rows = k_ref[...]
    values = v_ref[...]
    zero = jnp.zeros((), BF)
    for block in range(q_ref.shape[0] // block_rows):
        rows = slice(block * block_rows, (block + 1) * block_rows)
        queries = q_ref[rows, :] * jnp.asarray(DH**-0.5, BF)
        blended = []
        for head, mask in enumerate(masks):
            scores = lane_dot(jnp.where(mask, queries, zero), key_rows)
            peak = jnp.max(scores, 1, keepdims=True)
            shifted = jnp.exp(scores - peak)
            total = jnp.sum(shifted, 1, keepdims=True)
            part = jnp.dot(shifted.astype(BF), values, preferred_element_type=F32)
            blended.append(part * (1.0 / total))
            log_total = jnp.broadcast_to(peak + jnp.log(total), (block_rows, LANES))
            lse_ref[0, head : head + 1, rows] = jnp.transpose(log_total)[0:1, :]
        o_ref[rows, :] = jnp.where(masks[0], blended[0], blended[1]).astype(BF)


def attend_back_kernel(
    block_rows, q_ref, k_ref, v_ref, g_ref, lse_ref, out_ref, dk_acc, dv_acc
):
    masks = head_masks(LANES)
    key_rows = k_ref[...]
    values = v_ref[...]
    zero = jnp.zeros((), BF)
    factor = DH**-0.5
    key_heads = [jnp.where(mask, key_rows, zero) for mask in masks]
    for block in range(q_ref.shape[0] // block_rows):
        rows = slice(block * block_rows, (block + 1) * block_rows)
        queries = q_ref[rows, :] * jnp.asarray(factor, BF)
        grads = g_ref[rows, :]
        grad_query = None
        grad_keys = None
        grad_values = None
        for head, mask in enumerate(masks):
            query_head = jnp.where(mask, queries, zero)
            grad_head = jnp.where(mask, grads, zero)
            scores = lane_dot(key_rows, query_head)
            weights = jnp.exp(scores - lse_ref[0, head : head + 1, rows])
            value_part = jnp.dot(weights.astype(BF), grad_head, preferred_element_type=F32)
            grad_rows = lane_dot(values, grad_head)
            delta = jnp.sum(grad_rows * weights, 0, keepdims=True)
            grad_scores = (weights * (grad_rows - delta)).astype(BF)
            key_part = jnp.dot(grad_scores, query_head, preferred_element_type=F32)
            query_part = lax.dot_general(
                grad_scores, key_heads[head], (((0,), (0,)), ((), ())), preferred_element_type=F32
            )
            grad_query = query_part if head == 0 else grad_query + query_part
            grad_keys = key_part if head == 0 else grad_keys + key_part
            grad_values = value_part if head == 0 else grad_values + value_part
        out_ref[rows, 0:LANES] = (grad_query * factor).astype(BF)
        if block == 0:
            dk_acc[...] = grad_keys
            dv_acc[...] = grad_values
        else:
            dk_acc[...] += grad_keys
            dv_acc[...] += grad_values
    out_ref[:, LANES : 2 * LANES] = dk_acc[...].astype(BF)
    out_ref[:, 2 * LANES : 3 * LANES] = dv_acc[...].astype(BF)


def kind_spec(rows, kind):
    return pl.BlockSpec((rows, LANES), lambda p: (0, p * 3 + kind))


def attend(heads):
    rows, width = heads.shape
    pairs = width // LANES // 3
    return pl.pallas_call(
        functools.partial(attend_kernel, 256),
        grid=(pairs,),
        in_specs=[kind_spec(rows, kind) for kind in range(3)],
        out_specs=[
            pl.BlockSpec((rows, LANES), lambda p: (0, p)),
            pl.BlockSpec((1, 8, rows), lambda p: (p, 0, 0)),
        ],
        out_shape=[
            jax.ShapeDtypeStruct((rows, pairs * LANES), BF),
            jax.ShapeDtypeStruct((pairs, 8, rows), F32),
        ],
        compiler_params=pltpu.CompilerParams(vmem_limit_bytes=32 * 2**20),
        name="attend",
    )(heads, heads, heads)


def attend_back(heads, grad_blended, log_total):
    rows, width = heads.shape
    pairs = width // LANES // 3
    return pl.pallas_call(
        functools.partial(attend_back_kernel, 256),
        grid=(pairs,),
        in_specs=[kind_spec(rows, kind) for kind in range(3)]
        + [
            pl.BlockSpec((rows, LANES), lambda p: (0, p)),
            pl.BlockSpec((1, 8, rows), lambda p: (p, 0, 0)),
        ],
        out_specs=pl.BlockSpec((rows, 3 * LANES), lambda p: (0, p)),
        out_shape=jax.ShapeDtypeStruct((rows, width), BF),
        scratch_shapes=[pltpu.VMEM((rows, LANES), F32)] * 2,
        compiler_params=pltpu.CompilerParams(vmem_limit_bytes=32 * 2**20),
        name="attend_back",
    )(heads, heads, heads, grad_blended, log_total)


def dot_nn(left, right):
    return lax.dot_general(left, right, (((1,), (0,)), ((), ())), preferred_element_type=F32)


def dot_nt(left, right):
    return lax.dot_general(left, right, (((1,), (1,)), ((), ())), preferred_element_type=F32)


def dot_tn(left, right):
    return lax.dot_general(left, right, (((0,), (0,)), ((), ())), preferred_element_type=F32)


def local_image(
    tokens,
    cotangent,
    qkv_weight,
    qkv_first,
    qkv_second,
    out_weight,
    out_first,
    out_second,
    up_weight,
    up_first,
    up_second,
    down_weight,
    down_first,
    down_second,
    head_biases,
    bias_first,
    bias_second,
    vectors,
    vector_first,
    vector_second,
):
    dp_at = lax.axis_index("dp")
    mp_at = lax.axis_index("mp")
    units = up_weight.shape[1]
    half_units = units // 2
    block_width = qkv_weight.shape[2]
    depth = qkv_weight.shape[1]
    bias_width = head_biases.shape[1]
    chunk_rows, width = tokens.shape[2:]
    order = [((zk * YS) + yk) for yk in range(YS) for zk in range(ZS)]
    place = jnp.stack([dp_at ^ each for each in order] + [mp_at]).astype(jnp.int32)
    cores = (0, 1)

    def fetch_image(array):
        chunks = array[:, 0]

        def chunk(step):
            return lax.dynamic_index_in_dim(chunks, mp_at ^ step, 0, keepdims=False)

        return Chain(image_steps, jnp.stack([chunk(2), chunk(3)]), lambda: chunk(1))

    def send_back(low):
        chunks = low.reshape(MP, chunk_rows, width)
        return Chain(image_steps, chunks[2:], lambda: chunks[1])

    small_shard = jnp.concatenate(
        [vectors.astype(BF).reshape(-1), head_biases.astype(BF).reshape(-1)]
    ).reshape(1, -1)
    vector_size = vectors.size
    kinds = qkv_weight.shape[0]
    qkv_shard = qkv_weight.astype(BF).reshape(kinds, depth, 2, LANES).transpose(1, 2, 0, 3)
    qkv_shard = qkv_shard.reshape(depth, -1)
    rest_shard = jnp.concatenate(
        [
            out_weight.T.astype(BF),
            up_weight.astype(BF).reshape(depth, -1),
            down_weight.transpose(2, 0, 1).astype(BF).reshape(depth, -1),
        ],
        1,
    )
    both = ("xy", "yx")
    rows_qkv = [Chain(rows_z_steps, each) for each in jnp.split(qkv_shard, 2, 1)]
    small = Chain(small_steps, small_shard, vector_size)
    fetch_tokens = fetch_image(tokens)
    rest_shard = meet(rest_shard, rows_qkv[0], small)
    get_qkv = [Chain(gather_steps, [rows_qkv[0].result], ("yx",)), None]
    rest_shard = meet(rest_shard, small, rows_qkv[1])
    get_qkv[1] = Chain(gather_steps, [rows_qkv[1].result], ("xy",))
    rows_rest = Chain(rows_z_steps, rest_shard)
    meet((), small, get_qkv[0], fetch_tokens)
    tokens = meet(tokens, fetch_tokens)

    vector_full, bias_small = small.result
    vector_full = vector_full.reshape(DP, vectors.shape[0], LANES).transpose(1, 0, 2)
    vector_full = vector_full.reshape(vectors.shape[0], width).astype(F32)
    back_places = jnp.stack([((each ^ dp_at) & 1) * ZS + ((each ^ dp_at) >> 1) for each in range(DP)])
    bias_rows = jnp.take(bias_small, back_places, axis=1).reshape(2, 2, DP, -1, bias_width)
    bias_full = bias_rows.transpose(1, 3, 0, 2, 4).reshape(2, head_biases.shape[0], 2, block_width)
    bias_full = bias_full.astype(F32)

    base, normed_one = assemble_image(place, vector_full, tokens[:, 0], fetch_tokens.result, True)
    normed_one = meet(normed_one, *get_qkv)

    def project(core, half, weight):
        lanes = slice(half * LANES, (half + 1) * LANES)
        zero = jnp.zeros((2, LANES), F32)
        bias = jnp.stack([bias_full[core, 0, :, lanes], zero, bias_full[core, 1, :, lanes]], 1)
        return (dot_nn(normed_one, weight) + bias.reshape(-1)).astype(BF)

    heads, blended, log_total = ([[None, None], [None, None]] for _ in range(3))

    def forward_heads(core, half):
        blended[core][half], log_total[core][half] = attend(heads[core][half])

    heads[0][0] = project(0, 0, get_qkv[0].own[0])
    forward_heads(0, 0)
    blended[0][0], normed_one = meet((blended[0][0], normed_one), *get_qkv, rows_rest)
    out_rows, up_rows, down_rows = jnp.split(
        rows_rest.result, [block_width, block_width * (1 + units)], 1
    )
    get_out = Chain(gather_steps, [jnp.stack(jnp.split(out_rows, 2, 1))], ("yx",))
    get_up = Chain(gather_steps, jnp.split(up_rows, 2, 1), both)
    heads[0][1] = project(0, 1, get_qkv[1].own[0])
    forward_heads(0, 1)
    blended[0][1], normed_one, down_rows = meet(
        (blended[0][1], normed_one, down_rows), get_qkv[1], get_out, get_up
    )
    w_qkv = [[each.own[0] for each in get_qkv], [each.result[0] for each in get_qkv]]
    get_down = Chain(gather_steps, jnp.split(down_rows, 2, 1), both)
    heads[1][0] = project(1, 0, w_qkv[1][0])
    forward_heads(1, 0)
    blended[1][0], normed_one, cotangent = meet(
        (blended[1][0], normed_one, cotangent), get_up, get_out
    )
    fetch_cotangent = fetch_image(cotangent)
    heads[1][1] = project(1, 1, w_qkv[1][1])
    forward_heads(1, 1)
    blended = meet(blended, get_up, get_out, get_down, fetch_cotangent)
    w_up = [get_up.own, get_up.result]
    w_out = [[each[0][half] for half in (0, 1)] for each in (get_out.own, get_out.result)]
    pairs = [(core, half) for core in cores for half in (0, 1)]
    branch_one, hidden, normed_two = row_call(
        out_kernel,
        "out_norm",
        [blended[core][half] for core, half in pairs],
        [w_out[core][half] for core, half in pairs],
        vector_full,
        [base],
        [F32, F32, BF],
    )
    parts = [(half, core) for core in (1, 0) for half in (0, 1)]
    activ, slope = ({}, {})
    for half, core in parts:
        rows = bias_full[core, 2 + half * half_units : 2 + (half + 1) * half_units]
        unit_bias = rows.transpose(1, 0, 2).reshape(-1)
        activ[half, core], slope[half, core] = expand(normed_two, w_up[core][half], unit_bias)
        if (half, core) == (0, 0):
            activ, normed_two, cotangent = meet((activ, normed_two, cotangent), get_down, fetch_cotangent)
    activ, slope = meet((activ, slope))
    grad_out, grad_branch = assemble_image(
        place, vector_full, cotangent[:, 0], fetch_cotangent.result, False
    )

    def reduce_pairs(left, rights):
        chain = Chain(reduce_steps, [dot_tn(left, rights[half, 1]).astype(BF) for half in (0, 1)], both[::-1])
        chain.own = [dot_tn(left, rights[half, 0]).astype(BF) for half in (0, 1)]
        return chain

    sum_down = reduce_pairs(grad_branch, activ)
    grad_branch, activ = meet((grad_branch, activ), sum_down, get_down)
    w_down = [get_down.own, get_down.result]
    output, sums_two = row_call(
        down_kernel,
        "down_output",
        [activ[each] for each in parts],
        [w_down[core][half] for half, core in parts],
        vector_full,
        [hidden, grad_out],
        [BF, "sums"],
    )
    output, grad_branch, slope = meet((output, grad_branch, slope))
    send_output = send_back(output)
    grad_pre, unit_sums = ({}, {})
    for half, core in parts:
        grad_pre[half, core], unit_sums[half, core] = slope_product(
            grad_branch, w_down[core][half], slope[half, core]
        )
    grad_pre, normed_two = meet((grad_pre, normed_two), sum_down)
    sum_up = reduce_pairs(normed_two, grad_pre)
    grad_hidden, grad_projected, sums_one = row_call(
        up_back_kernel,
        "up_norm_back",
        [grad_pre[each] for each in parts],
        [w_up[core][half] for half, core in parts],
        vector_full,
        [hidden, branch_one, grad_out],
        [F32, BF, "sums"],
    )
    grad_projected = meet(grad_projected, sum_up, sum_down, send_output)
    rows_down = Chain(sum_z_halves_steps, jnp.concatenate(sum_down.result, 1))
    grad_w_out = [
        jnp.stack([dot_tn(grad_projected, each).astype(BF) for each in blended[core]]) for core in cores
    ]
    sum_out = Chain(reduce_steps, [grad_w_out[1]], ("xy",))
    sum_out.own = [grad_w_out[0]]
    grad_blended = [[dot_nn(grad_projected, each).astype(BF) for each in w_out[core]] for core in cores]
    grad_heads = [[None, None], [None, None]]

    def back_heads(core, half):
        grad_heads[core][half] = attend_back(
            heads[core][half], grad_blended[core][half], log_total[core][half]
        )
        return dot_tn(normed_one, grad_heads[core][half]).astype(BF)

    other = back_heads(1, 0)
    other, grad_blended = meet((other, grad_blended), sum_up, sum_out, rows_down, send_output)
    sum_qkv = [Chain(reduce_steps, [other], ("xy",)), None]
    sum_qkv[0].own = [back_heads(0, 0)]
    grad_heads[0][0], grad_blended = meet(
        (grad_heads[0][0], grad_blended), sum_qkv[0], sum_out, sum_up, rows_down
    )
    rows_up = Chain(sum_z_halves_steps, jnp.concatenate(sum_up.result, 1))
    other = back_heads(1, 1)
    other, grad_blended = meet((other, grad_blended), sum_out, sum_qkv[0])
    sum_qkv[1] = Chain(reduce_steps, [other], ("yx",))
    out_rows = jnp.concatenate([sum_out.result[0][0], sum_out.result[0][1]], 1)
    sum_qkv[1].own = [back_heads(0, 1)]
    grad_heads = meet(grad_heads, sum_qkv[0], sum_qkv[1], rows_up)

    def input_back(span, outs):
        return row_call(
            in_back_kernel,
            "in_norm_back",
            [grad_heads[core][half] for core, half in pairs],
            [w_qkv[core][half] for core, half in pairs],
            vector_full,
            [base, grad_hidden],
            outs,
            span,
            chunk_rows,
        )

    grad_far, sums_far = input_back((1, 1), [BF, "sums"])
    grad_near = []
    send_grad = Chain(
        image_steps, grad_far.reshape(2, chunk_rows, width), lambda: grad_near[0][chunk_rows:]
    )
    grad_heads = meet(grad_heads, sum_qkv[1])
    near, sums_near, own_grad = input_back((0, 1), [BF, "sums", "own"])
    grad_near.append(near)
    sums_input = sums_far + sums_near

    grad_vectors = jnp.stack(
        [
            sums_input[0],
            sums_input[1],
            sums_one[3] * vector_full[SCALE_ONE],
            sums_one[2],
            sums_one[0],
            sums_one[1],
            sums_two[1] * vector_full[SCALE_TWO],
            sums_two[0],
        ]
    )
    grad_vectors = grad_vectors.reshape(-1, DP, LANES).transpose(1, 0, 2).reshape(DP, -1)
    bias_parts = []
    for core in cores:
        head_part = [
            jnp.sum(each.astype(F32), 0).reshape(2, kinds, LANES) for each in grad_heads[core]
        ]
        rows = [jnp.concatenate([each[:, kind] for each in head_part], 1) for kind in (0, 2)]
        for half in (0, 1):
            unit_part = unit_sums[half, core][0].reshape(2, half_units, block_width)
            rows += [unit_part[:, at] for at in range(half_units)]
        bias_parts.append(jnp.stack(rows, 1))
    grad_biases = jnp.stack(bias_parts, 1).reshape(MP, -1, DP, bias_width).transpose(0, 2, 1, 3)
    grad_biases = jnp.take(grad_biases, place[:DP], axis=1).reshape(MP, DP, -1)
    sum_small = Chain(small_reduce_steps, grad_vectors, grad_biases)
    meet((), sum_qkv[1])
    rows_qkv = Chain(sum_z_steps, jnp.concatenate(sum_qkv[0].result + sum_qkv[1].result + [out_rows], 1))
    meet((), rows_up)
    meet((), send_grad)
    meet((), send_grad)
    meet((), rows_qkv)
    for _ in range(3):
        meet((), sum_small)
    layer_output = spread_image(place, output[:chunk_rows], send_output.result, BF)[:, None]
    input_grad = spread_image(place, own_grad, send_grad.result, F32)[:, None]

    small_total = sum_small.result
    vector_grad = small_total[:vector_size].reshape(vectors.shape)
    bias_grad = small_total[vector_size:].reshape(head_biases.shape)
    qkv_size = kinds * block_width
    qkv_grad = rows_qkv.result[:, :qkv_size].reshape(depth, 2, kinds, LANES).transpose(2, 0, 1, 3)
    grads = (
        qkv_grad.reshape(qkv_weight.shape),
        rows_qkv.result[:, qkv_size:].T,
        rows_up.result.reshape(depth, units, block_width),
        rows_down.result.reshape(depth, units, block_width).transpose(1, 2, 0),
        bias_grad,
        vector_grad,
    )
    params = (qkv_weight, out_weight, up_weight, down_weight, head_biases, vectors)
    firsts = (qkv_first, out_first, up_first, down_first, bias_first, vector_first)
    seconds = (qkv_second, out_second, up_second, down_second, bias_second, vector_second)
    results = [layer_output, input_grad]
    for slot in range(6):
        results.extend(
            adam_update(params[slot], firsts[slot], seconds[slot], grads[slot], RATES[slot])
        )
    return tuple(results)


def solution(mesh):
    whole_image = mesh.shape["mp"] == MICRO == MP and mesh.shape["dp"] == DP
    return jax.shard_map(
        local_image if whole_image else local_general,
        mesh=mesh,
        in_specs=(
            P(None, "dp", "mp", None),
            P(None, "dp", "mp", None),
            P(None, "dp", "mp"),
            P(None, "dp", "mp"),
            P(None, "dp", "mp"),
            P("mp", "dp"),
            P("mp", "dp"),
            P("mp", "dp"),
            P("dp", None, "mp"),
            P("dp", None, "mp"),
            P("dp", None, "mp"),
            P(None, "mp", "dp"),
            P(None, "mp", "dp"),
            P(None, "mp", "dp"),
            P(None, ("mp", "dp")),
            P(None, ("mp", "dp")),
            P(None, ("mp", "dp")),
            P(None, "dp"),
            P(None, "dp"),
            P(None, "dp"),
        ),
        out_specs=(
            P(None, "dp", "mp", None),
            P(None, "dp", "mp", None),
            P(None, "dp", "mp"),
            P(None, "dp", "mp"),
            P(None, "dp", "mp"),
            P("mp", "dp"),
            P("mp", "dp"),
            P("mp", "dp"),
            P("dp", None, "mp"),
            P("dp", None, "mp"),
            P("dp", None, "mp"),
            P(None, "mp", "dp"),
            P(None, "mp", "dp"),
            P(None, "mp", "dp"),
            P(None, ("mp", "dp")),
            P(None, ("mp", "dp")),
            P(None, ("mp", "dp")),
            P(None, "dp"),
            P(None, "dp"),
            P(None, "dp"),
        ),
        check_vma=False,
    )
```

```python
import functools

import jax
import jax.numpy as jnp
from jax import lax
from jax.experimental import pallas as pl
from jax.experimental.pallas import tpu as pltpu
from jax.sharding import PartitionSpec as P

DH = 64
MICRO = 4
STEP = 10


RATES = (0.05, 0.2, 0.05, 0.03, 0.5, 0.5)


def layer_norm(values, gain, shift):
    center = values - jnp.mean(values, -1, keepdims=True)
    spread = jnp.mean(center * center, -1, keepdims=True)
    return center * lax.rsqrt(spread + 1e-06) * gain + shift


def exact_gelu(values):
    return jax.nn.gelu(values, approximate=False)


def adam_update(weight, first, second, grad, rate):
    first_new = 0.9 * first + 0.1 * grad
    second_new = 0.999 * second + 0.001 * grad * grad
    corrected = first_new / (1.0 - 0.9**STEP)
    scaled = jnp.sqrt(second_new / (1.0 - 0.999**STEP))
    weight_new = weight - rate * (corrected / (scaled + 1e-08) + 0.05 * weight)
    return (weight_new, first_new, second_new)


def attend_forward(queries, key_rows, values, block_rows):
    images, seq_rows, head_count, head_width = queries.shape
    block_count = seq_rows // block_rows
    factor = head_width ** (-0.5)
    query_blocks = jnp.moveaxis(
        queries.reshape(images, block_count, block_rows, head_count, head_width), 1, 0
    )

    def one_block(query_part):
        scores = (
            jnp.einsum("iqhe,ikhe->ihqk", query_part, key_rows, preferred_element_type=jnp.float32)
            * factor
        )
        row_peak = jnp.max(scores, -1, keepdims=True)
        shifted = jnp.exp(scores - row_peak)
        row_total = jnp.sum(shifted, -1, keepdims=True)
        softmax_rows = (shifted / row_total).astype(jnp.bfloat16)
        blended = jnp.einsum(
            "ihqk,ikhe->iqhe", softmax_rows, values, preferred_element_type=jnp.float32
        )
        return (blended, row_peak[..., 0] + jnp.log(row_total[..., 0]))

    blended, log_total = lax.map(one_block, query_blocks)
    blended = jnp.moveaxis(blended, 0, 1).reshape(images, seq_rows, head_count * head_width)
    return (blended.astype(jnp.bfloat16), log_total)


def attend_backward(queries, key_rows, values, grad_blended, log_total, block_rows):
    images, seq_rows, head_count, head_width = queries.shape
    block_count = seq_rows // block_rows
    factor = head_width ** (-0.5)
    split_shape = (images, block_count, block_rows, head_count, head_width)
    query_blocks = jnp.moveaxis(queries.reshape(split_shape), 1, 0)
    grad_blocks = jnp.moveaxis(grad_blended.reshape(split_shape), 1, 0)

    def one_block(carry, inputs_part):
        query_part, grad_part, total_part = inputs_part
        grad_keys, grad_values = carry
        scores = (
            jnp.einsum("iqhe,ikhe->ihqk", query_part, key_rows, preferred_element_type=jnp.float32)
            * factor
        )
        softmax_rows = jnp.exp(scores - total_part[..., None])
        grad_values = grad_values + jnp.einsum(
            "ihqk,iqhe->ikhe",
            softmax_rows.astype(jnp.bfloat16),
            grad_part,
            preferred_element_type=jnp.float32,
        )
        grad_rows = jnp.einsum(
            "iqhe,ikhe->ihqk", grad_part, values, preferred_element_type=jnp.float32
        )
        grad_scores = softmax_rows * (
            grad_rows - jnp.sum(grad_rows * softmax_rows, -1, keepdims=True)
        )
        grad_scores = grad_scores.astype(jnp.bfloat16)
        grad_query = (
            jnp.einsum("ihqk,ikhe->iqhe", grad_scores, key_rows, preferred_element_type=jnp.float32)
            * factor
        )
        grad_keys = (
            grad_keys
            + jnp.einsum(
                "ihqk,iqhe->ikhe", grad_scores, query_part, preferred_element_type=jnp.float32
            )
            * factor
        )
        return ((grad_keys, grad_values), grad_query)

    zero_grad = jnp.zeros(queries.shape, jnp.float32)
    (grad_keys, grad_values), grad_query = lax.scan(
        one_block, (zero_grad, zero_grad), (query_blocks, grad_blocks, log_total)
    )
    flat_shape = (images, seq_rows, head_count * head_width)
    grad_query = jnp.moveaxis(grad_query, 0, 1).reshape(flat_shape)
    stacked = jnp.stack(
        [grad_query, grad_keys.reshape(flat_shape), grad_values.reshape(flat_shape)]
    )
    return stacked.astype(jnp.bfloat16)


def rows_forward(part):
    return lax.all_gather(part, "mp", axis=1, tiled=True)


def rows_sum_forward(part):
    return lax.psum_scatter(part, "mp", scatter_dimension=1, tiled=True)


def rows_backward(part):
    return lax.all_gather(part, "mp", axis=1, tiled=True)


def rows_sum_backward(part):
    return lax.psum_scatter(part, "mp", scatter_dimension=1, tiled=True)


def forward(inputs, params):
    qkv_full, out_full, up_full, down_full, bias_full, vector_full = params
    base = inputs.astype(jnp.float32)
    normed = layer_norm(base, vector_full[0], vector_full[1]).astype(jnp.bfloat16)
    normed_all = rows_forward(normed)
    images, seq_rows = (normed_all.shape[0], normed_all.shape[1])
    head_shape = (images, seq_rows, -1, DH)
    project = jnp.einsum("isd,tde->tise", normed_all, qkv_full, preferred_element_type=jnp.float32)
    queries = (project[0] + bias_full[0]).astype(jnp.bfloat16).reshape(head_shape)
    key_rows = project[1].astype(jnp.bfloat16).reshape(head_shape)
    values = (project[2] + bias_full[1]).astype(jnp.bfloat16).reshape(head_shape)
    blended, log_total = attend_forward(queries, key_rows, values, min(512, seq_rows))
    projected = rows_sum_forward(
        jnp.einsum("ise,ed->isd", blended, out_full, preferred_element_type=jnp.float32)
    )
    branch_one = projected + vector_full[2]
    hidden = base + vector_full[3] * branch_one
    normed_two = layer_norm(hidden, vector_full[4], vector_full[5]).astype(jnp.bfloat16)
    normed_two_all = rows_forward(normed_two)
    pre_act = jnp.einsum(
        "isd,df->isf", normed_two_all, up_full, preferred_element_type=jnp.float32
    ) + bias_full[2:].reshape(-1)
    activ = exact_gelu(pre_act).astype(jnp.bfloat16)
    branch_two = (
        rows_sum_forward(
            jnp.einsum("isf,fd->isd", activ, down_full, preferred_element_type=jnp.float32)
        )
        + vector_full[6]
    )
    output = hidden + vector_full[7] * branch_two
    saved = (
        base,
        hidden,
        branch_one,
        branch_two,
        normed_all,
        queries,
        key_rows,
        values,
        log_total,
        blended,
        normed_two_all,
        pre_act,
        activ,
    )
    return (output.astype(jnp.bfloat16), saved)


def backward(grad_output, saved, params):
    qkv_full, out_full, up_full, down_full, bias_full, vector_full = params
    (
        base,
        hidden,
        branch_one,
        branch_two,
        normed_all,
        queries,
        key_rows,
        values,
        log_total,
        blended,
        normed_two_all,
        pre_act,
        activ,
    ) = saved
    local_width = qkv_full.shape[2]
    grad_out = grad_output.astype(jnp.float32)
    grad_scale_two = jnp.sum(grad_out * branch_two, axis=(0, 1))
    grad_bias_two = jnp.sum(grad_out, axis=(0, 1)) * vector_full[7]
    grad_branch = rows_backward((grad_out * vector_full[7]).astype(jnp.bfloat16))
    grad_down = jnp.einsum("isf,isd->fd", activ, grad_branch, preferred_element_type=jnp.float32)
    grad_activ = jnp.einsum(
        "isd,fd->isf", grad_branch, down_full, preferred_element_type=jnp.float32
    )
    grad_pre = jax.vjp(exact_gelu, pre_act)[1](grad_activ)[0].astype(jnp.bfloat16)
    grad_up_bias = jnp.sum(grad_pre, axis=(0, 1), dtype=jnp.float32)
    grad_up = jnp.einsum(
        "isd,isf->df", normed_two_all, grad_pre, preferred_element_type=jnp.float32
    )
    grad_normed_two = rows_sum_backward(
        jnp.einsum("isf,df->isd", grad_pre, up_full, preferred_element_type=jnp.float32)
    )
    norm_back_two = jax.vjp(layer_norm, hidden, vector_full[4], vector_full[5])[1]
    grad_hidden, grad_gain_two, grad_shift_two = norm_back_two(grad_normed_two)
    grad_hidden = grad_out + grad_hidden
    grad_scale_one = jnp.sum(grad_hidden * branch_one, axis=(0, 1))
    grad_out_bias = jnp.sum(grad_hidden, axis=(0, 1)) * vector_full[3]
    grad_projected = rows_backward((grad_hidden * vector_full[3]).astype(jnp.bfloat16))
    grad_out_weight = jnp.einsum(
        "ise,isd->ed", blended, grad_projected, preferred_element_type=jnp.float32
    )
    grad_blended = jnp.einsum(
        "isd,ed->ise", grad_projected, out_full, preferred_element_type=jnp.float32
    ).astype(jnp.bfloat16)
    grad_project = attend_backward(
        queries, key_rows, values, grad_blended, log_total, min(512, queries.shape[1])
    )
    grad_query_bias = jnp.sum(grad_project[0], axis=(0, 1), dtype=jnp.float32)
    grad_value_bias = jnp.sum(grad_project[2], axis=(0, 1), dtype=jnp.float32)
    grad_qkv = jnp.einsum(
        "isd,tise->tde", normed_all, grad_project, preferred_element_type=jnp.float32
    )
    grad_normed = rows_sum_backward(
        jnp.einsum("tise,tde->isd", grad_project, qkv_full, preferred_element_type=jnp.float32)
    )
    norm_back_one = jax.vjp(layer_norm, base, vector_full[0], vector_full[1])[1]
    grad_input_part, grad_gain_one, grad_shift_one = norm_back_one(grad_normed)
    grad_input = grad_hidden + grad_input_part
    grad_vectors = jnp.stack(
        [
            grad_gain_one,
            grad_shift_one,
            grad_out_bias,
            grad_scale_one,
            grad_gain_two,
            grad_shift_two,
            grad_bias_two,
            grad_scale_two,
        ]
    )
    grad_biases = jnp.concatenate(
        [jnp.stack([grad_query_bias, grad_value_bias]), grad_up_bias.reshape(-1, local_width)], 0
    )
    return (grad_input, (grad_qkv, grad_out_weight, grad_up, grad_down, grad_biases, grad_vectors))


def local_general(
    tokens,
    cotangent,
    qkv_weight,
    qkv_first,
    qkv_second,
    out_weight,
    out_first,
    out_second,
    up_weight,
    up_first,
    up_second,
    down_weight,
    down_first,
    down_second,
    head_biases,
    bias_first,
    bias_second,
    vectors,
    vector_first,
    vector_second,
):

    def gather_params():
        gathered = (
            lax.all_gather(qkv_weight.astype(jnp.bfloat16), "dp", axis=1, tiled=True),
            lax.all_gather(out_weight.astype(jnp.bfloat16), "dp", axis=1, tiled=True),
            lax.all_gather(up_weight.astype(jnp.bfloat16), "dp", axis=0, tiled=True),
            lax.all_gather(down_weight.astype(jnp.bfloat16), "dp", axis=2, tiled=True),
            lax.all_gather(head_biases.astype(jnp.bfloat16), "dp", axis=1, tiled=True),
            lax.all_gather(vectors.astype(jnp.bfloat16), "dp", axis=1, tiled=True),
        )
        qkv_full, out_full, up_full, down_full, bias_full, vector_full = gathered
        return (
            qkv_full,
            out_full,
            up_full.reshape(up_full.shape[0], -1),
            down_full.reshape(-1, down_full.shape[2]),
            bias_full.astype(jnp.float32),
            vector_full.astype(jnp.float32),
        )

    grad_sums = None
    outputs = []
    input_grads = []
    for micro_step in range(MICRO):
        params_fwd = gather_params()
        output, saved = forward(tokens[micro_step], params_fwd)
        outputs.append(output)
        params_back = gather_params()
        grad_input, grads = backward(cotangent[micro_step], saved, params_back)
        input_grads.append(grad_input)
        if grad_sums is None:
            grad_sums = grads
        else:
            grad_sums = tuple((old_sum + new_part for old_sum, new_part in zip(grad_sums, grads)))
    grad_qkv, grad_out_weight, grad_up, grad_down, grad_biases, grad_vectors = grad_sums
    grad_up = grad_up.reshape(-1, up_weight.shape[1], up_weight.shape[2])
    grad_down = grad_down.reshape(down_weight.shape[0], down_weight.shape[1], -1)
    reduced = (
        lax.psum_scatter(grad_qkv, "dp", scatter_dimension=1, tiled=True),
        lax.psum_scatter(grad_out_weight, "dp", scatter_dimension=1, tiled=True),
        lax.psum_scatter(grad_up, "dp", scatter_dimension=0, tiled=True),
        lax.psum_scatter(grad_down, "dp", scatter_dimension=2, tiled=True),
        lax.psum_scatter(grad_biases, "dp", scatter_dimension=1, tiled=True),
        lax.psum_scatter(grad_vectors, "dp", scatter_dimension=1, tiled=True),
    )
    vector_grad = lax.psum(reduced[5], "mp")
    grads = (reduced[0], reduced[1], reduced[2], reduced[3], reduced[4], vector_grad)
    params = (qkv_weight, out_weight, up_weight, down_weight, head_biases, vectors)
    firsts = (qkv_first, out_first, up_first, down_first, bias_first, vector_first)
    seconds = (qkv_second, out_second, up_second, down_second, bias_second, vector_second)
    updated = [
        adam_update(params[slot], firsts[slot], seconds[slot], grads[slot], RATES[slot])
        for slot in range(6)
    ]
    return (
        jnp.stack(outputs),
        jnp.stack(input_grads),
        updated[0][0],
        updated[0][1],
        updated[0][2],
        updated[1][0],
        updated[1][1],
        updated[1][2],
        updated[2][0],
        updated[2][1],
        updated[2][2],
        updated[3][0],
        updated[3][1],
        updated[3][2],
        updated[4][0],
        updated[4][1],
        updated[4][2],
        updated[5][0],
        updated[5][1],
        updated[5][2],
    )


ZS, YS, MP = (4, 2, 4)
DP = ZS * YS
LANES = 128
BF = jnp.bfloat16
F32 = jnp.float32


def swap_z(part, step):
    return lax.ppermute(
        part, "dp", [(z * YS + y, (z ^ step) * YS + y) for z in range(ZS) for y in range(YS)]
    )


def swap_y(part):
    return lax.ppermute(part, "dp", [(each, each ^ 1) for each in range(DP)])


def swap_mp(part, step):
    return lax.ppermute(part, "mp", [(each, each ^ step) for each in range(MP)])


class Chain:
    def __init__(self, steps, *args):
        self.own = None
        self.result = None
        self.steps = steps(self, *args)
        self.flight = next(self.steps)

    def land(self, arrived):
        try:
            self.flight = self.steps.send(arrived)
        except StopIteration as end:
            self.flight = None
            self.result = end.value


def meet(values, *chains):
    values, flights = lax.optimization_barrier((values, [each.flight for each in chains]))
    for each, flight in zip(chains, flights):
        each.land(flight)
    return values


def join(rows, arrived, axis):
    return jnp.concatenate([rows, arrived], -2 if axis == "y" else -1)


def swap_plane(part, axis):
    return swap_y(part) if axis == "y" else swap_mp(part, 2)


def rows_z_steps(chain, shard):
    rows = shard
    for step in (1, 2):
        (arrived,) = yield [swap_z(rows, step)]
        rows = jnp.concatenate([rows, arrived], 0)
    return rows


def cut(part, axis, pieces):
    return jnp.split(part, pieces, -2 if axis == "y" else -1) if pieces > 1 else [part]


def gather_steps(chain, parts, orders, pieces=(1, 1)):
    for axes, count in zip(zip(*orders), pieces):
        sent = [cut(part, axis, count) for part, axis in zip(parts, axes)]
        for at in range(count):
            arrived = yield [swap_plane(each[at], axis) for each, axis in zip(sent, axes)]
            parts = [join(part, each, axis) for part, each, axis in zip(parts, arrived, axes)]
    chain.own = parts
    arrived = yield [swap_mp(part, 1) for part in parts]
    return arrived


def add_low(first, second):
    return (first.astype(F32) + second.astype(F32)).astype(BF)


def halve(total, axis):
    rows, width = total.shape[-2:]
    if axis == "y":
        return (total[..., : rows // 2, :], total[..., rows // 2 :, :])
    return (total[..., : width // 2], total[..., width // 2 :])


def reduce_steps(chain, other_parts, orders, pieces=(1, 1)):
    arrived = yield [swap_mp(part, 1) for part in other_parts]
    totals = [add_low(own, each) for own, each in zip(chain.own, arrived)]
    for axes, count in zip(zip(*orders), pieces):
        halves = [halve(total, axis) for total, axis in zip(totals, axes)]
        sent = [cut(half[1], axis, count) for half, axis in zip(halves, axes)]
        received = []
        for at in range(count):
            received.append((yield [swap_plane(each[at], axis) for each, axis in zip(sent, axes)]))
        totals = []
        for half, axis, each in zip(halves, axes, zip(*received)):
            whole = each[0] if count == 1 else jnp.concatenate(each, -2 if axis == "y" else -1)
            totals.append(add_low(half[0], whole))
    return totals


def sum_z_steps(chain, total):
    rows = total.shape[0] // ZS
    arrived = yield [swap_z(total[step * rows : (step + 1) * rows], step) for step in range(1, ZS)]
    total = total[:rows].astype(F32)
    for each in arrived:
        total = total + each.astype(F32)
    return total


def sum_z_halves_steps(chain, total):
    half = total.shape[0] // 2
    (arrived,) = yield [swap_z(total[half:], 2)]
    total = add_low(total[:half], arrived)
    (arrived,) = yield [swap_z(total[half // 2 :], 1)]
    return total[: half // 2].astype(F32) + arrived.astype(F32)


def image_steps(chain, far, near):
    (arrived,) = yield [swap_mp(far, 2)]
    second, passing = arrived
    (arrived,) = yield [swap_mp(jnp.stack([near(), passing]), 1)]
    return [arrived[0], second, arrived[1]]


def small_steps(chain, shard, vector_size):
    biases = shard[:, vector_size:]
    arrived = yield [swap_mp(biases, step) for step in range(1, MP)]
    rows = jnp.concatenate([shard] + arrived, 1)
    for step in (1, 2):
        arrived = yield [swap_z(rows, step)]
        rows = jnp.concatenate([rows] + arrived, 0)
    arrived = yield [swap_y(rows)]
    rows = jnp.concatenate([rows] + arrived, 0)
    biases = rows[:, vector_size:].reshape(DP, MP, -1).transpose(1, 0, 2)
    return (rows[:, :vector_size], biases)


def small_reduce_steps(chain, vector_part, bias_part):
    packed = [jnp.concatenate([vector_part, each], 1) for each in bias_part]
    arrived = yield [swap_mp(packed[step], step) for step in range(1, MP)]
    total = (packed[0] + arrived[0]) + (arrived[1] + arrived[2])
    arrived = yield [swap_y(total[ZS:])]
    total = total[:ZS] + arrived[0]
    arrived = yield [swap_z(total[step], step) for step in range(1, ZS)]
    total = total[0]
    for each in arrived:
        total = total + each
    return total


def norm_parts(values):
    center = values - jnp.mean(values, -1, keepdims=True)
    spread = lax.rsqrt(jnp.mean(center * center, -1, keepdims=True) + 1e-06)
    return (center * spread, spread)


def norm_back(grad, normal, spread, gain):
    scaled = grad * gain
    inner = scaled - jnp.mean(scaled, -1, keepdims=True)
    return spread * (inner - normal * jnp.mean(scaled * normal, -1, keepdims=True))


GAIN_ONE, SHIFT_ONE, OUT_BIAS, SCALE_ONE, GAIN_TWO, SHIFT_TWO, DOWN_BIAS, SCALE_TWO = range(8)


def vector_row(vector_ref, at):
    return vector_ref[at : at + 1, :]


def assemble_kernel(with_norm, place_ref, vector_ref, own_ref, *refs):
    out_ref, second_ref = refs[-2:]
    part_refs = [own_ref.at[0]] + list(refs[:-2])
    for at, part_ref in enumerate(part_refs):
        for block in range(DP):
            lanes = pl.ds(pl.multiple_of(place_ref[block] * LANES, LANES), LANES)
            out_ref[at, :, block * LANES : (block + 1) * LANES] = part_ref[:, lanes]
        values = out_ref[at].astype(F32)
        if with_norm:
            normal, _ = norm_parts(values)
            values = normal * vector_row(vector_ref, GAIN_ONE) + vector_row(vector_ref, SHIFT_ONE)
        else:
            values = values * vector_row(vector_ref, SCALE_TWO)
        second_ref[at] = values.astype(BF)


def assemble_image(place, vector_full, arrays, parts, with_norm):
    chunk_rows, width = parts[0].shape
    rows = chunk_rows // 4
    block = pl.BlockSpec((rows, width), lambda i, place_ref: (i, 0))
    result = pl.BlockSpec((MP, rows, width), lambda i, place_ref: (0, i, 0))
    shape = jax.ShapeDtypeStruct((MP, chunk_rows, width), BF)
    image, second = pl.pallas_call(
        functools.partial(assemble_kernel, with_norm),
        grid_spec=pltpu.PrefetchScalarGridSpec(
            num_scalar_prefetch=1,
            grid=(4,),
            in_specs=[
                pl.BlockSpec(vector_full.shape, lambda i, place_ref: (0, 0)),
                pl.BlockSpec((1, rows, width), lambda i, place_ref: (place_ref[DP], i, 0)),
            ]
            + [block] * len(parts),
            out_specs=[result] * 2,
        ),
        out_shape=[shape] * 2,
        compiler_params=pltpu.CompilerParams(vmem_limit_bytes=32 * 2**20),
        name="assemble_image",
    )(place, vector_full, arrays, *parts)
    return (image.reshape(-1, width), second.reshape(-1, width))


def spread_kernel(place_ref, own_ref, *refs):
    out_ref = refs[-1]
    mine = place_ref[DP]
    for at, part_ref in enumerate([own_ref] + list(refs[:-1])):
        for block in range(DP):
            lanes = pl.ds(pl.multiple_of(place_ref[block] * LANES, LANES), LANES)
            part = part_ref[:, block * LANES : (block + 1) * LANES]
            out_ref[mine ^ at, :, lanes] = part.astype(out_ref.dtype)


def spread_image(place, own, parts, dtype):
    chunk_rows, width = parts[0].shape
    rows = chunk_rows // 4
    block = pl.BlockSpec((rows, width), lambda i, place_ref: (i, 0))
    return pl.pallas_call(
        spread_kernel,
        grid_spec=pltpu.PrefetchScalarGridSpec(
            num_scalar_prefetch=1,
            grid=(4,),
            in_specs=[block] * (1 + len(parts)),
            out_specs=pl.BlockSpec((MP, rows, width), lambda i, place_ref: (0, i, 0)),
        ),
        out_shape=jax.ShapeDtypeStruct((MP, chunk_rows, width), dtype),
        compiler_params=pltpu.CompilerParams(vmem_limit_bytes=32 * 2**20),
        name="spread_image",
    )(place, own, *parts)


ROWS = 512


def product_nt(left_refs, right_refs):
    total = None
    for left_ref, right_ref in zip(left_refs, right_refs):
        part = lax.dot_general(
            left_ref[...], right_ref[...], (((1,), (1,)), ((), ())), preferred_element_type=F32
        )
        total = part if total is None else total + part
    return total


def add_rows(sums_ref, rows):
    @pl.when(pl.program_id(0) == 0)
    def _():
        sums_ref[...] = jnp.zeros_like(sums_ref)

    for at, each in enumerate(rows):
        sums_ref[at : at + 1, :] += jnp.sum(each, 0, keepdims=True)


def out_kernel(count, *refs):
    lefts, rights = (refs[:count], refs[count : 2 * count])
    vector_ref, base_ref, branch_ref, hidden_ref, normed_ref = refs[2 * count :]
    branch = product_nt(lefts, rights) + vector_row(vector_ref, OUT_BIAS)
    hidden = base_ref[...].astype(F32) + vector_row(vector_ref, SCALE_ONE) * branch
    normal, _ = norm_parts(hidden)
    branch_ref[...] = branch
    hidden_ref[...] = hidden
    normed = normal * vector_row(vector_ref, GAIN_TWO) + vector_row(vector_ref, SHIFT_TWO)
    normed_ref[...] = normed.astype(BF)


def down_kernel(count, *refs):
    lefts, rights = (refs[:count], refs[count : 2 * count])
    vector_ref, hidden_ref, output_ref, branch_ref = refs[2 * count :]
    branch = product_nt(lefts, rights) + vector_row(vector_ref, DOWN_BIAS)
    output = hidden_ref[...] + vector_row(vector_ref, SCALE_TWO) * branch
    output_ref[...] = output.astype(BF)
    branch_ref[...] = branch


def up_back_kernel(count, *refs):
    lefts, rights = (refs[:count], refs[count : 2 * count])
    vector_ref, hidden_ref, branch_ref, grad_ref, out_ref, low_ref, sums_ref = refs[2 * count :]
    grad_normed = product_nt(lefts, rights)
    normal, spread = norm_parts(hidden_ref[...])
    grad = norm_back(grad_normed, normal, spread, vector_row(vector_ref, GAIN_TWO))
    grad = grad + grad_ref[...].astype(F32)
    out_ref[...] = grad
    low_ref[...] = (grad * vector_row(vector_ref, SCALE_ONE)).astype(BF)
    add_rows(sums_ref, [grad_normed * normal, grad_normed, grad * branch_ref[...], grad])


def in_back_kernel(count, *refs):
    lefts, rights = (refs[:count], refs[count : 2 * count])
    vector_ref, base_ref, grad_ref, low_ref, sums_ref = refs[2 * count : 2 * count + 5]
    grad_normed = product_nt(lefts, rights)
    normal, spread = norm_parts(base_ref[...].astype(F32))
    grad = norm_back(grad_normed, normal, spread, vector_row(vector_ref, GAIN_ONE))
    grad = grad + grad_ref[...]
    low_ref[...] = grad.astype(BF)

    for own_ref in refs[2 * count + 5 :]:
        own_ref[...] = grad[: own_ref.shape[0]]
    add_rows(sums_ref, [grad_normed * normal, grad_normed])


def expand_kernel(left_ref, right_ref, bias_ref, activ_ref, slope_ref):
    values = jnp.dot(left_ref[...], right_ref[...], preferred_element_type=F32) + bias_ref[0:1, :]
    share = 0.5 * (1.0 + lax.erf(values * 0.7071067811865476))
    activ_ref[...] = (values * share).astype(BF)
    slope = share + values * (0.3989422804014327 * jnp.exp(-0.5 * values * values))
    slope_ref[...] = slope.astype(BF)


def expand(left, right, bias):
    rows, depth = left.shape
    width = right.shape[1]
    block = pl.BlockSpec((256, width), lambda i: (i, 0))
    return pl.pallas_call(
        expand_kernel,
        grid=(rows // 256,),
        in_specs=[
            pl.BlockSpec((256, depth), lambda i: (i, 0)),
            pl.BlockSpec((depth, width), lambda i: (0, 0), pipeline_mode=pl.Buffered(1)),
            pl.BlockSpec((1, width), lambda i: (0, 0)),
        ],
        out_specs=[block] * 2,
        out_shape=[jax.ShapeDtypeStruct((rows, width), BF)] * 2,
        compiler_params=pltpu.CompilerParams(vmem_limit_bytes=32 * 2**20),
        name="expand",
    )(left, right, bias.reshape(1, width))


def slope_kernel(left_ref, right_ref, slope_ref, grad_ref, sums_ref):
    grad = jnp.dot(left_ref[...], right_ref[...], preferred_element_type=F32)
    low = (grad * slope_ref[...].astype(F32)).astype(BF)
    grad_ref[...] = low
    add_rows(sums_ref, [low.astype(F32)])


def slope_product(left, right, slope):
    rows, depth = left.shape
    width = right.shape[1]
    block = pl.BlockSpec((256, width), lambda i: (i, 0))
    return pl.pallas_call(
        slope_kernel,
        grid=(rows // 256,),
        in_specs=[
            pl.BlockSpec((256, depth), lambda i: (i, 0)),
            pl.BlockSpec((depth, width), lambda i: (0, 0), pipeline_mode=pl.Buffered(1)),
            block,
        ],
        out_specs=[block, pl.BlockSpec((8, width), lambda i: (0, 0))],
        out_shape=[jax.ShapeDtypeStruct((rows, width), BF), jax.ShapeDtypeStruct((8, width), F32)],
        compiler_params=pltpu.CompilerParams(vmem_limit_bytes=32 * 2**20),
        name="slope_product",
    )(left, right, slope)


def row_call(kernel, name, lefts, rights, vector_full, row_inputs, outs, span=None, own_rows=0):
    rows, width = row_inputs[0].shape
    first, count = span or (0, rows // ROWS)
    rows = count * ROWS
    once = pl.Buffered(1)
    block = pl.BlockSpec((ROWS, width), lambda i: (i, 0))
    source = pl.BlockSpec((ROWS, width), lambda i: (i + first, 0))
    specs = {
        "sums": (pl.BlockSpec((8, width), lambda i: (0, 0)), jax.ShapeDtypeStruct((8, width), F32)),
        "own": (
            pl.BlockSpec((own_rows, width), lambda i: (0, 0)),
            jax.ShapeDtypeStruct((own_rows, width), F32),
        ),
    }
    pairs = [
        specs[each] if isinstance(each, str) else (block, jax.ShapeDtypeStruct((rows, width), each))
        for each in outs
    ]
    return pl.pallas_call(
        functools.partial(kernel, len(lefts)),
        grid=(count,),
        in_specs=[pl.BlockSpec((ROWS, each.shape[1]), lambda i: (i + first, 0)) for each in lefts]
        + [pl.BlockSpec(each.shape, lambda i: (0, 0), pipeline_mode=once) for each in rights]
        + [pl.BlockSpec(vector_full.shape, lambda i: (0, 0))]
        + [source] * len(row_inputs),
        out_specs=[each[0] for each in pairs],
        out_shape=[each[1] for each in pairs],
        compiler_params=pltpu.CompilerParams(vmem_limit_bytes=48 * 2**20),
        name=name,
    )(*lefts, *rights, vector_full, *row_inputs)


def lane_dot(left, right):
    return lax.dot_general(left, right, (((1,), (1,)), ((), ())), preferred_element_type=F32)


def head_masks(width):
    lane = lax.broadcasted_iota(jnp.int32, (1, width), 1)
    return [lane // DH == head for head in range(width // DH)]


def attend_kernel(block_rows, q_ref, k_ref, v_ref, o_ref, lse_ref):
    masks = head_masks(LANES)
    key_rows = k_ref[...]
    values = v_ref[...]
    zero = jnp.zeros((), BF)
    for block in range(q_ref.shape[0] // block_rows):
        rows = slice(block * block_rows, (block + 1) * block_rows)
        queries = q_ref[rows, :] * jnp.asarray(DH**-0.5, BF)
        blended = []
        for head, mask in enumerate(masks):
            scores = lane_dot(jnp.where(mask, queries, zero), key_rows)
            peak = jnp.max(scores, 1, keepdims=True)
            shifted = jnp.exp(scores - peak)
            total = jnp.sum(shifted, 1, keepdims=True)
            part = jnp.dot(shifted.astype(BF), values, preferred_element_type=F32)
            blended.append(part * (1.0 / total))
            log_total = jnp.broadcast_to(peak + jnp.log(total), (block_rows, LANES))
            lse_ref[0, head : head + 1, rows] = jnp.transpose(log_total)[0:1, :]
        o_ref[rows, :] = jnp.where(masks[0], blended[0], blended[1]).astype(BF)


def attend_back_kernel(
    block_rows, q_ref, k_ref, v_ref, g_ref, lse_ref, out_ref, dk_acc, dv_acc
):
    masks = head_masks(LANES)
    key_rows = k_ref[...]
    values = v_ref[...]
    zero = jnp.zeros((), BF)
    factor = DH**-0.5
    key_heads = [jnp.where(mask, key_rows, zero) for mask in masks]
    for block in range(q_ref.shape[0] // block_rows):
        rows = slice(block * block_rows, (block + 1) * block_rows)
        queries = q_ref[rows, :] * jnp.asarray(factor, BF)
        grads = g_ref[rows, :]
        grad_query = None
        grad_keys = None
        grad_values = None
        for head, mask in enumerate(masks):
            query_head = jnp.where(mask, queries, zero)
            grad_head = jnp.where(mask, grads, zero)
            scores = lane_dot(key_rows, query_head)
            weights = jnp.exp(scores - lse_ref[0, head : head + 1, rows])
            value_part = jnp.dot(weights.astype(BF), grad_head, preferred_element_type=F32)
            grad_rows = lane_dot(values, grad_head)
            delta = jnp.sum(grad_rows * weights, 0, keepdims=True)
            grad_scores = (weights * (grad_rows - delta)).astype(BF)
            key_part = jnp.dot(grad_scores, query_head, preferred_element_type=F32)
            query_part = lax.dot_general(
                grad_scores, key_heads[head], (((0,), (0,)), ((), ())), preferred_element_type=F32
            )
            grad_query = query_part if head == 0 else grad_query + query_part
            grad_keys = key_part if head == 0 else grad_keys + key_part
            grad_values = value_part if head == 0 else grad_values + value_part
        out_ref[rows, 0:LANES] = (grad_query * factor).astype(BF)
        if block == 0:
            dk_acc[...] = grad_keys
            dv_acc[...] = grad_values
        else:
            dk_acc[...] += grad_keys
            dv_acc[...] += grad_values
    out_ref[:, LANES : 2 * LANES] = dk_acc[...].astype(BF)
    out_ref[:, 2 * LANES : 3 * LANES] = dv_acc[...].astype(BF)


def kind_spec(rows, kind):
    return pl.BlockSpec((rows, LANES), lambda p: (0, p * 3 + kind))


def attend(heads):
    rows, width = heads.shape
    pairs = width // LANES // 3
    return pl.pallas_call(
        functools.partial(attend_kernel, 256),
        grid=(pairs,),
        in_specs=[kind_spec(rows, kind) for kind in range(3)],
        out_specs=[
            pl.BlockSpec((rows, LANES), lambda p: (0, p)),
            pl.BlockSpec((1, 8, rows), lambda p: (p, 0, 0)),
        ],
        out_shape=[
            jax.ShapeDtypeStruct((rows, pairs * LANES), BF),
            jax.ShapeDtypeStruct((pairs, 8, rows), F32),
        ],
        compiler_params=pltpu.CompilerParams(vmem_limit_bytes=32 * 2**20),
        name="attend",
    )(heads, heads, heads)


def attend_back(heads, grad_blended, log_total):
    rows, width = heads.shape
    pairs = width // LANES // 3
    return pl.pallas_call(
        functools.partial(attend_back_kernel, 256),
        grid=(pairs,),
        in_specs=[kind_spec(rows, kind) for kind in range(3)]
        + [
            pl.BlockSpec((rows, LANES), lambda p: (0, p)),
            pl.BlockSpec((1, 8, rows), lambda p: (p, 0, 0)),
        ],
        out_specs=pl.BlockSpec((rows, 3 * LANES), lambda p: (0, p)),
        out_shape=jax.ShapeDtypeStruct((rows, width), BF),
        scratch_shapes=[pltpu.VMEM((rows, LANES), F32)] * 2,
        compiler_params=pltpu.CompilerParams(vmem_limit_bytes=32 * 2**20),
        name="attend_back",
    )(heads, heads, heads, grad_blended, log_total)


def dot_nn(left, right):
    return lax.dot_general(left, right, (((1,), (0,)), ((), ())), preferred_element_type=F32)


def dot_nt(left, right):
    return lax.dot_general(left, right, (((1,), (1,)), ((), ())), preferred_element_type=F32)


def dot_tn(left, right):
    return lax.dot_general(left, right, (((0,), (0,)), ((), ())), preferred_element_type=F32)


def local_image(
    tokens,
    cotangent,
    qkv_weight,
    qkv_first,
    qkv_second,
    out_weight,
    out_first,
    out_second,
    up_weight,
    up_first,
    up_second,
    down_weight,
    down_first,
    down_second,
    head_biases,
    bias_first,
    bias_second,
    vectors,
    vector_first,
    vector_second,
):
    dp_at = lax.axis_index("dp")
    mp_at = lax.axis_index("mp")
    units = up_weight.shape[1]
    half_units = units // 2
    block_width = qkv_weight.shape[2]
    depth = qkv_weight.shape[1]
    bias_width = head_biases.shape[1]
    chunk_rows, width = tokens.shape[2:]
    order = [((zk * YS) + yk) for yk in range(YS) for zk in range(ZS)]
    place = jnp.stack([dp_at ^ each for each in order] + [mp_at]).astype(jnp.int32)
    cores = (0, 1)

    def fetch_image(array):
        chunks = array[:, 0]

        def chunk(step):
            return lax.dynamic_index_in_dim(chunks, mp_at ^ step, 0, keepdims=False)

        return Chain(image_steps, jnp.stack([chunk(2), chunk(3)]), lambda: chunk(1))

    def send_back(low):
        chunks = low.reshape(MP, chunk_rows, width)
        return Chain(image_steps, chunks[2:], lambda: chunks[1])

    small_shard = jnp.concatenate(
        [vectors.astype(BF).reshape(-1), head_biases.astype(BF).reshape(-1)]
    ).reshape(1, -1)
    vector_size = vectors.size
    kinds = qkv_weight.shape[0]
    qkv_shard = qkv_weight.astype(BF).reshape(kinds, depth, 2, LANES).transpose(1, 2, 0, 3)
    qkv_shard = qkv_shard.reshape(depth, -1)
    up_shard = jnp.concatenate(
        [out_weight.T.astype(BF), up_weight.astype(BF).reshape(depth, -1)], 1
    )
    down_shard = down_weight.transpose(2, 0, 1).astype(BF).reshape(depth, -1)
    both = ("xy", "yx")
    small = Chain(small_steps, small_shard, vector_size)
    rows_qkv = Chain(rows_z_steps, qkv_shard)
    rows_up = Chain(rows_z_steps, up_shard)
    tokens = meet(tokens, small, rows_qkv)
    fetch_tokens = fetch_image(tokens)
    meet((), small)
    meet((), small, rows_qkv, rows_up)
    part_a, part_b = jnp.split(rows_qkv.result, 2, 1)
    get_qkv = [Chain(gather_steps, [part_a], ("yx",)), Chain(gather_steps, [part_b], ("xy",))]
    meet((), small, get_qkv[0], fetch_tokens)
    tokens = meet(tokens, fetch_tokens)

    vector_full, bias_small = small.result
    vector_full = vector_full.reshape(DP, vectors.shape[0], LANES).transpose(1, 0, 2)
    vector_full = vector_full.reshape(vectors.shape[0], width).astype(F32)
    back_places = jnp.stack([((each ^ dp_at) & 1) * ZS + ((each ^ dp_at) >> 1) for each in range(DP)])
    bias_rows = jnp.take(bias_small, back_places, axis=1).reshape(2, 2, DP, -1, bias_width)
    bias_full = bias_rows.transpose(1, 3, 0, 2, 4).reshape(2, head_biases.shape[0], 2, block_width)
    bias_full = bias_full.astype(F32)

    base, normed_one = assemble_image(place, vector_full, tokens[:, 0], fetch_tokens.result, True)
    normed_one = meet(normed_one, *get_qkv)

    def project(core, half, weight):
        lanes = slice(half * LANES, (half + 1) * LANES)
        zero = jnp.zeros((2, LANES), F32)
        bias = jnp.stack([bias_full[core, 0, :, lanes], zero, bias_full[core, 1, :, lanes]], 1)
        return (dot_nn(normed_one, weight) + bias.reshape(-1)).astype(BF)

    heads, blended, log_total = ([[None, None], [None, None]] for _ in range(3))

    def forward_heads(core, half):
        blended[core][half], log_total[core][half] = attend(heads[core][half])

    heads[0][0] = project(0, 0, get_qkv[0].own[0])
    forward_heads(0, 0)
    blended[0][0], normed_one, down_shard = meet(
        (blended[0][0], normed_one, down_shard), *get_qkv, rows_up
    )
    out_rows, up_rows = jnp.split(rows_up.result, [block_width], 1)
    get_out = Chain(gather_steps, [jnp.stack(jnp.split(out_rows, 2, 1))], ("yx",))
    get_up = Chain(gather_steps, jnp.split(up_rows, 2, 1), both, (1, 2))
    rows_down = Chain(rows_z_steps, down_shard)
    heads[0][1] = project(0, 1, get_qkv[1].own[0])
    forward_heads(0, 1)
    blended[0][1], normed_one = meet(
        (blended[0][1], normed_one), get_qkv[1], get_out, get_up, rows_down
    )
    w_qkv = [[each.own[0] for each in get_qkv], [each.result[0] for each in get_qkv]]
    heads[1][0] = project(1, 0, w_qkv[1][0])
    forward_heads(1, 0)
    blended[1][0], normed_one = meet(
        (blended[1][0], normed_one), get_out, rows_down, get_up
    )
    get_down = Chain(gather_steps, jnp.split(rows_down.result, 2, 1), both)
    heads[1][1] = project(1, 1, w_qkv[1][1])
    forward_heads(1, 1)
    blended = meet(blended, get_up, get_out)
    w_out = [[each[0][half] for half in (0, 1)] for each in (get_out.own, get_out.result)]
    pairs = [(core, half) for core in cores for half in (0, 1)]
    branch_one, hidden, normed_two = row_call(
        out_kernel,
        "out_norm",
        [blended[core][half] for core, half in pairs],
        [w_out[core][half] for core, half in pairs],
        vector_full,
        [base],
        [F32, F32, BF],
    )
    activ, slope = ({}, {})

    def expand_units(core, weights):
        for half in (0, 1):
            rows = bias_full[core, 2 + half * half_units : 2 + (half + 1) * half_units]
            unit_bias = rows.transpose(1, 0, 2).reshape(-1)
            activ[half, core], slope[half, core] = expand(normed_two, weights[half], unit_bias)

    expand_units(0, get_up.own)
    activ, normed_two = meet((activ, normed_two), get_up, get_down)
    w_up = [get_up.own, get_up.result]
    expand_units(1, w_up[1])
    activ, slope, cotangent = meet((activ, slope, cotangent), get_down)
    fetch_cotangent = fetch_image(cotangent)
    activ = meet(activ, get_down)
    w_down = [get_down.own, get_down.result]
    parts = [(half, core) for core in (1, 0) for half in (0, 1)]
    output, branch_two = row_call(
        down_kernel,
        "down_output",
        [activ[each] for each in parts],
        [w_down[core][half] for half, core in parts],
        vector_full,
        [hidden],
        [BF, F32],
    )
    output = meet(output, fetch_cotangent)
    output, cotangent = meet((output, cotangent), fetch_cotangent)
    grad_out, grad_branch = assemble_image(
        place, vector_full, cotangent[:, 0], fetch_cotangent.result, False
    )

    def reduce_pairs(left, rights, pieces):
        chain = Chain(reduce_steps, [dot_tn(left, rights[half, 1]).astype(BF) for half in (0, 1)], both[::-1], pieces)
        chain.own = [dot_tn(left, rights[half, 0]).astype(BF) for half in (0, 1)]
        return chain

    sum_down = reduce_pairs(grad_branch, activ, (2, 1))
    grad_branch, output, slope = meet((grad_branch, output, slope), sum_down)
    send_output = send_back(output)
    grad_pre, unit_sums = ({}, {})
    for half, core in parts:
        grad_pre[half, core], unit_sums[half, core] = slope_product(
            grad_branch, w_down[core][half], slope[half, core]
        )
        if (half, core) == (0, 0):
            grad_pre, grad_branch = meet((grad_pre, grad_branch), sum_down)
    grad_pre, normed_two = meet((grad_pre, normed_two))
    sum_up = reduce_pairs(normed_two, grad_pre, (1, 1))
    grad_pre = meet(grad_pre, sum_down)
    grad_hidden, grad_projected, sums_one = row_call(
        up_back_kernel,
        "up_norm_back",
        [grad_pre[each] for each in parts],
        [w_up[core][half] for half, core in parts],
        vector_full,
        [hidden, branch_one, grad_out],
        [F32, BF, "sums"],
    )
    grad_projected = meet(grad_projected, sum_up, sum_down, send_output)
    rows_down = Chain(sum_z_halves_steps, jnp.concatenate(sum_down.result, 1))
    grad_w_out = [
        jnp.stack([dot_tn(grad_projected, each).astype(BF) for each in blended[core]]) for core in cores
    ]
    sum_out = Chain(reduce_steps, [grad_w_out[1]], ("xy",))
    sum_out.own = [grad_w_out[0]]
    grad_blended = [[dot_nn(grad_projected, each).astype(BF) for each in w_out[core]] for core in cores]
    grad_heads = [[None, None], [None, None]]

    def back_heads(core, half):
        grad_heads[core][half] = attend_back(
            heads[core][half], grad_blended[core][half], log_total[core][half]
        )
        return dot_tn(normed_one, grad_heads[core][half]).astype(BF)

    other = back_heads(1, 0)
    other, grad_blended = meet((other, grad_blended), sum_up, sum_out, rows_down, send_output)
    sum_qkv = [Chain(reduce_steps, [other], ("xy",)), None]
    sum_qkv[0].own = [back_heads(0, 0)]
    grad_heads[0][0], grad_blended = meet(
        (grad_heads[0][0], grad_blended), sum_qkv[0], sum_out, sum_up, rows_down
    )
    rows_up = Chain(sum_z_halves_steps, jnp.concatenate(sum_up.result, 1))
    other = back_heads(1, 1)
    other, grad_blended = meet((other, grad_blended), sum_out, sum_qkv[0])
    sum_qkv[1] = Chain(reduce_steps, [other], ("yx",))
    out_rows = jnp.concatenate([sum_out.result[0][0], sum_out.result[0][1]], 1)
    sum_qkv[1].own = [back_heads(0, 1)]
    grad_heads = meet(grad_heads, sum_qkv[0], sum_qkv[1], rows_up)

    def input_back(span, outs):
        return row_call(
            in_back_kernel,
            "in_norm_back",
            [grad_heads[core][half] for core, half in pairs],
            [w_qkv[core][half] for core, half in pairs],
            vector_full,
            [base, grad_hidden],
            outs,
            span,
            chunk_rows,
        )

    grad_far, sums_far = input_back((1, 1), [BF, "sums"])
    grad_near = []
    send_grad = Chain(
        image_steps, grad_far.reshape(2, chunk_rows, width), lambda: grad_near[0][chunk_rows:]
    )
    grad_heads = meet(grad_heads, sum_qkv[1])
    near, sums_near, own_grad = input_back((0, 1), [BF, "sums", "own"])
    grad_near.append(near)
    sums_input = sums_far + sums_near

    grad_vectors = jnp.stack(
        [
            sums_input[0],
            sums_input[1],
            sums_one[3] * vector_full[SCALE_ONE],
            sums_one[2],
            sums_one[0],
            sums_one[1],
            jnp.sum(grad_out.astype(F32), 0) * vector_full[SCALE_TWO],
            jnp.sum(grad_out.astype(F32) * branch_two, 0),
        ]
    )
    grad_vectors = grad_vectors.reshape(-1, DP, LANES).transpose(1, 0, 2).reshape(DP, -1)
    bias_parts = []
    for core in cores:
        head_part = [
            jnp.sum(each.astype(F32), 0).reshape(2, kinds, LANES) for each in grad_heads[core]
        ]
        rows = [jnp.concatenate([each[:, kind] for each in head_part], 1) for kind in (0, 2)]
        for half in (0, 1):
            unit_part = unit_sums[half, core][0].reshape(2, half_units, block_width)
            rows += [unit_part[:, at] for at in range(half_units)]
        bias_parts.append(jnp.stack(rows, 1))
    grad_biases = jnp.stack(bias_parts, 1).reshape(MP, -1, DP, bias_width).transpose(0, 2, 1, 3)
    grad_biases = jnp.take(grad_biases, place[:DP], axis=1).reshape(MP, DP, -1)
    sum_small = Chain(small_reduce_steps, grad_vectors, grad_biases)
    meet((), sum_qkv[1])
    rows_qkv = Chain(sum_z_steps, jnp.concatenate(sum_qkv[0].result + sum_qkv[1].result + [out_rows], 1))
    meet((), rows_up)
    meet((), send_grad)
    meet((), send_grad)
    meet((), rows_qkv)
    for _ in range(3):
        meet((), sum_small)
    layer_output = spread_image(place, output[:chunk_rows], send_output.result, BF)[:, None]
    input_grad = spread_image(place, own_grad, send_grad.result, F32)[:, None]

    small_total = sum_small.result
    vector_grad = small_total[:vector_size].reshape(vectors.shape)
    bias_grad = small_total[vector_size:].reshape(head_biases.shape)
    qkv_size = kinds * block_width
    qkv_grad = rows_qkv.result[:, :qkv_size].reshape(depth, 2, kinds, LANES).transpose(2, 0, 1, 3)
    grads = (
        qkv_grad.reshape(qkv_weight.shape),
        rows_qkv.result[:, qkv_size:].T,
        rows_up.result.reshape(depth, units, block_width),
        rows_down.result.reshape(depth, units, block_width).transpose(1, 2, 0),
        bias_grad,
        vector_grad,
    )
    params = (qkv_weight, out_weight, up_weight, down_weight, head_biases, vectors)
    firsts = (qkv_first, out_first, up_first, down_first, bias_first, vector_first)
    seconds = (qkv_second, out_second, up_second, down_second, bias_second, vector_second)
    results = [layer_output, input_grad]
    for slot in range(6):
        results.extend(
            adam_update(params[slot], firsts[slot], seconds[slot], grads[slot], RATES[slot])
        )
    return tuple(results)


def solution(mesh):
    whole_image = mesh.shape["mp"] == MICRO == MP and mesh.shape["dp"] == DP
    return jax.shard_map(
        local_image if whole_image else local_general,
        mesh=mesh,
        in_specs=(
            P(None, "dp", "mp", None),
            P(None, "dp", "mp", None),
            P(None, "dp", "mp"),
            P(None, "dp", "mp"),
            P(None, "dp", "mp"),
            P("mp", "dp"),
            P("mp", "dp"),
            P("mp", "dp"),
            P("dp", None, "mp"),
            P("dp", None, "mp"),
            P("dp", None, "mp"),
            P(None, "mp", "dp"),
            P(None, "mp", "dp"),
            P(None, "mp", "dp"),
            P(None, ("mp", "dp")),
            P(None, ("mp", "dp")),
            P(None, ("mp", "dp")),
            P(None, "dp"),
            P(None, "dp"),
            P(None, "dp"),
        ),
        out_specs=(
            P(None, "dp", "mp", None),
            P(None, "dp", "mp", None),
            P(None, "dp", "mp"),
            P(None, "dp", "mp"),
            P(None, "dp", "mp"),
            P("mp", "dp"),
            P("mp", "dp"),
            P("mp", "dp"),
            P("dp", None, "mp"),
            P("dp", None, "mp"),
            P("dp", None, "mp"),
            P(None, "mp", "dp"),
            P(None, "mp", "dp"),
            P(None, "mp", "dp"),
            P(None, ("mp", "dp")),
            P(None, ("mp", "dp")),
            P(None, ("mp", "dp")),
            P(None, "dp"),
            P(None, "dp"),
            P(None, "dp"),
        ),
        check_vma=False,
    )
```

```python
import functools

import jax
import jax.numpy as jnp
from jax import lax
from jax.experimental import pallas as pl
from jax.experimental.pallas import tpu as pltpu
from jax.sharding import PartitionSpec as P

DH = 64
MICRO = 4
STEP = 10


RATES = (0.05, 0.2, 0.05, 0.03, 0.5, 0.5)


def layer_norm(values, gain, shift):
    center = values - jnp.mean(values, -1, keepdims=True)
    spread = jnp.mean(center * center, -1, keepdims=True)
    return center * lax.rsqrt(spread + 1e-06) * gain + shift


def exact_gelu(values):
    return jax.nn.gelu(values, approximate=False)


def adam_update(weight, first, second, grad, rate):
    first_new = 0.9 * first + 0.1 * grad
    second_new = 0.999 * second + 0.001 * grad * grad
    corrected = first_new / (1.0 - 0.9**STEP)
    scaled = jnp.sqrt(second_new / (1.0 - 0.999**STEP))
    weight_new = weight - rate * (corrected / (scaled + 1e-08) + 0.05 * weight)
    return (weight_new, first_new, second_new)


def attend_forward(queries, key_rows, values, block_rows):
    images, seq_rows, head_count, head_width = queries.shape
    block_count = seq_rows // block_rows
    factor = head_width ** (-0.5)
    query_blocks = jnp.moveaxis(
        queries.reshape(images, block_count, block_rows, head_count, head_width), 1, 0
    )

    def one_block(query_part):
        scores = (
            jnp.einsum("iqhe,ikhe->ihqk", query_part, key_rows, preferred_element_type=jnp.float32)
            * factor
        )
        row_peak = jnp.max(scores, -1, keepdims=True)
        shifted = jnp.exp(scores - row_peak)
        row_total = jnp.sum(shifted, -1, keepdims=True)
        softmax_rows = (shifted / row_total).astype(jnp.bfloat16)
        blended = jnp.einsum(
            "ihqk,ikhe->iqhe", softmax_rows, values, preferred_element_type=jnp.float32
        )
        return (blended, row_peak[..., 0] + jnp.log(row_total[..., 0]))

    blended, log_total = lax.map(one_block, query_blocks)
    blended = jnp.moveaxis(blended, 0, 1).reshape(images, seq_rows, head_count * head_width)
    return (blended.astype(jnp.bfloat16), log_total)


def attend_backward(queries, key_rows, values, grad_blended, log_total, block_rows):
    images, seq_rows, head_count, head_width = queries.shape
    block_count = seq_rows // block_rows
    factor = head_width ** (-0.5)
    split_shape = (images, block_count, block_rows, head_count, head_width)
    query_blocks = jnp.moveaxis(queries.reshape(split_shape), 1, 0)
    grad_blocks = jnp.moveaxis(grad_blended.reshape(split_shape), 1, 0)

    def one_block(carry, inputs_part):
        query_part, grad_part, total_part = inputs_part
        grad_keys, grad_values = carry
        scores = (
            jnp.einsum("iqhe,ikhe->ihqk", query_part, key_rows, preferred_element_type=jnp.float32)
            * factor
        )
        softmax_rows = jnp.exp(scores - total_part[..., None])
        grad_values = grad_values + jnp.einsum(
            "ihqk,iqhe->ikhe",
            softmax_rows.astype(jnp.bfloat16),
            grad_part,
            preferred_element_type=jnp.float32,
        )
        grad_rows = jnp.einsum(
            "iqhe,ikhe->ihqk", grad_part, values, preferred_element_type=jnp.float32
        )
        grad_scores = softmax_rows * (
            grad_rows - jnp.sum(grad_rows * softmax_rows, -1, keepdims=True)
        )
        grad_scores = grad_scores.astype(jnp.bfloat16)
        grad_query = (
            jnp.einsum("ihqk,ikhe->iqhe", grad_scores, key_rows, preferred_element_type=jnp.float32)
            * factor
        )
        grad_keys = (
            grad_keys
            + jnp.einsum(
                "ihqk,iqhe->ikhe", grad_scores, query_part, preferred_element_type=jnp.float32
            )
            * factor
        )
        return ((grad_keys, grad_values), grad_query)

    zero_grad = jnp.zeros(queries.shape, jnp.float32)
    (grad_keys, grad_values), grad_query = lax.scan(
        one_block, (zero_grad, zero_grad), (query_blocks, grad_blocks, log_total)
    )
    flat_shape = (images, seq_rows, head_count * head_width)
    grad_query = jnp.moveaxis(grad_query, 0, 1).reshape(flat_shape)
    stacked = jnp.stack(
        [grad_query, grad_keys.reshape(flat_shape), grad_values.reshape(flat_shape)]
    )
    return stacked.astype(jnp.bfloat16)


def rows_forward(part):
    return lax.all_gather(part, "mp", axis=1, tiled=True)


def rows_sum_forward(part):
    return lax.psum_scatter(part, "mp", scatter_dimension=1, tiled=True)


def rows_backward(part):
    return lax.all_gather(part, "mp", axis=1, tiled=True)


def rows_sum_backward(part):
    return lax.psum_scatter(part, "mp", scatter_dimension=1, tiled=True)


def forward(inputs, params):
    qkv_full, out_full, up_full, down_full, bias_full, vector_full = params
    base = inputs.astype(jnp.float32)
    normed = layer_norm(base, vector_full[0], vector_full[1]).astype(jnp.bfloat16)
    normed_all = rows_forward(normed)
    images, seq_rows = (normed_all.shape[0], normed_all.shape[1])
    head_shape = (images, seq_rows, -1, DH)
    project = jnp.einsum("isd,tde->tise", normed_all, qkv_full, preferred_element_type=jnp.float32)
    queries = (project[0] + bias_full[0]).astype(jnp.bfloat16).reshape(head_shape)
    key_rows = project[1].astype(jnp.bfloat16).reshape(head_shape)
    values = (project[2] + bias_full[1]).astype(jnp.bfloat16).reshape(head_shape)
    blended, log_total = attend_forward(queries, key_rows, values, min(512, seq_rows))
    projected = rows_sum_forward(
        jnp.einsum("ise,ed->isd", blended, out_full, preferred_element_type=jnp.float32)
    )
    branch_one = projected + vector_full[2]
    hidden = base + vector_full[3] * branch_one
    normed_two = layer_norm(hidden, vector_full[4], vector_full[5]).astype(jnp.bfloat16)
    normed_two_all = rows_forward(normed_two)
    pre_act = jnp.einsum(
        "isd,df->isf", normed_two_all, up_full, preferred_element_type=jnp.float32
    ) + bias_full[2:].reshape(-1)
    activ = exact_gelu(pre_act).astype(jnp.bfloat16)
    branch_two = (
        rows_sum_forward(
            jnp.einsum("isf,fd->isd", activ, down_full, preferred_element_type=jnp.float32)
        )
        + vector_full[6]
    )
    output = hidden + vector_full[7] * branch_two
    saved = (
        base,
        hidden,
        branch_one,
        branch_two,
        normed_all,
        queries,
        key_rows,
        values,
        log_total,
        blended,
        normed_two_all,
        pre_act,
        activ,
    )
    return (output.astype(jnp.bfloat16), saved)


def backward(grad_output, saved, params):
    qkv_full, out_full, up_full, down_full, bias_full, vector_full = params
    (
        base,
        hidden,
        branch_one,
        branch_two,
        normed_all,
        queries,
        key_rows,
        values,
        log_total,
        blended,
        normed_two_all,
        pre_act,
        activ,
    ) = saved
    local_width = qkv_full.shape[2]
    grad_out = grad_output.astype(jnp.float32)
    grad_scale_two = jnp.sum(grad_out * branch_two, axis=(0, 1))
    grad_bias_two = jnp.sum(grad_out, axis=(0, 1)) * vector_full[7]
    grad_branch = rows_backward((grad_out * vector_full[7]).astype(jnp.bfloat16))
    grad_down = jnp.einsum("isf,isd->fd", activ, grad_branch, preferred_element_type=jnp.float32)
    grad_activ = jnp.einsum(
        "isd,fd->isf", grad_branch, down_full, preferred_element_type=jnp.float32
    )
    grad_pre = jax.vjp(exact_gelu, pre_act)[1](grad_activ)[0].astype(jnp.bfloat16)
    grad_up_bias = jnp.sum(grad_pre, axis=(0, 1), dtype=jnp.float32)
    grad_up = jnp.einsum(
        "isd,isf->df", normed_two_all, grad_pre, preferred_element_type=jnp.float32
    )
    grad_normed_two = rows_sum_backward(
        jnp.einsum("isf,df->isd", grad_pre, up_full, preferred_element_type=jnp.float32)
    )
    norm_back_two = jax.vjp(layer_norm, hidden, vector_full[4], vector_full[5])[1]
    grad_hidden, grad_gain_two, grad_shift_two = norm_back_two(grad_normed_two)
    grad_hidden = grad_out + grad_hidden
    grad_scale_one = jnp.sum(grad_hidden * branch_one, axis=(0, 1))
    grad_out_bias = jnp.sum(grad_hidden, axis=(0, 1)) * vector_full[3]
    grad_projected = rows_backward((grad_hidden * vector_full[3]).astype(jnp.bfloat16))
    grad_out_weight = jnp.einsum(
        "ise,isd->ed", blended, grad_projected, preferred_element_type=jnp.float32
    )
    grad_blended = jnp.einsum(
        "isd,ed->ise", grad_projected, out_full, preferred_element_type=jnp.float32
    ).astype(jnp.bfloat16)
    grad_project = attend_backward(
        queries, key_rows, values, grad_blended, log_total, min(512, queries.shape[1])
    )
    grad_query_bias = jnp.sum(grad_project[0], axis=(0, 1), dtype=jnp.float32)
    grad_value_bias = jnp.sum(grad_project[2], axis=(0, 1), dtype=jnp.float32)
    grad_qkv = jnp.einsum(
        "isd,tise->tde", normed_all, grad_project, preferred_element_type=jnp.float32
    )
    grad_normed = rows_sum_backward(
        jnp.einsum("tise,tde->isd", grad_project, qkv_full, preferred_element_type=jnp.float32)
    )
    norm_back_one = jax.vjp(layer_norm, base, vector_full[0], vector_full[1])[1]
    grad_input_part, grad_gain_one, grad_shift_one = norm_back_one(grad_normed)
    grad_input = grad_hidden + grad_input_part
    grad_vectors = jnp.stack(
        [
            grad_gain_one,
            grad_shift_one,
            grad_out_bias,
            grad_scale_one,
            grad_gain_two,
            grad_shift_two,
            grad_bias_two,
            grad_scale_two,
        ]
    )
    grad_biases = jnp.concatenate(
        [jnp.stack([grad_query_bias, grad_value_bias]), grad_up_bias.reshape(-1, local_width)], 0
    )
    return (grad_input, (grad_qkv, grad_out_weight, grad_up, grad_down, grad_biases, grad_vectors))


def local_general(
    tokens,
    cotangent,
    qkv_weight,
    qkv_first,
    qkv_second,
    out_weight,
    out_first,
    out_second,
    up_weight,
    up_first,
    up_second,
    down_weight,
    down_first,
    down_second,
    head_biases,
    bias_first,
    bias_second,
    vectors,
    vector_first,
    vector_second,
):

    def gather_params():
        gathered = (
            lax.all_gather(qkv_weight.astype(jnp.bfloat16), "dp", axis=1, tiled=True),
            lax.all_gather(out_weight.astype(jnp.bfloat16), "dp", axis=1, tiled=True),
            lax.all_gather(up_weight.astype(jnp.bfloat16), "dp", axis=0, tiled=True),
            lax.all_gather(down_weight.astype(jnp.bfloat16), "dp", axis=2, tiled=True),
            lax.all_gather(head_biases.astype(jnp.bfloat16), "dp", axis=1, tiled=True),
            lax.all_gather(vectors.astype(jnp.bfloat16), "dp", axis=1, tiled=True),
        )
        qkv_full, out_full, up_full, down_full, bias_full, vector_full = gathered
        return (
            qkv_full,
            out_full,
            up_full.reshape(up_full.shape[0], -1),
            down_full.reshape(-1, down_full.shape[2]),
            bias_full.astype(jnp.float32),
            vector_full.astype(jnp.float32),
        )

    grad_sums = None
    outputs = []
    input_grads = []
    for micro_step in range(MICRO):
        params_fwd = gather_params()
        output, saved = forward(tokens[micro_step], params_fwd)
        outputs.append(output)
        params_back = gather_params()
        grad_input, grads = backward(cotangent[micro_step], saved, params_back)
        input_grads.append(grad_input)
        if grad_sums is None:
            grad_sums = grads
        else:
            grad_sums = tuple((old_sum + new_part for old_sum, new_part in zip(grad_sums, grads)))
    grad_qkv, grad_out_weight, grad_up, grad_down, grad_biases, grad_vectors = grad_sums
    grad_up = grad_up.reshape(-1, up_weight.shape[1], up_weight.shape[2])
    grad_down = grad_down.reshape(down_weight.shape[0], down_weight.shape[1], -1)
    reduced = (
        lax.psum_scatter(grad_qkv, "dp", scatter_dimension=1, tiled=True),
        lax.psum_scatter(grad_out_weight, "dp", scatter_dimension=1, tiled=True),
        lax.psum_scatter(grad_up, "dp", scatter_dimension=0, tiled=True),
        lax.psum_scatter(grad_down, "dp", scatter_dimension=2, tiled=True),
        lax.psum_scatter(grad_biases, "dp", scatter_dimension=1, tiled=True),
        lax.psum_scatter(grad_vectors, "dp", scatter_dimension=1, tiled=True),
    )
    vector_grad = lax.psum(reduced[5], "mp")
    grads = (reduced[0], reduced[1], reduced[2], reduced[3], reduced[4], vector_grad)
    params = (qkv_weight, out_weight, up_weight, down_weight, head_biases, vectors)
    firsts = (qkv_first, out_first, up_first, down_first, bias_first, vector_first)
    seconds = (qkv_second, out_second, up_second, down_second, bias_second, vector_second)
    updated = [
        adam_update(params[slot], firsts[slot], seconds[slot], grads[slot], RATES[slot])
        for slot in range(6)
    ]
    return (
        jnp.stack(outputs),
        jnp.stack(input_grads),
        updated[0][0],
        updated[0][1],
        updated[0][2],
        updated[1][0],
        updated[1][1],
        updated[1][2],
        updated[2][0],
        updated[2][1],
        updated[2][2],
        updated[3][0],
        updated[3][1],
        updated[3][2],
        updated[4][0],
        updated[4][1],
        updated[4][2],
        updated[5][0],
        updated[5][1],
        updated[5][2],
    )


ZS, YS, MP = (4, 2, 4)
DP = ZS * YS
LANES = 128
BF = jnp.bfloat16
F32 = jnp.float32


def swap_z(part, step):
    return lax.ppermute(
        part, "dp", [(z * YS + y, (z ^ step) * YS + y) for z in range(ZS) for y in range(YS)]
    )


def swap_y(part):
    return lax.ppermute(part, "dp", [(each, each ^ 1) for each in range(DP)])


def swap_mp(part, step):
    return lax.ppermute(part, "mp", [(each, each ^ step) for each in range(MP)])


class Chain:
    def __init__(self, steps, *args):
        self.own = None
        self.result = None
        self.steps = steps(self, *args)
        self.flight = next(self.steps)

    def land(self, arrived):
        try:
            self.flight = self.steps.send(arrived)
        except StopIteration as end:
            self.flight = None
            self.result = end.value


def meet(values, *chains):
    values, flights = lax.optimization_barrier((values, [each.flight for each in chains]))
    for each, flight in zip(chains, flights):
        each.land(flight)
    return values


def join(rows, arrived, axis):
    return jnp.concatenate([rows, arrived], -2 if axis == "y" else -1)


def swap_plane(part, axis):
    return swap_y(part) if axis == "y" else swap_mp(part, 2)


def rows_z_steps(chain, shard):
    rows = shard
    for step in (1, 2):
        (arrived,) = yield [swap_z(rows, step)]
        rows = jnp.concatenate([rows, arrived], 0)
    return rows


def cut(part, axis, pieces):
    return jnp.split(part, pieces, -2 if axis == "y" else -1) if pieces > 1 else [part]


def gather_steps(chain, parts, orders, pieces=(1, 1)):
    for axes, count in zip(zip(*orders), pieces):
        sent = [cut(part, axis, count) for part, axis in zip(parts, axes)]
        for at in range(count):
            arrived = yield [swap_plane(each[at], axis) for each, axis in zip(sent, axes)]
            parts = [join(part, each, axis) for part, each, axis in zip(parts, arrived, axes)]
    chain.own = parts
    arrived = yield [swap_mp(part, 1) for part in parts]
    return arrived


def add_low(first, second):
    return (first.astype(F32) + second.astype(F32)).astype(BF)


def halve(total, axis):
    rows, width = total.shape[-2:]
    if axis == "y":
        return (total[..., : rows // 2, :], total[..., rows // 2 :, :])
    return (total[..., : width // 2], total[..., width // 2 :])


def reduce_steps(chain, other_parts, orders, pieces=(1, 1)):
    arrived = yield [swap_mp(part, 1) for part in other_parts]
    totals = [add_low(own, each) for own, each in zip(chain.own, arrived)]
    for axes, count in zip(zip(*orders), pieces):
        halves = [halve(total, axis) for total, axis in zip(totals, axes)]
        sent = [cut(half[1], axis, count) for half, axis in zip(halves, axes)]
        received = []
        for at in range(count):
            received.append((yield [swap_plane(each[at], axis) for each, axis in zip(sent, axes)]))
        totals = []
        for half, axis, each in zip(halves, axes, zip(*received)):
            whole = each[0] if count == 1 else jnp.concatenate(each, -2 if axis == "y" else -1)
            totals.append(add_low(half[0], whole))
    return totals


def sum_z_steps(chain, total):
    rows = total.shape[0] // ZS
    arrived = yield [swap_z(total[step * rows : (step + 1) * rows], step) for step in range(1, ZS)]
    total = total[:rows].astype(F32)
    for each in arrived:
        total = total + each.astype(F32)
    return total


def sum_z_halves_steps(chain, total):
    half = total.shape[0] // 2
    (arrived,) = yield [swap_z(total[half:], 2)]
    total = add_low(total[:half], arrived)
    (arrived,) = yield [swap_z(total[half // 2 :], 1)]
    return total[: half // 2].astype(F32) + arrived.astype(F32)


def image_steps(chain, far, near):
    (arrived,) = yield [swap_mp(far, 2)]
    second, passing = arrived
    (arrived,) = yield [swap_mp(jnp.stack([near(), passing]), 1)]
    return [arrived[0], second, arrived[1]]


def small_steps(chain, shard, vector_size):
    biases = shard[:, vector_size:]
    arrived = yield [swap_mp(biases, step) for step in range(1, MP)]
    rows = jnp.concatenate([shard] + arrived, 1)
    for step in (1, 2):
        arrived = yield [swap_z(rows, step)]
        rows = jnp.concatenate([rows] + arrived, 0)
    arrived = yield [swap_y(rows)]
    rows = jnp.concatenate([rows] + arrived, 0)
    biases = rows[:, vector_size:].reshape(DP, MP, -1).transpose(1, 0, 2)
    return (rows[:, :vector_size], biases)


def small_reduce_steps(chain, vector_part, bias_part):
    packed = [jnp.concatenate([vector_part, each], 1) for each in bias_part]
    arrived = yield [swap_mp(packed[step], step) for step in range(1, MP)]
    total = (packed[0] + arrived[0]) + (arrived[1] + arrived[2])
    arrived = yield [swap_y(total[ZS:])]
    total = total[:ZS] + arrived[0]
    arrived = yield [swap_z(total[step], step) for step in range(1, ZS)]
    total = total[0]
    for each in arrived:
        total = total + each
    return total


def norm_parts(values):
    center = values - jnp.mean(values, -1, keepdims=True)
    spread = lax.rsqrt(jnp.mean(center * center, -1, keepdims=True) + 1e-06)
    return (center * spread, spread)


def norm_back(grad, normal, spread, gain):
    scaled = grad * gain
    inner = scaled - jnp.mean(scaled, -1, keepdims=True)
    return spread * (inner - normal * jnp.mean(scaled * normal, -1, keepdims=True))


GAIN_ONE, SHIFT_ONE, OUT_BIAS, SCALE_ONE, GAIN_TWO, SHIFT_TWO, DOWN_BIAS, SCALE_TWO = range(8)


def vector_row(vector_ref, at):
    return vector_ref[at : at + 1, :]


def assemble_kernel(with_norm, place_ref, vector_ref, own_ref, *refs):
    out_ref, second_ref = refs[-2:]
    part_refs = [own_ref.at[0]] + list(refs[:-2])
    for at, part_ref in enumerate(part_refs):
        for block in range(DP):
            lanes = pl.ds(pl.multiple_of(place_ref[block] * LANES, LANES), LANES)
            out_ref[at, :, block * LANES : (block + 1) * LANES] = part_ref[:, lanes]
        values = out_ref[at].astype(F32)
        if with_norm:
            normal, _ = norm_parts(values)
            values = normal * vector_row(vector_ref, GAIN_ONE) + vector_row(vector_ref, SHIFT_ONE)
        else:
            values = values * vector_row(vector_ref, SCALE_TWO)
        second_ref[at] = values.astype(BF)


def assemble_image(place, vector_full, arrays, parts, with_norm):
    chunk_rows, width = parts[0].shape
    rows = chunk_rows // 4
    block = pl.BlockSpec((rows, width), lambda i, place_ref: (i, 0))
    result = pl.BlockSpec((MP, rows, width), lambda i, place_ref: (0, i, 0))
    shape = jax.ShapeDtypeStruct((MP, chunk_rows, width), BF)
    image, second = pl.pallas_call(
        functools.partial(assemble_kernel, with_norm),
        grid_spec=pltpu.PrefetchScalarGridSpec(
            num_scalar_prefetch=1,
            grid=(4,),
            in_specs=[
                pl.BlockSpec(vector_full.shape, lambda i, place_ref: (0, 0)),
                pl.BlockSpec((1, rows, width), lambda i, place_ref: (place_ref[DP], i, 0)),
            ]
            + [block] * len(parts),
            out_specs=[result] * 2,
        ),
        out_shape=[shape] * 2,
        compiler_params=pltpu.CompilerParams(vmem_limit_bytes=32 * 2**20),
        name="assemble_image",
    )(place, vector_full, arrays, *parts)
    return (image.reshape(-1, width), second.reshape(-1, width))


def spread_kernel(place_ref, own_ref, *refs):
    out_ref = refs[-1]
    mine = place_ref[DP]
    for at, part_ref in enumerate([own_ref] + list(refs[:-1])):
        for block in range(DP):
            lanes = pl.ds(pl.multiple_of(place_ref[block] * LANES, LANES), LANES)
            part = part_ref[:, block * LANES : (block + 1) * LANES]
            out_ref[mine ^ at, :, lanes] = part.astype(out_ref.dtype)


def spread_image(place, own, parts, dtype):
    chunk_rows, width = parts[0].shape
    rows = chunk_rows // 4
    block = pl.BlockSpec((rows, width), lambda i, place_ref: (i, 0))
    return pl.pallas_call(
        spread_kernel,
        grid_spec=pltpu.PrefetchScalarGridSpec(
            num_scalar_prefetch=1,
            grid=(4,),
            in_specs=[block] * (1 + len(parts)),
            out_specs=pl.BlockSpec((MP, rows, width), lambda i, place_ref: (0, i, 0)),
        ),
        out_shape=jax.ShapeDtypeStruct((MP, chunk_rows, width), dtype),
        compiler_params=pltpu.CompilerParams(vmem_limit_bytes=32 * 2**20),
        name="spread_image",
    )(place, own, *parts)


ROWS = 512


def product_nt(left_refs, right_refs):
    total = None
    for left_ref, right_ref in zip(left_refs, right_refs):
        part = lax.dot_general(
            left_ref[...], right_ref[...], (((1,), (1,)), ((), ())), preferred_element_type=F32
        )
        total = part if total is None else total + part
    return total


def add_rows(sums_ref, rows):
    @pl.when(pl.program_id(0) == 0)
    def _():
        sums_ref[...] = jnp.zeros_like(sums_ref)

    for at, each in enumerate(rows):
        sums_ref[at : at + 1, :] += jnp.sum(each, 0, keepdims=True)


def out_kernel(count, *refs):
    lefts, rights = (refs[:count], refs[count : 2 * count])
    vector_ref, base_ref, branch_ref, hidden_ref, normed_ref = refs[2 * count :]
    branch = product_nt(lefts, rights) + vector_row(vector_ref, OUT_BIAS)
    hidden = base_ref[...].astype(F32) + vector_row(vector_ref, SCALE_ONE) * branch
    normal, _ = norm_parts(hidden)
    branch_ref[...] = branch
    hidden_ref[...] = hidden
    normed = normal * vector_row(vector_ref, GAIN_TWO) + vector_row(vector_ref, SHIFT_TWO)
    normed_ref[...] = normed.astype(BF)


def down_kernel(count, *refs):
    lefts, rights = (refs[:count], refs[count : 2 * count])
    vector_ref, hidden_ref, output_ref, branch_ref = refs[2 * count :]
    branch = product_nt(lefts, rights) + vector_row(vector_ref, DOWN_BIAS)
    output = hidden_ref[...] + vector_row(vector_ref, SCALE_TWO) * branch
    output_ref[...] = output.astype(BF)
    branch_ref[...] = branch


def up_back_kernel(count, *refs):
    lefts, rights = (refs[:count], refs[count : 2 * count])
    vector_ref, hidden_ref, branch_ref, grad_ref, out_ref, low_ref, sums_ref = refs[2 * count :]
    grad_normed = product_nt(lefts, rights)
    normal, spread = norm_parts(hidden_ref[...])
    grad = norm_back(grad_normed, normal, spread, vector_row(vector_ref, GAIN_TWO))
    grad = grad + grad_ref[...].astype(F32)
    out_ref[...] = grad
    low_ref[...] = (grad * vector_row(vector_ref, SCALE_ONE)).astype(BF)
    add_rows(sums_ref, [grad_normed * normal, grad_normed, grad * branch_ref[...], grad])


def in_back_kernel(count, *refs):
    lefts, rights = (refs[:count], refs[count : 2 * count])
    vector_ref, base_ref, grad_ref, low_ref, sums_ref = refs[2 * count : 2 * count + 5]
    grad_normed = product_nt(lefts, rights)
    normal, spread = norm_parts(base_ref[...].astype(F32))
    grad = norm_back(grad_normed, normal, spread, vector_row(vector_ref, GAIN_ONE))
    grad = grad + grad_ref[...]
    low_ref[...] = grad.astype(BF)

    for own_ref in refs[2 * count + 5 :]:
        own_ref[...] = grad[: own_ref.shape[0]]
    add_rows(sums_ref, [grad_normed * normal, grad_normed])


def expand_kernel(left_ref, right_ref, bias_ref, activ_ref, slope_ref):
    values = jnp.dot(left_ref[...], right_ref[...], preferred_element_type=F32) + bias_ref[0:1, :]
    share = 0.5 * (1.0 + lax.erf(values * 0.7071067811865476))
    activ_ref[...] = (values * share).astype(BF)
    slope = share + values * (0.3989422804014327 * jnp.exp(-0.5 * values * values))
    slope_ref[...] = slope.astype(BF)


def expand(left, right, bias):
    rows, depth = left.shape
    width = right.shape[1]
    block = pl.BlockSpec((256, width), lambda i: (i, 0))
    return pl.pallas_call(
        expand_kernel,
        grid=(rows // 256,),
        in_specs=[
            pl.BlockSpec((256, depth), lambda i: (i, 0)),
            pl.BlockSpec((depth, width), lambda i: (0, 0), pipeline_mode=pl.Buffered(1)),
            pl.BlockSpec((1, width), lambda i: (0, 0)),
        ],
        out_specs=[block] * 2,
        out_shape=[jax.ShapeDtypeStruct((rows, width), BF)] * 2,
        compiler_params=pltpu.CompilerParams(vmem_limit_bytes=32 * 2**20),
        name="expand",
    )(left, right, bias.reshape(1, width))


def slope_kernel(left_ref, right_ref, slope_ref, grad_ref, sums_ref):
    grad = jnp.dot(left_ref[...], right_ref[...], preferred_element_type=F32)
    low = (grad * slope_ref[...].astype(F32)).astype(BF)
    grad_ref[...] = low
    add_rows(sums_ref, [low.astype(F32)])


def slope_product(left, right, slope):
    rows, depth = left.shape
    width = right.shape[1]
    block = pl.BlockSpec((256, width), lambda i: (i, 0))
    return pl.pallas_call(
        slope_kernel,
        grid=(rows // 256,),
        in_specs=[
            pl.BlockSpec((256, depth), lambda i: (i, 0)),
            pl.BlockSpec((depth, width), lambda i: (0, 0), pipeline_mode=pl.Buffered(1)),
            block,
        ],
        out_specs=[block, pl.BlockSpec((8, width), lambda i: (0, 0))],
        out_shape=[jax.ShapeDtypeStruct((rows, width), BF), jax.ShapeDtypeStruct((8, width), F32)],
        compiler_params=pltpu.CompilerParams(vmem_limit_bytes=32 * 2**20),
        name="slope_product",
    )(left, right, slope)


def row_call(kernel, name, lefts, rights, vector_full, row_inputs, outs, span=None, own_rows=0):
    rows, width = row_inputs[0].shape
    first, count = span or (0, rows // ROWS)
    rows = count * ROWS
    once = pl.Buffered(1)
    block = pl.BlockSpec((ROWS, width), lambda i: (i, 0))
    source = pl.BlockSpec((ROWS, width), lambda i: (i + first, 0))
    specs = {
        "sums": (pl.BlockSpec((8, width), lambda i: (0, 0)), jax.ShapeDtypeStruct((8, width), F32)),
        "own": (
            pl.BlockSpec((own_rows, width), lambda i: (0, 0)),
            jax.ShapeDtypeStruct((own_rows, width), F32),
        ),
    }
    pairs = [
        specs[each] if isinstance(each, str) else (block, jax.ShapeDtypeStruct((rows, width), each))
        for each in outs
    ]
    return pl.pallas_call(
        functools.partial(kernel, len(lefts)),
        grid=(count,),
        in_specs=[pl.BlockSpec((ROWS, each.shape[1]), lambda i: (i + first, 0)) for each in lefts]
        + [pl.BlockSpec(each.shape, lambda i: (0, 0), pipeline_mode=once) for each in rights]
        + [pl.BlockSpec(vector_full.shape, lambda i: (0, 0))]
        + [source] * len(row_inputs),
        out_specs=[each[0] for each in pairs],
        out_shape=[each[1] for each in pairs],
        compiler_params=pltpu.CompilerParams(vmem_limit_bytes=48 * 2**20),
        name=name,
    )(*lefts, *rights, vector_full, *row_inputs)


def lane_dot(left, right):
    return lax.dot_general(left, right, (((1,), (1,)), ((), ())), preferred_element_type=F32)


def head_masks(width):
    lane = lax.broadcasted_iota(jnp.int32, (1, width), 1)
    return [lane // DH == head for head in range(width // DH)]


def attend_kernel(block_rows, q_ref, k_ref, v_ref, o_ref, lse_ref):
    masks = head_masks(LANES)
    key_rows = k_ref[...]
    values = v_ref[...]
    zero = jnp.zeros((), BF)
    for block in range(q_ref.shape[0] // block_rows):
        rows = slice(block * block_rows, (block + 1) * block_rows)
        queries = q_ref[rows, :] * jnp.asarray(DH**-0.5, BF)
        blended = []
        for head, mask in enumerate(masks):
            scores = lane_dot(jnp.where(mask, queries, zero), key_rows)
            peak = jnp.max(scores, 1, keepdims=True)
            shifted = jnp.exp(scores - peak)
            total = jnp.sum(shifted, 1, keepdims=True)
            part = jnp.dot(shifted.astype(BF), values, preferred_element_type=F32)
            blended.append(part * (1.0 / total))
            log_total = jnp.broadcast_to(peak + jnp.log(total), (block_rows, LANES))
            lse_ref[0, head : head + 1, rows] = jnp.transpose(log_total)[0:1, :]
        o_ref[rows, :] = jnp.where(masks[0], blended[0], blended[1]).astype(BF)


def attend_back_kernel(
    block_rows, q_ref, k_ref, v_ref, g_ref, lse_ref, out_ref, dk_acc, dv_acc
):
    masks = head_masks(LANES)
    key_rows = k_ref[...]
    values = v_ref[...]
    zero = jnp.zeros((), BF)
    factor = DH**-0.5
    key_heads = [jnp.where(mask, key_rows, zero) for mask in masks]
    for block in range(q_ref.shape[0] // block_rows):
        rows = slice(block * block_rows, (block + 1) * block_rows)
        queries = q_ref[rows, :] * jnp.asarray(factor, BF)
        grads = g_ref[rows, :]
        grad_query = None
        grad_keys = None
        grad_values = None
        for head, mask in enumerate(masks):
            query_head = jnp.where(mask, queries, zero)
            grad_head = jnp.where(mask, grads, zero)
            scores = lane_dot(key_rows, query_head)
            weights = jnp.exp(scores - lse_ref[0, head : head + 1, rows])
            value_part = jnp.dot(weights.astype(BF), grad_head, preferred_element_type=F32)
            grad_rows = lane_dot(values, grad_head)
            delta = jnp.sum(grad_rows * weights, 0, keepdims=True)
            grad_scores = (weights * (grad_rows - delta)).astype(BF)
            key_part = jnp.dot(grad_scores, query_head, preferred_element_type=F32)
            query_part = lax.dot_general(
                grad_scores, key_heads[head], (((0,), (0,)), ((), ())), preferred_element_type=F32
            )
            grad_query = query_part if head == 0 else grad_query + query_part
            grad_keys = key_part if head == 0 else grad_keys + key_part
            grad_values = value_part if head == 0 else grad_values + value_part
        out_ref[rows, 0:LANES] = (grad_query * factor).astype(BF)
        if block == 0:
            dk_acc[...] = grad_keys
            dv_acc[...] = grad_values
        else:
            dk_acc[...] += grad_keys
            dv_acc[...] += grad_values
    out_ref[:, LANES : 2 * LANES] = dk_acc[...].astype(BF)
    out_ref[:, 2 * LANES : 3 * LANES] = dv_acc[...].astype(BF)


def kind_spec(rows, kind):
    return pl.BlockSpec((rows, LANES), lambda p: (0, p * 3 + kind))


def attend(heads):
    rows, width = heads.shape
    pairs = width // LANES // 3
    return pl.pallas_call(
        functools.partial(attend_kernel, 256),
        grid=(pairs,),
        in_specs=[kind_spec(rows, kind) for kind in range(3)],
        out_specs=[
            pl.BlockSpec((rows, LANES), lambda p: (0, p)),
            pl.BlockSpec((1, 8, rows), lambda p: (p, 0, 0)),
        ],
        out_shape=[
            jax.ShapeDtypeStruct((rows, pairs * LANES), BF),
            jax.ShapeDtypeStruct((pairs, 8, rows), F32),
        ],
        compiler_params=pltpu.CompilerParams(vmem_limit_bytes=32 * 2**20),
        name="attend",
    )(heads, heads, heads)


def attend_back(heads, grad_blended, log_total):
    rows, width = heads.shape
    pairs = width // LANES // 3
    return pl.pallas_call(
        functools.partial(attend_back_kernel, 256),
        grid=(pairs,),
        in_specs=[kind_spec(rows, kind) for kind in range(3)]
        + [
            pl.BlockSpec((rows, LANES), lambda p: (0, p)),
            pl.BlockSpec((1, 8, rows), lambda p: (p, 0, 0)),
        ],
        out_specs=pl.BlockSpec((rows, 3 * LANES), lambda p: (0, p)),
        out_shape=jax.ShapeDtypeStruct((rows, width), BF),
        scratch_shapes=[pltpu.VMEM((rows, LANES), F32)] * 2,
        compiler_params=pltpu.CompilerParams(vmem_limit_bytes=32 * 2**20),
        name="attend_back",
    )(heads, heads, heads, grad_blended, log_total)


def dot_nn(left, right):
    return lax.dot_general(left, right, (((1,), (0,)), ((), ())), preferred_element_type=F32)


def dot_nt(left, right):
    return lax.dot_general(left, right, (((1,), (1,)), ((), ())), preferred_element_type=F32)


def dot_tn(left, right):
    return lax.dot_general(left, right, (((0,), (0,)), ((), ())), preferred_element_type=F32)


def local_image(
    tokens,
    cotangent,
    qkv_weight,
    qkv_first,
    qkv_second,
    out_weight,
    out_first,
    out_second,
    up_weight,
    up_first,
    up_second,
    down_weight,
    down_first,
    down_second,
    head_biases,
    bias_first,
    bias_second,
    vectors,
    vector_first,
    vector_second,
):
    dp_at = lax.axis_index("dp")
    mp_at = lax.axis_index("mp")
    units = up_weight.shape[1]
    half_units = units // 2
    block_width = qkv_weight.shape[2]
    depth = qkv_weight.shape[1]
    bias_width = head_biases.shape[1]
    chunk_rows, width = tokens.shape[2:]
    order = [((zk * YS) + yk) for yk in range(YS) for zk in range(ZS)]
    place = jnp.stack([dp_at ^ each for each in order] + [mp_at]).astype(jnp.int32)
    cores = (0, 1)

    def fetch_image(array):
        chunks = array[:, 0]

        def chunk(step):
            return lax.dynamic_index_in_dim(chunks, mp_at ^ step, 0, keepdims=False)

        return Chain(image_steps, jnp.stack([chunk(2), chunk(3)]), lambda: chunk(1))

    def send_back(low):
        chunks = low.reshape(MP, chunk_rows, width)
        return Chain(image_steps, chunks[2:], lambda: chunks[1])

    small_shard = jnp.concatenate(
        [vectors.astype(BF).reshape(-1), head_biases.astype(BF).reshape(-1)]
    ).reshape(1, -1)
    vector_size = vectors.size
    kinds = qkv_weight.shape[0]
    qkv_shard = qkv_weight.astype(BF).reshape(kinds, depth, 2, LANES).transpose(1, 2, 0, 3)
    qkv_shard = qkv_shard.reshape(depth, -1)
    up_shard = jnp.concatenate(
        [out_weight.T.astype(BF), up_weight.astype(BF).reshape(depth, -1)], 1
    )
    down_shard = down_weight.transpose(2, 0, 1).astype(BF).reshape(depth, -1)
    both = ("xy", "yx")
    small = Chain(small_steps, small_shard, vector_size)
    rows_qkv = Chain(rows_z_steps, qkv_shard)
    rows_up = Chain(rows_z_steps, up_shard)
    tokens = meet(tokens, small, rows_qkv)
    fetch_tokens = fetch_image(tokens)
    meet((), small)
    meet((), small, rows_qkv, rows_up)
    part_a, part_b = jnp.split(rows_qkv.result, 2, 1)
    get_qkv = [Chain(gather_steps, [part_a], ("yx",)), Chain(gather_steps, [part_b], ("xy",))]
    meet((), small, get_qkv[0], fetch_tokens)
    tokens = meet(tokens, fetch_tokens)

    vector_full, bias_small = small.result
    vector_full = vector_full.reshape(DP, vectors.shape[0], LANES).transpose(1, 0, 2)
    vector_full = vector_full.reshape(vectors.shape[0], width).astype(F32)
    back_places = jnp.stack([((each ^ dp_at) & 1) * ZS + ((each ^ dp_at) >> 1) for each in range(DP)])
    bias_rows = jnp.take(bias_small, back_places, axis=1).reshape(2, 2, DP, -1, bias_width)
    bias_full = bias_rows.transpose(1, 3, 0, 2, 4).reshape(2, head_biases.shape[0], 2, block_width)
    bias_full = bias_full.astype(F32)

    base, normed_one = assemble_image(place, vector_full, tokens[:, 0], fetch_tokens.result, True)
    normed_one, down_shard = meet((normed_one, down_shard), *get_qkv, rows_up)
    out_rows, up_rows = jnp.split(rows_up.result, [block_width], 1)
    get_out = Chain(gather_steps, [jnp.stack(jnp.split(out_rows, 2, 1))], ("yx",))
    get_up = Chain(gather_steps, jnp.split(up_rows, 2, 1), both, (1, 2))

    def project(core, half, weight):
        lanes = slice(half * LANES, (half + 1) * LANES)
        zero = jnp.zeros((2, LANES), F32)
        bias = jnp.stack([bias_full[core, 0, :, lanes], zero, bias_full[core, 1, :, lanes]], 1)
        return (dot_nn(normed_one, weight) + bias.reshape(-1)).astype(BF)

    heads, blended, log_total = ([[None, None], [None, None]] for _ in range(3))

    def forward_heads(core, half):
        blended[core][half], log_total[core][half] = attend(heads[core][half])

    heads[0][0] = project(0, 0, get_qkv[0].own[0])
    forward_heads(0, 0)
    blended[0][0], normed_one, down_shard = meet(
        (blended[0][0], normed_one, down_shard), *get_qkv, get_out, get_up
    )
    rows_down = Chain(rows_z_steps, down_shard)
    heads[0][1] = project(0, 1, get_qkv[1].own[0])
    forward_heads(0, 1)
    blended[0][1], normed_one = meet(
        (blended[0][1], normed_one), get_qkv[1], get_out, get_up, rows_down
    )
    w_qkv = [[each.own[0] for each in get_qkv], [each.result[0] for each in get_qkv]]
    heads[1][0] = project(1, 0, w_qkv[1][0])
    forward_heads(1, 0)
    blended[1][0], normed_one = meet(
        (blended[1][0], normed_one), get_out, rows_down, get_up
    )
    get_down = Chain(gather_steps, jnp.split(rows_down.result, 2, 1), both)
    heads[1][1] = project(1, 1, w_qkv[1][1])
    forward_heads(1, 1)
    blended = meet(blended, get_up, get_down)
    w_out = [[each[0][half] for half in (0, 1)] for each in (get_out.own, get_out.result)]
    pairs = [(core, half) for core in cores for half in (0, 1)]
    branch_one, hidden, normed_two = row_call(
        out_kernel,
        "out_norm",
        [blended[core][half] for core, half in pairs],
        [w_out[core][half] for core, half in pairs],
        vector_full,
        [base],
        [F32, F32, BF],
    )
    activ, slope = ({}, {})

    def expand_units(core, weights):
        for half in (0, 1):
            rows = bias_full[core, 2 + half * half_units : 2 + (half + 1) * half_units]
            unit_bias = rows.transpose(1, 0, 2).reshape(-1)
            activ[half, core], slope[half, core] = expand(normed_two, weights[half], unit_bias)

    w_up = [get_up.own, get_up.result]
    expand_units(0, w_up[0])
    activ, normed_two, cotangent = meet((activ, normed_two, cotangent), get_down)
    fetch_cotangent = fetch_image(cotangent)
    expand_units(1, w_up[1])
    activ = meet(activ, get_down)
    w_down = [get_down.own, get_down.result]
    parts = [(half, core) for core in (1, 0) for half in (0, 1)]
    output, branch_two = row_call(
        down_kernel,
        "down_output",
        [activ[each] for each in parts],
        [w_down[core][half] for half, core in parts],
        vector_full,
        [hidden],
        [BF, F32],
    )
    output = meet(output, fetch_cotangent)
    output, cotangent = meet((output, cotangent), fetch_cotangent)
    grad_out, grad_branch = assemble_image(
        place, vector_full, cotangent[:, 0], fetch_cotangent.result, False
    )

    def reduce_pairs(left, rights, pieces):
        chain = Chain(reduce_steps, [dot_tn(left, rights[half, 1]).astype(BF) for half in (0, 1)], both[::-1], pieces)
        chain.own = [dot_tn(left, rights[half, 0]).astype(BF) for half in (0, 1)]
        return chain

    sum_down = reduce_pairs(grad_branch, activ, (2, 1))
    grad_branch, output, slope = meet((grad_branch, output, slope), sum_down)
    send_output = send_back(output)
    grad_pre, unit_sums = ({}, {})
    for half, core in parts:
        grad_pre[half, core], unit_sums[half, core] = slope_product(
            grad_branch, w_down[core][half], slope[half, core]
        )
        if (half, core) == (0, 0):
            grad_pre, grad_branch = meet((grad_pre, grad_branch), sum_down)
    grad_pre, normed_two = meet((grad_pre, normed_two))
    sum_up = reduce_pairs(normed_two, grad_pre, (1, 1))
    grad_pre = meet(grad_pre, sum_down)
    grad_hidden, grad_projected, sums_one = row_call(
        up_back_kernel,
        "up_norm_back",
        [grad_pre[each] for each in parts],
        [w_up[core][half] for half, core in parts],
        vector_full,
        [hidden, branch_one, grad_out],
        [F32, BF, "sums"],
    )
    grad_projected = meet(grad_projected, sum_up, sum_down, send_output)
    rows_down = Chain(sum_z_halves_steps, jnp.concatenate(sum_down.result, 1))
    grad_w_out = [
        jnp.stack([dot_tn(grad_projected, each).astype(BF) for each in blended[core]]) for core in cores
    ]
    sum_out = Chain(reduce_steps, [grad_w_out[1]], ("xy",))
    sum_out.own = [grad_w_out[0]]
    grad_blended = [[dot_nn(grad_projected, each).astype(BF) for each in w_out[core]] for core in cores]
    grad_heads = [[None, None], [None, None]]

    def back_heads(core, half):
        grad_heads[core][half] = attend_back(
            heads[core][half], grad_blended[core][half], log_total[core][half]
        )
        return dot_tn(normed_one, grad_heads[core][half]).astype(BF)

    other = back_heads(1, 0)
    other, grad_blended = meet((other, grad_blended), sum_up, sum_out, rows_down, send_output)
    sum_qkv = [Chain(reduce_steps, [other], ("xy",)), None]
    sum_qkv[0].own = [back_heads(0, 0)]
    grad_heads[0][0], grad_blended = meet(
        (grad_heads[0][0], grad_blended), sum_qkv[0], sum_out, sum_up, rows_down
    )
    rows_up = Chain(sum_z_halves_steps, jnp.concatenate(sum_up.result, 1))
    other = back_heads(1, 1)
    other, grad_blended = meet((other, grad_blended), sum_out, sum_qkv[0])
    sum_qkv[1] = Chain(reduce_steps, [other], ("yx",))
    out_rows = jnp.concatenate([sum_out.result[0][0], sum_out.result[0][1]], 1)
    sum_qkv[1].own = [back_heads(0, 1)]
    grad_heads = meet(grad_heads, sum_qkv[0], sum_qkv[1], rows_up)

    def input_back(span, outs):
        return row_call(
            in_back_kernel,
            "in_norm_back",
            [grad_heads[core][half] for core, half in pairs],
            [w_qkv[core][half] for core, half in pairs],
            vector_full,
            [base, grad_hidden],
            outs,
            span,
            chunk_rows,
        )

    grad_far, sums_far = input_back((1, 1), [BF, "sums"])
    grad_near = []
    send_grad = Chain(
        image_steps, grad_far.reshape(2, chunk_rows, width), lambda: grad_near[0][chunk_rows:]
    )
    grad_heads = meet(grad_heads, sum_qkv[1])
    near, sums_near, own_grad = input_back((0, 1), [BF, "sums", "own"])
    near, sums_near, own_grad = meet((near, sums_near, own_grad), sum_qkv[1])
    grad_near.append(near)
    sums_input = sums_far + sums_near

    grad_vectors = jnp.stack(
        [
            sums_input[0],
            sums_input[1],
            sums_one[3] * vector_full[SCALE_ONE],
            sums_one[2],
            sums_one[0],
            sums_one[1],
            jnp.sum(grad_out.astype(F32), 0) * vector_full[SCALE_TWO],
            jnp.sum(grad_out.astype(F32) * branch_two, 0),
        ]
    )
    grad_vectors = grad_vectors.reshape(-1, DP, LANES).transpose(1, 0, 2).reshape(DP, -1)
    bias_parts = []
    for core in cores:
        head_part = [
            jnp.sum(each.astype(F32), 0).reshape(2, kinds, LANES) for each in grad_heads[core]
        ]
        rows = [jnp.concatenate([each[:, kind] for each in head_part], 1) for kind in (0, 2)]
        for half in (0, 1):
            unit_part = unit_sums[half, core][0].reshape(2, half_units, block_width)
            rows += [unit_part[:, at] for at in range(half_units)]
        bias_parts.append(jnp.stack(rows, 1))
    grad_biases = jnp.stack(bias_parts, 1).reshape(MP, -1, DP, bias_width).transpose(0, 2, 1, 3)
    grad_biases = jnp.take(grad_biases, place[:DP], axis=1).reshape(MP, DP, -1)
    sum_small = Chain(small_reduce_steps, grad_vectors, grad_biases)
    rows_qkv = Chain(sum_z_steps, jnp.concatenate(sum_qkv[0].result + sum_qkv[1].result + [out_rows], 1))
    meet((), rows_up)
    meet((), send_grad)
    meet((), send_grad)
    meet((), rows_qkv)
    for _ in range(3):
        meet((), sum_small)
    layer_output = spread_image(place, output[:chunk_rows], send_output.result, BF)[:, None]
    input_grad = spread_image(place, own_grad, send_grad.result, F32)[:, None]

    small_total = sum_small.result
    vector_grad = small_total[:vector_size].reshape(vectors.shape)
    bias_grad = small_total[vector_size:].reshape(head_biases.shape)
    qkv_size = kinds * block_width
    qkv_grad = rows_qkv.result[:, :qkv_size].reshape(depth, 2, kinds, LANES).transpose(2, 0, 1, 3)
    grads = (
        qkv_grad.reshape(qkv_weight.shape),
        rows_qkv.result[:, qkv_size:].T,
        rows_up.result.reshape(depth, units, block_width),
        rows_down.result.reshape(depth, units, block_width).transpose(1, 2, 0),
        bias_grad,
        vector_grad,
    )
    params = (qkv_weight, out_weight, up_weight, down_weight, head_biases, vectors)
    firsts = (qkv_first, out_first, up_first, down_first, bias_first, vector_first)
    seconds = (qkv_second, out_second, up_second, down_second, bias_second, vector_second)
    results = [layer_output, input_grad]
    for slot in range(6):
        results.extend(
            adam_update(params[slot], firsts[slot], seconds[slot], grads[slot], RATES[slot])
        )
    return tuple(results)


def solution(mesh):
    whole_image = mesh.shape["mp"] == MICRO == MP and mesh.shape["dp"] == DP
    return jax.shard_map(
        local_image if whole_image else local_general,
        mesh=mesh,
        in_specs=(
            P(None, "dp", "mp", None),
            P(None, "dp", "mp", None),
            P(None, "dp", "mp"),
            P(None, "dp", "mp"),
            P(None, "dp", "mp"),
            P("mp", "dp"),
            P("mp", "dp"),
            P("mp", "dp"),
            P("dp", None, "mp"),
            P("dp", None, "mp"),
            P("dp", None, "mp"),
            P(None, "mp", "dp"),
            P(None, "mp", "dp"),
            P(None, "mp", "dp"),
            P(None, ("mp", "dp")),
            P(None, ("mp", "dp")),
            P(None, ("mp", "dp")),
            P(None, "dp"),
            P(None, "dp"),
            P(None, "dp"),
        ),
        out_specs=(
            P(None, "dp", "mp", None),
            P(None, "dp", "mp", None),
            P(None, "dp", "mp"),
            P(None, "dp", "mp"),
            P(None, "dp", "mp"),
            P("mp", "dp"),
            P("mp", "dp"),
            P("mp", "dp"),
            P("dp", None, "mp"),
            P("dp", None, "mp"),
            P("dp", None, "mp"),
            P(None, "mp", "dp"),
            P(None, "mp", "dp"),
            P(None, "mp", "dp"),
            P(None, ("mp", "dp")),
            P(None, ("mp", "dp")),
            P(None, ("mp", "dp")),
            P(None, "dp"),
            P(None, "dp"),
            P(None, "dp"),
        ),
        check_vma=False,
    )
```

```python
import functools

import jax
import jax.numpy as jnp
from jax import lax
from jax.experimental import pallas as pl
from jax.experimental.pallas import tpu as pltpu
from jax.sharding import PartitionSpec as P

DH = 64
MICRO = 4
STEP = 10


RATES = (0.05, 0.2, 0.05, 0.03, 0.5, 0.5)


def layer_norm(values, gain, shift):
    center = values - jnp.mean(values, -1, keepdims=True)
    spread = jnp.mean(center * center, -1, keepdims=True)
    return center * lax.rsqrt(spread + 1e-06) * gain + shift


def exact_gelu(values):
    return jax.nn.gelu(values, approximate=False)


def adam_update(weight, first, second, grad, rate):
    first_new = 0.9 * first + 0.1 * grad
    second_new = 0.999 * second + 0.001 * grad * grad
    corrected = first_new / (1.0 - 0.9**STEP)
    scaled = jnp.sqrt(second_new / (1.0 - 0.999**STEP))
    weight_new = weight - rate * (corrected / (scaled + 1e-08) + 0.05 * weight)
    return (weight_new, first_new, second_new)


def attend_forward(queries, key_rows, values, block_rows):
    images, seq_rows, head_count, head_width = queries.shape
    block_count = seq_rows // block_rows
    factor = head_width ** (-0.5)
    query_blocks = jnp.moveaxis(
        queries.reshape(images, block_count, block_rows, head_count, head_width), 1, 0
    )

    def one_block(query_part):
        scores = (
            jnp.einsum("iqhe,ikhe->ihqk", query_part, key_rows, preferred_element_type=jnp.float32)
            * factor
        )
        row_peak = jnp.max(scores, -1, keepdims=True)
        shifted = jnp.exp(scores - row_peak)
        row_total = jnp.sum(shifted, -1, keepdims=True)
        softmax_rows = (shifted / row_total).astype(jnp.bfloat16)
        blended = jnp.einsum(
            "ihqk,ikhe->iqhe", softmax_rows, values, preferred_element_type=jnp.float32
        )
        return (blended, row_peak[..., 0] + jnp.log(row_total[..., 0]))

    blended, log_total = lax.map(one_block, query_blocks)
    blended = jnp.moveaxis(blended, 0, 1).reshape(images, seq_rows, head_count * head_width)
    return (blended.astype(jnp.bfloat16), log_total)


def attend_backward(queries, key_rows, values, grad_blended, log_total, block_rows):
    images, seq_rows, head_count, head_width = queries.shape
    block_count = seq_rows // block_rows
    factor = head_width ** (-0.5)
    split_shape = (images, block_count, block_rows, head_count, head_width)
    query_blocks = jnp.moveaxis(queries.reshape(split_shape), 1, 0)
    grad_blocks = jnp.moveaxis(grad_blended.reshape(split_shape), 1, 0)

    def one_block(carry, inputs_part):
        query_part, grad_part, total_part = inputs_part
        grad_keys, grad_values = carry
        scores = (
            jnp.einsum("iqhe,ikhe->ihqk", query_part, key_rows, preferred_element_type=jnp.float32)
            * factor
        )
        softmax_rows = jnp.exp(scores - total_part[..., None])
        grad_values = grad_values + jnp.einsum(
            "ihqk,iqhe->ikhe",
            softmax_rows.astype(jnp.bfloat16),
            grad_part,
            preferred_element_type=jnp.float32,
        )
        grad_rows = jnp.einsum(
            "iqhe,ikhe->ihqk", grad_part, values, preferred_element_type=jnp.float32
        )
        grad_scores = softmax_rows * (
            grad_rows - jnp.sum(grad_rows * softmax_rows, -1, keepdims=True)
        )
        grad_scores = grad_scores.astype(jnp.bfloat16)
        grad_query = (
            jnp.einsum("ihqk,ikhe->iqhe", grad_scores, key_rows, preferred_element_type=jnp.float32)
            * factor
        )
        grad_keys = (
            grad_keys
            + jnp.einsum(
                "ihqk,iqhe->ikhe", grad_scores, query_part, preferred_element_type=jnp.float32
            )
            * factor
        )
        return ((grad_keys, grad_values), grad_query)

    zero_grad = jnp.zeros(queries.shape, jnp.float32)
    (grad_keys, grad_values), grad_query = lax.scan(
        one_block, (zero_grad, zero_grad), (query_blocks, grad_blocks, log_total)
    )
    flat_shape = (images, seq_rows, head_count * head_width)
    grad_query = jnp.moveaxis(grad_query, 0, 1).reshape(flat_shape)
    stacked = jnp.stack(
        [grad_query, grad_keys.reshape(flat_shape), grad_values.reshape(flat_shape)]
    )
    return stacked.astype(jnp.bfloat16)


def rows_forward(part):
    return lax.all_gather(part, "mp", axis=1, tiled=True)


def rows_sum_forward(part):
    return lax.psum_scatter(part, "mp", scatter_dimension=1, tiled=True)


def rows_backward(part):
    return lax.all_gather(part, "mp", axis=1, tiled=True)


def rows_sum_backward(part):
    return lax.psum_scatter(part, "mp", scatter_dimension=1, tiled=True)


def forward(inputs, params):
    qkv_full, out_full, up_full, down_full, bias_full, vector_full = params
    base = inputs.astype(jnp.float32)
    normed = layer_norm(base, vector_full[0], vector_full[1]).astype(jnp.bfloat16)
    normed_all = rows_forward(normed)
    images, seq_rows = (normed_all.shape[0], normed_all.shape[1])
    head_shape = (images, seq_rows, -1, DH)
    project = jnp.einsum("isd,tde->tise", normed_all, qkv_full, preferred_element_type=jnp.float32)
    queries = (project[0] + bias_full[0]).astype(jnp.bfloat16).reshape(head_shape)
    key_rows = project[1].astype(jnp.bfloat16).reshape(head_shape)
    values = (project[2] + bias_full[1]).astype(jnp.bfloat16).reshape(head_shape)
    blended, log_total = attend_forward(queries, key_rows, values, min(512, seq_rows))
    projected = rows_sum_forward(
        jnp.einsum("ise,ed->isd", blended, out_full, preferred_element_type=jnp.float32)
    )
    branch_one = projected + vector_full[2]
    hidden = base + vector_full[3] * branch_one
    normed_two = layer_norm(hidden, vector_full[4], vector_full[5]).astype(jnp.bfloat16)
    normed_two_all = rows_forward(normed_two)
    pre_act = jnp.einsum(
        "isd,df->isf", normed_two_all, up_full, preferred_element_type=jnp.float32
    ) + bias_full[2:].reshape(-1)
    activ = exact_gelu(pre_act).astype(jnp.bfloat16)
    branch_two = (
        rows_sum_forward(
            jnp.einsum("isf,fd->isd", activ, down_full, preferred_element_type=jnp.float32)
        )
        + vector_full[6]
    )
    output = hidden + vector_full[7] * branch_two
    saved = (
        base,
        hidden,
        branch_one,
        branch_two,
        normed_all,
        queries,
        key_rows,
        values,
        log_total,
        blended,
        normed_two_all,
        pre_act,
        activ,
    )
    return (output.astype(jnp.bfloat16), saved)


def backward(grad_output, saved, params):
    qkv_full, out_full, up_full, down_full, bias_full, vector_full = params
    (
        base,
        hidden,
        branch_one,
        branch_two,
        normed_all,
        queries,
        key_rows,
        values,
        log_total,
        blended,
        normed_two_all,
        pre_act,
        activ,
    ) = saved
    local_width = qkv_full.shape[2]
    grad_out = grad_output.astype(jnp.float32)
    grad_scale_two = jnp.sum(grad_out * branch_two, axis=(0, 1))
    grad_bias_two = jnp.sum(grad_out, axis=(0, 1)) * vector_full[7]
    grad_branch = rows_backward((grad_out * vector_full[7]).astype(jnp.bfloat16))
    grad_down = jnp.einsum("isf,isd->fd", activ, grad_branch, preferred_element_type=jnp.float32)
    grad_activ = jnp.einsum(
        "isd,fd->isf", grad_branch, down_full, preferred_element_type=jnp.float32
    )
    grad_pre = jax.vjp(exact_gelu, pre_act)[1](grad_activ)[0].astype(jnp.bfloat16)
    grad_up_bias = jnp.sum(grad_pre, axis=(0, 1), dtype=jnp.float32)
    grad_up = jnp.einsum(
        "isd,isf->df", normed_two_all, grad_pre, preferred_element_type=jnp.float32
    )
    grad_normed_two = rows_sum_backward(
        jnp.einsum("isf,df->isd", grad_pre, up_full, preferred_element_type=jnp.float32)
    )
    norm_back_two = jax.vjp(layer_norm, hidden, vector_full[4], vector_full[5])[1]
    grad_hidden, grad_gain_two, grad_shift_two = norm_back_two(grad_normed_two)
    grad_hidden = grad_out + grad_hidden
    grad_scale_one = jnp.sum(grad_hidden * branch_one, axis=(0, 1))
    grad_out_bias = jnp.sum(grad_hidden, axis=(0, 1)) * vector_full[3]
    grad_projected = rows_backward((grad_hidden * vector_full[3]).astype(jnp.bfloat16))
    grad_out_weight = jnp.einsum(
        "ise,isd->ed", blended, grad_projected, preferred_element_type=jnp.float32
    )
    grad_blended = jnp.einsum(
        "isd,ed->ise", grad_projected, out_full, preferred_element_type=jnp.float32
    ).astype(jnp.bfloat16)
    grad_project = attend_backward(
        queries, key_rows, values, grad_blended, log_total, min(512, queries.shape[1])
    )
    grad_query_bias = jnp.sum(grad_project[0], axis=(0, 1), dtype=jnp.float32)
    grad_value_bias = jnp.sum(grad_project[2], axis=(0, 1), dtype=jnp.float32)
    grad_qkv = jnp.einsum(
        "isd,tise->tde", normed_all, grad_project, preferred_element_type=jnp.float32
    )
    grad_normed = rows_sum_backward(
        jnp.einsum("tise,tde->isd", grad_project, qkv_full, preferred_element_type=jnp.float32)
    )
    norm_back_one = jax.vjp(layer_norm, base, vector_full[0], vector_full[1])[1]
    grad_input_part, grad_gain_one, grad_shift_one = norm_back_one(grad_normed)
    grad_input = grad_hidden + grad_input_part
    grad_vectors = jnp.stack(
        [
            grad_gain_one,
            grad_shift_one,
            grad_out_bias,
            grad_scale_one,
            grad_gain_two,
            grad_shift_two,
            grad_bias_two,
            grad_scale_two,
        ]
    )
    grad_biases = jnp.concatenate(
        [jnp.stack([grad_query_bias, grad_value_bias]), grad_up_bias.reshape(-1, local_width)], 0
    )
    return (grad_input, (grad_qkv, grad_out_weight, grad_up, grad_down, grad_biases, grad_vectors))


def local_general(
    tokens,
    cotangent,
    qkv_weight,
    qkv_first,
    qkv_second,
    out_weight,
    out_first,
    out_second,
    up_weight,
    up_first,
    up_second,
    down_weight,
    down_first,
    down_second,
    head_biases,
    bias_first,
    bias_second,
    vectors,
    vector_first,
    vector_second,
):

    def gather_params():
        gathered = (
            lax.all_gather(qkv_weight.astype(jnp.bfloat16), "dp", axis=1, tiled=True),
            lax.all_gather(out_weight.astype(jnp.bfloat16), "dp", axis=1, tiled=True),
            lax.all_gather(up_weight.astype(jnp.bfloat16), "dp", axis=0, tiled=True),
            lax.all_gather(down_weight.astype(jnp.bfloat16), "dp", axis=2, tiled=True),
            lax.all_gather(head_biases.astype(jnp.bfloat16), "dp", axis=1, tiled=True),
            lax.all_gather(vectors.astype(jnp.bfloat16), "dp", axis=1, tiled=True),
        )
        qkv_full, out_full, up_full, down_full, bias_full, vector_full = gathered
        return (
            qkv_full,
            out_full,
            up_full.reshape(up_full.shape[0], -1),
            down_full.reshape(-1, down_full.shape[2]),
            bias_full.astype(jnp.float32),
            vector_full.astype(jnp.float32),
        )

    grad_sums = None
    outputs = []
    input_grads = []
    for micro_step in range(MICRO):
        params_fwd = gather_params()
        output, saved = forward(tokens[micro_step], params_fwd)
        outputs.append(output)
        params_back = gather_params()
        grad_input, grads = backward(cotangent[micro_step], saved, params_back)
        input_grads.append(grad_input)
        if grad_sums is None:
            grad_sums = grads
        else:
            grad_sums = tuple((old_sum + new_part for old_sum, new_part in zip(grad_sums, grads)))
    grad_qkv, grad_out_weight, grad_up, grad_down, grad_biases, grad_vectors = grad_sums
    grad_up = grad_up.reshape(-1, up_weight.shape[1], up_weight.shape[2])
    grad_down = grad_down.reshape(down_weight.shape[0], down_weight.shape[1], -1)
    reduced = (
        lax.psum_scatter(grad_qkv, "dp", scatter_dimension=1, tiled=True),
        lax.psum_scatter(grad_out_weight, "dp", scatter_dimension=1, tiled=True),
        lax.psum_scatter(grad_up, "dp", scatter_dimension=0, tiled=True),
        lax.psum_scatter(grad_down, "dp", scatter_dimension=2, tiled=True),
        lax.psum_scatter(grad_biases, "dp", scatter_dimension=1, tiled=True),
        lax.psum_scatter(grad_vectors, "dp", scatter_dimension=1, tiled=True),
    )
    vector_grad = lax.psum(reduced[5], "mp")
    grads = (reduced[0], reduced[1], reduced[2], reduced[3], reduced[4], vector_grad)
    params = (qkv_weight, out_weight, up_weight, down_weight, head_biases, vectors)
    firsts = (qkv_first, out_first, up_first, down_first, bias_first, vector_first)
    seconds = (qkv_second, out_second, up_second, down_second, bias_second, vector_second)
    updated = [
        adam_update(params[slot], firsts[slot], seconds[slot], grads[slot], RATES[slot])
        for slot in range(6)
    ]
    return (
        jnp.stack(outputs),
        jnp.stack(input_grads),
        updated[0][0],
        updated[0][1],
        updated[0][2],
        updated[1][0],
        updated[1][1],
        updated[1][2],
        updated[2][0],
        updated[2][1],
        updated[2][2],
        updated[3][0],
        updated[3][1],
        updated[3][2],
        updated[4][0],
        updated[4][1],
        updated[4][2],
        updated[5][0],
        updated[5][1],
        updated[5][2],
    )


ZS, YS, MP = (4, 2, 4)
DP = ZS * YS
LANES = 128
BF = jnp.bfloat16
F32 = jnp.float32


def swap_z(part, step):
    return lax.ppermute(
        part, "dp", [(z * YS + y, (z ^ step) * YS + y) for z in range(ZS) for y in range(YS)]
    )


def swap_y(part):
    return lax.ppermute(part, "dp", [(each, each ^ 1) for each in range(DP)])


def swap_mp(part, step):
    return lax.ppermute(part, "mp", [(each, each ^ step) for each in range(MP)])


class Chain:
    def __init__(self, steps, *args):
        self.own = None
        self.result = None
        self.steps = steps(self, *args)
        self.flight = next(self.steps)

    def land(self, arrived):
        try:
            self.flight = self.steps.send(arrived)
        except StopIteration as end:
            self.flight = None
            self.result = end.value


def meet(values, *chains):
    values, flights = lax.optimization_barrier((values, [each.flight for each in chains]))
    for each, flight in zip(chains, flights):
        each.land(flight)
    return values


def join(rows, arrived, axis):
    return jnp.concatenate([rows, arrived], -2 if axis == "y" else -1)


def swap_plane(part, axis):
    return swap_y(part) if axis == "y" else swap_mp(part, 2)


def rows_z_steps(chain, shard):
    rows = shard
    for step in (1, 2):
        (arrived,) = yield [swap_z(rows, step)]
        rows = jnp.concatenate([rows, arrived], 0)
    return rows


def cut(part, axis, pieces):
    return jnp.split(part, pieces, -2 if axis == "y" else -1) if pieces > 1 else [part]


def gather_steps(chain, parts, orders, pieces=(1, 1)):
    for axes, count in zip(zip(*orders), pieces):
        sent = [cut(part, axis, count) for part, axis in zip(parts, axes)]
        for at in range(count):
            arrived = yield [swap_plane(each[at], axis) for each, axis in zip(sent, axes)]
            parts = [join(part, each, axis) for part, each, axis in zip(parts, arrived, axes)]
    chain.own = parts
    arrived = yield [swap_mp(part, 1) for part in parts]
    return arrived


def add_low(first, second):
    return (first.astype(F32) + second.astype(F32)).astype(BF)


def halve(total, axis):
    rows, width = total.shape[-2:]
    if axis == "y":
        return (total[..., : rows // 2, :], total[..., rows // 2 :, :])
    return (total[..., : width // 2], total[..., width // 2 :])


def reduce_steps(chain, other_parts, orders, pieces=(1, 1)):
    arrived = yield [swap_mp(part, 1) for part in other_parts]
    totals = [add_low(own, each) for own, each in zip(chain.own, arrived)]
    for axes, count in zip(zip(*orders), pieces):
        halves = [halve(total, axis) for total, axis in zip(totals, axes)]
        sent = [cut(half[1], axis, count) for half, axis in zip(halves, axes)]
        received = []
        for at in range(count):
            received.append((yield [swap_plane(each[at], axis) for each, axis in zip(sent, axes)]))
        totals = []
        for half, axis, each in zip(halves, axes, zip(*received)):
            whole = each[0] if count == 1 else jnp.concatenate(each, -2 if axis == "y" else -1)
            totals.append(add_low(half[0], whole))
    return totals


def sum_z_steps(chain, total):
    rows = total.shape[0] // ZS
    arrived = yield [swap_z(total[step * rows : (step + 1) * rows], step) for step in range(1, ZS)]
    total = total[:rows].astype(F32)
    for each in arrived:
        total = total + each.astype(F32)
    return total


def sum_z_halves_steps(chain, total):
    half = total.shape[0] // 2
    (arrived,) = yield [swap_z(total[half:], 2)]
    total = add_low(total[:half], arrived)
    (arrived,) = yield [swap_z(total[half // 2 :], 1)]
    return total[: half // 2].astype(F32) + arrived.astype(F32)


def image_steps(chain, far, near):
    (arrived,) = yield [swap_mp(far, 2)]
    second, passing = arrived
    (arrived,) = yield [swap_mp(jnp.stack([near(), passing]), 1)]
    return [arrived[0], second, arrived[1]]


def small_steps(chain, shard, vector_size):
    biases = shard[:, vector_size:]
    arrived = yield [swap_mp(biases, step) for step in range(1, MP)]
    rows = jnp.concatenate([shard] + arrived, 1)
    for step in (1, 2):
        arrived = yield [swap_z(rows, step)]
        rows = jnp.concatenate([rows] + arrived, 0)
    arrived = yield [swap_y(rows)]
    rows = jnp.concatenate([rows] + arrived, 0)
    biases = rows[:, vector_size:].reshape(DP, MP, -1).transpose(1, 0, 2)
    return (rows[:, :vector_size], biases)


def small_reduce_steps(chain, vector_part, bias_part):
    near = jnp.concatenate([vector_part, bias_part[0], bias_part[2]], 1)
    far = jnp.concatenate([vector_part, bias_part[1], bias_part[3]], 1)
    (arrived,) = yield [swap_mp(far, 1)]
    total = near + arrived
    kept = vector_part.shape[1] + bias_part.shape[2]
    far = jnp.concatenate([total[:, : vector_part.shape[1]], total[:, kept:]], 1)
    (arrived,) = yield [swap_mp(far, 2)]
    total = total[:, :kept] + arrived
    arrived = yield [swap_y(total[ZS:])]
    total = total[:ZS] + arrived[0]
    arrived = yield [swap_z(total[step], step) for step in range(1, ZS)]
    total = total[0]
    for each in arrived:
        total = total + each
    return total


def norm_parts(values):
    center = values - jnp.mean(values, -1, keepdims=True)
    spread = lax.rsqrt(jnp.mean(center * center, -1, keepdims=True) + 1e-06)
    return (center * spread, spread)


def norm_back(grad, normal, spread, gain):
    scaled = grad * gain
    inner = scaled - jnp.mean(scaled, -1, keepdims=True)
    return spread * (inner - normal * jnp.mean(scaled * normal, -1, keepdims=True))


GAIN_ONE, SHIFT_ONE, OUT_BIAS, SCALE_ONE, GAIN_TWO, SHIFT_TWO, DOWN_BIAS, SCALE_TWO = range(8)


def vector_row(vector_ref, at):
    return vector_ref[at : at + 1, :]


def assemble_kernel(with_norm, place_ref, vector_ref, own_ref, *refs):
    out_ref, second_ref = refs[-2:]
    part_refs = [own_ref.at[0]] + list(refs[:-2])
    for at, part_ref in enumerate(part_refs):
        for block in range(DP):
            lanes = pl.ds(pl.multiple_of(place_ref[block] * LANES, LANES), LANES)
            out_ref[at, :, block * LANES : (block + 1) * LANES] = part_ref[:, lanes]
        values = out_ref[at].astype(F32)
        if with_norm:
            normal, _ = norm_parts(values)
            values = normal * vector_row(vector_ref, GAIN_ONE) + vector_row(vector_ref, SHIFT_ONE)
        else:
            values = values * vector_row(vector_ref, SCALE_TWO)
        second_ref[at] = values.astype(BF)


def assemble_image(place, vector_full, arrays, parts, with_norm):
    chunk_rows, width = parts[0].shape
    rows = chunk_rows // 4
    block = pl.BlockSpec((rows, width), lambda i, place_ref: (i, 0))
    result = pl.BlockSpec((MP, rows, width), lambda i, place_ref: (0, i, 0))
    shape = jax.ShapeDtypeStruct((MP, chunk_rows, width), BF)
    image, second = pl.pallas_call(
        functools.partial(assemble_kernel, with_norm),
        grid_spec=pltpu.PrefetchScalarGridSpec(
            num_scalar_prefetch=1,
            grid=(4,),
            in_specs=[
                pl.BlockSpec(vector_full.shape, lambda i, place_ref: (0, 0)),
                pl.BlockSpec((1, rows, width), lambda i, place_ref: (place_ref[DP], i, 0)),
            ]
            + [block] * len(parts),
            out_specs=[result] * 2,
        ),
        out_shape=[shape] * 2,
        compiler_params=pltpu.CompilerParams(vmem_limit_bytes=32 * 2**20),
        name="assemble_image",
    )(place, vector_full, arrays, *parts)
    return (image.reshape(-1, width), second.reshape(-1, width))


def spread_kernel(place_ref, own_ref, *refs):
    out_ref = refs[-1]
    mine = place_ref[DP]
    for at, part_ref in enumerate([own_ref] + list(refs[:-1])):
        for block in range(DP):
            lanes = pl.ds(pl.multiple_of(place_ref[block] * LANES, LANES), LANES)
            part = part_ref[:, block * LANES : (block + 1) * LANES]
            out_ref[mine ^ at, :, lanes] = part.astype(out_ref.dtype)


def spread_image(place, own, parts, dtype):
    chunk_rows, width = parts[0].shape
    rows = chunk_rows // 4
    block = pl.BlockSpec((rows, width), lambda i, place_ref: (i, 0))
    return pl.pallas_call(
        spread_kernel,
        grid_spec=pltpu.PrefetchScalarGridSpec(
            num_scalar_prefetch=1,
            grid=(4,),
            in_specs=[block] * (1 + len(parts)),
            out_specs=pl.BlockSpec((MP, rows, width), lambda i, place_ref: (0, i, 0)),
        ),
        out_shape=jax.ShapeDtypeStruct((MP, chunk_rows, width), dtype),
        compiler_params=pltpu.CompilerParams(vmem_limit_bytes=32 * 2**20),
        name="spread_image",
    )(place, own, *parts)


ROWS = 512


def product_nt(left_refs, right_refs):
    total = None
    for left_ref, right_ref in zip(left_refs, right_refs):
        part = lax.dot_general(
            left_ref[...], right_ref[...], (((1,), (1,)), ((), ())), preferred_element_type=F32
        )
        total = part if total is None else total + part
    return total


def add_rows(sums_ref, rows):
    @pl.when(pl.program_id(0) == 0)
    def _():
        sums_ref[...] = jnp.zeros_like(sums_ref)

    for at, each in enumerate(rows):
        sums_ref[at : at + 1, :] += jnp.sum(each, 0, keepdims=True)


def out_kernel(count, *refs):
    lefts, rights = (refs[:count], refs[count : 2 * count])
    vector_ref, base_ref, branch_ref, hidden_ref, normed_ref = refs[2 * count :]
    branch = product_nt(lefts, rights) + vector_row(vector_ref, OUT_BIAS)
    hidden = base_ref[...].astype(F32) + vector_row(vector_ref, SCALE_ONE) * branch
    normal, _ = norm_parts(hidden)
    branch_ref[...] = branch
    hidden_ref[...] = hidden
    normed = normal * vector_row(vector_ref, GAIN_TWO) + vector_row(vector_ref, SHIFT_TWO)
    normed_ref[...] = normed.astype(BF)


def down_kernel(count, *refs):
    lefts, rights = (refs[:count], refs[count : 2 * count])
    vector_ref, hidden_ref, output_ref, branch_ref = refs[2 * count :]
    branch = product_nt(lefts, rights) + vector_row(vector_ref, DOWN_BIAS)
    output = hidden_ref[...] + vector_row(vector_ref, SCALE_TWO) * branch
    output_ref[...] = output.astype(BF)
    branch_ref[...] = branch


def up_back_kernel(count, *refs):
    lefts, rights = (refs[:count], refs[count : 2 * count])
    vector_ref, hidden_ref, branch_ref, grad_ref, out_ref, low_ref, sums_ref = refs[2 * count :]
    grad_normed = product_nt(lefts, rights)
    normal, spread = norm_parts(hidden_ref[...])
    grad = norm_back(grad_normed, normal, spread, vector_row(vector_ref, GAIN_TWO))
    grad = grad + grad_ref[...].astype(F32)
    out_ref[...] = grad
    low_ref[...] = (grad * vector_row(vector_ref, SCALE_ONE)).astype(BF)
    add_rows(sums_ref, [grad_normed * normal, grad_normed, grad * branch_ref[...], grad])


def in_back_kernel(count, *refs):
    lefts, rights = (refs[:count], refs[count : 2 * count])
    vector_ref, base_ref, grad_ref, low_ref, sums_ref = refs[2 * count : 2 * count + 5]
    grad_normed = product_nt(lefts, rights)
    normal, spread = norm_parts(base_ref[...].astype(F32))
    grad = norm_back(grad_normed, normal, spread, vector_row(vector_ref, GAIN_ONE))
    grad = grad + grad_ref[...]
    low_ref[...] = grad.astype(BF)

    for own_ref in refs[2 * count + 5 :]:
        own_ref[...] = grad[: own_ref.shape[0]]
    add_rows(sums_ref, [grad_normed * normal, grad_normed])


def expand_kernel(left_ref, right_ref, bias_ref, activ_ref, slope_ref):
    values = jnp.dot(left_ref[...], right_ref[...], preferred_element_type=F32) + bias_ref[0:1, :]
    share = 0.5 * (1.0 + lax.erf(values * 0.7071067811865476))
    activ_ref[...] = (values * share).astype(BF)
    slope = share + values * (0.3989422804014327 * jnp.exp(-0.5 * values * values))
    slope_ref[...] = slope.astype(BF)


def expand(left, right, bias):
    rows, depth = left.shape
    width = right.shape[1]
    block = pl.BlockSpec((256, width), lambda i: (i, 0))
    return pl.pallas_call(
        expand_kernel,
        grid=(rows // 256,),
        in_specs=[
            pl.BlockSpec((256, depth), lambda i: (i, 0)),
            pl.BlockSpec((depth, width), lambda i: (0, 0), pipeline_mode=pl.Buffered(1)),
            pl.BlockSpec((1, width), lambda i: (0, 0)),
        ],
        out_specs=[block] * 2,
        out_shape=[jax.ShapeDtypeStruct((rows, width), BF)] * 2,
        compiler_params=pltpu.CompilerParams(vmem_limit_bytes=32 * 2**20),
        name="expand",
    )(left, right, bias.reshape(1, width))


def slope_kernel(left_ref, right_ref, slope_ref, grad_ref, sums_ref):
    grad = jnp.dot(left_ref[...], right_ref[...], preferred_element_type=F32)
    low = (grad * slope_ref[...].astype(F32)).astype(BF)
    grad_ref[...] = low
    add_rows(sums_ref, [low.astype(F32)])


def slope_product(left, right, slope):
    rows, depth = left.shape
    width = right.shape[1]
    block = pl.BlockSpec((256, width), lambda i: (i, 0))
    return pl.pallas_call(
        slope_kernel,
        grid=(rows // 256,),
        in_specs=[
            pl.BlockSpec((256, depth), lambda i: (i, 0)),
            pl.BlockSpec((depth, width), lambda i: (0, 0), pipeline_mode=pl.Buffered(1)),
            block,
        ],
        out_specs=[block, pl.BlockSpec((8, width), lambda i: (0, 0))],
        out_shape=[jax.ShapeDtypeStruct((rows, width), BF), jax.ShapeDtypeStruct((8, width), F32)],
        compiler_params=pltpu.CompilerParams(vmem_limit_bytes=32 * 2**20),
        name="slope_product",
    )(left, right, slope)


def row_call(kernel, name, lefts, rights, vector_full, row_inputs, outs, span=None, own_rows=0):
    rows, width = row_inputs[0].shape
    first, count = span or (0, rows // ROWS)
    rows = count * ROWS
    once = pl.Buffered(1)
    block = pl.BlockSpec((ROWS, width), lambda i: (i, 0))
    source = pl.BlockSpec((ROWS, width), lambda i: (i + first, 0))
    specs = {
        "sums": (pl.BlockSpec((8, width), lambda i: (0, 0)), jax.ShapeDtypeStruct((8, width), F32)),
        "own": (
            pl.BlockSpec((own_rows, width), lambda i: (0, 0)),
            jax.ShapeDtypeStruct((own_rows, width), F32),
        ),
    }
    pairs = [
        specs[each] if isinstance(each, str) else (block, jax.ShapeDtypeStruct((rows, width), each))
        for each in outs
    ]
    return pl.pallas_call(
        functools.partial(kernel, len(lefts)),
        grid=(count,),
        in_specs=[pl.BlockSpec((ROWS, each.shape[1]), lambda i: (i + first, 0)) for each in lefts]
        + [pl.BlockSpec(each.shape, lambda i: (0, 0), pipeline_mode=once) for each in rights]
        + [pl.BlockSpec(vector_full.shape, lambda i: (0, 0))]
        + [source] * len(row_inputs),
        out_specs=[each[0] for each in pairs],
        out_shape=[each[1] for each in pairs],
        compiler_params=pltpu.CompilerParams(vmem_limit_bytes=48 * 2**20),
        name=name,
    )(*lefts, *rights, vector_full, *row_inputs)


def lane_dot(left, right):
    return lax.dot_general(left, right, (((1,), (1,)), ((), ())), preferred_element_type=F32)


def head_masks(width):
    lane = lax.broadcasted_iota(jnp.int32, (1, width), 1)
    return [lane // DH == head for head in range(width // DH)]


def attend_kernel(block_rows, q_ref, k_ref, v_ref, o_ref, lse_ref):
    masks = head_masks(LANES)
    key_rows = k_ref[...]
    values = v_ref[...]
    zero = jnp.zeros((), BF)
    for block in range(q_ref.shape[0] // block_rows):
        rows = slice(block * block_rows, (block + 1) * block_rows)
        queries = q_ref[rows, :] * jnp.asarray(DH**-0.5, BF)
        blended = []
        for head, mask in enumerate(masks):
            scores = lane_dot(jnp.where(mask, queries, zero), key_rows)
            peak = jnp.max(scores, 1, keepdims=True)
            shifted = jnp.exp(scores - peak)
            total = jnp.sum(shifted, 1, keepdims=True)
            part = jnp.dot(shifted.astype(BF), values, preferred_element_type=F32)
            blended.append(part * (1.0 / total))
            log_total = jnp.broadcast_to(peak + jnp.log(total), (block_rows, LANES))
            lse_ref[0, head : head + 1, rows] = jnp.transpose(log_total)[0:1, :]
        o_ref[rows, :] = jnp.where(masks[0], blended[0], blended[1]).astype(BF)


def attend_back_kernel(
    block_rows, q_ref, k_ref, v_ref, g_ref, lse_ref, out_ref, dk_acc, dv_acc
):
    masks = head_masks(LANES)
    key_rows = k_ref[...]
    values = v_ref[...]
    zero = jnp.zeros((), BF)
    factor = DH**-0.5
    key_heads = [jnp.where(mask, key_rows, zero) for mask in masks]
    for block in range(q_ref.shape[0] // block_rows):
        rows = slice(block * block_rows, (block + 1) * block_rows)
        queries = q_ref[rows, :] * jnp.asarray(factor, BF)
        grads = g_ref[rows, :]
        grad_query = None
        grad_keys = None
        grad_values = None
        for head, mask in enumerate(masks):
            query_head = jnp.where(mask, queries, zero)
            grad_head = jnp.where(mask, grads, zero)
            scores = lane_dot(key_rows, query_head)
            weights = jnp.exp(scores - lse_ref[0, head : head + 1, rows])
            value_part = jnp.dot(weights.astype(BF), grad_head, preferred_element_type=F32)
            grad_rows = lane_dot(values, grad_head)
            delta = jnp.sum(grad_rows * weights, 0, keepdims=True)
            grad_scores = (weights * (grad_rows - delta)).astype(BF)
            key_part = jnp.dot(grad_scores, query_head, preferred_element_type=F32)
            query_part = lax.dot_general(
                grad_scores, key_heads[head], (((0,), (0,)), ((), ())), preferred_element_type=F32
            )
            grad_query = query_part if head == 0 else grad_query + query_part
            grad_keys = key_part if head == 0 else grad_keys + key_part
            grad_values = value_part if head == 0 else grad_values + value_part
        out_ref[rows, 0:LANES] = (grad_query * factor).astype(BF)
        if block == 0:
            dk_acc[...] = grad_keys
            dv_acc[...] = grad_values
        else:
            dk_acc[...] += grad_keys
            dv_acc[...] += grad_values
    out_ref[:, LANES : 2 * LANES] = dk_acc[...].astype(BF)
    out_ref[:, 2 * LANES : 3 * LANES] = dv_acc[...].astype(BF)


def kind_spec(rows, kind):
    return pl.BlockSpec((rows, LANES), lambda p: (0, p * 3 + kind))


def attend(heads):
    rows, width = heads.shape
    pairs = width // LANES // 3
    return pl.pallas_call(
        functools.partial(attend_kernel, 512),
        grid=(pairs,),
        in_specs=[kind_spec(rows, kind) for kind in range(3)],
        out_specs=[
            pl.BlockSpec((rows, LANES), lambda p: (0, p)),
            pl.BlockSpec((1, 8, rows), lambda p: (p, 0, 0)),
        ],
        out_shape=[
            jax.ShapeDtypeStruct((rows, pairs * LANES), BF),
            jax.ShapeDtypeStruct((pairs, 8, rows), F32),
        ],
        compiler_params=pltpu.CompilerParams(vmem_limit_bytes=32 * 2**20),
        name="attend",
    )(heads, heads, heads)


def attend_back(heads, grad_blended, log_total):
    rows, width = heads.shape
    pairs = width // LANES // 3
    return pl.pallas_call(
        functools.partial(attend_back_kernel, 512),
        grid=(pairs,),
        in_specs=[kind_spec(rows, kind) for kind in range(3)]
        + [
            pl.BlockSpec((rows, LANES), lambda p: (0, p)),
            pl.BlockSpec((1, 8, rows), lambda p: (p, 0, 0)),
        ],
        out_specs=pl.BlockSpec((rows, 3 * LANES), lambda p: (0, p)),
        out_shape=jax.ShapeDtypeStruct((rows, width), BF),
        scratch_shapes=[pltpu.VMEM((rows, LANES), F32)] * 2,
        compiler_params=pltpu.CompilerParams(vmem_limit_bytes=32 * 2**20),
        name="attend_back",
    )(heads, heads, heads, grad_blended, log_total)


def dot_nn(left, right):
    return lax.dot_general(left, right, (((1,), (0,)), ((), ())), preferred_element_type=F32)


def dot_nt(left, right):
    return lax.dot_general(left, right, (((1,), (1,)), ((), ())), preferred_element_type=F32)


def dot_tn(left, right):
    return lax.dot_general(left, right, (((0,), (0,)), ((), ())), preferred_element_type=F32)


def local_image(
    tokens,
    cotangent,
    qkv_weight,
    qkv_first,
    qkv_second,
    out_weight,
    out_first,
    out_second,
    up_weight,
    up_first,
    up_second,
    down_weight,
    down_first,
    down_second,
    head_biases,
    bias_first,
    bias_second,
    vectors,
    vector_first,
    vector_second,
):
    dp_at = lax.axis_index("dp")
    mp_at = lax.axis_index("mp")
    units = up_weight.shape[1]
    half_units = units // 2
    block_width = qkv_weight.shape[2]
    depth = qkv_weight.shape[1]
    bias_width = head_biases.shape[1]
    chunk_rows, width = tokens.shape[2:]
    order = [((zk * YS) + yk) for yk in range(YS) for zk in range(ZS)]
    place = jnp.stack([dp_at ^ each for each in order] + [mp_at]).astype(jnp.int32)
    cores = (0, 1)

    def fetch_image(array):
        chunks = array[:, 0]

        def chunk(step):
            return lax.dynamic_index_in_dim(chunks, mp_at ^ step, 0, keepdims=False)

        return Chain(image_steps, jnp.stack([chunk(2), chunk(3)]), lambda: chunk(1))

    def send_back(low):
        chunks = low.reshape(MP, chunk_rows, width)
        return Chain(image_steps, chunks[2:], lambda: chunks[1])

    small_shard = jnp.concatenate(
        [vectors.astype(BF).reshape(-1), head_biases.astype(BF).reshape(-1)]
    ).reshape(1, -1)
    vector_size = vectors.size
    kinds = qkv_weight.shape[0]
    qkv_shard = qkv_weight.astype(BF).reshape(kinds, depth, 2, LANES).transpose(1, 2, 0, 3)
    qkv_shard = qkv_shard.reshape(depth, -1)
    up_shard = jnp.concatenate(
        [out_weight.T.astype(BF), up_weight.astype(BF).reshape(depth, -1)], 1
    )
    down_shard = down_weight.transpose(2, 0, 1).astype(BF).reshape(depth, -1)
    both = ("xy", "yx")
    small = Chain(small_steps, small_shard, vector_size)
    rows_qkv = Chain(rows_z_steps, qkv_shard)
    rows_up = Chain(rows_z_steps, up_shard)
    tokens = meet(tokens, small, rows_qkv)
    fetch_tokens = fetch_image(tokens)
    meet((), small)
    meet((), small, rows_qkv, rows_up)
    part_a, part_b = jnp.split(rows_qkv.result, 2, 1)
    get_qkv = [Chain(gather_steps, [part_a], ("xy",)), Chain(gather_steps, [part_b], ("yx",))]
    meet((), small, get_qkv[1], fetch_tokens)
    tokens = meet(tokens, fetch_tokens, get_qkv[0])

    vector_full, bias_small = small.result
    vector_full = vector_full.reshape(DP, vectors.shape[0], LANES).transpose(1, 0, 2)
    vector_full = vector_full.reshape(vectors.shape[0], width).astype(F32)
    back_places = jnp.stack([((each ^ dp_at) & 1) * ZS + ((each ^ dp_at) >> 1) for each in range(DP)])
    bias_rows = jnp.take(bias_small, back_places, axis=1).reshape(2, 2, DP, -1, bias_width)
    bias_full = bias_rows.transpose(1, 3, 0, 2, 4).reshape(2, head_biases.shape[0], 2, block_width)
    bias_full = bias_full.astype(F32)

    base, normed_one = assemble_image(place, vector_full, tokens[:, 0], fetch_tokens.result, True)
    normed_one = meet(normed_one, *get_qkv, rows_up)
    out_rows, up_rows = jnp.split(rows_up.result, [block_width], 1)
    get_out = Chain(gather_steps, [jnp.stack(jnp.split(out_rows, 2, 1))], ("yx",))
    get_up = Chain(gather_steps, jnp.split(up_rows, 2, 1), both, (1, 2))

    def project(core, half, weight):
        lanes = slice(half * LANES, (half + 1) * LANES)
        zero = jnp.zeros((2, LANES), F32)
        bias = jnp.stack([bias_full[core, 0, :, lanes], zero, bias_full[core, 1, :, lanes]], 1)
        return (dot_nn(normed_one, weight) + bias.reshape(-1)).astype(BF)

    heads, blended, log_total = ([[None, None], [None, None]] for _ in range(3))

    def forward_heads(core, half):
        blended[core][half], log_total[core][half] = attend(heads[core][half])

    heads[0][0] = project(0, 0, get_qkv[0].own[0])
    heads[0][0], down_shard = meet((heads[0][0], down_shard), *get_qkv)
    w_qkv = [[each.own[0] for each in get_qkv], [each.result[0] for each in get_qkv]]
    rows_down = Chain(rows_z_steps, down_shard)
    forward_heads(0, 0)
    blended[0][0], normed_one = meet((blended[0][0], normed_one), get_out, get_up, rows_down)
    heads[0][1] = project(0, 1, w_qkv[0][1])
    forward_heads(0, 1)
    blended[0][1], normed_one = meet((blended[0][1], normed_one), get_out, get_up)
    heads[1][0] = project(1, 0, w_qkv[1][0])
    forward_heads(1, 0)
    blended[1][0], normed_one = meet(
        (blended[1][0], normed_one), get_out, rows_down, get_up
    )
    get_down = Chain(gather_steps, jnp.split(rows_down.result, 2, 1), both)
    heads[1][1] = project(1, 1, w_qkv[1][1])
    forward_heads(1, 1)
    blended = meet(blended, get_up, get_down)
    w_out = [[each[0][half] for half in (0, 1)] for each in (get_out.own, get_out.result)]
    pairs = [(core, half) for core in cores for half in (0, 1)]
    branch_one, hidden, normed_two = row_call(
        out_kernel,
        "out_norm",
        [blended[core][half] for core, half in pairs],
        [w_out[core][half] for core, half in pairs],
        vector_full,
        [base],
        [F32, F32, BF],
    )
    activ, slope = ({}, {})

    def expand_units(core, weights):
        for half in (0, 1):
            rows = bias_full[core, 2 + half * half_units : 2 + (half + 1) * half_units]
            unit_bias = rows.transpose(1, 0, 2).reshape(-1)
            activ[half, core], slope[half, core] = expand(normed_two, weights[half], unit_bias)

    w_up = [get_up.own, get_up.result]
    expand_units(0, w_up[0])
    activ, normed_two, cotangent = meet((activ, normed_two, cotangent), get_down)
    fetch_cotangent = fetch_image(cotangent)
    expand_units(1, w_up[1])
    activ = meet(activ, get_down)
    w_down = [get_down.own, get_down.result]
    parts = [(half, core) for core in (1, 0) for half in (0, 1)]
    output, branch_two = row_call(
        down_kernel,
        "down_output",
        [activ[each] for each in parts],
        [w_down[core][half] for half, core in parts],
        vector_full,
        [hidden],
        [BF, F32],
    )
    output = meet(output, fetch_cotangent)
    output, cotangent = meet((output, cotangent), fetch_cotangent)
    grad_out, grad_branch = assemble_image(
        place, vector_full, cotangent[:, 0], fetch_cotangent.result, False
    )

    def reduce_pairs(left, rights, pieces):
        chain = Chain(reduce_steps, [dot_tn(left, rights[half, 1]).astype(BF) for half in (0, 1)], both[::-1], pieces)
        chain.own = [dot_tn(left, rights[half, 0]).astype(BF) for half in (0, 1)]
        return chain

    sum_down = reduce_pairs(grad_branch, activ, (2, 1))
    grad_branch, output, slope = meet((grad_branch, output, slope), sum_down)
    send_output = send_back(output)
    grad_pre, unit_sums = ({}, {})
    for half, core in parts:
        grad_pre[half, core], unit_sums[half, core] = slope_product(
            grad_branch, w_down[core][half], slope[half, core]
        )
        if (half, core) == (0, 0):
            grad_pre, grad_branch = meet((grad_pre, grad_branch), sum_down)
    grad_pre, normed_two = meet((grad_pre, normed_two))
    sum_up = reduce_pairs(normed_two, grad_pre, (1, 1))
    grad_pre = meet(grad_pre, sum_down)
    grad_hidden, grad_projected, sums_one = row_call(
        up_back_kernel,
        "up_norm_back",
        [grad_pre[each] for each in parts],
        [w_up[core][half] for half, core in parts],
        vector_full,
        [hidden, branch_one, grad_out],
        [F32, BF, "sums"],
    )
    grad_projected = meet(grad_projected, sum_up, sum_down, send_output)
    rows_down = Chain(sum_z_halves_steps, jnp.concatenate(sum_down.result, 1))
    grad_w_out = [
        jnp.stack([dot_tn(grad_projected, each).astype(BF) for each in blended[core]]) for core in cores
    ]
    sum_out = Chain(reduce_steps, [grad_w_out[1]], ("xy",))
    sum_out.own = [grad_w_out[0]]
    grad_blended = [[dot_nn(grad_projected, each).astype(BF) for each in w_out[core]] for core in cores]
    grad_heads = [[None, None], [None, None]]

    def back_heads(core, half):
        grad_heads[core][half] = attend_back(
            heads[core][half], grad_blended[core][half], log_total[core][half]
        )
        return dot_tn(normed_one, grad_heads[core][half]).astype(BF)

    other = back_heads(1, 0)
    other, grad_blended = meet((other, grad_blended), sum_up, sum_out, rows_down, send_output)
    sum_qkv = [Chain(reduce_steps, [other], ("xy",)), None]
    sum_qkv[0].own = [back_heads(0, 0)]
    grad_heads[0][0], grad_blended = meet(
        (grad_heads[0][0], grad_blended), sum_qkv[0], sum_out, sum_up, rows_down
    )
    rows_up = Chain(sum_z_halves_steps, jnp.concatenate(sum_up.result, 1))
    other = back_heads(1, 1)
    other, grad_blended = meet((other, grad_blended), sum_out, sum_qkv[0])
    sum_qkv[1] = Chain(reduce_steps, [other], ("yx",))
    out_rows = jnp.concatenate([sum_out.result[0][0], sum_out.result[0][1]], 1)
    sum_qkv[1].own = [back_heads(0, 1)]
    grad_heads = meet(grad_heads, sum_qkv[0], sum_qkv[1], rows_up)

    def input_back(span, outs):
        return row_call(
            in_back_kernel,
            "in_norm_back",
            [grad_heads[core][half] for core, half in pairs],
            [w_qkv[core][half] for core, half in pairs],
            vector_full,
            [base, grad_hidden],
            outs,
            span,
            chunk_rows,
        )

    grad_far, sums_far = input_back((1, 1), [BF, "sums"])
    grad_near = []
    send_grad = Chain(
        image_steps, grad_far.reshape(2, chunk_rows, width), lambda: grad_near[0][chunk_rows:]
    )
    grad_heads = meet(grad_heads, sum_qkv[1])
    near, sums_near, own_grad = input_back((0, 1), [BF, "sums", "own"])
    grad_near.append(near)
    sums_near, own_grad = meet((sums_near, own_grad), sum_qkv[1], send_grad)
    sums_input = sums_far + sums_near

    grad_vectors = jnp.stack(
        [
            sums_input[0],
            sums_input[1],
            sums_one[3] * vector_full[SCALE_ONE],
            sums_one[2],
            sums_one[0],
            sums_one[1],
            jnp.sum(grad_out.astype(F32), 0) * vector_full[SCALE_TWO],
            jnp.sum(grad_out.astype(F32) * branch_two, 0),
        ]
    )
    grad_vectors = grad_vectors.reshape(-1, DP, LANES).transpose(1, 0, 2).reshape(DP, -1)
    bias_parts = []
    for core in cores:
        head_part = [
            jnp.sum(each.astype(F32), 0).reshape(2, kinds, LANES) for each in grad_heads[core]
        ]
        rows = [jnp.concatenate([each[:, kind] for each in head_part], 1) for kind in (0, 2)]
        for half in (0, 1):
            unit_part = unit_sums[half, core][0].reshape(2, half_units, block_width)
            rows += [unit_part[:, at] for at in range(half_units)]
        bias_parts.append(jnp.stack(rows, 1))
    grad_biases = jnp.stack(bias_parts, 1).reshape(MP, -1, DP, bias_width).transpose(0, 2, 1, 3)
    grad_biases = jnp.take(grad_biases, place[:DP], axis=1).reshape(MP, DP, -1)
    sum_small = Chain(small_reduce_steps, grad_vectors, grad_biases)
    rows_qkv = Chain(sum_z_steps, jnp.concatenate(sum_qkv[0].result + sum_qkv[1].result + [out_rows], 1))
    meet((), rows_up)
    meet((), send_grad)
    meet((), rows_qkv)
    for _ in range(4):
        meet((), sum_small)
    layer_output = spread_image(place, output[:chunk_rows], send_output.result, BF)[:, None]
    input_grad = spread_image(place, own_grad, send_grad.result, F32)[:, None]

    small_total = sum_small.result
    vector_grad = small_total[:vector_size].reshape(vectors.shape)
    bias_grad = small_total[vector_size:].reshape(head_biases.shape)
    qkv_size = kinds * block_width
    qkv_grad = rows_qkv.result[:, :qkv_size].reshape(depth, 2, kinds, LANES).transpose(2, 0, 1, 3)
    grads = (
        qkv_grad.reshape(qkv_weight.shape),
        rows_qkv.result[:, qkv_size:].T,
        rows_up.result.reshape(depth, units, block_width),
        rows_down.result.reshape(depth, units, block_width).transpose(1, 2, 0),
        bias_grad,
        vector_grad,
    )
    params = (qkv_weight, out_weight, up_weight, down_weight, head_biases, vectors)
    firsts = (qkv_first, out_first, up_first, down_first, bias_first, vector_first)
    seconds = (qkv_second, out_second, up_second, down_second, bias_second, vector_second)
    results = [layer_output, input_grad]
    for slot in range(6):
        results.extend(
            adam_update(params[slot], firsts[slot], seconds[slot], grads[slot], RATES[slot])
        )
    return tuple(results)


def solution(mesh):
    whole_image = mesh.shape["mp"] == MICRO == MP and mesh.shape["dp"] == DP
    return jax.shard_map(
        local_image if whole_image else local_general,
        mesh=mesh,
        in_specs=(
            P(None, "dp", "mp", None),
            P(None, "dp", "mp", None),
            P(None, "dp", "mp"),
            P(None, "dp", "mp"),
            P(None, "dp", "mp"),
            P("mp", "dp"),
            P("mp", "dp"),
            P("mp", "dp"),
            P("dp", None, "mp"),
            P("dp", None, "mp"),
            P("dp", None, "mp"),
            P(None, "mp", "dp"),
            P(None, "mp", "dp"),
            P(None, "mp", "dp"),
            P(None, ("mp", "dp")),
            P(None, ("mp", "dp")),
            P(None, ("mp", "dp")),
            P(None, "dp"),
            P(None, "dp"),
            P(None, "dp"),
        ),
        out_specs=(
            P(None, "dp", "mp", None),
            P(None, "dp", "mp", None),
            P(None, "dp", "mp"),
            P(None, "dp", "mp"),
            P(None, "dp", "mp"),
            P("mp", "dp"),
            P("mp", "dp"),
            P("mp", "dp"),
            P("dp", None, "mp"),
            P("dp", None, "mp"),
            P("dp", None, "mp"),
            P(None, "mp", "dp"),
            P(None, "mp", "dp"),
            P(None, "mp", "dp"),
            P(None, ("mp", "dp")),
            P(None, ("mp", "dp")),
            P(None, ("mp", "dp")),
            P(None, "dp"),
            P(None, "dp"),
            P(None, "dp"),
        ),
        check_vma=False,
    )
```

```python
import functools

import jax
import jax.numpy as jnp
from jax import lax
from jax.experimental import pallas as pl
from jax.experimental.pallas import tpu as pltpu
from jax.sharding import PartitionSpec as P

DH = 64
MICRO = 4
STEP = 10


RATES = (0.05, 0.2, 0.05, 0.03, 0.5, 0.5)


def layer_norm(values, gain, shift):
    center = values - jnp.mean(values, -1, keepdims=True)
    spread = jnp.mean(center * center, -1, keepdims=True)
    return center * lax.rsqrt(spread + 1e-06) * gain + shift


def exact_gelu(values):
    return jax.nn.gelu(values, approximate=False)


def adam_update(weight, first, second, grad, rate):
    first_new = 0.9 * first + 0.1 * grad
    second_new = 0.999 * second + 0.001 * grad * grad
    corrected = first_new / (1.0 - 0.9**STEP)
    scaled = jnp.sqrt(second_new / (1.0 - 0.999**STEP))
    weight_new = weight - rate * (corrected / (scaled + 1e-08) + 0.05 * weight)
    return (weight_new, first_new, second_new)


def attend_forward(queries, key_rows, values, block_rows):
    images, seq_rows, head_count, head_width = queries.shape
    block_count = seq_rows // block_rows
    factor = head_width ** (-0.5)
    query_blocks = jnp.moveaxis(
        queries.reshape(images, block_count, block_rows, head_count, head_width), 1, 0
    )

    def one_block(query_part):
        scores = (
            jnp.einsum("iqhe,ikhe->ihqk", query_part, key_rows, preferred_element_type=jnp.float32)
            * factor
        )
        row_peak = jnp.max(scores, -1, keepdims=True)
        shifted = jnp.exp(scores - row_peak)
        row_total = jnp.sum(shifted, -1, keepdims=True)
        softmax_rows = (shifted / row_total).astype(jnp.bfloat16)
        blended = jnp.einsum(
            "ihqk,ikhe->iqhe", softmax_rows, values, preferred_element_type=jnp.float32
        )
        return (blended, row_peak[..., 0] + jnp.log(row_total[..., 0]))

    blended, log_total = lax.map(one_block, query_blocks)
    blended = jnp.moveaxis(blended, 0, 1).reshape(images, seq_rows, head_count * head_width)
    return (blended.astype(jnp.bfloat16), log_total)


def attend_backward(queries, key_rows, values, grad_blended, log_total, block_rows):
    images, seq_rows, head_count, head_width = queries.shape
    block_count = seq_rows // block_rows
    factor = head_width ** (-0.5)
    split_shape = (images, block_count, block_rows, head_count, head_width)
    query_blocks = jnp.moveaxis(queries.reshape(split_shape), 1, 0)
    grad_blocks = jnp.moveaxis(grad_blended.reshape(split_shape), 1, 0)

    def one_block(carry, inputs_part):
        query_part, grad_part, total_part = inputs_part
        grad_keys, grad_values = carry
        scores = (
            jnp.einsum("iqhe,ikhe->ihqk", query_part, key_rows, preferred_element_type=jnp.float32)
            * factor
        )
        softmax_rows = jnp.exp(scores - total_part[..., None])
        grad_values = grad_values + jnp.einsum(
            "ihqk,iqhe->ikhe",
            softmax_rows.astype(jnp.bfloat16),
            grad_part,
            preferred_element_type=jnp.float32,
        )
        grad_rows = jnp.einsum(
            "iqhe,ikhe->ihqk", grad_part, values, preferred_element_type=jnp.float32
        )
        grad_scores = softmax_rows * (
            grad_rows - jnp.sum(grad_rows * softmax_rows, -1, keepdims=True)
        )
        grad_scores = grad_scores.astype(jnp.bfloat16)
        grad_query = (
            jnp.einsum("ihqk,ikhe->iqhe", grad_scores, key_rows, preferred_element_type=jnp.float32)
            * factor
        )
        grad_keys = (
            grad_keys
            + jnp.einsum(
                "ihqk,iqhe->ikhe", grad_scores, query_part, preferred_element_type=jnp.float32
            )
            * factor
        )
        return ((grad_keys, grad_values), grad_query)

    zero_grad = jnp.zeros(queries.shape, jnp.float32)
    (grad_keys, grad_values), grad_query = lax.scan(
        one_block, (zero_grad, zero_grad), (query_blocks, grad_blocks, log_total)
    )
    flat_shape = (images, seq_rows, head_count * head_width)
    grad_query = jnp.moveaxis(grad_query, 0, 1).reshape(flat_shape)
    stacked = jnp.stack(
        [grad_query, grad_keys.reshape(flat_shape), grad_values.reshape(flat_shape)]
    )
    return stacked.astype(jnp.bfloat16)


def rows_forward(part):
    return lax.all_gather(part, "mp", axis=1, tiled=True)


def rows_sum_forward(part):
    return lax.psum_scatter(part, "mp", scatter_dimension=1, tiled=True)


def rows_backward(part):
    return lax.all_gather(part, "mp", axis=1, tiled=True)


def rows_sum_backward(part):
    return lax.psum_scatter(part, "mp", scatter_dimension=1, tiled=True)


def forward(inputs, params):
    qkv_full, out_full, up_full, down_full, bias_full, vector_full = params
    base = inputs.astype(jnp.float32)
    normed = layer_norm(base, vector_full[0], vector_full[1]).astype(jnp.bfloat16)
    normed_all = rows_forward(normed)
    images, seq_rows = (normed_all.shape[0], normed_all.shape[1])
    head_shape = (images, seq_rows, -1, DH)
    project = jnp.einsum("isd,tde->tise", normed_all, qkv_full, preferred_element_type=jnp.float32)
    queries = (project[0] + bias_full[0]).astype(jnp.bfloat16).reshape(head_shape)
    key_rows = project[1].astype(jnp.bfloat16).reshape(head_shape)
    values = (project[2] + bias_full[1]).astype(jnp.bfloat16).reshape(head_shape)
    blended, log_total = attend_forward(queries, key_rows, values, min(512, seq_rows))
    projected = rows_sum_forward(
        jnp.einsum("ise,ed->isd", blended, out_full, preferred_element_type=jnp.float32)
    )
    branch_one = projected + vector_full[2]
    hidden = base + vector_full[3] * branch_one
    normed_two = layer_norm(hidden, vector_full[4], vector_full[5]).astype(jnp.bfloat16)
    normed_two_all = rows_forward(normed_two)
    pre_act = jnp.einsum(
        "isd,df->isf", normed_two_all, up_full, preferred_element_type=jnp.float32
    ) + bias_full[2:].reshape(-1)
    activ = exact_gelu(pre_act).astype(jnp.bfloat16)
    branch_two = (
        rows_sum_forward(
            jnp.einsum("isf,fd->isd", activ, down_full, preferred_element_type=jnp.float32)
        )
        + vector_full[6]
    )
    output = hidden + vector_full[7] * branch_two
    saved = (
        base,
        hidden,
        branch_one,
        branch_two,
        normed_all,
        queries,
        key_rows,
        values,
        log_total,
        blended,
        normed_two_all,
        pre_act,
        activ,
    )
    return (output.astype(jnp.bfloat16), saved)


def backward(grad_output, saved, params):
    qkv_full, out_full, up_full, down_full, bias_full, vector_full = params
    (
        base,
        hidden,
        branch_one,
        branch_two,
        normed_all,
        queries,
        key_rows,
        values,
        log_total,
        blended,
        normed_two_all,
        pre_act,
        activ,
    ) = saved
    local_width = qkv_full.shape[2]
    grad_out = grad_output.astype(jnp.float32)
    grad_scale_two = jnp.sum(grad_out * branch_two, axis=(0, 1))
    grad_bias_two = jnp.sum(grad_out, axis=(0, 1)) * vector_full[7]
    grad_branch = rows_backward((grad_out * vector_full[7]).astype(jnp.bfloat16))
    grad_down = jnp.einsum("isf,isd->fd", activ, grad_branch, preferred_element_type=jnp.float32)
    grad_activ = jnp.einsum(
        "isd,fd->isf", grad_branch, down_full, preferred_element_type=jnp.float32
    )
    grad_pre = jax.vjp(exact_gelu, pre_act)[1](grad_activ)[0].astype(jnp.bfloat16)
    grad_up_bias = jnp.sum(grad_pre, axis=(0, 1), dtype=jnp.float32)
    grad_up = jnp.einsum(
        "isd,isf->df", normed_two_all, grad_pre, preferred_element_type=jnp.float32
    )
    grad_normed_two = rows_sum_backward(
        jnp.einsum("isf,df->isd", grad_pre, up_full, preferred_element_type=jnp.float32)
    )
    norm_back_two = jax.vjp(layer_norm, hidden, vector_full[4], vector_full[5])[1]
    grad_hidden, grad_gain_two, grad_shift_two = norm_back_two(grad_normed_two)
    grad_hidden = grad_out + grad_hidden
    grad_scale_one = jnp.sum(grad_hidden * branch_one, axis=(0, 1))
    grad_out_bias = jnp.sum(grad_hidden, axis=(0, 1)) * vector_full[3]
    grad_projected = rows_backward((grad_hidden * vector_full[3]).astype(jnp.bfloat16))
    grad_out_weight = jnp.einsum(
        "ise,isd->ed", blended, grad_projected, preferred_element_type=jnp.float32
    )
    grad_blended = jnp.einsum(
        "isd,ed->ise", grad_projected, out_full, preferred_element_type=jnp.float32
    ).astype(jnp.bfloat16)
    grad_project = attend_backward(
        queries, key_rows, values, grad_blended, log_total, min(512, queries.shape[1])
    )
    grad_query_bias = jnp.sum(grad_project[0], axis=(0, 1), dtype=jnp.float32)
    grad_value_bias = jnp.sum(grad_project[2], axis=(0, 1), dtype=jnp.float32)
    grad_qkv = jnp.einsum(
        "isd,tise->tde", normed_all, grad_project, preferred_element_type=jnp.float32
    )
    grad_normed = rows_sum_backward(
        jnp.einsum("tise,tde->isd", grad_project, qkv_full, preferred_element_type=jnp.float32)
    )
    norm_back_one = jax.vjp(layer_norm, base, vector_full[0], vector_full[1])[1]
    grad_input_part, grad_gain_one, grad_shift_one = norm_back_one(grad_normed)
    grad_input = grad_hidden + grad_input_part
    grad_vectors = jnp.stack(
        [
            grad_gain_one,
            grad_shift_one,
            grad_out_bias,
            grad_scale_one,
            grad_gain_two,
            grad_shift_two,
            grad_bias_two,
            grad_scale_two,
        ]
    )
    grad_biases = jnp.concatenate(
        [jnp.stack([grad_query_bias, grad_value_bias]), grad_up_bias.reshape(-1, local_width)], 0
    )
    return (grad_input, (grad_qkv, grad_out_weight, grad_up, grad_down, grad_biases, grad_vectors))


def local_general(
    tokens,
    cotangent,
    qkv_weight,
    qkv_first,
    qkv_second,
    out_weight,
    out_first,
    out_second,
    up_weight,
    up_first,
    up_second,
    down_weight,
    down_first,
    down_second,
    head_biases,
    bias_first,
    bias_second,
    vectors,
    vector_first,
    vector_second,
):

    def gather_params():
        gathered = (
            lax.all_gather(qkv_weight.astype(jnp.bfloat16), "dp", axis=1, tiled=True),
            lax.all_gather(out_weight.astype(jnp.bfloat16), "dp", axis=1, tiled=True),
            lax.all_gather(up_weight.astype(jnp.bfloat16), "dp", axis=0, tiled=True),
            lax.all_gather(down_weight.astype(jnp.bfloat16), "dp", axis=2, tiled=True),
            lax.all_gather(head_biases.astype(jnp.bfloat16), "dp", axis=1, tiled=True),
            lax.all_gather(vectors.astype(jnp.bfloat16), "dp", axis=1, tiled=True),
        )
        qkv_full, out_full, up_full, down_full, bias_full, vector_full = gathered
        return (
            qkv_full,
            out_full,
            up_full.reshape(up_full.shape[0], -1),
            down_full.reshape(-1, down_full.shape[2]),
            bias_full.astype(jnp.float32),
            vector_full.astype(jnp.float32),
        )

    grad_sums = None
    outputs = []
    input_grads = []
    for micro_step in range(MICRO):
        params_fwd = gather_params()
        output, saved = forward(tokens[micro_step], params_fwd)
        outputs.append(output)
        params_back = gather_params()
        grad_input, grads = backward(cotangent[micro_step], saved, params_back)
        input_grads.append(grad_input)
        if grad_sums is None:
            grad_sums = grads
        else:
            grad_sums = tuple((old_sum + new_part for old_sum, new_part in zip(grad_sums, grads)))
    grad_qkv, grad_out_weight, grad_up, grad_down, grad_biases, grad_vectors = grad_sums
    grad_up = grad_up.reshape(-1, up_weight.shape[1], up_weight.shape[2])
    grad_down = grad_down.reshape(down_weight.shape[0], down_weight.shape[1], -1)
    reduced = (
        lax.psum_scatter(grad_qkv, "dp", scatter_dimension=1, tiled=True),
        lax.psum_scatter(grad_out_weight, "dp", scatter_dimension=1, tiled=True),
        lax.psum_scatter(grad_up, "dp", scatter_dimension=0, tiled=True),
        lax.psum_scatter(grad_down, "dp", scatter_dimension=2, tiled=True),
        lax.psum_scatter(grad_biases, "dp", scatter_dimension=1, tiled=True),
        lax.psum_scatter(grad_vectors, "dp", scatter_dimension=1, tiled=True),
    )
    vector_grad = lax.psum(reduced[5], "mp")
    grads = (reduced[0], reduced[1], reduced[2], reduced[3], reduced[4], vector_grad)
    params = (qkv_weight, out_weight, up_weight, down_weight, head_biases, vectors)
    firsts = (qkv_first, out_first, up_first, down_first, bias_first, vector_first)
    seconds = (qkv_second, out_second, up_second, down_second, bias_second, vector_second)
    updated = [
        adam_update(params[slot], firsts[slot], seconds[slot], grads[slot], RATES[slot])
        for slot in range(6)
    ]
    return (
        jnp.stack(outputs),
        jnp.stack(input_grads),
        updated[0][0],
        updated[0][1],
        updated[0][2],
        updated[1][0],
        updated[1][1],
        updated[1][2],
        updated[2][0],
        updated[2][1],
        updated[2][2],
        updated[3][0],
        updated[3][1],
        updated[3][2],
        updated[4][0],
        updated[4][1],
        updated[4][2],
        updated[5][0],
        updated[5][1],
        updated[5][2],
    )


ZS, YS, MP = (4, 2, 4)
DP = ZS * YS
LANES = 128
BF = jnp.bfloat16
F32 = jnp.float32


def swap_z(part, step):
    return lax.ppermute(
        part, "dp", [(z * YS + y, (z ^ step) * YS + y) for z in range(ZS) for y in range(YS)]
    )


def swap_y(part):
    return lax.ppermute(part, "dp", [(each, each ^ 1) for each in range(DP)])


def swap_mp(part, step):
    return lax.ppermute(part, "mp", [(each, each ^ step) for each in range(MP)])


class Chain:
    def __init__(self, steps, *args):
        self.own = None
        self.result = None
        self.steps = steps(self, *args)
        self.flight = next(self.steps)

    def land(self, arrived):
        try:
            self.flight = self.steps.send(arrived)
        except StopIteration as end:
            self.flight = None
            self.result = end.value


def meet(values, *chains):
    values, flights = lax.optimization_barrier((values, [each.flight for each in chains]))
    for each, flight in zip(chains, flights):
        each.land(flight)
    return values


def join(rows, arrived, axis):
    return jnp.concatenate([rows, arrived], -2 if axis == "y" else -1)


def swap_plane(part, axis):
    return swap_y(part) if axis == "y" else swap_mp(part, 2)


def rows_z_steps(chain, shard):
    rows = shard
    for step in (1, 2):
        (arrived,) = yield [swap_z(rows, step)]
        rows = jnp.concatenate([rows, arrived], 0)
    return rows


def cut(part, axis, pieces):
    return jnp.split(part, pieces, -2 if axis == "y" else -1) if pieces > 1 else [part]


def gather_steps(chain, parts, orders, pieces=(1, 1)):
    for axes, count in zip(zip(*orders), pieces):
        sent = [cut(part, axis, count) for part, axis in zip(parts, axes)]
        for at in range(count):
            arrived = yield [swap_plane(each[at], axis) for each, axis in zip(sent, axes)]
            parts = [join(part, each, axis) for part, each, axis in zip(parts, arrived, axes)]
    chain.own = parts
    arrived = yield [swap_mp(part, 1) for part in parts]
    return arrived


def add_low(first, second):
    return (first.astype(F32) + second.astype(F32)).astype(BF)


def halve(total, axis):
    rows, width = total.shape[-2:]
    if axis == "y":
        return (total[..., : rows // 2, :], total[..., rows // 2 :, :])
    return (total[..., : width // 2], total[..., width // 2 :])


def reduce_steps(chain, other_parts, orders, pieces=(1, 1)):
    arrived = yield [swap_mp(part, 1) for part in other_parts]
    totals = [add_low(own, each) for own, each in zip(chain.own, arrived)]
    for axes, count in zip(zip(*orders), pieces):
        halves = [halve(total, axis) for total, axis in zip(totals, axes)]
        sent = [cut(half[1], axis, count) for half, axis in zip(halves, axes)]
        received = []
        for at in range(count):
            received.append((yield [swap_plane(each[at], axis) for each, axis in zip(sent, axes)]))
        totals = []
        for half, axis, each in zip(halves, axes, zip(*received)):
            whole = each[0] if count == 1 else jnp.concatenate(each, -2 if axis == "y" else -1)
            totals.append(add_low(half[0], whole))
    return totals


def sum_z_steps(chain, total):
    rows = total.shape[0] // ZS
    arrived = yield [swap_z(total[step * rows : (step + 1) * rows], step) for step in range(1, ZS)]
    total = total[:rows].astype(F32)
    for each in arrived:
        total = total + each.astype(F32)
    return total


def sum_z_halves_steps(chain, total):
    half = total.shape[0] // 2
    (arrived,) = yield [swap_z(total[half:], 2)]
    total = add_low(total[:half], arrived)
    (arrived,) = yield [swap_z(total[half // 2 :], 1)]
    return total[: half // 2].astype(F32) + arrived.astype(F32)


def image_steps(chain, far, near):
    (arrived,) = yield [swap_mp(far, 2)]
    second, passing = arrived
    (arrived,) = yield [swap_mp(jnp.stack([near(), passing]), 1)]
    return [arrived[0], second, arrived[1]]


def small_steps(chain, shard, vector_size):
    biases = shard[:, vector_size:]
    arrived = yield [swap_mp(biases, step) for step in range(1, MP)]
    rows = jnp.concatenate([shard] + arrived, 1)
    for step in (1, 2):
        arrived = yield [swap_z(rows, step)]
        rows = jnp.concatenate([rows] + arrived, 0)
    arrived = yield [swap_y(rows)]
    rows = jnp.concatenate([rows] + arrived, 0)
    biases = rows[:, vector_size:].reshape(DP, MP, -1).transpose(1, 0, 2)
    return (rows[:, :vector_size], biases)


def small_reduce_steps(chain, vector_part, bias_part):
    near = jnp.concatenate([vector_part, bias_part[0], bias_part[2]], 1)
    far = jnp.concatenate([vector_part, bias_part[1], bias_part[3]], 1)
    (arrived,) = yield [swap_mp(far, 1)]
    total = near + arrived
    kept = vector_part.shape[1] + bias_part.shape[2]
    far = jnp.concatenate([total[:, : vector_part.shape[1]], total[:, kept:]], 1)
    (arrived,) = yield [swap_mp(far, 2)]
    total = total[:, :kept] + arrived
    arrived = yield [swap_y(total[ZS:])]
    total = total[:ZS] + arrived[0]
    arrived = yield [swap_z(total[step], step) for step in range(1, ZS)]
    total = total[0]
    for each in arrived:
        total = total + each
    return total


def norm_parts(values):
    center = values - jnp.mean(values, -1, keepdims=True)
    spread = lax.rsqrt(jnp.mean(center * center, -1, keepdims=True) + 1e-06)
    return (center * spread, spread)


def norm_back(grad, normal, spread, gain):
    scaled = grad * gain
    inner = scaled - jnp.mean(scaled, -1, keepdims=True)
    return spread * (inner - normal * jnp.mean(scaled * normal, -1, keepdims=True))


GAIN_ONE, SHIFT_ONE, OUT_BIAS, SCALE_ONE, GAIN_TWO, SHIFT_TWO, DOWN_BIAS, SCALE_TWO = range(8)


def vector_row(vector_ref, at):
    return vector_ref[at : at + 1, :]


def assemble_kernel(with_norm, place_ref, vector_ref, own_ref, *refs):
    out_ref, second_ref = refs[-2:]
    part_refs = [own_ref.at[0]] + list(refs[:-2])
    for at, part_ref in enumerate(part_refs):
        for block in range(DP):
            lanes = pl.ds(pl.multiple_of(place_ref[block] * LANES, LANES), LANES)
            out_ref[at, :, block * LANES : (block + 1) * LANES] = part_ref[:, lanes]
        values = out_ref[at].astype(F32)
        if with_norm:
            normal, _ = norm_parts(values)
            values = normal * vector_row(vector_ref, GAIN_ONE) + vector_row(vector_ref, SHIFT_ONE)
        else:
            values = values * vector_row(vector_ref, SCALE_TWO)
        second_ref[at] = values.astype(BF)


def assemble_image(place, vector_full, arrays, parts, with_norm):
    chunk_rows, width = parts[0].shape
    rows = chunk_rows // 4
    block = pl.BlockSpec((rows, width), lambda i, place_ref: (i, 0))
    result = pl.BlockSpec((MP, rows, width), lambda i, place_ref: (0, i, 0))
    shape = jax.ShapeDtypeStruct((MP, chunk_rows, width), BF)
    image, second = pl.pallas_call(
        functools.partial(assemble_kernel, with_norm),
        grid_spec=pltpu.PrefetchScalarGridSpec(
            num_scalar_prefetch=1,
            grid=(4,),
            in_specs=[
                pl.BlockSpec(vector_full.shape, lambda i, place_ref: (0, 0)),
                pl.BlockSpec((1, rows, width), lambda i, place_ref: (place_ref[DP], i, 0)),
            ]
            + [block] * len(parts),
            out_specs=[result] * 2,
        ),
        out_shape=[shape] * 2,
        compiler_params=pltpu.CompilerParams(vmem_limit_bytes=32 * 2**20),
        name="assemble_image",
    )(place, vector_full, arrays, *parts)
    return (image.reshape(-1, width), second.reshape(-1, width))


def spread_kernel(place_ref, own_ref, *refs):
    out_ref = refs[-1]
    mine = place_ref[DP]
    for at, part_ref in enumerate([own_ref] + list(refs[:-1])):
        for block in range(DP):
            lanes = pl.ds(pl.multiple_of(place_ref[block] * LANES, LANES), LANES)
            part = part_ref[:, block * LANES : (block + 1) * LANES]
            out_ref[mine ^ at, :, lanes] = part.astype(out_ref.dtype)


def spread_image(place, own, parts, dtype):
    chunk_rows, width = parts[0].shape
    rows = chunk_rows // 4
    block = pl.BlockSpec((rows, width), lambda i, place_ref: (i, 0))
    return pl.pallas_call(
        spread_kernel,
        grid_spec=pltpu.PrefetchScalarGridSpec(
            num_scalar_prefetch=1,
            grid=(4,),
            in_specs=[block] * (1 + len(parts)),
            out_specs=pl.BlockSpec((MP, rows, width), lambda i, place_ref: (0, i, 0)),
        ),
        out_shape=jax.ShapeDtypeStruct((MP, chunk_rows, width), dtype),
        compiler_params=pltpu.CompilerParams(vmem_limit_bytes=32 * 2**20),
        name="spread_image",
    )(place, own, *parts)


ROWS = 512


def product_nt(left_refs, right_refs):
    total = None
    for left_ref, right_ref in zip(left_refs, right_refs):
        part = lax.dot_general(
            left_ref[...], right_ref[...], (((1,), (1,)), ((), ())), preferred_element_type=F32
        )
        total = part if total is None else total + part
    return total


def add_rows(sums_ref, rows):
    @pl.when(pl.program_id(0) == 0)
    def _():
        sums_ref[...] = jnp.zeros_like(sums_ref)

    for at, each in enumerate(rows):
        sums_ref[at : at + 1, :] += jnp.sum(each, 0, keepdims=True)


def out_kernel(count, *refs):
    lefts, rights = (refs[:count], refs[count : 2 * count])
    vector_ref, base_ref, branch_ref, hidden_ref, normed_ref = refs[2 * count :]
    branch = product_nt(lefts, rights) + vector_row(vector_ref, OUT_BIAS)
    hidden = base_ref[...].astype(F32) + vector_row(vector_ref, SCALE_ONE) * branch
    normal, _ = norm_parts(hidden)
    branch_ref[...] = branch
    hidden_ref[...] = hidden
    normed = normal * vector_row(vector_ref, GAIN_TWO) + vector_row(vector_ref, SHIFT_TWO)
    normed_ref[...] = normed.astype(BF)


def down_kernel(count, *refs):
    lefts, rights = (refs[:count], refs[count : 2 * count])
    vector_ref, hidden_ref, output_ref, branch_ref = refs[2 * count :]
    branch = product_nt(lefts, rights) + vector_row(vector_ref, DOWN_BIAS)
    output = hidden_ref[...] + vector_row(vector_ref, SCALE_TWO) * branch
    output_ref[...] = output.astype(BF)
    branch_ref[...] = branch


def up_back_kernel(count, *refs):
    lefts, rights = (refs[:count], refs[count : 2 * count])
    vector_ref, hidden_ref, branch_ref, grad_ref, out_ref, low_ref, sums_ref = refs[2 * count :]
    grad_normed = product_nt(lefts, rights)
    normal, spread = norm_parts(hidden_ref[...])
    grad = norm_back(grad_normed, normal, spread, vector_row(vector_ref, GAIN_TWO))
    grad = grad + grad_ref[...].astype(F32)
    out_ref[...] = grad
    low_ref[...] = (grad * vector_row(vector_ref, SCALE_ONE)).astype(BF)
    add_rows(sums_ref, [grad_normed * normal, grad_normed, grad * branch_ref[...], grad])


def in_back_kernel(count, *refs):
    lefts, rights = (refs[:count], refs[count : 2 * count])
    vector_ref, base_ref, grad_ref, low_ref, sums_ref = refs[2 * count : 2 * count + 5]
    grad_normed = product_nt(lefts, rights)
    normal, spread = norm_parts(base_ref[...].astype(F32))
    grad = norm_back(grad_normed, normal, spread, vector_row(vector_ref, GAIN_ONE))
    grad = grad + grad_ref[...]
    low_ref[...] = grad.astype(BF)

    for own_ref in refs[2 * count + 5 :]:
        own_ref[...] = grad[: own_ref.shape[0]]
    add_rows(sums_ref, [grad_normed * normal, grad_normed])


def expand_kernel(left_ref, right_ref, bias_ref, activ_ref, slope_ref):
    values = jnp.dot(left_ref[...], right_ref[...], preferred_element_type=F32) + bias_ref[0:1, :]
    share = 0.5 * (1.0 + lax.erf(values * 0.7071067811865476))
    activ_ref[...] = (values * share).astype(BF)
    slope = share + values * (0.3989422804014327 * jnp.exp(-0.5 * values * values))
    slope_ref[...] = slope.astype(BF)


def expand(left, right, bias):
    rows, depth = left.shape
    width = right.shape[1]
    block = pl.BlockSpec((256, width), lambda i: (i, 0))
    return pl.pallas_call(
        expand_kernel,
        grid=(rows // 256,),
        in_specs=[
            pl.BlockSpec((256, depth), lambda i: (i, 0)),
            pl.BlockSpec((depth, width), lambda i: (0, 0), pipeline_mode=pl.Buffered(1)),
            pl.BlockSpec((1, width), lambda i: (0, 0)),
        ],
        out_specs=[block] * 2,
        out_shape=[jax.ShapeDtypeStruct((rows, width), BF)] * 2,
        compiler_params=pltpu.CompilerParams(vmem_limit_bytes=32 * 2**20),
        name="expand",
    )(left, right, bias.reshape(1, width))


def slope_kernel(left_ref, right_ref, slope_ref, grad_ref, sums_ref):
    grad = jnp.dot(left_ref[...], right_ref[...], preferred_element_type=F32)
    low = (grad * slope_ref[...].astype(F32)).astype(BF)
    grad_ref[...] = low
    add_rows(sums_ref, [low.astype(F32)])


def slope_product(left, right, slope):
    rows, depth = left.shape
    width = right.shape[1]
    block = pl.BlockSpec((256, width), lambda i: (i, 0))
    return pl.pallas_call(
        slope_kernel,
        grid=(rows // 256,),
        in_specs=[
            pl.BlockSpec((256, depth), lambda i: (i, 0)),
            pl.BlockSpec((depth, width), lambda i: (0, 0), pipeline_mode=pl.Buffered(1)),
            block,
        ],
        out_specs=[block, pl.BlockSpec((8, width), lambda i: (0, 0))],
        out_shape=[jax.ShapeDtypeStruct((rows, width), BF), jax.ShapeDtypeStruct((8, width), F32)],
        compiler_params=pltpu.CompilerParams(vmem_limit_bytes=32 * 2**20),
        name="slope_product",
    )(left, right, slope)


def row_call(kernel, name, lefts, rights, vector_full, row_inputs, outs, span=None, own_rows=0):
    rows, width = row_inputs[0].shape
    first, count = span or (0, rows // ROWS)
    rows = count * ROWS
    once = pl.Buffered(1)
    block = pl.BlockSpec((ROWS, width), lambda i: (i, 0))
    source = pl.BlockSpec((ROWS, width), lambda i: (i + first, 0))
    specs = {
        "sums": (pl.BlockSpec((8, width), lambda i: (0, 0)), jax.ShapeDtypeStruct((8, width), F32)),
        "own": (
            pl.BlockSpec((own_rows, width), lambda i: (0, 0)),
            jax.ShapeDtypeStruct((own_rows, width), F32),
        ),
    }
    pairs = [
        specs[each] if isinstance(each, str) else (block, jax.ShapeDtypeStruct((rows, width), each))
        for each in outs
    ]
    return pl.pallas_call(
        functools.partial(kernel, len(lefts)),
        grid=(count,),
        in_specs=[pl.BlockSpec((ROWS, each.shape[1]), lambda i: (i + first, 0)) for each in lefts]
        + [pl.BlockSpec(each.shape, lambda i: (0, 0), pipeline_mode=once) for each in rights]
        + [pl.BlockSpec(vector_full.shape, lambda i: (0, 0))]
        + [source] * len(row_inputs),
        out_specs=[each[0] for each in pairs],
        out_shape=[each[1] for each in pairs],
        compiler_params=pltpu.CompilerParams(vmem_limit_bytes=48 * 2**20),
        name=name,
    )(*lefts, *rights, vector_full, *row_inputs)


def lane_dot(left, right):
    return lax.dot_general(left, right, (((1,), (1,)), ((), ())), preferred_element_type=F32)


def head_masks(width):
    lane = lax.broadcasted_iota(jnp.int32, (1, width), 1)
    return [lane // DH == head for head in range(width // DH)]


def attend_kernel(block_rows, q_ref, k_ref, v_ref, o_ref, lse_ref):
    masks = head_masks(LANES)
    key_rows = k_ref[...]
    values = v_ref[...]
    zero = jnp.zeros((), BF)
    for block in range(q_ref.shape[0] // block_rows):
        rows = slice(block * block_rows, (block + 1) * block_rows)
        queries = q_ref[rows, :] * jnp.asarray(DH**-0.5, BF)
        blended = []
        for head, mask in enumerate(masks):
            scores = lane_dot(jnp.where(mask, queries, zero), key_rows)
            peak = jnp.max(scores, 1, keepdims=True)
            shifted = jnp.exp(scores - peak)
            total = jnp.sum(shifted, 1, keepdims=True)
            part = jnp.dot(shifted.astype(BF), values, preferred_element_type=F32)
            blended.append(part * (1.0 / total))
            log_total = jnp.broadcast_to(peak + jnp.log(total), (block_rows, LANES))
            lse_ref[0, head : head + 1, rows] = jnp.transpose(log_total)[0:1, :]
        o_ref[rows, :] = jnp.where(masks[0], blended[0], blended[1]).astype(BF)


def attend_back_kernel(
    block_rows, q_ref, k_ref, v_ref, g_ref, lse_ref, out_ref, dk_acc, dv_acc
):
    masks = head_masks(LANES)
    key_rows = k_ref[...]
    values = v_ref[...]
    zero = jnp.zeros((), BF)
    factor = DH**-0.5
    key_heads = [jnp.where(mask, key_rows, zero) for mask in masks]
    for block in range(q_ref.shape[0] // block_rows):
        rows = slice(block * block_rows, (block + 1) * block_rows)
        queries = q_ref[rows, :] * jnp.asarray(factor, BF)
        grads = g_ref[rows, :]
        grad_query = None
        grad_keys = None
        grad_values = None
        for head, mask in enumerate(masks):
            query_head = jnp.where(mask, queries, zero)
            grad_head = jnp.where(mask, grads, zero)
            scores = lane_dot(key_rows, query_head)
            weights = jnp.exp(scores - lse_ref[0, head : head + 1, rows])
            value_part = jnp.dot(weights.astype(BF), grad_head, preferred_element_type=F32)
            grad_rows = lane_dot(values, grad_head)
            delta = jnp.sum(grad_rows * weights, 0, keepdims=True)
            grad_scores = (weights * (grad_rows - delta)).astype(BF)
            key_part = jnp.dot(grad_scores, query_head, preferred_element_type=F32)
            query_part = lax.dot_general(
                grad_scores, key_heads[head], (((0,), (0,)), ((), ())), preferred_element_type=F32
            )
            grad_query = query_part if head == 0 else grad_query + query_part
            grad_keys = key_part if head == 0 else grad_keys + key_part
            grad_values = value_part if head == 0 else grad_values + value_part
        out_ref[rows, 0:LANES] = (grad_query * factor).astype(BF)
        if block == 0:
            dk_acc[...] = grad_keys
            dv_acc[...] = grad_values
        else:
            dk_acc[...] += grad_keys
            dv_acc[...] += grad_values
    out_ref[:, LANES : 2 * LANES] = dk_acc[...].astype(BF)
    out_ref[:, 2 * LANES : 3 * LANES] = dv_acc[...].astype(BF)


def kind_spec(rows, kind):
    return pl.BlockSpec((rows, LANES), lambda p: (0, p * 3 + kind))


def attend(heads):
    rows, width = heads.shape
    pairs = width // LANES // 3
    return pl.pallas_call(
        functools.partial(attend_kernel, 1024),
        grid=(pairs,),
        in_specs=[kind_spec(rows, kind) for kind in range(3)],
        out_specs=[
            pl.BlockSpec((rows, LANES), lambda p: (0, p)),
            pl.BlockSpec((1, 8, rows), lambda p: (p, 0, 0)),
        ],
        out_shape=[
            jax.ShapeDtypeStruct((rows, pairs * LANES), BF),
            jax.ShapeDtypeStruct((pairs, 8, rows), F32),
        ],
        compiler_params=pltpu.CompilerParams(vmem_limit_bytes=40 * 2**20),
        name="attend",
    )(heads, heads, heads)


def attend_back(heads, grad_blended, log_total):
    rows, width = heads.shape
    pairs = width // LANES // 3
    return pl.pallas_call(
        functools.partial(attend_back_kernel, 1024),
        grid=(pairs,),
        in_specs=[kind_spec(rows, kind) for kind in range(3)]
        + [
            pl.BlockSpec((rows, LANES), lambda p: (0, p)),
            pl.BlockSpec((1, 8, rows), lambda p: (p, 0, 0)),
        ],
        out_specs=pl.BlockSpec((rows, 3 * LANES), lambda p: (0, p)),
        out_shape=jax.ShapeDtypeStruct((rows, width), BF),
        scratch_shapes=[pltpu.VMEM((rows, LANES), F32)] * 2,
        compiler_params=pltpu.CompilerParams(vmem_limit_bytes=48 * 2**20),
        name="attend_back",
    )(heads, heads, heads, grad_blended, log_total)


def dot_nn(left, right):
    return lax.dot_general(left, right, (((1,), (0,)), ((), ())), preferred_element_type=F32)


def dot_nt(left, right):
    return lax.dot_general(left, right, (((1,), (1,)), ((), ())), preferred_element_type=F32)


def dot_tn(left, right):
    return lax.dot_general(left, right, (((0,), (0,)), ((), ())), preferred_element_type=F32)


def local_image(
    tokens,
    cotangent,
    qkv_weight,
    qkv_first,
    qkv_second,
    out_weight,
    out_first,
    out_second,
    up_weight,
    up_first,
    up_second,
    down_weight,
    down_first,
    down_second,
    head_biases,
    bias_first,
    bias_second,
    vectors,
    vector_first,
    vector_second,
):
    dp_at = lax.axis_index("dp")
    mp_at = lax.axis_index("mp")
    units = up_weight.shape[1]
    half_units = units // 2
    block_width = qkv_weight.shape[2]
    depth = qkv_weight.shape[1]
    bias_width = head_biases.shape[1]
    chunk_rows, width = tokens.shape[2:]
    order = [((zk * YS) + yk) for yk in range(YS) for zk in range(ZS)]
    place = jnp.stack([dp_at ^ each for each in order] + [mp_at]).astype(jnp.int32)
    cores = (0, 1)

    def fetch_image(array):
        chunks = array[:, 0]

        def chunk(step):
            return lax.dynamic_index_in_dim(chunks, mp_at ^ step, 0, keepdims=False)

        return Chain(image_steps, jnp.stack([chunk(2), chunk(3)]), lambda: chunk(1))

    def send_back(low):
        chunks = low.reshape(MP, chunk_rows, width)
        return Chain(image_steps, chunks[2:], lambda: chunks[1])

    small_shard = jnp.concatenate(
        [vectors.astype(BF).reshape(-1), head_biases.astype(BF).reshape(-1)]
    ).reshape(1, -1)
    vector_size = vectors.size
    kinds = qkv_weight.shape[0]
    qkv_shard = qkv_weight.astype(BF).reshape(kinds, depth, 2, LANES).transpose(1, 2, 0, 3)
    qkv_shard = qkv_shard.reshape(depth, -1)
    up_low = up_weight.astype(BF)
    up_shards = [
        jnp.concatenate([out_weight.T.astype(BF), up_low[:, :half_units].reshape(depth, -1)], 1),
        up_low[:, half_units:].reshape(depth, -1),
    ]
    down_low = down_weight.transpose(2, 0, 1).astype(BF)
    down_shards = [
        down_low[:, at : at + half_units].reshape(depth, -1) for at in (0, half_units)
    ]
    both = ("xy", "yx")
    small = Chain(small_steps, small_shard, vector_size)
    rows_qkv = Chain(rows_z_steps, qkv_shard)
    rows_up = [Chain(rows_z_steps, each) for each in up_shards]
    tokens = meet(tokens, small, rows_qkv)
    fetch_tokens = fetch_image(tokens)
    meet((), small)
    meet((), small, rows_qkv, *rows_up)
    part_a, part_b = jnp.split(rows_qkv.result, 2, 1)
    get_qkv = [Chain(gather_steps, [part_a], ("xy",)), Chain(gather_steps, [part_b], ("yx",))]
    meet((), small, get_qkv[1], fetch_tokens)
    tokens = meet(tokens, fetch_tokens, get_qkv[0], rows_up[0])

    vector_full, bias_small = small.result
    vector_full = vector_full.reshape(DP, vectors.shape[0], LANES).transpose(1, 0, 2)
    vector_full = vector_full.reshape(vectors.shape[0], width).astype(F32)
    back_places = jnp.stack([((each ^ dp_at) & 1) * ZS + ((each ^ dp_at) >> 1) for each in range(DP)])
    bias_rows = jnp.take(bias_small, back_places, axis=1).reshape(2, 2, DP, -1, bias_width)
    bias_full = bias_rows.transpose(1, 3, 0, 2, 4).reshape(2, head_biases.shape[0], 2, block_width)
    bias_full = bias_full.astype(F32)

    base, normed_one = assemble_image(place, vector_full, tokens[:, 0], fetch_tokens.result, True)
    normed_one = meet(normed_one, *get_qkv, rows_up[1])
    out_rows, up_rows = jnp.split(rows_up[0].result, [block_width], 1)
    get_out = Chain(gather_steps, [jnp.stack(jnp.split(out_rows, 2, 1))], ("yx",))
    get_up = Chain(gather_steps, [up_rows, rows_up[1].result], both, (1, 2))

    def project(core, half, weight):
        lanes = slice(half * LANES, (half + 1) * LANES)
        zero = jnp.zeros((2, LANES), F32)
        bias = jnp.stack([bias_full[core, 0, :, lanes], zero, bias_full[core, 1, :, lanes]], 1)
        return (dot_nn(normed_one, weight) + bias.reshape(-1)).astype(BF)

    heads, blended, log_total = ([[None, None], [None, None]] for _ in range(3))

    def forward_heads(core, half):
        blended[core][half], log_total[core][half] = attend(heads[core][half])

    heads[0][0] = project(0, 0, get_qkv[0].own[0])
    heads[0][0], down_shards = meet((heads[0][0], down_shards), *get_qkv)
    w_qkv = [[each.own[0] for each in get_qkv], [each.result[0] for each in get_qkv]]
    rows_down = [Chain(rows_z_steps, each) for each in down_shards]
    forward_heads(0, 0)
    blended[0][0], normed_one = meet(
        (blended[0][0], normed_one), get_out, get_up, *rows_down
    )
    heads[0][1] = project(0, 1, w_qkv[0][1])
    forward_heads(0, 1)
    blended[0][1], normed_one = meet(
        (blended[0][1], normed_one), get_up, rows_down[0]
    )
    heads[1][0] = project(1, 0, w_qkv[1][0])
    forward_heads(1, 0)
    blended[1][0], normed_one = meet(
        (blended[1][0], normed_one), get_out, rows_down[1], get_up
    )
    get_down = Chain(gather_steps, [each.result for each in rows_down], both)
    heads[1][1] = project(1, 1, w_qkv[1][1])
    forward_heads(1, 1)
    blended = meet(blended, get_up, get_down, get_out)
    w_out = [[each[0][half] for half in (0, 1)] for each in (get_out.own, get_out.result)]
    pairs = [(core, half) for core in cores for half in (0, 1)]
    branch_one, hidden, normed_two = row_call(
        out_kernel,
        "out_norm",
        [blended[core][half] for core, half in pairs],
        [w_out[core][half] for core, half in pairs],
        vector_full,
        [base],
        [F32, F32, BF],
    )
    activ, slope = ({}, {})

    def expand_units(core, weights):
        for half in (0, 1):
            rows = bias_full[core, 2 + half * half_units : 2 + (half + 1) * half_units]
            unit_bias = rows.transpose(1, 0, 2).reshape(-1)
            activ[half, core], slope[half, core] = expand(normed_two, weights[half], unit_bias)

    w_up = [get_up.own, get_up.result]
    expand_units(0, w_up[0])
    activ, normed_two, cotangent = meet((activ, normed_two, cotangent), get_down)
    fetch_cotangent = fetch_image(cotangent)
    expand_units(1, w_up[1])
    activ = meet(activ, get_down)
    w_down = [get_down.own, get_down.result]
    parts = [(half, core) for core in (1, 0) for half in (0, 1)]
    output, branch_two = row_call(
        down_kernel,
        "down_output",
        [activ[each] for each in parts],
        [w_down[core][half] for half, core in parts],
        vector_full,
        [hidden],
        [BF, F32],
    )
    output = meet(output, fetch_cotangent)
    output, cotangent = meet((output, cotangent), fetch_cotangent)
    grad_out, grad_branch = assemble_image(
        place, vector_full, cotangent[:, 0], fetch_cotangent.result, False
    )

    def reduce_pairs(left, rights, pieces):
        chain = Chain(reduce_steps, [dot_tn(left, rights[half, 1]).astype(BF) for half in (0, 1)], both[::-1], pieces)
        chain.own = [dot_tn(left, rights[half, 0]).astype(BF) for half in (0, 1)]
        return chain

    sum_down = reduce_pairs(grad_branch, activ, (2, 1))
    grad_branch, output, slope = meet((grad_branch, output, slope), sum_down)
    send_output = send_back(output)
    grad_pre, unit_sums = ({}, {})
    for half, core in parts:
        grad_pre[half, core], unit_sums[half, core] = slope_product(
            grad_branch, w_down[core][half], slope[half, core]
        )
        if (half, core) == (0, 0):
            grad_pre, grad_branch = meet((grad_pre, grad_branch), sum_down)
    grad_pre, normed_two = meet((grad_pre, normed_two))
    sum_up = reduce_pairs(normed_two, grad_pre, (1, 1))
    grad_pre = meet(grad_pre, sum_down)
    grad_hidden, grad_projected, sums_one = row_call(
        up_back_kernel,
        "up_norm_back",
        [grad_pre[each] for each in parts],
        [w_up[core][half] for half, core in parts],
        vector_full,
        [hidden, branch_one, grad_out],
        [F32, BF, "sums"],
    )
    grad_projected = meet(grad_projected, sum_up, sum_down, send_output)
    rows_down = Chain(sum_z_halves_steps, jnp.concatenate(sum_down.result, 1))
    grad_w_out = [
        jnp.stack([dot_tn(grad_projected, each).astype(BF) for each in blended[core]]) for core in cores
    ]
    sum_out = Chain(reduce_steps, [grad_w_out[1]], ("xy",))
    sum_out.own = [grad_w_out[0]]
    grad_blended = [[dot_nn(grad_projected, each).astype(BF) for each in w_out[core]] for core in cores]
    grad_heads = [[None, None], [None, None]]

    def back_heads(core, half):
        grad_heads[core][half] = attend_back(
            heads[core][half], grad_blended[core][half], log_total[core][half]
        )
        return dot_tn(normed_one, grad_heads[core][half]).astype(BF)

    other = back_heads(1, 0)
    other, grad_blended = meet((other, grad_blended), sum_up, sum_out, rows_down, send_output)
    sum_qkv = [Chain(reduce_steps, [other], ("xy",)), None]
    sum_qkv[0].own = [back_heads(0, 0)]
    grad_heads[0][0], grad_blended = meet(
        (grad_heads[0][0], grad_blended), sum_qkv[0], sum_out, sum_up, rows_down
    )
    rows_up = Chain(sum_z_halves_steps, jnp.concatenate(sum_up.result, 1))
    other = back_heads(1, 1)
    other, grad_blended = meet((other, grad_blended), sum_out, sum_qkv[0])
    sum_qkv[1] = Chain(reduce_steps, [other], ("yx",))
    out_rows = jnp.concatenate([sum_out.result[0][0], sum_out.result[0][1]], 1)
    sum_qkv[1].own = [back_heads(0, 1)]
    grad_heads = meet(grad_heads, sum_qkv[0], sum_qkv[1], rows_up)

    def input_back(span, outs):
        return row_call(
            in_back_kernel,
            "in_norm_back",
            [grad_heads[core][half] for core, half in pairs],
            [w_qkv[core][half] for core, half in pairs],
            vector_full,
            [base, grad_hidden],
            outs,
            span,
            chunk_rows,
        )

    grad_far, sums_far = input_back((1, 1), [BF, "sums"])
    grad_near = []
    send_grad = Chain(
        image_steps, grad_far.reshape(2, chunk_rows, width), lambda: grad_near[0][chunk_rows:]
    )
    grad_heads = meet(grad_heads, sum_qkv[1])
    near, sums_near, own_grad = input_back((0, 1), [BF, "sums", "own"])
    grad_near.append(near)
    sums_near, own_grad = meet((sums_near, own_grad), sum_qkv[1], send_grad)
    sums_input = sums_far + sums_near

    grad_vectors = jnp.stack(
        [
            sums_input[0],
            sums_input[1],
            sums_one[3] * vector_full[SCALE_ONE],
            sums_one[2],
            sums_one[0],
            sums_one[1],
            jnp.sum(grad_out.astype(F32), 0) * vector_full[SCALE_TWO],
            jnp.sum(grad_out.astype(F32) * branch_two, 0),
        ]
    )
    grad_vectors = grad_vectors.reshape(-1, DP, LANES).transpose(1, 0, 2).reshape(DP, -1)
    bias_parts = []
    for core in cores:
        head_part = [
            jnp.sum(each.astype(F32), 0).reshape(2, kinds, LANES) for each in grad_heads[core]
        ]
        rows = [jnp.concatenate([each[:, kind] for each in head_part], 1) for kind in (0, 2)]
        for half in (0, 1):
            unit_part = unit_sums[half, core][0].reshape(2, half_units, block_width)
            rows += [unit_part[:, at] for at in range(half_units)]
        bias_parts.append(jnp.stack(rows, 1))
    grad_biases = jnp.stack(bias_parts, 1).reshape(MP, -1, DP, bias_width).transpose(0, 2, 1, 3)
    grad_biases = jnp.take(grad_biases, place[:DP], axis=1).reshape(MP, DP, -1)
    sum_small = Chain(small_reduce_steps, grad_vectors, grad_biases)
    rows_qkv = Chain(sum_z_steps, jnp.concatenate(sum_qkv[0].result + sum_qkv[1].result + [out_rows], 1))
    meet((), rows_up)
    meet((), send_grad)
    meet((), rows_qkv)
    for _ in range(4):
        meet((), sum_small)
    layer_output = spread_image(place, output[:chunk_rows], send_output.result, BF)[:, None]
    input_grad = spread_image(place, own_grad, send_grad.result, F32)[:, None]

    small_total = sum_small.result
    vector_grad = small_total[:vector_size].reshape(vectors.shape)
    bias_grad = small_total[vector_size:].reshape(head_biases.shape)
    qkv_size = kinds * block_width
    qkv_grad = rows_qkv.result[:, :qkv_size].reshape(depth, 2, kinds, LANES).transpose(2, 0, 1, 3)
    grads = (
        qkv_grad.reshape(qkv_weight.shape),
        rows_qkv.result[:, qkv_size:].T,
        rows_up.result.reshape(depth, units, block_width),
        rows_down.result.reshape(depth, units, block_width).transpose(1, 2, 0),
        bias_grad,
        vector_grad,
    )
    params = (qkv_weight, out_weight, up_weight, down_weight, head_biases, vectors)
    firsts = (qkv_first, out_first, up_first, down_first, bias_first, vector_first)
    seconds = (qkv_second, out_second, up_second, down_second, bias_second, vector_second)
    results = [layer_output, input_grad]
    for slot in range(6):
        results.extend(
            adam_update(params[slot], firsts[slot], seconds[slot], grads[slot], RATES[slot])
        )
    return tuple(results)


def solution(mesh):
    whole_image = mesh.shape["mp"] == MICRO == MP and mesh.shape["dp"] == DP
    return jax.shard_map(
        local_image if whole_image else local_general,
        mesh=mesh,
        in_specs=(
            P(None, "dp", "mp", None),
            P(None, "dp", "mp", None),
            P(None, "dp", "mp"),
            P(None, "dp", "mp"),
            P(None, "dp", "mp"),
            P("mp", "dp"),
            P("mp", "dp"),
            P("mp", "dp"),
            P("dp", None, "mp"),
            P("dp", None, "mp"),
            P("dp", None, "mp"),
            P(None, "mp", "dp"),
            P(None, "mp", "dp"),
            P(None, "mp", "dp"),
            P(None, ("mp", "dp")),
            P(None, ("mp", "dp")),
            P(None, ("mp", "dp")),
            P(None, "dp"),
            P(None, "dp"),
            P(None, "dp"),
        ),
        out_specs=(
            P(None, "dp", "mp", None),
            P(None, "dp", "mp", None),
            P(None, "dp", "mp"),
            P(None, "dp", "mp"),
            P(None, "dp", "mp"),
            P("mp", "dp"),
            P("mp", "dp"),
            P("mp", "dp"),
            P("dp", None, "mp"),
            P("dp", None, "mp"),
            P("dp", None, "mp"),
            P(None, "mp", "dp"),
            P(None, "mp", "dp"),
            P(None, "mp", "dp"),
            P(None, ("mp", "dp")),
            P(None, ("mp", "dp")),
            P(None, ("mp", "dp")),
            P(None, "dp"),
            P(None, "dp"),
            P(None, "dp"),
        ),
        check_vma=False,
    )
```

```python
import functools

import jax
import jax.numpy as jnp
from jax import lax
from jax.experimental import pallas as pl
from jax.experimental.pallas import tpu as pltpu
from jax.sharding import PartitionSpec as P

DH = 64
MICRO = 4
STEP = 10


RATES = (0.05, 0.2, 0.05, 0.03, 0.5, 0.5)


def layer_norm(values, gain, shift):
    center = values - jnp.mean(values, -1, keepdims=True)
    spread = jnp.mean(center * center, -1, keepdims=True)
    return center * lax.rsqrt(spread + 1e-06) * gain + shift


def exact_gelu(values):
    return jax.nn.gelu(values, approximate=False)


def adam_update(weight, first, second, grad, rate):
    first_new = 0.9 * first + 0.1 * grad
    second_new = 0.999 * second + 0.001 * grad * grad
    corrected = first_new / (1.0 - 0.9**STEP)
    scaled = jnp.sqrt(second_new / (1.0 - 0.999**STEP))
    weight_new = weight - rate * (corrected / (scaled + 1e-08) + 0.05 * weight)
    return (weight_new, first_new, second_new)


def attend_forward(queries, key_rows, values, block_rows):
    images, seq_rows, head_count, head_width = queries.shape
    block_count = seq_rows // block_rows
    factor = head_width ** (-0.5)
    query_blocks = jnp.moveaxis(
        queries.reshape(images, block_count, block_rows, head_count, head_width), 1, 0
    )

    def one_block(query_part):
        scores = (
            jnp.einsum("iqhe,ikhe->ihqk", query_part, key_rows, preferred_element_type=jnp.float32)
            * factor
        )
        row_peak = jnp.max(scores, -1, keepdims=True)
        shifted = jnp.exp(scores - row_peak)
        row_total = jnp.sum(shifted, -1, keepdims=True)
        softmax_rows = (shifted / row_total).astype(jnp.bfloat16)
        blended = jnp.einsum(
            "ihqk,ikhe->iqhe", softmax_rows, values, preferred_element_type=jnp.float32
        )
        return (blended, row_peak[..., 0] + jnp.log(row_total[..., 0]))

    blended, log_total = lax.map(one_block, query_blocks)
    blended = jnp.moveaxis(blended, 0, 1).reshape(images, seq_rows, head_count * head_width)
    return (blended.astype(jnp.bfloat16), log_total)


def attend_backward(queries, key_rows, values, grad_blended, log_total, block_rows):
    images, seq_rows, head_count, head_width = queries.shape
    block_count = seq_rows // block_rows
    factor = head_width ** (-0.5)
    split_shape = (images, block_count, block_rows, head_count, head_width)
    query_blocks = jnp.moveaxis(queries.reshape(split_shape), 1, 0)
    grad_blocks = jnp.moveaxis(grad_blended.reshape(split_shape), 1, 0)

    def one_block(carry, inputs_part):
        query_part, grad_part, total_part = inputs_part
        grad_keys, grad_values = carry
        scores = (
            jnp.einsum("iqhe,ikhe->ihqk", query_part, key_rows, preferred_element_type=jnp.float32)
            * factor
        )
        softmax_rows = jnp.exp(scores - total_part[..., None])
        grad_values = grad_values + jnp.einsum(
            "ihqk,iqhe->ikhe",
            softmax_rows.astype(jnp.bfloat16),
            grad_part,
            preferred_element_type=jnp.float32,
        )
        grad_rows = jnp.einsum(
            "iqhe,ikhe->ihqk", grad_part, values, preferred_element_type=jnp.float32
        )
        grad_scores = softmax_rows * (
            grad_rows - jnp.sum(grad_rows * softmax_rows, -1, keepdims=True)
        )
        grad_scores = grad_scores.astype(jnp.bfloat16)
        grad_query = (
            jnp.einsum("ihqk,ikhe->iqhe", grad_scores, key_rows, preferred_element_type=jnp.float32)
            * factor
        )
        grad_keys = (
            grad_keys
            + jnp.einsum(
                "ihqk,iqhe->ikhe", grad_scores, query_part, preferred_element_type=jnp.float32
            )
            * factor
        )
        return ((grad_keys, grad_values), grad_query)

    zero_grad = jnp.zeros(queries.shape, jnp.float32)
    (grad_keys, grad_values), grad_query = lax.scan(
        one_block, (zero_grad, zero_grad), (query_blocks, grad_blocks, log_total)
    )
    flat_shape = (images, seq_rows, head_count * head_width)
    grad_query = jnp.moveaxis(grad_query, 0, 1).reshape(flat_shape)
    stacked = jnp.stack(
        [grad_query, grad_keys.reshape(flat_shape), grad_values.reshape(flat_shape)]
    )
    return stacked.astype(jnp.bfloat16)


def rows_forward(part):
    return lax.all_gather(part, "mp", axis=1, tiled=True)


def rows_sum_forward(part):
    return lax.psum_scatter(part, "mp", scatter_dimension=1, tiled=True)


def rows_backward(part):
    return lax.all_gather(part, "mp", axis=1, tiled=True)


def rows_sum_backward(part):
    return lax.psum_scatter(part, "mp", scatter_dimension=1, tiled=True)


def forward(inputs, params):
    qkv_full, out_full, up_full, down_full, bias_full, vector_full = params
    base = inputs.astype(jnp.float32)
    normed = layer_norm(base, vector_full[0], vector_full[1]).astype(jnp.bfloat16)
    normed_all = rows_forward(normed)
    images, seq_rows = (normed_all.shape[0], normed_all.shape[1])
    head_shape = (images, seq_rows, -1, DH)
    project = jnp.einsum("isd,tde->tise", normed_all, qkv_full, preferred_element_type=jnp.float32)
    queries = (project[0] + bias_full[0]).astype(jnp.bfloat16).reshape(head_shape)
    key_rows = project[1].astype(jnp.bfloat16).reshape(head_shape)
    values = (project[2] + bias_full[1]).astype(jnp.bfloat16).reshape(head_shape)
    blended, log_total = attend_forward(queries, key_rows, values, min(512, seq_rows))
    projected = rows_sum_forward(
        jnp.einsum("ise,ed->isd", blended, out_full, preferred_element_type=jnp.float32)
    )
    branch_one = projected + vector_full[2]
    hidden = base + vector_full[3] * branch_one
    normed_two = layer_norm(hidden, vector_full[4], vector_full[5]).astype(jnp.bfloat16)
    normed_two_all = rows_forward(normed_two)
    pre_act = jnp.einsum(
        "isd,df->isf", normed_two_all, up_full, preferred_element_type=jnp.float32
    ) + bias_full[2:].reshape(-1)
    activ = exact_gelu(pre_act).astype(jnp.bfloat16)
    branch_two = (
        rows_sum_forward(
            jnp.einsum("isf,fd->isd", activ, down_full, preferred_element_type=jnp.float32)
        )
        + vector_full[6]
    )
    output = hidden + vector_full[7] * branch_two
    saved = (
        base,
        hidden,
        branch_one,
        branch_two,
        normed_all,
        queries,
        key_rows,
        values,
        log_total,
        blended,
        normed_two_all,
        pre_act,
        activ,
    )
    return (output.astype(jnp.bfloat16), saved)


def backward(grad_output, saved, params):
    qkv_full, out_full, up_full, down_full, bias_full, vector_full = params
    (
        base,
        hidden,
        branch_one,
        branch_two,
        normed_all,
        queries,
        key_rows,
        values,
        log_total,
        blended,
        normed_two_all,
        pre_act,
        activ,
    ) = saved
    local_width = qkv_full.shape[2]
    grad_out = grad_output.astype(jnp.float32)
    grad_scale_two = jnp.sum(grad_out * branch_two, axis=(0, 1))
    grad_bias_two = jnp.sum(grad_out, axis=(0, 1)) * vector_full[7]
    grad_branch = rows_backward((grad_out * vector_full[7]).astype(jnp.bfloat16))
    grad_down = jnp.einsum("isf,isd->fd", activ, grad_branch, preferred_element_type=jnp.float32)
    grad_activ = jnp.einsum(
        "isd,fd->isf", grad_branch, down_full, preferred_element_type=jnp.float32
    )
    grad_pre = jax.vjp(exact_gelu, pre_act)[1](grad_activ)[0].astype(jnp.bfloat16)
    grad_up_bias = jnp.sum(grad_pre, axis=(0, 1), dtype=jnp.float32)
    grad_up = jnp.einsum(
        "isd,isf->df", normed_two_all, grad_pre, preferred_element_type=jnp.float32
    )
    grad_normed_two = rows_sum_backward(
        jnp.einsum("isf,df->isd", grad_pre, up_full, preferred_element_type=jnp.float32)
    )
    norm_back_two = jax.vjp(layer_norm, hidden, vector_full[4], vector_full[5])[1]
    grad_hidden, grad_gain_two, grad_shift_two = norm_back_two(grad_normed_two)
    grad_hidden = grad_out + grad_hidden
    grad_scale_one = jnp.sum(grad_hidden * branch_one, axis=(0, 1))
    grad_out_bias = jnp.sum(grad_hidden, axis=(0, 1)) * vector_full[3]
    grad_projected = rows_backward((grad_hidden * vector_full[3]).astype(jnp.bfloat16))
    grad_out_weight = jnp.einsum(
        "ise,isd->ed", blended, grad_projected, preferred_element_type=jnp.float32
    )
    grad_blended = jnp.einsum(
        "isd,ed->ise", grad_projected, out_full, preferred_element_type=jnp.float32
    ).astype(jnp.bfloat16)
    grad_project = attend_backward(
        queries, key_rows, values, grad_blended, log_total, min(512, queries.shape[1])
    )
    grad_query_bias = jnp.sum(grad_project[0], axis=(0, 1), dtype=jnp.float32)
    grad_value_bias = jnp.sum(grad_project[2], axis=(0, 1), dtype=jnp.float32)
    grad_qkv = jnp.einsum(
        "isd,tise->tde", normed_all, grad_project, preferred_element_type=jnp.float32
    )
    grad_normed = rows_sum_backward(
        jnp.einsum("tise,tde->isd", grad_project, qkv_full, preferred_element_type=jnp.float32)
    )
    norm_back_one = jax.vjp(layer_norm, base, vector_full[0], vector_full[1])[1]
    grad_input_part, grad_gain_one, grad_shift_one = norm_back_one(grad_normed)
    grad_input = grad_hidden + grad_input_part
    grad_vectors = jnp.stack(
        [
            grad_gain_one,
            grad_shift_one,
            grad_out_bias,
            grad_scale_one,
            grad_gain_two,
            grad_shift_two,
            grad_bias_two,
            grad_scale_two,
        ]
    )
    grad_biases = jnp.concatenate(
        [jnp.stack([grad_query_bias, grad_value_bias]), grad_up_bias.reshape(-1, local_width)], 0
    )
    return (grad_input, (grad_qkv, grad_out_weight, grad_up, grad_down, grad_biases, grad_vectors))


def local_general(
    tokens,
    cotangent,
    qkv_weight,
    qkv_first,
    qkv_second,
    out_weight,
    out_first,
    out_second,
    up_weight,
    up_first,
    up_second,
    down_weight,
    down_first,
    down_second,
    head_biases,
    bias_first,
    bias_second,
    vectors,
    vector_first,
    vector_second,
):

    def gather_params():
        gathered = (
            lax.all_gather(qkv_weight.astype(jnp.bfloat16), "dp", axis=1, tiled=True),
            lax.all_gather(out_weight.astype(jnp.bfloat16), "dp", axis=1, tiled=True),
            lax.all_gather(up_weight.astype(jnp.bfloat16), "dp", axis=0, tiled=True),
            lax.all_gather(down_weight.astype(jnp.bfloat16), "dp", axis=2, tiled=True),
            lax.all_gather(head_biases.astype(jnp.bfloat16), "dp", axis=1, tiled=True),
            lax.all_gather(vectors.astype(jnp.bfloat16), "dp", axis=1, tiled=True),
        )
        qkv_full, out_full, up_full, down_full, bias_full, vector_full = gathered
        return (
            qkv_full,
            out_full,
            up_full.reshape(up_full.shape[0], -1),
            down_full.reshape(-1, down_full.shape[2]),
            bias_full.astype(jnp.float32),
            vector_full.astype(jnp.float32),
        )

    grad_sums = None
    outputs = []
    input_grads = []
    for micro_step in range(MICRO):
        params_fwd = gather_params()
        output, saved = forward(tokens[micro_step], params_fwd)
        outputs.append(output)
        params_back = gather_params()
        grad_input, grads = backward(cotangent[micro_step], saved, params_back)
        input_grads.append(grad_input)
        if grad_sums is None:
            grad_sums = grads
        else:
            grad_sums = tuple((old_sum + new_part for old_sum, new_part in zip(grad_sums, grads)))
    grad_qkv, grad_out_weight, grad_up, grad_down, grad_biases, grad_vectors = grad_sums
    grad_up = grad_up.reshape(-1, up_weight.shape[1], up_weight.shape[2])
    grad_down = grad_down.reshape(down_weight.shape[0], down_weight.shape[1], -1)
    reduced = (
        lax.psum_scatter(grad_qkv, "dp", scatter_dimension=1, tiled=True),
        lax.psum_scatter(grad_out_weight, "dp", scatter_dimension=1, tiled=True),
        lax.psum_scatter(grad_up, "dp", scatter_dimension=0, tiled=True),
        lax.psum_scatter(grad_down, "dp", scatter_dimension=2, tiled=True),
        lax.psum_scatter(grad_biases, "dp", scatter_dimension=1, tiled=True),
        lax.psum_scatter(grad_vectors, "dp", scatter_dimension=1, tiled=True),
    )
    vector_grad = lax.psum(reduced[5], "mp")
    grads = (reduced[0], reduced[1], reduced[2], reduced[3], reduced[4], vector_grad)
    params = (qkv_weight, out_weight, up_weight, down_weight, head_biases, vectors)
    firsts = (qkv_first, out_first, up_first, down_first, bias_first, vector_first)
    seconds = (qkv_second, out_second, up_second, down_second, bias_second, vector_second)
    updated = [
        adam_update(params[slot], firsts[slot], seconds[slot], grads[slot], RATES[slot])
        for slot in range(6)
    ]
    return (
        jnp.stack(outputs),
        jnp.stack(input_grads),
        updated[0][0],
        updated[0][1],
        updated[0][2],
        updated[1][0],
        updated[1][1],
        updated[1][2],
        updated[2][0],
        updated[2][1],
        updated[2][2],
        updated[3][0],
        updated[3][1],
        updated[3][2],
        updated[4][0],
        updated[4][1],
        updated[4][2],
        updated[5][0],
        updated[5][1],
        updated[5][2],
    )


ZS, YS, MP = (4, 2, 4)
DP = ZS * YS
LANES = 128
BF = jnp.bfloat16
F32 = jnp.float32


def swap_z(part, step):
    return lax.ppermute(
        part, "dp", [(z * YS + y, (z ^ step) * YS + y) for z in range(ZS) for y in range(YS)]
    )


def swap_y(part):
    return lax.ppermute(part, "dp", [(each, each ^ 1) for each in range(DP)])


def swap_mp(part, step):
    return lax.ppermute(part, "mp", [(each, each ^ step) for each in range(MP)])


class Chain:
    def __init__(self, steps, *args):
        self.own = None
        self.result = None
        self.steps = steps(self, *args)
        self.flight = next(self.steps)

    def land(self, arrived):
        try:
            self.flight = self.steps.send(arrived)
        except StopIteration as end:
            self.flight = None
            self.result = end.value


def meet(values, *chains):
    values, flights = lax.optimization_barrier((values, [each.flight for each in chains]))
    for each, flight in zip(chains, flights):
        each.land(flight)
    return values


def join(rows, arrived, axis):
    return jnp.concatenate([rows, arrived], -2 if axis == "y" else -1)


def swap_plane(part, axis):
    return swap_y(part) if axis == "y" else swap_mp(part, 2)


def rows_z_steps(chain, shard):
    rows = shard
    for step in (1, 2):
        (arrived,) = yield [swap_z(rows, step)]
        rows = jnp.concatenate([rows, arrived], 0)
    return rows


def cut(part, axis, pieces):
    return jnp.split(part, pieces, -2 if axis == "y" else -1) if pieces > 1 else [part]


def gather_steps(chain, parts, orders, pieces=(1, 1)):
    for axes, count in zip(zip(*orders), pieces):
        sent = [cut(part, axis, count) for part, axis in zip(parts, axes)]
        for at in range(count):
            arrived = yield [swap_plane(each[at], axis) for each, axis in zip(sent, axes)]
            parts = [join(part, each, axis) for part, each, axis in zip(parts, arrived, axes)]
    chain.own = parts
    arrived = yield [swap_mp(part, 1) for part in parts]
    return arrived


def add_low(first, second):
    return (first.astype(F32) + second.astype(F32)).astype(BF)


def halve(total, axis):
    rows, width = total.shape[-2:]
    if axis == "y":
        return (total[..., : rows // 2, :], total[..., rows // 2 :, :])
    return (total[..., : width // 2], total[..., width // 2 :])


def reduce_steps(chain, other_parts, orders, pieces=(1, 1)):
    arrived = yield [swap_mp(part, 1) for part in other_parts]
    totals = [add_low(own, each) for own, each in zip(chain.own, arrived)]
    for axes, count in zip(zip(*orders), pieces):
        halves = [halve(total, axis) for total, axis in zip(totals, axes)]
        sent = [cut(half[1], axis, count) for half, axis in zip(halves, axes)]
        received = []
        for at in range(count):
            received.append((yield [swap_plane(each[at], axis) for each, axis in zip(sent, axes)]))
        totals = []
        for half, axis, each in zip(halves, axes, zip(*received)):
            whole = each[0] if count == 1 else jnp.concatenate(each, -2 if axis == "y" else -1)
            totals.append(add_low(half[0], whole))
    return totals


def sum_z_steps(chain, total):
    rows = total.shape[0] // ZS
    arrived = yield [swap_z(total[step * rows : (step + 1) * rows], step) for step in range(1, ZS)]
    total = total[:rows].astype(F32)
    for each in arrived:
        total = total + each.astype(F32)
    return total


def sum_z_halves_steps(chain, total):
    half = total.shape[0] // 2
    (arrived,) = yield [swap_z(total[half:], 2)]
    total = add_low(total[:half], arrived)
    (arrived,) = yield [swap_z(total[half // 2 :], 1)]
    return total[: half // 2].astype(F32) + arrived.astype(F32)


def image_steps(chain, far, near):
    (arrived,) = yield [swap_mp(far, 2)]
    second, passing = arrived
    (arrived,) = yield [swap_mp(jnp.stack([near(), passing]), 1)]
    return [arrived[0], second, arrived[1]]


def small_steps(chain, shard, vector_size):
    biases = shard[:, vector_size:]
    arrived = yield [swap_mp(biases, step) for step in range(1, MP)]
    rows = jnp.concatenate([shard] + arrived, 1)
    for step in (1, 2):
        arrived = yield [swap_z(rows, step)]
        rows = jnp.concatenate([rows] + arrived, 0)
    arrived = yield [swap_y(rows)]
    rows = jnp.concatenate([rows] + arrived, 0)
    biases = rows[:, vector_size:].reshape(DP, MP, -1).transpose(1, 0, 2)
    return (rows[:, :vector_size], biases)


def small_reduce_steps(chain, vector_part, bias_part):
    near = jnp.concatenate([vector_part, bias_part[0], bias_part[2]], 1)
    far = jnp.concatenate([vector_part, bias_part[1], bias_part[3]], 1)
    (arrived,) = yield [swap_mp(far, 1)]
    total = near + arrived
    kept = vector_part.shape[1] + bias_part.shape[2]
    far = jnp.concatenate([total[:, : vector_part.shape[1]], total[:, kept:]], 1)
    (arrived,) = yield [swap_mp(far, 2)]
    total = total[:, :kept] + arrived
    arrived = yield [swap_y(total[ZS:])]
    total = total[:ZS] + arrived[0]
    arrived = yield [swap_z(total[step], step) for step in range(1, ZS)]
    total = total[0]
    for each in arrived:
        total = total + each
    return total


def norm_parts(values):
    center = values - jnp.mean(values, -1, keepdims=True)
    spread = lax.rsqrt(jnp.mean(center * center, -1, keepdims=True) + 1e-06)
    return (center * spread, spread)


def norm_back(grad, normal, spread, gain):
    scaled = grad * gain
    inner = scaled - jnp.mean(scaled, -1, keepdims=True)
    return spread * (inner - normal * jnp.mean(scaled * normal, -1, keepdims=True))


GAIN_ONE, SHIFT_ONE, OUT_BIAS, SCALE_ONE, GAIN_TWO, SHIFT_TWO, DOWN_BIAS, SCALE_TWO = range(8)


def vector_row(vector_ref, at):
    return vector_ref[at : at + 1, :]


def assemble_kernel(with_norm, place_ref, vector_ref, own_ref, *refs):
    out_ref, second_ref = refs[-2:]
    part_refs = [own_ref.at[0]] + list(refs[:-2])
    for at, part_ref in enumerate(part_refs):
        for block in range(DP):
            lanes = pl.ds(pl.multiple_of(place_ref[block] * LANES, LANES), LANES)
            out_ref[at, :, block * LANES : (block + 1) * LANES] = part_ref[:, lanes]
        values = out_ref[at].astype(F32)
        if with_norm:
            normal, _ = norm_parts(values)
            values = normal * vector_row(vector_ref, GAIN_ONE) + vector_row(vector_ref, SHIFT_ONE)
        else:
            values = values * vector_row(vector_ref, SCALE_TWO)
        second_ref[at] = values.astype(BF)


def assemble_image(place, vector_full, arrays, parts, with_norm):
    chunk_rows, width = parts[0].shape
    rows = chunk_rows // 4
    block = pl.BlockSpec((rows, width), lambda i, place_ref: (i, 0))
    result = pl.BlockSpec((MP, rows, width), lambda i, place_ref: (0, i, 0))
    shape = jax.ShapeDtypeStruct((MP, chunk_rows, width), BF)
    image, second = pl.pallas_call(
        functools.partial(assemble_kernel, with_norm),
        grid_spec=pltpu.PrefetchScalarGridSpec(
            num_scalar_prefetch=1,
            grid=(4,),
            in_specs=[
                pl.BlockSpec(vector_full.shape, lambda i, place_ref: (0, 0)),
                pl.BlockSpec((1, rows, width), lambda i, place_ref: (place_ref[DP], i, 0)),
            ]
            + [block] * len(parts),
            out_specs=[result] * 2,
        ),
        out_shape=[shape] * 2,
        compiler_params=pltpu.CompilerParams(vmem_limit_bytes=32 * 2**20),
        name="assemble_image",
    )(place, vector_full, arrays, *parts)
    return (image.reshape(-1, width), second.reshape(-1, width))


def spread_kernel(place_ref, own_ref, *refs):
    out_ref = refs[-1]
    mine = place_ref[DP]
    for at, part_ref in enumerate([own_ref] + list(refs[:-1])):
        for block in range(DP):
            lanes = pl.ds(pl.multiple_of(place_ref[block] * LANES, LANES), LANES)
            part = part_ref[:, block * LANES : (block + 1) * LANES]
            out_ref[mine ^ at, :, lanes] = part.astype(out_ref.dtype)


def spread_image(place, own, parts, dtype):
    chunk_rows, width = parts[0].shape
    rows = chunk_rows // 4
    block = pl.BlockSpec((rows, width), lambda i, place_ref: (i, 0))
    return pl.pallas_call(
        spread_kernel,
        grid_spec=pltpu.PrefetchScalarGridSpec(
            num_scalar_prefetch=1,
            grid=(4,),
            in_specs=[block] * (1 + len(parts)),
            out_specs=pl.BlockSpec((MP, rows, width), lambda i, place_ref: (0, i, 0)),
        ),
        out_shape=jax.ShapeDtypeStruct((MP, chunk_rows, width), dtype),
        compiler_params=pltpu.CompilerParams(vmem_limit_bytes=32 * 2**20),
        name="spread_image",
    )(place, own, *parts)


ROWS = 512


def product_nt(left_refs, right_refs):
    total = None
    for left_ref, right_ref in zip(left_refs, right_refs):
        part = lax.dot_general(
            left_ref[...], right_ref[...], (((1,), (1,)), ((), ())), preferred_element_type=F32
        )
        total = part if total is None else total + part
    return total


def add_rows(sums_ref, rows):
    @pl.when(pl.program_id(0) == 0)
    def _():
        sums_ref[...] = jnp.zeros_like(sums_ref)

    for at, each in enumerate(rows):
        sums_ref[at : at + 1, :] += jnp.sum(each, 0, keepdims=True)


def out_kernel(count, *refs):
    lefts, rights = (refs[:count], refs[count : 2 * count])
    vector_ref, base_ref, branch_ref, hidden_ref, normed_ref = refs[2 * count :]
    branch = product_nt(lefts, rights) + vector_row(vector_ref, OUT_BIAS)
    hidden = base_ref[...].astype(F32) + vector_row(vector_ref, SCALE_ONE) * branch
    normal, _ = norm_parts(hidden)
    branch_ref[...] = branch
    hidden_ref[...] = hidden
    normed = normal * vector_row(vector_ref, GAIN_TWO) + vector_row(vector_ref, SHIFT_TWO)
    normed_ref[...] = normed.astype(BF)


def down_kernel(count, *refs):
    lefts, rights = (refs[:count], refs[count : 2 * count])
    vector_ref, hidden_ref, output_ref, branch_ref = refs[2 * count :]
    branch = product_nt(lefts, rights) + vector_row(vector_ref, DOWN_BIAS)
    output = hidden_ref[...] + vector_row(vector_ref, SCALE_TWO) * branch
    output_ref[...] = output.astype(BF)
    branch_ref[...] = branch


def up_back_kernel(count, *refs):
    lefts, rights = (refs[:count], refs[count : 2 * count])
    vector_ref, hidden_ref, branch_ref, grad_ref, out_ref, low_ref, sums_ref = refs[2 * count :]
    grad_normed = product_nt(lefts, rights)
    normal, spread = norm_parts(hidden_ref[...])
    grad = norm_back(grad_normed, normal, spread, vector_row(vector_ref, GAIN_TWO))
    grad = grad + grad_ref[...].astype(F32)
    out_ref[...] = grad
    low_ref[...] = (grad * vector_row(vector_ref, SCALE_ONE)).astype(BF)
    add_rows(sums_ref, [grad_normed * normal, grad_normed, grad * branch_ref[...], grad])


def in_back_kernel(count, *refs):
    lefts, rights = (refs[:count], refs[count : 2 * count])
    vector_ref, base_ref, grad_ref, low_ref, sums_ref = refs[2 * count : 2 * count + 5]
    grad_normed = product_nt(lefts, rights)
    normal, spread = norm_parts(base_ref[...].astype(F32))
    grad = norm_back(grad_normed, normal, spread, vector_row(vector_ref, GAIN_ONE))
    grad = grad + grad_ref[...]
    low_ref[...] = grad.astype(BF)

    for own_ref in refs[2 * count + 5 :]:
        own_ref[...] = grad[: own_ref.shape[0]]
    add_rows(sums_ref, [grad_normed * normal, grad_normed])


def expand_kernel(left_ref, right_ref, bias_ref, activ_ref, slope_ref):
    values = jnp.dot(left_ref[...], right_ref[...], preferred_element_type=F32) + bias_ref[0:1, :]
    share = 0.5 * (1.0 + lax.erf(values * 0.7071067811865476))
    activ_ref[...] = (values * share).astype(BF)
    slope = share + values * (0.3989422804014327 * jnp.exp(-0.5 * values * values))
    slope_ref[...] = slope.astype(BF)


def expand(left, right, bias):
    rows, depth = left.shape
    width = right.shape[1]
    block = pl.BlockSpec((256, width), lambda i: (i, 0))
    return pl.pallas_call(
        expand_kernel,
        grid=(rows // 256,),
        in_specs=[
            pl.BlockSpec((256, depth), lambda i: (i, 0)),
            pl.BlockSpec((depth, width), lambda i: (0, 0), pipeline_mode=pl.Buffered(1)),
            pl.BlockSpec((1, width), lambda i: (0, 0)),
        ],
        out_specs=[block] * 2,
        out_shape=[jax.ShapeDtypeStruct((rows, width), BF)] * 2,
        compiler_params=pltpu.CompilerParams(vmem_limit_bytes=32 * 2**20),
        name="expand",
    )(left, right, bias.reshape(1, width))


def slope_kernel(left_ref, right_ref, slope_ref, grad_ref, sums_ref):
    grad = jnp.dot(left_ref[...], right_ref[...], preferred_element_type=F32)
    low = (grad * slope_ref[...].astype(F32)).astype(BF)
    grad_ref[...] = low
    add_rows(sums_ref, [low.astype(F32)])


def slope_product(left, right, slope):
    rows, depth = left.shape
    width = right.shape[1]
    block = pl.BlockSpec((256, width), lambda i: (i, 0))
    return pl.pallas_call(
        slope_kernel,
        grid=(rows // 256,),
        in_specs=[
            pl.BlockSpec((256, depth), lambda i: (i, 0)),
            pl.BlockSpec((depth, width), lambda i: (0, 0), pipeline_mode=pl.Buffered(1)),
            block,
        ],
        out_specs=[block, pl.BlockSpec((8, width), lambda i: (0, 0))],
        out_shape=[jax.ShapeDtypeStruct((rows, width), BF), jax.ShapeDtypeStruct((8, width), F32)],
        compiler_params=pltpu.CompilerParams(vmem_limit_bytes=32 * 2**20),
        name="slope_product",
    )(left, right, slope)


def row_call(kernel, name, lefts, rights, vector_full, row_inputs, outs, span=None, own_rows=0):
    rows, width = row_inputs[0].shape
    first, count = span or (0, rows // ROWS)
    rows = count * ROWS
    once = pl.Buffered(1)
    block = pl.BlockSpec((ROWS, width), lambda i: (i, 0))
    source = pl.BlockSpec((ROWS, width), lambda i: (i + first, 0))
    specs = {
        "sums": (pl.BlockSpec((8, width), lambda i: (0, 0)), jax.ShapeDtypeStruct((8, width), F32)),
        "own": (
            pl.BlockSpec((own_rows, width), lambda i: (0, 0)),
            jax.ShapeDtypeStruct((own_rows, width), F32),
        ),
    }
    pairs = [
        specs[each] if isinstance(each, str) else (block, jax.ShapeDtypeStruct((rows, width), each))
        for each in outs
    ]
    return pl.pallas_call(
        functools.partial(kernel, len(lefts)),
        grid=(count,),
        in_specs=[pl.BlockSpec((ROWS, each.shape[1]), lambda i: (i + first, 0)) for each in lefts]
        + [pl.BlockSpec(each.shape, lambda i: (0, 0), pipeline_mode=once) for each in rights]
        + [pl.BlockSpec(vector_full.shape, lambda i: (0, 0))]
        + [source] * len(row_inputs),
        out_specs=[each[0] for each in pairs],
        out_shape=[each[1] for each in pairs],
        compiler_params=pltpu.CompilerParams(vmem_limit_bytes=48 * 2**20),
        name=name,
    )(*lefts, *rights, vector_full, *row_inputs)


def lane_dot(left, right):
    return lax.dot_general(left, right, (((1,), (1,)), ((), ())), preferred_element_type=F32)


def head_masks(width):
    lane = lax.broadcasted_iota(jnp.int32, (1, width), 1)
    return [lane // DH == head for head in range(width // DH)]


def attend_kernel(block_rows, q_ref, k_ref, v_ref, o_ref, lse_ref):
    masks = head_masks(LANES)
    key_rows = k_ref[...]
    values = v_ref[...]
    zero = jnp.zeros((), BF)
    for block in range(q_ref.shape[0] // block_rows):
        rows = slice(block * block_rows, (block + 1) * block_rows)
        queries = q_ref[rows, :] * jnp.asarray(DH**-0.5, BF)
        blended = []
        for head, mask in enumerate(masks):
            scores = lane_dot(jnp.where(mask, queries, zero), key_rows)
            peak = jnp.max(scores, 1, keepdims=True)
            shifted = jnp.exp(scores - peak)
            total = jnp.sum(shifted, 1, keepdims=True)
            part = jnp.dot(shifted.astype(BF), values, preferred_element_type=F32)
            blended.append(part * (1.0 / total))
            log_total = jnp.broadcast_to(peak + jnp.log(total), (block_rows, LANES))
            lse_ref[0, head : head + 1, rows] = jnp.transpose(log_total)[0:1, :]
        o_ref[rows, :] = jnp.where(masks[0], blended[0], blended[1]).astype(BF)


def attend_back_kernel(
    block_rows, q_ref, k_ref, v_ref, g_ref, lse_ref, out_ref, dk_acc, dv_acc
):
    masks = head_masks(LANES)
    key_rows = k_ref[...]
    values = v_ref[...]
    zero = jnp.zeros((), BF)
    factor = DH**-0.5
    key_heads = [jnp.where(mask, key_rows, zero) for mask in masks]
    for block in range(q_ref.shape[0] // block_rows):
        rows = slice(block * block_rows, (block + 1) * block_rows)
        queries = q_ref[rows, :] * jnp.asarray(factor, BF)
        grads = g_ref[rows, :]
        grad_query = None
        grad_keys = None
        grad_values = None
        for head, mask in enumerate(masks):
            query_head = jnp.where(mask, queries, zero)
            grad_head = jnp.where(mask, grads, zero)
            scores = lane_dot(key_rows, query_head)
            weights = jnp.exp(scores - lse_ref[0, head : head + 1, rows])
            value_part = jnp.dot(weights.astype(BF), grad_head, preferred_element_type=F32)
            grad_rows = lane_dot(values, grad_head)
            delta = jnp.sum(grad_rows * weights, 0, keepdims=True)
            grad_scores = (weights * (grad_rows - delta)).astype(BF)
            key_part = jnp.dot(grad_scores, query_head, preferred_element_type=F32)
            query_part = lax.dot_general(
                grad_scores, key_heads[head], (((0,), (0,)), ((), ())), preferred_element_type=F32
            )
            grad_query = query_part if head == 0 else grad_query + query_part
            grad_keys = key_part if head == 0 else grad_keys + key_part
            grad_values = value_part if head == 0 else grad_values + value_part
        out_ref[rows, 0:LANES] = (grad_query * factor).astype(BF)
        if block == 0:
            dk_acc[...] = grad_keys
            dv_acc[...] = grad_values
        else:
            dk_acc[...] += grad_keys
            dv_acc[...] += grad_values
    out_ref[:, LANES : 2 * LANES] = dk_acc[...].astype(BF)
    out_ref[:, 2 * LANES : 3 * LANES] = dv_acc[...].astype(BF)


def kind_spec(rows, kind):
    return pl.BlockSpec((rows, LANES), lambda p: (0, p * 3 + kind))


def attend(heads):
    rows, width = heads.shape
    pairs = width // LANES // 3
    return pl.pallas_call(
        functools.partial(attend_kernel, 512),
        grid=(pairs,),
        in_specs=[kind_spec(rows, kind) for kind in range(3)],
        out_specs=[
            pl.BlockSpec((rows, LANES), lambda p: (0, p)),
            pl.BlockSpec((1, 8, rows), lambda p: (p, 0, 0)),
        ],
        out_shape=[
            jax.ShapeDtypeStruct((rows, pairs * LANES), BF),
            jax.ShapeDtypeStruct((pairs, 8, rows), F32),
        ],
        compiler_params=pltpu.CompilerParams(vmem_limit_bytes=32 * 2**20),
        name="attend",
    )(heads, heads, heads)


def attend_back(heads, grad_blended, log_total):
    rows, width = heads.shape
    pairs = width // LANES // 3
    return pl.pallas_call(
        functools.partial(attend_back_kernel, 512),
        grid=(pairs,),
        in_specs=[kind_spec(rows, kind) for kind in range(3)]
        + [
            pl.BlockSpec((rows, LANES), lambda p: (0, p)),
            pl.BlockSpec((1, 8, rows), lambda p: (p, 0, 0)),
        ],
        out_specs=pl.BlockSpec((rows, 3 * LANES), lambda p: (0, p)),
        out_shape=jax.ShapeDtypeStruct((rows, width), BF),
        scratch_shapes=[pltpu.VMEM((rows, LANES), F32)] * 2,
        compiler_params=pltpu.CompilerParams(vmem_limit_bytes=32 * 2**20),
        name="attend_back",
    )(heads, heads, heads, grad_blended, log_total)


def dot_nn(left, right):
    return lax.dot_general(left, right, (((1,), (0,)), ((), ())), preferred_element_type=F32)


def dot_nt(left, right):
    return lax.dot_general(left, right, (((1,), (1,)), ((), ())), preferred_element_type=F32)


def dot_tn(left, right):
    return lax.dot_general(left, right, (((0,), (0,)), ((), ())), preferred_element_type=F32)


def local_image(
    tokens,
    cotangent,
    qkv_weight,
    qkv_first,
    qkv_second,
    out_weight,
    out_first,
    out_second,
    up_weight,
    up_first,
    up_second,
    down_weight,
    down_first,
    down_second,
    head_biases,
    bias_first,
    bias_second,
    vectors,
    vector_first,
    vector_second,
):
    dp_at = lax.axis_index("dp")
    mp_at = lax.axis_index("mp")
    units = up_weight.shape[1]
    half_units = units // 2
    block_width = qkv_weight.shape[2]
    depth = qkv_weight.shape[1]
    bias_width = head_biases.shape[1]
    chunk_rows, width = tokens.shape[2:]
    order = [((zk * YS) + yk) for yk in range(YS) for zk in range(ZS)]
    place = jnp.stack([dp_at ^ each for each in order] + [mp_at]).astype(jnp.int32)
    cores = (0, 1)

    def fetch_image(array):
        chunks = array[:, 0]

        def chunk(step):
            return lax.dynamic_index_in_dim(chunks, mp_at ^ step, 0, keepdims=False)

        return Chain(image_steps, jnp.stack([chunk(2), chunk(3)]), lambda: chunk(1))

    def send_back(low):
        chunks = low.reshape(MP, chunk_rows, width)
        return Chain(image_steps, chunks[2:], lambda: chunks[1])

    small_shard = jnp.concatenate(
        [vectors.astype(BF).reshape(-1), head_biases.astype(BF).reshape(-1)]
    ).reshape(1, -1)
    vector_size = vectors.size
    kinds = qkv_weight.shape[0]
    qkv_shard = qkv_weight.astype(BF).reshape(kinds, depth, 2, LANES).transpose(1, 2, 0, 3)
    qkv_shard = qkv_shard.reshape(depth, -1)
    up_shard = jnp.concatenate(
        [out_weight.T.astype(BF), up_weight.astype(BF).reshape(depth, -1)], 1
    )
    down_low = down_weight.transpose(2, 0, 1).astype(BF)
    down_shards = [
        down_low[:, at : at + half_units].reshape(depth, -1) for at in (0, half_units)
    ]
    both = ("xy", "yx")
    small = Chain(small_steps, small_shard, vector_size)
    rows_qkv = Chain(rows_z_steps, qkv_shard)
    rows_up = Chain(rows_z_steps, up_shard)
    tokens = meet(tokens, small, rows_qkv)
    fetch_tokens = fetch_image(tokens)
    meet((), small)
    meet((), small, rows_qkv, rows_up)
    part_a, part_b = jnp.split(rows_qkv.result, 2, 1)
    get_qkv = [Chain(gather_steps, [part_a], ("xy",)), Chain(gather_steps, [part_b], ("yx",))]
    meet((), small, get_qkv[1], fetch_tokens)
    tokens = meet(tokens, fetch_tokens, get_qkv[0])

    vector_full, bias_small = small.result
    vector_full = vector_full.reshape(DP, vectors.shape[0], LANES).transpose(1, 0, 2)
    vector_full = vector_full.reshape(vectors.shape[0], width).astype(F32)
    back_places = jnp.stack([((each ^ dp_at) & 1) * ZS + ((each ^ dp_at) >> 1) for each in range(DP)])
    bias_rows = jnp.take(bias_small, back_places, axis=1).reshape(2, 2, DP, -1, bias_width)
    bias_full = bias_rows.transpose(1, 3, 0, 2, 4).reshape(2, head_biases.shape[0], 2, block_width)
    bias_full = bias_full.astype(F32)

    base, normed_one = assemble_image(place, vector_full, tokens[:, 0], fetch_tokens.result, True)
    normed_one = meet(normed_one, *get_qkv, rows_up)
    out_rows, up_rows = jnp.split(rows_up.result, [block_width], 1)
    get_out = Chain(gather_steps, [jnp.stack(jnp.split(out_rows, 2, 1))], ("yx",))
    get_up = Chain(gather_steps, jnp.split(up_rows, 2, 1), both, (1, 2))

    def project(core, half, weight):
        lanes = slice(half * LANES, (half + 1) * LANES)
        zero = jnp.zeros((2, LANES), F32)
        bias = jnp.stack([bias_full[core, 0, :, lanes], zero, bias_full[core, 1, :, lanes]], 1)
        return (dot_nn(normed_one, weight) + bias.reshape(-1)).astype(BF)

    heads, blended, log_total = ([[None, None], [None, None]] for _ in range(3))

    def forward_heads(core, half):
        blended[core][half], log_total[core][half] = attend(heads[core][half])

    heads[0][0] = project(0, 0, get_qkv[0].own[0])
    heads[0][0], down_shards = meet((heads[0][0], down_shards), *get_qkv)
    w_qkv = [[each.own[0] for each in get_qkv], [each.result[0] for each in get_qkv]]
    rows_down = [Chain(rows_z_steps, each) for each in down_shards]
    forward_heads(0, 0)
    blended[0][0], normed_one = meet(
        (blended[0][0], normed_one), get_out, get_up, *rows_down
    )
    heads[0][1] = project(0, 1, w_qkv[0][1])
    forward_heads(0, 1)
    blended[0][1], normed_one = meet(
        (blended[0][1], normed_one), get_up, rows_down[0]
    )
    heads[1][0] = project(1, 0, w_qkv[1][0])
    forward_heads(1, 0)
    blended[1][0], normed_one = meet(
        (blended[1][0], normed_one), get_out, rows_down[1], get_up
    )
    get_down = Chain(gather_steps, [each.result for each in rows_down], both)
    heads[1][1] = project(1, 1, w_qkv[1][1])
    forward_heads(1, 1)
    blended = meet(blended, get_up, get_down, get_out)
    w_out = [[each[0][half] for half in (0, 1)] for each in (get_out.own, get_out.result)]
    pairs = [(core, half) for core in cores for half in (0, 1)]
    branch_one, hidden, normed_two = row_call(
        out_kernel,
        "out_norm",
        [blended[core][half] for core, half in pairs],
        [w_out[core][half] for core, half in pairs],
        vector_full,
        [base],
        [F32, F32, BF],
    )
    activ, slope = ({}, {})

    def expand_units(core, weights):
        for half in (0, 1):
            rows = bias_full[core, 2 + half * half_units : 2 + (half + 1) * half_units]
            unit_bias = rows.transpose(1, 0, 2).reshape(-1)
            activ[half, core], slope[half, core] = expand(normed_two, weights[half], unit_bias)

    w_up = [get_up.own, get_up.result]
    expand_units(0, w_up[0])
    activ, normed_two, cotangent = meet((activ, normed_two, cotangent), get_down)
    fetch_cotangent = fetch_image(cotangent)
    expand_units(1, w_up[1])
    activ = meet(activ, get_down)
    w_down = [get_down.own, get_down.result]
    parts = [(half, core) for core in (1, 0) for half in (0, 1)]
    output, branch_two = row_call(
        down_kernel,
        "down_output",
        [activ[each] for each in parts],
        [w_down[core][half] for half, core in parts],
        vector_full,
        [hidden],
        [BF, F32],
    )
    output = meet(output, fetch_cotangent)
    output, cotangent = meet((output, cotangent), fetch_cotangent)
    grad_out, grad_branch = assemble_image(
        place, vector_full, cotangent[:, 0], fetch_cotangent.result, False
    )

    def reduce_pairs(left, rights, pieces):
        chain = Chain(reduce_steps, [dot_tn(left, rights[half, 1]).astype(BF) for half in (0, 1)], both[::-1], pieces)
        chain.own = [dot_tn(left, rights[half, 0]).astype(BF) for half in (0, 1)]
        return chain

    sum_down = reduce_pairs(grad_branch, activ, (2, 1))
    grad_branch, output, slope = meet((grad_branch, output, slope), sum_down)
    send_output = send_back(output)
    grad_pre, unit_sums = ({}, {})
    for half, core in parts:
        grad_pre[half, core], unit_sums[half, core] = slope_product(
            grad_branch, w_down[core][half], slope[half, core]
        )
        if (half, core) == (0, 0):
            grad_pre, grad_branch = meet((grad_pre, grad_branch), sum_down)
    grad_pre, normed_two = meet((grad_pre, normed_two))
    sum_up = reduce_pairs(normed_two, grad_pre, (1, 1))
    grad_pre = meet(grad_pre, sum_down)
    grad_hidden, grad_projected, sums_one = row_call(
        up_back_kernel,
        "up_norm_back",
        [grad_pre[each] for each in parts],
        [w_up[core][half] for half, core in parts],
        vector_full,
        [hidden, branch_one, grad_out],
        [F32, BF, "sums"],
    )
    grad_projected = meet(grad_projected, sum_up, sum_down, send_output)
    rows_down = Chain(sum_z_halves_steps, jnp.concatenate(sum_down.result, 1))
    grad_w_out = [
        jnp.stack([dot_tn(grad_projected, each).astype(BF) for each in blended[core]]) for core in cores
    ]
    sum_out = Chain(reduce_steps, [grad_w_out[1]], ("xy",))
    sum_out.own = [grad_w_out[0]]
    grad_blended = [[dot_nn(grad_projected, each).astype(BF) for each in w_out[core]] for core in cores]
    grad_heads = [[None, None], [None, None]]

    def back_heads(core, half):
        grad_heads[core][half] = attend_back(
            heads[core][half], grad_blended[core][half], log_total[core][half]
        )
        return dot_tn(normed_one, grad_heads[core][half]).astype(BF)

    other = back_heads(1, 0)
    other, grad_blended = meet((other, grad_blended), sum_up, sum_out, rows_down, send_output)
    sum_qkv = [Chain(reduce_steps, [other], ("xy",)), None]
    sum_qkv[0].own = [back_heads(0, 0)]
    grad_heads[0][0], grad_blended = meet(
        (grad_heads[0][0], grad_blended), sum_qkv[0], sum_out, sum_up, rows_down
    )
    rows_up = Chain(sum_z_halves_steps, jnp.concatenate(sum_up.result, 1))
    other = back_heads(1, 1)
    other, grad_blended = meet((other, grad_blended), sum_out, sum_qkv[0])
    sum_qkv[1] = Chain(reduce_steps, [other], ("yx",))
    out_rows = jnp.concatenate([sum_out.result[0][0], sum_out.result[0][1]], 1)
    sum_qkv[1].own = [back_heads(0, 1)]
    grad_heads = meet(grad_heads, sum_qkv[0], sum_qkv[1], rows_up)

    def input_back(span, outs):
        return row_call(
            in_back_kernel,
            "in_norm_back",
            [grad_heads[core][half] for core, half in pairs],
            [w_qkv[core][half] for core, half in pairs],
            vector_full,
            [base, grad_hidden],
            outs,
            span,
            chunk_rows,
        )

    grad_far, sums_far = input_back((1, 1), [BF, "sums"])
    grad_near = []
    send_grad = Chain(
        image_steps, grad_far.reshape(2, chunk_rows, width), lambda: grad_near[0][chunk_rows:]
    )
    grad_heads = meet(grad_heads, sum_qkv[1])
    near, sums_near, own_grad = input_back((0, 1), [BF, "sums", "own"])
    grad_near.append(near)
    sums_near, own_grad = meet((sums_near, own_grad), sum_qkv[1], send_grad)
    sums_input = sums_far + sums_near

    grad_vectors = jnp.stack(
        [
            sums_input[0],
            sums_input[1],
            sums_one[3] * vector_full[SCALE_ONE],
            sums_one[2],
            sums_one[0],
            sums_one[1],
            jnp.sum(grad_out.astype(F32), 0) * vector_full[SCALE_TWO],
            jnp.sum(grad_out.astype(F32) * branch_two, 0),
        ]
    )
    grad_vectors = grad_vectors.reshape(-1, DP, LANES).transpose(1, 0, 2).reshape(DP, -1)
    bias_parts = []
    for core in cores:
        head_part = [
            jnp.sum(each.astype(F32), 0).reshape(2, kinds, LANES) for each in grad_heads[core]
        ]
        rows = [jnp.concatenate([each[:, kind] for each in head_part], 1) for kind in (0, 2)]
        for half in (0, 1):
            unit_part = unit_sums[half, core][0].reshape(2, half_units, block_width)
            rows += [unit_part[:, at] for at in range(half_units)]
        bias_parts.append(jnp.stack(rows, 1))
    grad_biases = jnp.stack(bias_parts, 1).reshape(MP, -1, DP, bias_width).transpose(0, 2, 1, 3)
    grad_biases = jnp.take(grad_biases, place[:DP], axis=1).reshape(MP, DP, -1)
    sum_small = Chain(small_reduce_steps, grad_vectors, grad_biases)
    rows_qkv = Chain(sum_z_steps, jnp.concatenate(sum_qkv[0].result + sum_qkv[1].result + [out_rows], 1))
    meet((), rows_up)
    meet((), send_grad)
    meet((), rows_qkv)
    for _ in range(4):
        meet((), sum_small)
    layer_output = spread_image(place, output[:chunk_rows], send_output.result, BF)[:, None]
    input_grad = spread_image(place, own_grad, send_grad.result, F32)[:, None]

    small_total = sum_small.result
    vector_grad = small_total[:vector_size].reshape(vectors.shape)
    bias_grad = small_total[vector_size:].reshape(head_biases.shape)
    qkv_size = kinds * block_width
    qkv_grad = rows_qkv.result[:, :qkv_size].reshape(depth, 2, kinds, LANES).transpose(2, 0, 1, 3)
    grads = (
        qkv_grad.reshape(qkv_weight.shape),
        rows_qkv.result[:, qkv_size:].T,
        rows_up.result.reshape(depth, units, block_width),
        rows_down.result.reshape(depth, units, block_width).transpose(1, 2, 0),
        bias_grad,
        vector_grad,
    )
    params = (qkv_weight, out_weight, up_weight, down_weight, head_biases, vectors)
    firsts = (qkv_first, out_first, up_first, down_first, bias_first, vector_first)
    seconds = (qkv_second, out_second, up_second, down_second, bias_second, vector_second)
    results = [layer_output, input_grad]
    for slot in range(6):
        results.extend(
            adam_update(params[slot], firsts[slot], seconds[slot], grads[slot], RATES[slot])
        )
    return tuple(results)


def solution(mesh):
    whole_image = mesh.shape["mp"] == MICRO == MP and mesh.shape["dp"] == DP
    return jax.shard_map(
        local_image if whole_image else local_general,
        mesh=mesh,
        in_specs=(
            P(None, "dp", "mp", None),
            P(None, "dp", "mp", None),
            P(None, "dp", "mp"),
            P(None, "dp", "mp"),
            P(None, "dp", "mp"),
            P("mp", "dp"),
            P("mp", "dp"),
            P("mp", "dp"),
            P("dp", None, "mp"),
            P("dp", None, "mp"),
            P("dp", None, "mp"),
            P(None, "mp", "dp"),
            P(None, "mp", "dp"),
            P(None, "mp", "dp"),
            P(None, ("mp", "dp")),
            P(None, ("mp", "dp")),
            P(None, ("mp", "dp")),
            P(None, "dp"),
            P(None, "dp"),
            P(None, "dp"),
        ),
        out_specs=(
            P(None, "dp", "mp", None),
            P(None, "dp", "mp", None),
            P(None, "dp", "mp"),
            P(None, "dp", "mp"),
            P(None, "dp", "mp"),
            P("mp", "dp"),
            P("mp", "dp"),
            P("mp", "dp"),
            P("dp", None, "mp"),
            P("dp", None, "mp"),
            P("dp", None, "mp"),
            P(None, "mp", "dp"),
            P(None, "mp", "dp"),
            P(None, "mp", "dp"),
            P(None, ("mp", "dp")),
            P(None, ("mp", "dp")),
            P(None, ("mp", "dp")),
            P(None, "dp"),
            P(None, "dp"),
            P(None, "dp"),
        ),
        check_vma=False,
    )
```
